32 devices in a mesh: tile: 4 (over z), chan: 8 (over y, x, core).
Axes of the slice: x: 2, y: 2, z: 4, core: 2. Of those that a mesh axis runs over, the one named last changes fastest.
Arguments:
- fields: float32 [32, 128, 411], P('chan', 'tile'), may hold values from -12 to 12
- diffusivity: float32 [32, 128], P('chan', 'tile'), may hold values from 0.02 to 0.24
- owners: int32 [256, 1], replicated, may hold values from 0 to 3; in each aligned block of 64 rows (0 to 63, 64 to 127, ...) at most 32 rows name the same one
- observed: bfloat16 [512, 6144], P('tile', 'chan'), may hold values from -6 to 6
- usable: int32 [512], P('tile'), may hold values 0 or 1
- w_hidden: bfloat16 [411, 2048], P(None, 'chan'), may hold values from -0.3125 to 0.3125
- b_hidden: float32 [2048], P('chan'), may hold values from -3 to 3
- w_radiance: bfloat16 [2048, 6144], P(None, 'chan'), may hold values from -0.125 to 0.125
- b_radiance: float32 [6144], P('chan'), may hold values from -3 to 3
- inv_cov: bfloat16 [6144, 6144], P('tile', 'chan'), may hold values from -6 to 22
Outputs:
- gradient: float32 [32, 128, 411], P('chan', 'tile')
The draws below stay inside these ranges and needn't reach their ends.
Inputs may be any that keep to these rules, and one draw needn't show every extreme that they name: `owners`: in each tile's block of 64 consecutive entries no owner appears more than 32 times, and in some blocks one appears exactly 32 times.
All inputs are finite; a program needn't handle non-finite values. No bound on the sum of `usable` on one device may be relied on, other than what follows from the above.
Results may differ from the reference program's by a relative error of at most 0.0045.
Values may be sent and summed in bfloat16 or wider, within the bound.
No kernel may reach another device: no remote copies, remote signals or barrier semaphores. Data moves between devices by JAX's collectives and lax.ppermute only.
A program may use at most 64 MiB of HBM per device.

```python
import math
import jax
import jax.numpy as jnp
import numpy as np
from jax import lax

FEAT = 411
HID = 2048
NCH = 6144
NX = 32
NY = 128
SRC_COLS = 8
COLS = 256
CAPACITY = 32
SLOTS = 128
PROFILES = 512
N_TILE = 4
N_CHAN = 8


def draw_inv_cov(key, part):
    first, second = jax.random.split(key)
    entries = jax.random.truncated_normal(first, -4.0, 4.0, (NCH, NCH), jnp.float32)
    coupling = (entries + entries.T) * (0.45 / math.sqrt(2.0 * NCH))
    scales = jnp.exp(jax.random.uniform(second, (NCH,), jnp.float32, 0.0, math.log(16.0)) * 0.5)
    matrix = scales[:, None] * (jnp.eye(NCH, dtype=jnp.float32) + coupling) * scales[None, :]
    return matrix.astype(jnp.bfloat16)


def place_ends(values, own_key, low, largest):
    extent = values.shape
    index_at = [jax.random.randint(jax.random.fold_in(own_key, axis), (), 0, extent[axis]) for axis in range(len(extent))]
    values = values.at[tuple(index_at)].set(low)
    longest = extent.index(max(extent))
    index_at[longest] = (index_at[longest] + 1) % extent[longest]
    return values.at[tuple(index_at)].set(largest)


def levels(stream_key, shape, shards, smallest, high):
    loudness, own = 1.0, jax.random.fold_in(stream_key, 6)
    for position, shards_of in shards:
        steps = jnp.exp(jax.random.uniform(jax.random.fold_in(own, position), (shards_of,), jnp.float32, smallest / len(shards), high / len(shards)))
        loudness = loudness * jnp.repeat(steps, shape[position] // shards_of).reshape([-1 if axis == position else 1 for axis in range(len(shape))])
    return loudness


def assign_block(rng, own, number, rows, number_of, top, limit, slope):
    sequence = jax.random.permutation(rng, number_of)
    crowded, common = portions_of(number_of, rows * top, limit, slope, True), portions_of(number_of, rows * top, limit, slope, False)
    places = jnp.arange(number_of)

    def named(lengths, rotation):
        used = int((lengths > 0).sum())
        fixed = max(1, used // 4)
        passed = fixed + (places - fixed + rotation * (used - fixed)) % max(1, number_of - fixed)
        return jnp.zeros((number_of,), jnp.int32).at[sequence[jnp.where(places < fixed, places, passed)]].set(jnp.asarray(lengths, jnp.int32))

    lengths = jnp.where(number % 4 == 0, named(crowded, number // 4), named(common, number - number // 4 - 1))
    mixed = jax.random.permutation(jax.random.fold_in(own, 3), number_of)
    source_of, sink = mixed[0:number_of // 2 * 2:2], mixed[1:number_of // 2 * 2:2]
    room = jnp.minimum(lengths[source_of] - 1, limit - lengths[sink]) // 2
    room = jnp.where((source_of == sequence[0]) | (sink == sequence[0]) | (lengths[sink] == 0), 0, jnp.maximum(room, 0))
    passed = jax.random.randint(jax.random.fold_in(own, 4), (number_of // 2,), 0, 1 << 20) % (room + 1)
    lengths = lengths.at[source_of].add(-passed).at[sink].add(passed)
    items = jnp.searchsorted(jnp.cumsum(lengths), jnp.arange(rows * top), side="right").astype(jnp.int32)
    listing = items.reshape(top, rows).T
    listing = listing[jax.random.permutation(jax.random.fold_in(own, 1), rows)]
    rotation = jax.random.randint(jax.random.fold_in(own, 2), (rows, 1), 0, top)
    return jnp.take_along_axis(listing, (jnp.arange(top)[None, :] + rotation) % top, axis=1)


def portions_of(number_of, total, reach, lean, full):
    loads = [(1 << 20) // math.isqrt(grade ** lean) + 1 for grade in range(1, number_of + 1)]
    largest = reach if full else min(reach, max(-(-total // number_of), total * loads[0] // sum(loads)))
    least = 1 if total - largest >= number_of - 1 else 0
    given, surplus = [largest] + [least] * (number_of - 1), total - largest - least * (number_of - 1)
    while surplus > 0:
        free = [i for i in range(1, number_of) if given[i] < largest] or [i for i in range(1, number_of) if given[i] < reach]
        whole, budget = sum([loads[i] for i in free]), surplus
        for i in free:
            more = min(reach - given[i], max(1, budget * loads[i] // whole), surplus)
            given[i] = given[i] + more
            surplus = surplus - more
    return np.array(given)


def gaussian(stream_key, extent, scale, bound, cuts=(), kind=jnp.bfloat16):
    values = scale * jax.random.normal(stream_key, extent, jnp.float32)
    if cuts:
        values = values * levels(stream_key, extent, cuts, -0.22, 0.18)
    return jnp.clip(values, -bound, bound).astype(kind)


def setup_inputs(seed: int = 0) -> dict:
    seeds = jax.random.split(jax.random.key(seed), 11)
    fields = gaussian(seeds[0], (NX, NY, FEAT), 2.0, 12.0, ((0, 8), (1, 4)), jnp.float32)
    diffusivity = jnp.clip(jnp.exp(math.log(0.24) - 2.4849066 * jax.random.uniform(seeds[1], (NX, NY), jnp.float32) ** levels(seeds[1], (NX, NY), ((0, 8), (1, 4)), -0.2, 0.2)), 0.02, 0.24)
    owners_keys = jax.random.split(jax.random.fold_in(seeds[2], 1), COLS // (N_CHAN * SRC_COLS))
    owners_turns = jax.random.permutation(jax.random.fold_in(seeds[2], 3), COLS // (N_CHAN * SRC_COLS))
    owners = jax.vmap(lambda own, number: assign_block(jax.random.fold_in(seeds[2], 2), own, number, N_CHAN * SRC_COLS, N_TILE, 1, CAPACITY, 2))(owners_keys, owners_turns).reshape((COLS, 1))
    observed = gaussian(seeds[3], (PROFILES, NCH), 1.0, 6.0, ((0, 4), (1, 8)))
    usable = place_ends((jax.random.randint(seeds[4], (PROFILES,), 0, 4) < 3).astype(jnp.int32), jax.random.fold_in(seeds[4], 1), 0, 1)
    w_hidden = gaussian(seeds[5], (FEAT, HID), FEAT ** -0.5, 0.3125, ((1, 8),))
    b_hidden = gaussian(seeds[6], (HID,), 0.5, 3.0, ((0, 8),), jnp.float32)
    w_radiance = gaussian(seeds[7], (HID, NCH), HID ** -0.5, 0.125, ((1, 8),))
    b_radiance = gaussian(seeds[8], (NCH,), 0.5, 3.0, ((0, 8),), jnp.float32)
    inv_cov = draw_inv_cov(jax.random.fold_in(seeds[10], 71), 0)
    return {"fields": fields, "diffusivity": diffusivity, "owners": owners, "observed": observed, "usable": usable, "w_hidden": w_hidden, "b_hidden": b_hidden, "w_radiance": w_radiance, "b_radiance": b_radiance, "inv_cov": inv_cov}


def diffuse(adjoint, kappa_root):
    root_pad = jnp.pad(kappa_root, ((1, 1), (0, 0)))
    coef_north = (kappa_root * root_pad[2:])[:, :, None]
    coef_south = (kappa_root * root_pad[:-2])[:, :, None]
    coef_east = (kappa_root * jnp.roll(kappa_root, -1, axis=1))[:, :, None]
    coef_west = (kappa_root * jnp.roll(kappa_root, 1, axis=1))[:, :, None]
    for sweep_index in range(2):
        padded = jnp.pad(adjoint, ((1, 1), (0, 0), (0, 0)))
        adjoint = adjoint + coef_north * (padded[2:] - adjoint) + coef_south * (padded[:-2] - adjoint) + coef_east * (jnp.roll(adjoint, -1, axis=1) - adjoint) + coef_west * (jnp.roll(adjoint, 1, axis=1) - adjoint)
    return adjoint

def reference(fields, diffusivity, owners, observed, usable, w_hidden, b_hidden, w_radiance, b_radiance, inv_cov):
    tile_cols = N_CHAN * SRC_COLS
    grouped = fields.reshape(N_CHAN, 4, N_TILE * SRC_COLS, 4, FEAT)
    averaged = lax.optimization_barrier(jnp.sum(grouped, axis=(1, 3))) * 0.0625
    ordered = averaged.reshape(N_CHAN, N_TILE, SRC_COLS, FEAT).transpose(1, 0, 2, 3).reshape(COLS, FEAT)
    ordered = ordered.astype(jnp.bfloat16)
    owner_table = owners[:, 0].reshape(N_TILE, tile_cols)
    owner_hits = (owner_table[:, :, None] == jnp.arange(N_TILE, dtype=jnp.int32)[None, None, :]).astype(jnp.int32)
    before = lax.optimization_barrier(jnp.sum((jnp.cumsum(owner_hits, axis=1) - owner_hits) * owner_hits, axis=2))
    tallies = lax.optimization_barrier(jnp.sum(owner_hits, axis=1))
    source_tile = jnp.arange(N_TILE, dtype=jnp.int32)[:, None]
    slot_index = (owner_table * SLOTS + source_tile * CAPACITY + before).reshape(COLS).astype(jnp.int32)
    stacked = jnp.zeros((PROFILES, FEAT), jnp.bfloat16).at[slot_index].set(ordered)
    occupied = (jnp.arange(CAPACITY, dtype=jnp.int32)[None, None, :] < tallies.T[:, :, None]).reshape(PROFILES)
    in_use = usable.astype(jnp.float32) * occupied.astype(jnp.float32)
    preact = jnp.dot(stacked, w_hidden, preferred_element_type=jnp.float32) + b_hidden[None, :]
    squash = jax.nn.sigmoid(preact)
    active = (preact * squash).astype(jnp.bfloat16)
    radiance = jnp.dot(active, w_radiance, preferred_element_type=jnp.float32) + b_radiance[None, :]
    departure = ((radiance - observed.astype(jnp.float32)) * in_use[:, None]).astype(jnp.bfloat16)
    cotangent = jnp.dot(departure, inv_cov, preferred_element_type=jnp.float32).astype(jnp.bfloat16)
    grad_hidden = jnp.dot(cotangent, w_radiance.T, preferred_element_type=jnp.float32)
    slope_term = squash * (1.0 + preact * (1.0 - squash))
    grad_pre = (grad_hidden * slope_term).astype(jnp.bfloat16)
    profile_grad = jnp.dot(grad_pre, w_hidden.T, preferred_element_type=jnp.float32)
    column_grad = profile_grad[slot_index]
    column_grad = column_grad.reshape(N_TILE, N_CHAN, SRC_COLS, FEAT).transpose(1, 0, 2, 3)
    column_grad = column_grad.reshape(N_CHAN, N_TILE * SRC_COLS, FEAT)
    spread = jnp.repeat(jnp.repeat(column_grad, 4, axis=0), 4, axis=1) * 0.0625
    return diffuse(spread, jnp.sqrt(diffusivity))
```

```python
import functools

import jax
import jax.numpy as jnp
import numpy as np
from jax import lax
from jax.experimental import pallas as pl
from jax.experimental.pallas import tpu as pltpu
from jax.sharding import PartitionSpec as P

VMEM_BYTES = 40 * 1024 * 1024
NT_DIMS = (((1,), (1,)), ((), ()))


def padded_2(value, sides, width, wrap):
    for axis, dim in sides:
        devices, length = (lax.axis_size(axis), value.shape[dim])
        up = [(i, (i + 1) % devices) for i in range(devices if wrap else devices - 1)]
        down = [(j, i) for i, j in up]
        last = lax.slice_in_dim(value, length - width, length, axis=dim)
        first = lax.slice_in_dim(value, 0, width, axis=dim)
        before = lax.ppermute(last, axis, up)
        after = lax.ppermute(first, axis, down)
        value = jnp.concatenate([before, value, after], axis=dim)
    return value


def add_rims(values):
    rowwise = padded_2(values, (("chan", 0),), 1, False)
    return padded_2(rowwise, (("tile", 1),), 1, True)


def body_by_owner(
    fields,
    diffusivity,
    owners,
    observed,
    usable,
    w_hidden,
    b_hidden,
    w_radiance,
    b_radiance,
    inv_cov,
):
    tile_count = lax.axis_size("tile")
    chan_count = lax.axis_size("chan")
    tile_index = lax.axis_index("tile")
    chan_index = lax.axis_index("chan")
    slot_count = observed.shape[0]
    capacity = slot_count // tile_count
    cells_across, cells_along, features = fields.shape
    own_cols = cells_across // 4 * (cells_along // 4)
    tile_cols = chan_count * own_cols
    hidden_dev = w_hidden.shape[1]
    owner_table = owners[:, 0].reshape(tile_count, tile_cols)
    owner_hits = (
        owner_table[:, :, None] == jnp.arange(tile_count, dtype=jnp.int32)[None, None, :]
    ).astype(jnp.int32)
    before = jnp.sum((jnp.cumsum(owner_hits, axis=1) - owner_hits) * owner_hits, axis=2)
    tallies = jnp.sum(owner_hits, axis=1)
    slot_of = lax.dynamic_index_in_dim(
        owner_table * capacity + before, tile_index, 0, keepdims=False
    )
    arriving = lax.dynamic_index_in_dim(tallies, tile_index, 1, keepdims=False)
    occupied = (jnp.arange(capacity, dtype=jnp.int32)[None, :] < arriving[:, None]).reshape(
        slot_count
    )
    grouped = fields.reshape(cells_across // 4, 4, cells_along // 4, 4, features)
    columns = (
        (jnp.sum(grouped, axis=(1, 3)) * 0.0625).reshape(own_cols, features).astype(jnp.bfloat16)
    )
    placer = (slot_of[None, :] == jnp.arange(slot_count, dtype=jnp.int32)[:, None]).astype(
        jnp.bfloat16
    )
    outgoing = jnp.dot(
        placer,
        lax.all_gather(columns, "chan", axis=0, tiled=True),
        preferred_element_type=jnp.float32,
    )
    incoming = lax.all_to_all(
        outgoing.astype(jnp.bfloat16), "tile", split_axis=0, concat_axis=0, tiled=True
    )
    preact = lax.dot_general(
        w_hidden, incoming, (((0,), (1,)), ((), ())), preferred_element_type=jnp.float32
    )
    preact = preact + b_hidden[:, None]
    squash = jax.nn.sigmoid(preact)
    active = (preact * squash).astype(jnp.bfloat16)
    radiance = lax.dot_general(
        lax.all_gather(active, "chan", axis=0, tiled=True),
        w_radiance,
        (((0,), (0,)), ((), ())),
        preferred_element_type=jnp.float32,
    )
    radiance = radiance + b_radiance[None, :]
    in_use = usable.astype(jnp.float32) * occupied.astype(jnp.float32)
    departure = ((radiance - observed.astype(jnp.float32)) * in_use[:, None]).astype(jnp.bfloat16)
    cotangent = jnp.dot(
        lax.all_gather(departure, "chan", axis=1, tiled=True),
        lax.all_gather(inv_cov, "tile", axis=0, tiled=True),
        preferred_element_type=jnp.float32,
    )
    cotangent = cotangent.astype(jnp.bfloat16)
    full_sum = lax.psum(
        lax.dot_general(w_radiance, cotangent, NT_DIMS, preferred_element_type=jnp.float32),
        "chan",
    )
    grad_hidden = lax.dynamic_slice_in_dim(full_sum, chan_index * hidden_dev, hidden_dev, 0)
    slope_term = squash * (1.0 + preact * (1.0 - squash))
    grad_pre = (grad_hidden * slope_term).astype(jnp.bfloat16)
    part_grad = lax.dot_general(
        grad_pre, w_hidden, (((0,), (1,)), ((), ())), preferred_element_type=jnp.float32
    )
    returned = lax.all_to_all(part_grad, "tile", split_axis=0, concat_axis=0, tiled=True)
    column_grad = lax.psum_scatter(
        jnp.take(returned, slot_of, axis=0), "chan", scatter_dimension=0, tiled=True
    )
    spread = jnp.repeat(
        column_grad.reshape(cells_across // 4, cells_along // 4, features), 4, axis=0
    )
    adjoint = jnp.repeat(spread, 4, axis=1) * 0.0625
    kappa_root = jnp.sqrt(diffusivity)
    root_rim = add_rims(kappa_root)
    coef_north = (kappa_root * root_rim[2:, 1:-1])[:, :, None]
    coef_south = (kappa_root * root_rim[:-2, 1:-1])[:, :, None]
    coef_east = (kappa_root * root_rim[1:-1, 2:])[:, :, None]
    coef_west = (kappa_root * root_rim[1:-1, :-2])[:, :, None]
    for sweep_index in range(2):
        padded = add_rims(adjoint)
        adjoint = (
            adjoint
            + coef_north * (padded[2:, 1:-1] - adjoint)
            + coef_south * (padded[:-2, 1:-1] - adjoint)
            + coef_east * (padded[1:-1, 2:] - adjoint)
            + coef_west * (padded[1:-1, :-2] - adjoint)
        )
    return adjoint


def up_to(value, multiple):
    return -(-value // multiple) * multiple


def in_three(value):
    high = lax.reduce_precision(value, 8, 7)
    middle = lax.reduce_precision(value - high, 8, 7)
    low = lax.reduce_precision(value - high - middle, 8, 7)
    return [part.astype(jnp.bfloat16) for part in (high, middle, low)]


def as_rows(flat, width):
    length = up_to(flat.shape[0], width)
    return jnp.pad(flat, (0, length - flat.shape[0])).reshape(-1, width)


def flip(value, mask):
    count = lax.axis_size("chan")
    return lax.ppermute(value, "chan", [(i, i ^ mask) for i in range(count)])


def dot(left, right):
    return jnp.dot(left, right, preferred_element_type=jnp.float32)


def call(kernel, out_shape, args, scalars, scratch=(), flops=0):
    bytes_accessed = sum(a.size * a.dtype.itemsize for a in args)
    return pl.pallas_call(
        kernel,
        out_shape=out_shape,
        in_specs=[pl.BlockSpec(memory_space=pltpu.SMEM)] * scalars
        + [pl.BlockSpec(memory_space=pltpu.VMEM)] * (len(args) - scalars),
        out_specs=jax.tree.map(lambda _: pl.BlockSpec(memory_space=pltpu.VMEM), out_shape),
        scratch_shapes=list(scratch),
        compiler_params=pltpu.CompilerParams(vmem_limit_bytes=VMEM_BYTES),
        cost_estimate=pl.CostEstimate(
            flops=flops, bytes_accessed=bytes_accessed, transcendentals=0
        ),
    )(*args)


def forward_kernel(
    tiles, group, block, own_cols, order_ref, gathered_ref, spot_ref, place_ref, usable_ref, bias_ref,
    w_radiance_ref, *rest,
):
    observed_refs = rest[:tiles]
    near_refs = rest[tiles:-4]
    far_ref, departure_ref, slope_ref, active_ref = rest[-4:]
    rows = spot_ref.shape[0]
    chips = len(near_refs)
    hidden = near_refs[0].shape[1]
    slots = observed_refs[0].shape[0]
    row = lax.broadcasted_iota(jnp.int32, (rows, gathered_ref.shape[0]), 0)
    source = lax.broadcasted_iota(jnp.int32, (rows, gathered_ref.shape[0]), 1)
    pick = (source == row // own_cols * block + row % own_cols).astype(jnp.bfloat16)
    columns = dot(pick, gathered_ref[...]).astype(jnp.bfloat16)
    for chip in range(chips):
        for member in range(group):
            k = chip * group + member
            weights = near_refs[chip][...] if member == 0 else far_ref[member - 1, chip]
            preact = dot(columns, weights)
            squash = jax.nn.sigmoid(preact)
            slope_ref[k] = squash * (1.0 + preact * (1.0 - squash))
            at = pl.multiple_of(order_ref[k] * hidden, hidden)
            active_ref[:, pl.ds(at, hidden)] = (preact * squash).astype(jnp.bfloat16)
    slot = lax.broadcasted_iota(jnp.int32, (rows, slots), 1)
    in_use = jnp.zeros((rows, 1), jnp.float32)
    seen = jnp.zeros(departure_ref.shape, jnp.float32)
    for k in range(tiles):
        hit = spot_ref[...] == slot + k * slots
        in_use = in_use + jnp.sum(
            jnp.where(hit, usable_ref[k : k + 1, :], 0.0), axis=1, keepdims=True
        )
        hit = place_ref[...] == slot + k * slots
        seen = seen + dot(hit.astype(jnp.bfloat16), observed_refs[k][...])
    radiance = dot(active_ref[...], w_radiance_ref[...]) + bias_ref[...]
    departure_ref[...] = ((radiance - seen) * in_use).astype(jnp.bfloat16)


def backward_kernel(
    tiles, group, own_cols, steps, order_ref, at_ref, inv_cov_ref, w_radiance_ref, slope_ref, *rest
):
    chan_width = w_radiance_ref.shape[1]
    own_refs, other_ref = rest[: steps], rest[steps]
    near_refs = rest[steps + 1 : -3]
    far_ref, out_ref, pre_ref = rest[-3:]
    chips = len(near_refs)
    hidden = near_refs[0].shape[1]
    own = jnp.concatenate([r[...] for r in own_refs], axis=0)
    rows = own.shape[0]
    at = pl.multiple_of(at_ref[0] * chan_width, chan_width)
    cotangent = dot(own, inv_cov_ref[pl.ds(at, chan_width), :])
    for member in range(1, group):
        at = pl.multiple_of(at_ref[member] * chan_width, chan_width)
        cotangent = cotangent + dot(other_ref[member - 1], inv_cov_ref[pl.ds(at, chan_width), :])
    cotangent = cotangent.astype(jnp.bfloat16)
    total = jnp.zeros((rows, near_refs[0].shape[0]), jnp.float32)
    for chip in range(chips):
        for member in range(group):
            k = chip * group + member
            at = pl.multiple_of(order_ref[k] * hidden, hidden)
            grad_hidden = lax.dot_general(
                cotangent,
                w_radiance_ref[pl.ds(at, hidden), :],
                NT_DIMS,
                preferred_element_type=jnp.float32,
            )
            grad_pre = (grad_hidden * slope_ref[k]).astype(jnp.bfloat16)
            weights = near_refs[chip][...] if member == 0 else far_ref[member - 1, chip]
            total = total + lax.dot_general(
                grad_pre, weights, NT_DIMS, preferred_element_type=jnp.float32
            )
    wide = out_ref.shape[0] // tiles
    per_row = wide // (rows // tiles // own_cols)
    target = lax.broadcasted_iota(jnp.int32, (out_ref.shape[0], rows), 0)
    source = lax.broadcasted_iota(jnp.int32, (out_ref.shape[0], rows), 1)
    tile, inner = target // wide, target % wide
    row, along = inner // per_row, inner % per_row - 1 + own_cols
    tile = (tile + along // own_cols - 1 + tiles) % tiles
    wanted = tile * (rows // tiles) + row * own_cols + along % own_cols
    pick = (source == wanted).astype(jnp.bfloat16)
    out_ref[...] = dot(pick, total.astype(jnp.bfloat16)).astype(jnp.bfloat16)


def middle_kernel(chans, per_row, in_ref, out_ref):
    total = in_ref[0].astype(jnp.float32)
    for k in range(1, in_ref.shape[0]):
        total = total + in_ref[k].astype(jnp.float32)
    shape = (out_ref.shape[0], total.shape[0])
    block = out_ref.shape[0] // chans
    target = lax.broadcasted_iota(jnp.int32, shape, 0)
    source = lax.broadcasted_iota(jnp.int32, shape, 1)
    chan, inner = target // block, target % block
    wanted = (chan + inner // per_row - 1) * per_row + inner % per_row
    pick = (source == wanted) & (inner < 3 * per_row)
    out_ref[...] = dot(pick.astype(jnp.bfloat16), total.astype(jnp.bfloat16)).astype(jnp.bfloat16)


def diffuse_kernel(per_row, edge, in_ref, root_ref, out_ref):
    total = in_ref[0].astype(jnp.float32)
    for k in range(1, in_ref.shape[0]):
        total = total + in_ref[k].astype(jnp.float32)
    cells_across, cells_along, features = out_ref.shape
    length = cells_along + 2 * edge
    total = total * 0.0625
    shape = (length, total.shape[0])
    cell = lax.broadcasted_iota(jnp.int32, shape, 0)
    source = lax.broadcasted_iota(jnp.int32, shape, 1)
    column = (cell - edge + 4) // 4
    spread = []
    for k in range(3):
        pick = (source == column + k * per_row) & (column >= 0) & (column < per_row)
        spread.append(
            jnp.dot(
                pick.astype(jnp.float32),
                total,
                precision=lax.Precision.HIGHEST,
                preferred_element_type=jnp.float32,
            )
        )
    root = root_ref[...]
    state = [spread[(row + 2) // 4] for row in range(cells_across + 4)]
    east_of = functools.partial(pltpu.roll, shift=length - 1, axis=0)
    west_of = functools.partial(pltpu.roll, shift=1, axis=0)
    root_east, root_west = east_of(root), west_of(root)
    north = root[:, :-1] * root[:, 1:]
    east, west = root * root_east, root * root_west
    for sweep in range(2):
        fresh = list(state)
        for row in range(1 + sweep, cells_across + 3 - sweep):
            here = state[row]
            fresh[row] = (
                here
                + north[:, row : row + 1] * (state[row + 1] - here)
                + north[:, row - 1 : row] * (state[row - 1] - here)
                + east[:, row : row + 1] * (east_of(here) - here)
                + west[:, row : row + 1] * (west_of(here) - here)
            )
        state = fresh
    for row in range(cells_across):
        out_ref[row] = state[row + 2][edge : edge + cells_along, :features]


def body_by_column(
    fields,
    diffusivity,
    owners,
    observed,
    usable,
    w_hidden,
    b_hidden,
    w_radiance,
    b_radiance,
    inv_cov,
):
    tiles = lax.axis_size("tile")
    chans = lax.axis_size("chan")
    t = lax.axis_index("tile")
    c = lax.axis_index("chan")
    slots = observed.shape[0]
    capacity = slots // tiles
    cells_across, cells_along, features = fields.shape
    own_cols = cells_across // 4 * (cells_along // 4)
    hidden = w_hidden.shape[1]
    rows = owners.shape[0]
    tile_cols = rows // tiles
    group = chans // tiles
    chips = chans // group
    steps = chips.bit_length() - 1
    width = up_to(features + 3, 16)
    both = ("tile", "chan")

    w_own = jnp.concatenate(
        [w_hidden]
        + [part[None, :] for part in in_three(b_hidden)]
        + [jnp.zeros((width - features - 3, hidden), jnp.bfloat16)],
        axis=0,
    )
    near = [w_own] + [flip(w_own, k * group) for k in range(1, chips)]

    seen = [observed]
    for k in range(1, tiles):
        pairs = [
            ((j // group + k) % tiles * chans + j, j // group * chans + j) for j in range(chans)
        ]
        seen.append(lax.ppermute(observed, both, pairs))

    grouped = fields.reshape(cells_across // 4, 4, cells_along // 4, 4, features)
    averaged = (jnp.sum(grouped, axis=(1, 3)) * 0.0625).reshape(own_cols, features)
    columns = jnp.concatenate(
        [
            averaged.astype(jnp.bfloat16),
            jnp.ones((own_cols, 3), jnp.bfloat16),
            jnp.zeros((own_cols, width - features - 3), jnp.bfloat16),
        ],
        axis=1,
    )
    cells = as_rows(jnp.concatenate(in_three(diffusivity.reshape(-1))), width)
    flags = as_rows(usable.astype(jnp.bfloat16), width)
    block = up_to(own_cols + cells.shape[0] + flags.shape[0], 16)
    packed = jnp.concatenate([columns, cells, flags], axis=0)
    packed = jnp.pad(packed, ((0, block - packed.shape[0]), (0, 0)))
    gathered = lax.all_gather(packed, both, axis=0, tiled=True)

    stack = jnp.stack(near)
    far = jnp.stack([flip(stack, k) for k in range(1, group)])

    owner = owners[:, 0]
    number = jnp.arange(rows, dtype=jnp.int32)
    same = (
        (owner[:, None] == owner[None, :])
        & (number[:, None] // tile_cols == number[None, :] // tile_cols)
        & (number[None, :] < number[:, None])
    )
    rank = jnp.sum(same.astype(jnp.int32), axis=1, keepdims=True)
    within = number[:, None] // tile_cols * capacity + rank
    spot = owners * slots + within
    place = (owners + tiles - t) % tiles * slots + within
    order = jnp.bitwise_xor(jnp.arange(chans, dtype=jnp.int32), c)

    by_device = gathered.reshape(tiles, chans, block, width)
    low = own_cols + cells.shape[0]
    usable_all = by_device[:, 0, low : low + flags.shape[0]].reshape(tiles, -1)[:, :slots]
    usable_all = usable_all.astype(jnp.float32)

    departure, slope = call(
        functools.partial(forward_kernel, tiles, group, block, own_cols),
        (
            jax.ShapeDtypeStruct((rows, observed.shape[1]), jnp.bfloat16),
            jax.ShapeDtypeStruct((chans, rows, hidden), jnp.float32),
        ),
        [order, gathered, spot, place, usable_all, b_radiance[None, :], w_radiance]
        + seen
        + near
        + [far],
        1,
        scratch=[pltpu.VMEM((rows, hidden * chans), jnp.bfloat16)],
        flops=2 * rows * hidden * chans * (width + observed.shape[1]),
    )

    parts = jnp.split(departure, steps, axis=0)
    source = lax.div(c, jnp.int32(group)) ^ t
    for step in range(steps):
        moved = []
        for j in range(steps):
            reached = sum(1 << (j + k) % steps for k in range(step))
            bit = 1 << (j + step) % steps
            pairs = [
                (a * chans + b, a * chans + (b ^ bit * group))
                for a in range(tiles)
                for b in range(chans)
                if (b // group ^ a) & ~reached == 0
            ]
            arrived = lax.ppermute(parts[j], both, pairs)
            is_new = (source & ~jnp.int32(reached)) == bit
            moved.append(jnp.where(is_new, arrived, parts[j]))
        parts = moved
    joined = jnp.concatenate(parts, axis=0)
    others = jnp.stack([flip(joined, k) for k in range(1, group)])
    at = jnp.bitwise_xor(jnp.arange(group, dtype=jnp.int32), c % group)

    per_row = own_cols + 2
    partial = call(
        functools.partial(backward_kernel, tiles, group, own_cols, steps),
        jax.ShapeDtypeStruct((tiles * chans * per_row, width), jnp.bfloat16),
        [order, at, inv_cov, w_radiance, slope] + parts + [others] + near + [far],
        2,
        scratch=[pltpu.VMEM((16, 128), jnp.bfloat16)],
        flops=2 * rows * (hidden * chans * (width + observed.shape[1]) + inv_cov.size),
    )
    partial = lax.all_to_all(
        partial.reshape(tiles, chans * per_row, width), "tile", 0, 0, tiled=True
    )
    room = up_to(3 * per_row, 16)
    partial = call(
        functools.partial(middle_kernel, chans, per_row),
        jax.ShapeDtypeStruct((chans * room, width), jnp.bfloat16),
        [partial],
        0,
        flops=2 * chans * room * chans * per_row * width,
    )
    partial = lax.all_to_all(partial.reshape(chans, room, width), "chan", 0, 0, tiled=True)

    edge = 8
    cell_rows = by_device[:, :, own_cols:low].reshape(tiles, chans, -1)
    cell_rows = cell_rows[:, :, : 3 * cells_across * cells_along].astype(jnp.float32)
    kappa = jnp.sum(cell_rows.reshape(tiles, chans, 3, cells_across, cells_along), axis=2)
    kappa = kappa.transpose(0, 3, 1, 2).reshape(tiles * cells_along, chans * cells_across)
    kappa = jnp.concatenate([kappa[-edge:], kappa, kappa[:edge]], axis=0)
    kappa = jnp.pad(kappa, ((0, 0), (2, 2)))
    root = jnp.sqrt(
        lax.dynamic_slice(
            kappa,
            (t * cells_along, c * cells_across),
            (cells_along + 2 * edge, cells_across + 4),
        )
    )
    return call(
        functools.partial(diffuse_kernel, per_row, edge),
        jax.ShapeDtypeStruct(fields.shape, jnp.float32),
        [partial, root],
        0,
        flops=100 * fields.size,
    )


def solution(mesh):
    tiles, chans = mesh.shape["tile"], mesh.shape["chan"]
    by_column = chans % tiles == 0 and chans & (chans - 1) == 0 and chans // tiles > 1
    placed = (
        P("chan", "tile", None),
        P("chan", "tile"),
        P(),
        P("tile", "chan"),
        P("tile"),
        P(None, "chan"),
        P("chan"),
        P(None, "chan"),
        P("chan"),
        P("tile", "chan"),
    )
    return jax.shard_map(
        body_by_column if by_column else body_by_owner,
        mesh=mesh,
        in_specs=placed,
        out_specs=P("chan", "tile", None),
        check_vma=False,
    )
```

```python
import functools

import jax
import jax.numpy as jnp
from jax import lax
from jax.experimental import pallas as pl
from jax.experimental.pallas import tpu as pltpu
from jax.sharding import PartitionSpec as P

VMEM_BYTES = 24 * 1024 * 1024
NT_DIMS = (((1,), (1,)), ((), ()))


def padded_2(value, sides, width, wrap):
    for axis, dim in sides:
        devices, length = (lax.axis_size(axis), value.shape[dim])
        up = [(i, (i + 1) % devices) for i in range(devices if wrap else devices - 1)]
        down = [(j, i) for i, j in up]
        last = lax.slice_in_dim(value, length - width, length, axis=dim)
        first = lax.slice_in_dim(value, 0, width, axis=dim)
        before = lax.ppermute(last, axis, up)
        after = lax.ppermute(first, axis, down)
        value = jnp.concatenate([before, value, after], axis=dim)
    return value


def add_rims(values):
    rowwise = padded_2(values, (("chan", 0),), 1, False)
    return padded_2(rowwise, (("tile", 1),), 1, True)


def body_by_owner(
    fields,
    diffusivity,
    owners,
    observed,
    usable,
    w_hidden,
    b_hidden,
    w_radiance,
    b_radiance,
    inv_cov,
):
    tile_count = lax.axis_size("tile")
    chan_count = lax.axis_size("chan")
    tile_index = lax.axis_index("tile")
    chan_index = lax.axis_index("chan")
    slot_count = observed.shape[0]
    capacity = slot_count // tile_count
    cells_across, cells_along, features = fields.shape
    own_cols = cells_across // 4 * (cells_along // 4)
    tile_cols = chan_count * own_cols
    hidden_dev = w_hidden.shape[1]
    owner_table = owners[:, 0].reshape(tile_count, tile_cols)
    owner_hits = (
        owner_table[:, :, None] == jnp.arange(tile_count, dtype=jnp.int32)[None, None, :]
    ).astype(jnp.int32)
    before = jnp.sum((jnp.cumsum(owner_hits, axis=1) - owner_hits) * owner_hits, axis=2)
    tallies = jnp.sum(owner_hits, axis=1)
    slot_of = lax.dynamic_index_in_dim(
        owner_table * capacity + before, tile_index, 0, keepdims=False
    )
    arriving = lax.dynamic_index_in_dim(tallies, tile_index, 1, keepdims=False)
    occupied = (jnp.arange(capacity, dtype=jnp.int32)[None, :] < arriving[:, None]).reshape(
        slot_count
    )
    grouped = fields.reshape(cells_across // 4, 4, cells_along // 4, 4, features)
    columns = (
        (jnp.sum(grouped, axis=(1, 3)) * 0.0625).reshape(own_cols, features).astype(jnp.bfloat16)
    )
    placer = (slot_of[None, :] == jnp.arange(slot_count, dtype=jnp.int32)[:, None]).astype(
        jnp.bfloat16
    )
    outgoing = jnp.dot(
        placer,
        lax.all_gather(columns, "chan", axis=0, tiled=True),
        preferred_element_type=jnp.float32,
    )
    incoming = lax.all_to_all(
        outgoing.astype(jnp.bfloat16), "tile", split_axis=0, concat_axis=0, tiled=True
    )
    preact = lax.dot_general(
        w_hidden, incoming, (((0,), (1,)), ((), ())), preferred_element_type=jnp.float32
    )
    preact = preact + b_hidden[:, None]
    squash = jax.nn.sigmoid(preact)
    active = (preact * squash).astype(jnp.bfloat16)
    radiance = lax.dot_general(
        lax.all_gather(active, "chan", axis=0, tiled=True),
        w_radiance,
        (((0,), (0,)), ((), ())),
        preferred_element_type=jnp.float32,
    )
    radiance = radiance + b_radiance[None, :]
    in_use = usable.astype(jnp.float32) * occupied.astype(jnp.float32)
    departure = ((radiance - observed.astype(jnp.float32)) * in_use[:, None]).astype(jnp.bfloat16)
    cotangent = jnp.dot(
        lax.all_gather(departure, "chan", axis=1, tiled=True),
        lax.all_gather(inv_cov, "tile", axis=0, tiled=True),
        preferred_element_type=jnp.float32,
    )
    cotangent = cotangent.astype(jnp.bfloat16)
    full_sum = lax.psum(
        lax.dot_general(w_radiance, cotangent, NT_DIMS, preferred_element_type=jnp.float32),
        "chan",
    )
    grad_hidden = lax.dynamic_slice_in_dim(full_sum, chan_index * hidden_dev, hidden_dev, 0)
    slope_term = squash * (1.0 + preact * (1.0 - squash))
    grad_pre = (grad_hidden * slope_term).astype(jnp.bfloat16)
    part_grad = lax.dot_general(
        grad_pre, w_hidden, (((0,), (1,)), ((), ())), preferred_element_type=jnp.float32
    )
    returned = lax.all_to_all(part_grad, "tile", split_axis=0, concat_axis=0, tiled=True)
    column_grad = lax.psum_scatter(
        jnp.take(returned, slot_of, axis=0), "chan", scatter_dimension=0, tiled=True
    )
    spread = jnp.repeat(
        column_grad.reshape(cells_across // 4, cells_along // 4, features), 4, axis=0
    )
    adjoint = jnp.repeat(spread, 4, axis=1) * 0.0625
    kappa_root = jnp.sqrt(diffusivity)
    root_rim = add_rims(kappa_root)
    coef_north = (kappa_root * root_rim[2:, 1:-1])[:, :, None]
    coef_south = (kappa_root * root_rim[:-2, 1:-1])[:, :, None]
    coef_east = (kappa_root * root_rim[1:-1, 2:])[:, :, None]
    coef_west = (kappa_root * root_rim[1:-1, :-2])[:, :, None]
    for sweep_index in range(2):
        padded = add_rims(adjoint)
        adjoint = (
            adjoint
            + coef_north * (padded[2:, 1:-1] - adjoint)
            + coef_south * (padded[:-2, 1:-1] - adjoint)
            + coef_east * (padded[1:-1, 2:] - adjoint)
            + coef_west * (padded[1:-1, :-2] - adjoint)
        )
    return adjoint


def up_to(value, multiple):
    return -(-value // multiple) * multiple


def dot(left, right):
    return jnp.dot(left, right, preferred_element_type=jnp.float32)


def dot_nt(left, right):
    return lax.dot_general(left, right, NT_DIMS, preferred_element_type=jnp.float32)


def split_three(value):
    high = value.astype(jnp.bfloat16).astype(jnp.float32)
    middle = (value - high).astype(jnp.bfloat16).astype(jnp.float32)
    return high, middle, value - high - middle


def call(kernel, out_shape, args, in_hbm=(), out_hbm=False, scratch=(), flops=0):
    far, near = pl.BlockSpec(memory_space=pl.ANY), pl.BlockSpec(memory_space=pltpu.VMEM)
    bytes_accessed = sum(a.size * a.dtype.itemsize for a in args)
    return pl.pallas_call(
        kernel,
        out_shape=out_shape,
        in_specs=[far if k in in_hbm else near for k in range(len(args))],
        out_specs=jax.tree.map(lambda _: far if out_hbm else near, out_shape),
        scratch_shapes=list(scratch),
        compiler_params=pltpu.CompilerParams(vmem_limit_bytes=VMEM_BYTES),
        cost_estimate=pl.CostEstimate(
            flops=flops, bytes_accessed=bytes_accessed, transcendentals=0
        ),
    )(*args)


class Plan:
    def __init__(self, tiles, chans, fields, owners, observed, w_hidden):
        self.tiles, self.chans = tiles, chans
        self.across, self.along, self.features = fields
        self.own_cols = self.across // 4 * (self.along // 4)
        self.rows = owners[0]
        self.tile_cols = self.rows // tiles
        self.slots = observed[0]
        self.shard = observed[1]
        self.capacity = self.slots // tiles
        self.hidden = w_hidden[1]
        self.group = chans // tiles
        self.chips = chans // self.group
        self.steps = self.chips.bit_length() - 1
        self.lane = up_to(self.along, 128)
        self.flag_at = up_to(self.hidden, 128)
        self.width = max(
            up_to(self.features, 128),
            2 * self.flag_at,
            self.flag_at + up_to(self.slots, 128),
            3 * self.lane,
        )
        self.block = up_to(self.own_cols + 2 + self.across, 16)
        self.per_row = self.own_cols + 2
        self.room = up_to(3 * self.per_row, 16)
        self.patch = 3 * tiles * self.own_cols


def prepare_kernel(p, fields_ref, diffusivity_ref, usable_ref, bias_ref, out_ref, flat, packed, sem):
    flat[...] = jnp.zeros(flat.shape, jnp.float32)
    shape = (p.own_cols, p.along)
    row = lax.broadcasted_iota(jnp.int32, shape, 0)
    member = row == lax.broadcasted_iota(jnp.int32, shape, 1) // 4
    total = jnp.dot(
        member.astype(jnp.float32),
        fields_ref[0] + fields_ref[1] + fields_ref[2] + fields_ref[3],
        precision=lax.Precision.HIGHEST,
        preferred_element_type=jnp.float32,
    )
    flat[: p.own_cols, : p.features] = total * 0.0625
    at = p.own_cols
    high, middle, low = split_three(bias_ref[...].reshape(1, p.hidden))
    flat[at : at + 1, : p.hidden] = high
    flat[at : at + 1, p.flag_at : p.flag_at + p.hidden] = middle
    flat[at + 1 : at + 2, : p.hidden] = low
    flags = usable_ref[...].reshape(1, p.slots).astype(jnp.float32)
    flat[at + 1 : at + 2, p.flag_at : p.flag_at + p.slots] = flags
    for k, part in enumerate(split_three(diffusivity_ref[...])):
        flat[at + 2 : at + 2 + p.across, k * p.lane : k * p.lane + p.along] = part
    packed[...] = flat[...].astype(jnp.bfloat16)
    copy = pltpu.make_async_copy(packed, out_ref, sem)
    copy.start()
    copy.wait()


def place_kernel(p, owners_ref, out_ref):
    owner = owners_ref[...]
    shape = (p.rows, p.rows)
    row = lax.broadcasted_iota(jnp.int32, shape, 0)
    other = lax.broadcasted_iota(jnp.int32, shape, 1)
    across = jnp.sum(jnp.where(row == other, owner, 0), axis=0, keepdims=True)
    same = (owner == across) & (row // p.tile_cols == other // p.tile_cols) & (other < row)
    rank = jnp.sum(jnp.where(same, 1, 0), axis=1, keepdims=True)
    number = lax.broadcasted_iota(jnp.int32, owner.shape, 0)
    near = (owner + p.tiles - lax.axis_index("tile")) % p.tiles
    out_ref[...] = near * p.slots + number // p.tile_cols * p.capacity + rank


def join_kernel(*refs):
    count = (len(refs) - 2) // 1
    ins, out_ref, sems = refs[:count], refs[count], refs[count + 1]
    size = ins[0].shape[0]
    copies = [
        pltpu.make_async_copy(ref, out_ref.at[pl.ds(k * size, size)], sems.at[k])
        for k, ref in enumerate(ins)
    ]
    for copy in copies:
        copy.start()
    for copy in copies:
        copy.wait()


def forward_kernel(p, *refs):
    refs = list(refs)
    take = lambda n: [refs.pop(0) for _ in range(n)]
    place_ref, bias_ref, w_radiance_ref = take(3)
    gathered_refs, seen_refs, weight_refs = take(p.chans), take(p.tiles), take(p.chans)
    *part_refs, slope_out, kappa_out = take(p.steps + 2)
    stack, seen, weights, slope, active, departure, kappa, sems = take(8)
    t, c = lax.axis_index("tile"), lax.axis_index("chan")
    count = iter(range(3 * p.chans + p.tiles + p.steps + 1))

    def begin(source, target):
        copy = pltpu.make_async_copy(source, target, sems.at[next(count)])
        copy.start()
        return copy

    wide = p.tiles * p.block
    packs = [
        begin(ref, stack.at[pl.ds(k * wide, wide)]) for k, ref in enumerate(gathered_refs)
    ]
    loads = [begin(ref, weights.at[k]) for k, ref in enumerate(weight_refs)]
    views = [begin(ref, seen.at[k]) for k, ref in enumerate(seen_refs)]
    for copy in packs:
        copy.wait()
    shape = (p.rows, p.chans * wide)
    row = lax.broadcasted_iota(jnp.int32, shape, 0)
    source = lax.broadcasted_iota(jnp.int32, shape, 1)
    tile = (row // p.tile_cols + p.tiles - t) % p.tiles
    chan = (row % p.tile_cols // p.own_cols) ^ c
    pick = source == chan * wide + tile * p.block + row % p.own_cols
    everything = stack[...]
    columns = dot(pick.astype(jnp.bfloat16), everything).astype(jnp.bfloat16)[:, : p.features]
    out = []
    for k in range(p.chans):
        loads[k].wait()
        low = stack[k * wide + p.own_cols : k * wide + p.own_cols + 2, :].astype(jnp.float32)
        bias = (
            low[:1, : p.hidden]
            + low[:1, p.flag_at : p.flag_at + p.hidden]
            + low[1:, : p.hidden]
        )
        preact = dot(columns, weights[k]) + bias
        squash = jax.nn.sigmoid(preact)
        slope[k] = squash * (1.0 + preact * (1.0 - squash))
        out.append(begin(slope.at[k], slope_out.at[k]))
        at = pl.multiple_of((c ^ k) * p.hidden, p.hidden)
        active[:, pl.ds(at, p.hidden)] = (preact * squash).astype(jnp.bfloat16)
    for copy in views:
        copy.wait()
    part = p.rows // p.steps
    slot = lax.broadcasted_iota(jnp.int32, (part, p.slots), 1)
    for j, part_ref in enumerate(part_refs):
        at = slice(j * part, (j + 1) * part)
        in_use = jnp.zeros((part, 1), jnp.float32)
        observed = jnp.zeros((part, p.shard), jnp.float32)
        for k in range(p.tiles):
            hit = place_ref[at, :] == slot + k * p.slots
            low = k * p.block + p.own_cols + 1
            flags = stack[low : low + 1, p.flag_at : p.flag_at + p.slots].astype(jnp.float32)
            in_use = in_use + jnp.sum(jnp.where(hit, flags, 0.0), axis=1, keepdims=True)
            observed = observed + dot(hit.astype(jnp.bfloat16), seen[k])
        radiance = dot(active[at, :], w_radiance_ref[...]) + bias_ref[...].reshape(1, p.shard)
        departure[at, :] = ((radiance - observed) * in_use).astype(jnp.bfloat16)
        out.append(begin(departure.at[pl.ds(j * part, part)], part_ref))
    reach = p.across + 4
    shape = (3 * reach, p.chans * wide)
    row = lax.broadcasted_iota(jnp.int32, shape, 0)
    source = lax.broadcasted_iota(jnp.int32, shape, 1)
    tile = (row // reach - 1 + p.tiles) % p.tiles
    cell = c * p.across - 2 + row % reach
    inside = (cell >= 0) & (cell < p.chans * p.across)
    cell = jnp.where(inside, cell, 0)
    wanted = (cell // p.across ^ c) * wide + tile * p.block + p.own_cols + 2 + cell % p.across
    pick = (source == wanted) & inside
    parts = dot(pick.astype(jnp.bfloat16), everything)
    kappa[...] = sum(parts[:, k * p.lane : (k + 1) * p.lane] for k in range(3))
    out.append(begin(kappa, kappa_out))
    for copy in out:
        copy.wait()


def choose_kernel(p, choices, *refs):
    refs, out_ref, sems = refs[:-2], refs[-2], refs[-1]
    size = refs[0].shape[0]
    role = (lax.axis_index("chan") // p.group) ^ lax.axis_index("tile")
    for place in range(p.chips):

        @pl.when(role == place)
        def _():
            copies = [
                pltpu.make_async_copy(
                    refs[choices[place, j]], out_ref.at[pl.ds(j * size, size)], sems.at[j]
                )
                for j in range(p.steps)
            ]
            for copy in copies:
                copy.start()
            for copy in copies:
                copy.wait()


def backward_kernel(p, *refs):
    refs = list(refs)
    take = lambda n: [refs.pop(0) for _ in range(n)]
    (w_radiance_ref,) = take(1)
    inv_cov_ref, slope_ref = take(2)
    depart_refs, weight_refs, out_refs = take(p.group), take(p.chans), take(p.group)
    inv_cov, slope, depart, weights, result, sems = take(6)
    t, c = lax.axis_index("tile"), lax.axis_index("chan")
    count = iter(range(2 * p.group + 2 * p.chans + p.group))

    def begin(source, target):
        copy = pltpu.make_async_copy(source, target, sems.at[next(count)])
        copy.start()
        return copy

    loads = []
    for k, ref in enumerate(depart_refs):
        at = pl.multiple_of((c % p.group ^ k) * p.shard, p.shard)
        loads.append(
            (
                begin(ref, depart.at[k]),
                begin(inv_cov_ref.at[pl.ds(at, p.shard)], inv_cov.at[k]),
            )
        )
    slopes = [begin(slope_ref.at[k], slope.at[k]) for k in range(p.chans)]
    firsts = [begin(ref, weights.at[k]) for k, ref in enumerate(weight_refs)]
    cotangent = None
    for k, copies in enumerate(loads):
        for copy in copies:
            copy.wait()
        term = dot(depart[k], inv_cov[k])
        cotangent = term if cotangent is None else cotangent + term
    cotangent = cotangent.astype(jnp.bfloat16)
    total = jnp.zeros((p.rows, p.features), jnp.float32)
    for k in range(p.chans):
        at = pl.multiple_of((c ^ k) * p.hidden, p.hidden)
        grad_hidden = dot_nt(cotangent, w_radiance_ref[pl.ds(at, p.hidden), :])
        slopes[k].wait()
        firsts[k].wait()
        grad_pre = (grad_hidden * slope[k]).astype(jnp.bfloat16)
        total = total + dot_nt(grad_pre, weights[k])
    total = total.astype(jnp.bfloat16)
    shape = (p.chips * p.patch, p.rows)
    target = lax.broadcasted_iota(jnp.int32, shape, 0)
    source = lax.broadcasted_iota(jnp.int32, shape, 1)
    chip, inner = target // p.patch, target % p.patch
    beside, inner = inner // (p.patch // 3) - 1, inner % (p.patch // 3)
    tile, along = inner // p.own_cols, inner % p.own_cols
    copies = []
    for k in range(p.group):
        row = ((chip ^ (c // p.group)) * p.group + (c % p.group ^ k)) + beside
        wanted = tile * p.tile_cols + row * p.own_cols + along
        pick = (source == wanted) & (row >= 0) & (row < p.chans)
        result[k] = dot(pick.astype(jnp.bfloat16), total).astype(jnp.bfloat16)
        copies.append(begin(result.at[k], out_refs[k]))
    for copy in copies:
        copy.wait()


def add(refs, at=slice(None)):
    total = refs[0][at, :].astype(jnp.float32)
    for ref in refs[1:]:
        total = total + ref[at, :].astype(jnp.float32)
    return total


def add_group_kernel(p, *refs):
    ins, outs = refs[: p.group], refs[p.group :]
    for k, out_ref in enumerate(outs):
        out_ref[...] = add(ins, slice(k * p.patch, (k + 1) * p.patch)).astype(jnp.bfloat16)


def add_chips_kernel(p, *refs):
    ins, outs = refs[: p.chips], refs[p.chips :]
    total = add(ins).astype(jnp.bfloat16)
    shape = (p.room, p.patch)
    target = lax.broadcasted_iota(jnp.int32, shape, 0)
    source = lax.broadcasted_iota(jnp.int32, shape, 1)
    row, along = target // p.per_row, target % p.per_row - 1
    for k, out_ref in enumerate(outs):
        tile = (lax.axis_index("tile") + k) % p.tiles
        cell = (tile * p.own_cols + along + p.tiles * p.own_cols) % (p.tiles * p.own_cols)
        pick = (source == row * (p.tiles * p.own_cols) + cell) & (row < 3)
        out_ref[...] = dot(pick.astype(jnp.bfloat16), total).astype(jnp.bfloat16)


def diffuse_kernel(p, edge, *refs):
    ins, root_ref, out_ref = refs[: p.tiles], refs[-2], refs[-1]
    total = add(ins) * 0.0625
    length = p.along + 2 * edge
    shape = (length, p.room)
    cell = lax.broadcasted_iota(jnp.int32, shape, 0)
    source = lax.broadcasted_iota(jnp.int32, shape, 1)
    column = (cell - edge + 4) // 4
    spread = []
    for k in range(3):
        pick = (source == column + k * p.per_row) & (column >= 0) & (column < p.per_row)
        spread.append(
            jnp.dot(
                pick.astype(jnp.float32),
                total,
                precision=lax.Precision.HIGHEST,
                preferred_element_type=jnp.float32,
            )
        )
    root = root_ref[...]
    state = [spread[(row + 2) // 4] for row in range(p.across + 4)]
    east_of = functools.partial(pltpu.roll, shift=length - 1, axis=0)
    west_of = functools.partial(pltpu.roll, shift=1, axis=0)
    north = root[:, :-1] * root[:, 1:]
    east, west = root * east_of(root), root * west_of(root)
    for sweep in range(2):
        fresh = list(state)
        for row in range(1 + sweep, p.across + 3 - sweep):
            here = state[row]
            fresh[row] = (
                here
                + north[:, row : row + 1] * (state[row + 1] - here)
                + north[:, row - 1 : row] * (state[row - 1] - here)
                + east[:, row : row + 1] * (east_of(here) - here)
                + west[:, row : row + 1] * (west_of(here) - here)
            )
        state = fresh
    for row in range(p.across):
        out_ref[row] = state[row + 2][edge : edge + p.along, : p.features]


def body_by_column(
    fields,
    diffusivity,
    owners,
    observed,
    usable,
    w_hidden,
    b_hidden,
    w_radiance,
    b_radiance,
    inv_cov,
):
    p = Plan(
        lax.axis_size("tile"),
        lax.axis_size("chan"),
        fields.shape,
        owners.shape,
        observed.shape,
        w_hidden.shape,
    )
    half, single = jnp.bfloat16, jnp.float32
    shape = jax.ShapeDtypeStruct
    both = ("tile", "chan")
    everyone = [(a, b) for a in range(p.tiles) for b in range(p.chans)]

    def flip(value, mask):
        return lax.ppermute(value, "chan", [(b, b ^ mask) for b in range(p.chans)])

    def shift(value, by):
        return lax.ppermute(value, "tile", [(a, (a + by) % p.tiles) for a in range(p.tiles)])

    def send(value, wanted):
        pairs = dict(wanted)
        pairs.update({target: source for source, target in wanted.items()})
        for a, b in everyone:
            if (a, b) not in pairs:
                pairs[a, b] = (a, b ^ 1)
        number = lambda place: place[0] * p.chans + place[1]
        return lax.ppermute(
            value, both, sorted((number(a), number(b)) for a, b in pairs.items())
        )

    weights = [None] * p.chans
    weights[0] = w_hidden
    for chip in range(1, p.chips):
        weights[chip * p.group] = flip(w_hidden, chip * p.group)

    seen = [observed] + [
        send(
            observed,
            {((b // p.group + k) % p.tiles, b): (b // p.group, b) for b in range(p.chans)},
        )
        for k in range(1, p.tiles)
    ]

    packed = call(
        functools.partial(prepare_kernel, p),
        shape((p.block, p.width), half),
        [fields, diffusivity, usable, b_hidden],
        out_hbm=True,
        scratch=[
            pltpu.VMEM((p.block, p.width), single),
            pltpu.VMEM((p.block, p.width), half),
            pltpu.SemaphoreType.DMA,
        ],
    )
    strips = [packed] + [shift(packed, p.tiles - k) for k in range(1, p.tiles)]
    joined = call(
        join_kernel,
        shape((p.tiles * p.block, p.width), half),
        strips,
        in_hbm=range(p.tiles),
        out_hbm=True,
        scratch=[pltpu.SemaphoreType.DMA((p.tiles,))],
    )
    gathered = [joined] + [None] * (p.chans - 1)
    for chip in range(1, p.chips):
        gathered[chip * p.group] = flip(joined, chip * p.group)
    for held in (weights, gathered):
        for k in range(p.chans):
            if k % p.group:
                held[k] = flip(held[k - k % p.group], k % p.group)
    place = call(functools.partial(place_kernel, p), shape((p.rows, 1), jnp.int32), [owners])

    reach = p.across + 4
    *parts, slope, kappa = call(
        functools.partial(forward_kernel, p),
        [shape((p.rows // p.steps, p.shard), half)] * p.steps
        + [shape((p.chans, p.rows, p.hidden), single), shape((3 * reach, p.lane), single)],
        [place, b_radiance, w_radiance] + gathered + seen + weights,
        in_hbm=range(3, 3 + 2 * p.chans + p.tiles),
        out_hbm=True,
        scratch=[
            pltpu.VMEM((p.chans * p.tiles * p.block, p.width), half),
            pltpu.VMEM((p.tiles, p.slots, p.shard), half),
            pltpu.VMEM((p.chans, p.features, p.hidden), half),
            pltpu.VMEM((p.chans, p.rows, p.hidden), single),
            pltpu.VMEM((p.rows, p.hidden * p.chans), half),
            pltpu.VMEM((p.rows, p.shard), half),
            pltpu.VMEM((3 * reach, p.lane), single),
            pltpu.SemaphoreType.DMA((3 * p.chans + p.tiles + p.steps + 1,)),
        ],
        flops=2 * p.rows * p.hidden * p.chans * (p.features + p.shard),
    )

    pool, held, choices = list(parts), {}, {}
    for j in range(p.steps):
        held[0, j] = choices[0, j] = j
    for step in range(p.steps):
        for since in range(-1, step):
            for j in range(p.steps):
                order = [1 << (j + k) % p.steps for k in range(p.steps)]
                roles = [0] if since < 0 else [
                    order[since] + rest
                    for rest in range(p.chips)
                    if rest & ~sum(order[:since]) == 0
                ]
                wanted = {
                    (a, b): (a, b ^ order[step] * p.group)
                    for a, b in everyone
                    if (b // p.group ^ a) in roles
                }
                source = pool[choices[roles[0], j]]
                for role in roles:
                    choices[role + order[step], j] = len(pool)
                pool.append(send(source, wanted))
    chosen = call(
        functools.partial(choose_kernel, p, choices),
        shape((p.rows, p.shard), half),
        pool,
        in_hbm=range(len(pool)),
        out_hbm=True,
        scratch=[pltpu.SemaphoreType.DMA((p.steps,))],
    )
    depart = [chosen] + [flip(chosen, k) for k in range(1, p.group)]

    count = p.group + p.chans
    partial = call(
        functools.partial(backward_kernel, p),
        [shape((p.chips * p.patch, p.features), half)] * p.group,
        [w_radiance, inv_cov, slope] + depart + weights,
        in_hbm=range(1, 3 + count),
        out_hbm=True,
        scratch=[
            pltpu.VMEM((p.group, p.shard, p.shard), half),
            pltpu.VMEM((p.chans, p.rows, p.hidden), single),
            pltpu.VMEM((p.group, p.rows, p.shard), half),
            pltpu.VMEM((p.chans, p.features, p.hidden), half),
            pltpu.VMEM((p.group, p.chips * p.patch, p.features), half),
            pltpu.SemaphoreType.DMA((2 * p.group + 2 * p.chans + p.group,)),
        ],
        flops=2 * p.rows * (p.hidden * p.chans * (p.features + p.shard) + inv_cov.size),
    )
    partial = [partial[0]] + [flip(partial[k], k) for k in range(1, p.group)]
    partial = call(
        functools.partial(add_group_kernel, p),
        [shape((p.patch, p.features), half)] * p.chips,
        partial,
    )
    partial = [partial[0]] + [flip(partial[k], k * p.group) for k in range(1, p.chips)]
    partial = call(
        functools.partial(add_chips_kernel, p),
        [shape((p.room, p.features), half)] * p.tiles,
        partial,
    )
    partial = [partial[0]] + [shift(partial[k], k) for k in range(1, p.tiles)]

    edge = 8
    kappa = kappa.reshape(3, reach, p.lane)
    root = jnp.sqrt(
        jnp.concatenate(
            [kappa[0, :, p.along - edge : p.along], kappa[1, :, : p.along], kappa[2, :, :edge]],
            axis=1,
        ).T
    )
    return call(
        functools.partial(diffuse_kernel, p, edge),
        shape(fields.shape, single),
        partial + [root],
        flops=100 * fields.size,
    )


def solution(mesh):
    tiles, chans = mesh.shape["tile"], mesh.shape["chan"]
    by_column = chans % tiles == 0 and chans & (chans - 1) == 0 and chans // tiles > 1
    placed = (
        P("chan", "tile", None),
        P("chan", "tile"),
        P(),
        P("tile", "chan"),
        P("tile"),
        P(None, "chan"),
        P("chan"),
        P(None, "chan"),
        P("chan"),
        P("tile", "chan"),
    )
    return jax.shard_map(
        body_by_column if by_column else body_by_owner,
        mesh=mesh,
        in_specs=placed,
        out_specs=P("chan", "tile", None),
        check_vma=False,
    )
```

```python
import functools

import jax
import jax.numpy as jnp
from jax import lax
from jax.experimental import pallas as pl
from jax.experimental.pallas import tpu as pltpu
from jax.sharding import PartitionSpec as P

VMEM_BYTES = 24 * 1024 * 1024
WHOLE_VMEM_BYTES = 63 * 1024 * 1024
SLACK_FLOPS = 5 * 10**9
NT_DIMS = (((1,), (1,)), ((), ()))


def padded_2(value, sides, width, wrap):
    for axis, dim in sides:
        devices, length = (lax.axis_size(axis), value.shape[dim])
        up = [(i, (i + 1) % devices) for i in range(devices if wrap else devices - 1)]
        down = [(j, i) for i, j in up]
        last = lax.slice_in_dim(value, length - width, length, axis=dim)
        first = lax.slice_in_dim(value, 0, width, axis=dim)
        before = lax.ppermute(last, axis, up)
        after = lax.ppermute(first, axis, down)
        value = jnp.concatenate([before, value, after], axis=dim)
    return value


def add_rims(values):
    rowwise = padded_2(values, (("chan", 0),), 1, False)
    return padded_2(rowwise, (("tile", 1),), 1, True)


def body_by_owner(
    fields,
    diffusivity,
    owners,
    observed,
    usable,
    w_hidden,
    b_hidden,
    w_radiance,
    b_radiance,
    inv_cov,
):
    tile_count = lax.axis_size("tile")
    chan_count = lax.axis_size("chan")
    tile_index = lax.axis_index("tile")
    chan_index = lax.axis_index("chan")
    slot_count = observed.shape[0]
    capacity = slot_count // tile_count
    cells_across, cells_along, features = fields.shape
    own_cols = cells_across // 4 * (cells_along // 4)
    tile_cols = chan_count * own_cols
    hidden_dev = w_hidden.shape[1]
    owner_table = owners[:, 0].reshape(tile_count, tile_cols)
    owner_hits = (
        owner_table[:, :, None] == jnp.arange(tile_count, dtype=jnp.int32)[None, None, :]
    ).astype(jnp.int32)
    before = jnp.sum((jnp.cumsum(owner_hits, axis=1) - owner_hits) * owner_hits, axis=2)
    tallies = jnp.sum(owner_hits, axis=1)
    slot_of = lax.dynamic_index_in_dim(
        owner_table * capacity + before, tile_index, 0, keepdims=False
    )
    arriving = lax.dynamic_index_in_dim(tallies, tile_index, 1, keepdims=False)
    occupied = (jnp.arange(capacity, dtype=jnp.int32)[None, :] < arriving[:, None]).reshape(
        slot_count
    )
    grouped = fields.reshape(cells_across // 4, 4, cells_along // 4, 4, features)
    columns = (
        (jnp.sum(grouped, axis=(1, 3)) * 0.0625).reshape(own_cols, features).astype(jnp.bfloat16)
    )
    placer = (slot_of[None, :] == jnp.arange(slot_count, dtype=jnp.int32)[:, None]).astype(
        jnp.bfloat16
    )
    outgoing = jnp.dot(
        placer,
        lax.all_gather(columns, "chan", axis=0, tiled=True),
        preferred_element_type=jnp.float32,
    )
    incoming = lax.all_to_all(
        outgoing.astype(jnp.bfloat16), "tile", split_axis=0, concat_axis=0, tiled=True
    )
    preact = lax.dot_general(
        w_hidden, incoming, (((0,), (1,)), ((), ())), preferred_element_type=jnp.float32
    )
    preact = preact + b_hidden[:, None]
    squash = jax.nn.sigmoid(preact)
    active = (preact * squash).astype(jnp.bfloat16)
    radiance = lax.dot_general(
        lax.all_gather(active, "chan", axis=0, tiled=True),
        w_radiance,
        (((0,), (0,)), ((), ())),
        preferred_element_type=jnp.float32,
    )
    radiance = radiance + b_radiance[None, :]
    in_use = usable.astype(jnp.float32) * occupied.astype(jnp.float32)
    departure = ((radiance - observed.astype(jnp.float32)) * in_use[:, None]).astype(jnp.bfloat16)
    cotangent = jnp.dot(
        lax.all_gather(departure, "chan", axis=1, tiled=True),
        lax.all_gather(inv_cov, "tile", axis=0, tiled=True),
        preferred_element_type=jnp.float32,
    )
    cotangent = cotangent.astype(jnp.bfloat16)
    full_sum = lax.psum(
        lax.dot_general(w_radiance, cotangent, NT_DIMS, preferred_element_type=jnp.float32),
        "chan",
    )
    grad_hidden = lax.dynamic_slice_in_dim(full_sum, chan_index * hidden_dev, hidden_dev, 0)
    slope_term = squash * (1.0 + preact * (1.0 - squash))
    grad_pre = (grad_hidden * slope_term).astype(jnp.bfloat16)
    part_grad = lax.dot_general(
        grad_pre, w_hidden, (((0,), (1,)), ((), ())), preferred_element_type=jnp.float32
    )
    returned = lax.all_to_all(part_grad, "tile", split_axis=0, concat_axis=0, tiled=True)
    column_grad = lax.psum_scatter(
        jnp.take(returned, slot_of, axis=0), "chan", scatter_dimension=0, tiled=True
    )
    spread = jnp.repeat(
        column_grad.reshape(cells_across // 4, cells_along // 4, features), 4, axis=0
    )
    adjoint = jnp.repeat(spread, 4, axis=1) * 0.0625
    kappa_root = jnp.sqrt(diffusivity)
    root_rim = add_rims(kappa_root)
    coef_north = (kappa_root * root_rim[2:, 1:-1])[:, :, None]
    coef_south = (kappa_root * root_rim[:-2, 1:-1])[:, :, None]
    coef_east = (kappa_root * root_rim[1:-1, 2:])[:, :, None]
    coef_west = (kappa_root * root_rim[1:-1, :-2])[:, :, None]
    for sweep_index in range(2):
        padded = add_rims(adjoint)
        adjoint = (
            adjoint
            + coef_north * (padded[2:, 1:-1] - adjoint)
            + coef_south * (padded[:-2, 1:-1] - adjoint)
            + coef_east * (padded[1:-1, 2:] - adjoint)
            + coef_west * (padded[1:-1, :-2] - adjoint)
        )
    return adjoint


def up_to(value, multiple):
    return -(-value // multiple) * multiple


def dot(left, right):
    return jnp.dot(left, right, preferred_element_type=jnp.float32)


def dot_nt(left, right):
    return lax.dot_general(left, right, NT_DIMS, preferred_element_type=jnp.float32)


def split_three(value):
    high = value.astype(jnp.bfloat16).astype(jnp.float32)
    middle = (value - high).astype(jnp.bfloat16).astype(jnp.float32)
    return high, middle, value - high - middle


def call(
    kernel, out_shape, args, in_hbm=(), out_hbm=False, scratch=(), flops=0, vmem=VMEM_BYTES
):
    far, near = pl.BlockSpec(memory_space=pl.ANY), pl.BlockSpec(memory_space=pltpu.VMEM)
    bytes_accessed = sum(a.size * a.dtype.itemsize for a in args)
    return pl.pallas_call(
        kernel,
        out_shape=out_shape,
        in_specs=[far if k in in_hbm else near for k in range(len(args))],
        out_specs=jax.tree.map(lambda _: far if out_hbm else near, out_shape),
        scratch_shapes=list(scratch),
        compiler_params=pltpu.CompilerParams(vmem_limit_bytes=vmem),
        cost_estimate=pl.CostEstimate(
            flops=flops, bytes_accessed=bytes_accessed, transcendentals=0
        ),
    )(*args)


class Plan:
    def __init__(self, tiles, chans, fields, owners, observed, w_hidden):
        self.tiles, self.chans = tiles, chans
        self.across, self.along, self.features = fields
        self.own_cols = self.across // 4 * (self.along // 4)
        self.rows = owners[0]
        self.tile_cols = self.rows // tiles
        self.slots = observed[0]
        self.shard = observed[1]
        self.capacity = self.slots // tiles
        self.hidden = w_hidden[1]
        self.group = chans // tiles
        self.chips = chans // self.group
        self.steps = self.chips.bit_length() - 1
        self.lane = up_to(self.along, 128)
        self.flag_at = up_to(self.hidden, 128)
        self.width = max(
            up_to(self.features, 128),
            2 * self.flag_at,
            self.flag_at + up_to(self.slots, 128),
            3 * self.lane,
        )
        self.block = up_to(self.own_cols + 2 + self.across, 16)
        self.per_row = self.own_cols + 2
        self.room = up_to(3 * self.per_row, 16)
        self.patch = 3 * tiles * self.own_cols
        self.deep = up_to(self.features, 16)
        self.strips = self.chips * tiles * self.block

    def order(self, mask):
        return mask % self.group * self.chips + mask // self.group

    def layer(self, refs, k):
        at = k % self.chips * self.deep
        return refs[k // self.chips][at : at + self.features, :]

    def mask(self, k):
        return k % self.chips * self.group + k // self.chips


def prepare_kernel(p, *refs):
    ins, out_ref = refs[:4], refs[4]
    fields_ref, diffusivity_ref, usable_ref, bias_ref, flat, packed, sems = refs[5:]
    copies = [
        pltpu.make_async_copy(source, target, sems.at[k])
        for k, (source, target) in enumerate(zip(ins, refs[5:9]))
    ]
    for copy in copies:
        copy.start()
    flat[...] = jnp.zeros(flat.shape, jnp.float32)
    for copy in copies:
        copy.wait()
    shape = (p.own_cols, p.along)
    row = lax.broadcasted_iota(jnp.int32, shape, 0)
    member = row == lax.broadcasted_iota(jnp.int32, shape, 1) // 4
    total = jnp.dot(
        member.astype(jnp.float32),
        fields_ref[0] + fields_ref[1] + fields_ref[2] + fields_ref[3],
        precision=lax.Precision.HIGHEST,
        preferred_element_type=jnp.float32,
    )
    flat[: p.own_cols, : p.features] = total * 0.0625
    at = p.own_cols
    high, middle, low = split_three(bias_ref[...].reshape(1, p.hidden))
    flat[at : at + 1, : p.hidden] = high
    flat[at : at + 1, p.flag_at : p.flag_at + p.hidden] = middle
    flat[at + 1 : at + 2, : p.hidden] = low
    flags = usable_ref[...].reshape(1, p.slots).astype(jnp.float32)
    flat[at + 1 : at + 2, p.flag_at : p.flag_at + p.slots] = flags
    for k, part in enumerate(split_three(diffusivity_ref[...])):
        flat[at + 2 : at + 2 + p.across, k * p.lane : k * p.lane + p.along] = part
    packed[...] = flat[...].astype(jnp.bfloat16)
    copy = pltpu.make_async_copy(packed, out_ref, sems.at[4])
    copy.start()
    copy.wait()


def place_kernel(p, owners_ref, place_ref, source_ref, cell_ref, *target_refs):
    t, c = lax.axis_index("tile"), lax.axis_index("chan")
    owner = owners_ref[...]
    shape = (p.rows, p.rows)
    row = lax.broadcasted_iota(jnp.int32, shape, 0)
    other = lax.broadcasted_iota(jnp.int32, shape, 1)
    across = jnp.sum(jnp.where(row == other, owner, 0), axis=0, keepdims=True)
    first = lax.broadcasted_iota(jnp.int32, owner.shape, 0)
    begin = first // p.tile_cols * p.tile_cols
    same = (owner == across) & (other >= begin) & (other < row)
    rank = jnp.sum(jnp.where(same, 1, 0), axis=1, keepdims=True)
    tile = first // p.tile_cols
    place_ref[...] = (owner ^ t) * p.slots + tile * p.capacity + rank

    def strip(tile, chan):
        other = chan ^ c
        return p.order(other) * p.tiles + (tile ^ t)

    source_ref[...] = (
        strip(tile, first % p.tile_cols // p.own_cols) * p.block + first % p.own_cols
    )

    row = lax.broadcasted_iota(jnp.int32, cell_ref.shape, 0)
    reach = p.across + 4
    tile = (t + row // reach - 1 + p.tiles) % p.tiles
    cell = c * p.across - 2 + row % reach
    inside = (cell >= 0) & (cell < p.chans * p.across)
    cell = jnp.where(inside, cell, 0)
    wanted = strip(tile, cell // p.across) * p.block + p.own_cols + 2 + cell % p.across
    cell_ref[...] = jnp.where(inside, wanted, -1)

    target = lax.broadcasted_iota(jnp.int32, target_refs[0].shape, 0)
    chip, inner = target // p.patch, target % p.patch
    beside, inner = inner // (p.patch // 3) - 1, inner % (p.patch // 3)
    tile, along = inner // p.own_cols, inner % p.own_cols
    for k, target_ref in enumerate(target_refs):
        row = ((chip ^ (c // p.group)) * p.group + (c % p.group ^ k)) + beside
        wanted = tile * p.tile_cols + row * p.own_cols + along
        target_ref[...] = jnp.where((row >= 0) & (row < p.chans), wanted, -1)


def join_kernel(count, *refs):
    ins, out_ref, sems = refs[:count], refs[-2], refs[-1]
    size = out_ref.shape[0] // count
    copies = [
        pltpu.make_async_copy(
            ref, out_ref.at[k] if ref.ndim < out_ref.ndim else out_ref.at[pl.ds(k * size, size)],
            sems.at[k],
        )
        for k, ref in enumerate(ins)
    ]
    for copy in copies:
        copy.start()
    for copy in copies:
        copy.wait()


def stack_kernel(p, *refs):
    for k, ref in enumerate(refs[: p.chips]):
        refs[-1][k * p.deep : k * p.deep + p.features, :] = ref[...]
        refs[-1][k * p.deep + p.features : (k + 1) * p.deep, :] = jnp.zeros(
            (p.deep - p.features, p.hidden), jnp.bfloat16
        )


def one_hot(wanted, first, count):
    source = lax.broadcasted_iota(jnp.int32, (wanted.shape[0], count), 1)
    return (source + first == wanted).astype(jnp.bfloat16)


def forward_kernel(p, *refs):
    refs = list(refs)
    take = lambda n: [refs.pop(0) for _ in range(n)]
    place_ref, source_ref, cell_ref, bias_ref, w_radiance_ref = take(5)
    strip_refs, weight_refs, seen_refs = take(p.group), take(p.group), take(2)
    part_refs = take(p.steps)
    slope_ref, kappa_ref, active = refs
    c = lax.axis_index("chan")
    gathered = [ref[...] for ref in strip_refs]
    columns = sum(
        dot(one_hot(source_ref[...], k * p.strips, p.strips), strips)
        for k, strips in enumerate(gathered)
    )
    columns = columns.astype(jnp.bfloat16)[:, : p.features]
    for k in range(p.chans):
        member, chip = k // p.chips, k % p.chips
        at = chip * p.tiles * p.block + p.own_cols
        low = strip_refs[member][at : at + 2, :].astype(jnp.float32)
        bias = (
            low[:1, : p.hidden]
            + low[:1, p.flag_at : p.flag_at + p.hidden]
            + low[1:, : p.hidden]
        )
        preact = dot(columns, p.layer(weight_refs, k)) + bias
        squash = jax.nn.sigmoid(preact)
        slope_ref[k] = squash * (1.0 + preact * (1.0 - squash))
        at = pl.multiple_of((c ^ p.mask(k)) * p.hidden, p.hidden)
        active[:, pl.ds(at, p.hidden)] = (preact * squash).astype(jnp.bfloat16)
    part = p.rows // p.steps
    count = seen_refs[0].shape[0]
    for j, part_ref in enumerate(part_refs):
        at = slice(j * part, (j + 1) * part)
        in_use = jnp.zeros((part, 1), jnp.float32)
        for k in range(p.tiles):
            slot = lax.broadcasted_iota(jnp.int32, (part, p.slots), 1) + k * p.slots
            low = k * p.block + p.own_cols + 1
            flags = strip_refs[0][low : low + 1, p.flag_at : p.flag_at + p.slots]
            flags = jnp.where(place_ref[at, :] == slot, flags.astype(jnp.float32), 0.0)
            in_use = in_use + jnp.sum(flags, axis=1, keepdims=True)
        observed = sum(
            dot(one_hot(place_ref[at, :], k * count, count), ref[...])
            for k, ref in enumerate(seen_refs)
        )
        radiance = dot(active[at, :], w_radiance_ref[...]) + bias_ref[...].reshape(1, p.shard)
        part_ref[...] = ((radiance - observed) * in_use).astype(jnp.bfloat16)
    parts = sum(
        dot(one_hot(cell_ref[...], k * p.strips, p.strips), strips)
        for k, strips in enumerate(gathered)
    )
    kappa_ref[...] = sum(parts[:, k * p.lane : (k + 1) * p.lane] for k in range(3))


def choose_kernel(p, choices, *refs):
    refs, out_ref, sems = refs[:-2], refs[-2], refs[-1]
    size = refs[0].shape[0]
    role = (lax.axis_index("chan") // p.group) ^ lax.axis_index("tile")
    for place in range(p.chips):

        @pl.when(role == place)
        def _():
            copies = [
                pltpu.make_async_copy(
                    refs[choices[place, j]], out_ref.at[pl.ds(j * size, size)], sems.at[j]
                )
                for j in range(p.steps)
            ]
            for copy in copies:
                copy.start()
            for copy in copies:
                copy.wait()


def backward_kernel(p, *refs):
    refs = list(refs)
    take = lambda n: [refs.pop(0) for _ in range(n)]
    w_radiance_ref, inv_cov_ref, slope_ref = take(3)
    depart_refs, weight_refs, target_refs = take(p.group), take(p.group), take(p.group)
    out_refs = refs
    c = lax.axis_index("chan")
    cotangent = None
    for k, ref in enumerate(depart_refs):
        at = pl.multiple_of((c % p.group ^ k) * p.shard, p.shard)
        term = dot(ref[...], inv_cov_ref[pl.ds(at, p.shard), :])
        cotangent = term if cotangent is None else cotangent + term
    cotangent = cotangent.astype(jnp.bfloat16)
    total = jnp.zeros((p.rows, p.features), jnp.float32)
    for k in range(p.chans):
        at = pl.multiple_of((c ^ p.mask(k)) * p.hidden, p.hidden)
        grad_hidden = dot_nt(cotangent, w_radiance_ref[pl.ds(at, p.hidden), :])
        grad_pre = (grad_hidden * slope_ref[k]).astype(jnp.bfloat16)
        total = total + dot_nt(grad_pre, p.layer(weight_refs, k))
    total = total.astype(jnp.bfloat16)
    for target_ref, out_ref in zip(target_refs, out_refs):
        out_ref[...] = dot(one_hot(target_ref[...], 0, p.rows), total).astype(jnp.bfloat16)


def add(refs, at=slice(None)):
    total = refs[0][at, :].astype(jnp.float32)
    for ref in refs[1:]:
        total = total + ref[at, :].astype(jnp.float32)
    return total


def add_group_kernel(p, *refs):
    ins, outs = refs[: p.group], refs[p.group :]
    for k, out_ref in enumerate(outs):
        out_ref[...] = add(ins, slice(k * p.patch, (k + 1) * p.patch)).astype(jnp.bfloat16)


def add_chips_kernel(p, *refs):
    ins, outs = refs[: p.chips], refs[p.chips :]
    total = add(ins).astype(jnp.bfloat16)
    shape = (p.room, p.patch)
    target = lax.broadcasted_iota(jnp.int32, shape, 0)
    source = lax.broadcasted_iota(jnp.int32, shape, 1)
    row, along = target // p.per_row, target % p.per_row - 1
    for k, out_ref in enumerate(outs):
        tile = (lax.axis_index("tile") + k) % p.tiles
        cell = (tile * p.own_cols + along + p.tiles * p.own_cols) % (p.tiles * p.own_cols)
        pick = (source == row * (p.tiles * p.own_cols) + cell) & (row < 3)
        out_ref[...] = dot(pick.astype(jnp.bfloat16), total).astype(jnp.bfloat16)


def diffuse_kernel(p, edge, *refs):
    ins, root_ref, out_ref = refs[: p.tiles], refs[-2], refs[-1]
    total = add(ins) * 0.0625
    length = p.along + 2 * edge
    shape = (length, p.room)
    cell = lax.broadcasted_iota(jnp.int32, shape, 0)
    source = lax.broadcasted_iota(jnp.int32, shape, 1)
    column = (cell - edge + 4) // 4
    spread = []
    for k in range(3):
        pick = (source == column + k * p.per_row) & (column >= 0) & (column < p.per_row)
        spread.append(
            jnp.dot(
                pick.astype(jnp.float32),
                total,
                precision=lax.Precision.HIGHEST,
                preferred_element_type=jnp.float32,
            )
        )
    root = root_ref[...]
    state = [spread[(row + 2) // 4] for row in range(p.across + 4)]
    east_of = functools.partial(pltpu.roll, shift=length - 1, axis=0)
    west_of = functools.partial(pltpu.roll, shift=1, axis=0)
    north = root[:, :-1] * root[:, 1:]
    east, west = root * east_of(root), root * west_of(root)
    for sweep in range(2):
        fresh = list(state)
        for row in range(1 + sweep, p.across + 3 - sweep):
            here = state[row]
            fresh[row] = (
                here
                + north[:, row : row + 1] * (state[row + 1] - here)
                + north[:, row - 1 : row] * (state[row - 1] - here)
                + east[:, row : row + 1] * (east_of(here) - here)
                + west[:, row : row + 1] * (west_of(here) - here)
            )
        state = fresh
    for row in range(p.across):
        out_ref[row] = state[row + 2][edge : edge + p.along, : p.features]


def body_by_column(
    fields,
    diffusivity,
    owners,
    observed,
    usable,
    w_hidden,
    b_hidden,
    w_radiance,
    b_radiance,
    inv_cov,
):
    p = Plan(
        lax.axis_size("tile"),
        lax.axis_size("chan"),
        fields.shape,
        owners.shape,
        observed.shape,
        w_hidden.shape,
    )
    half, single = jnp.bfloat16, jnp.float32
    shape = jax.ShapeDtypeStruct
    both = ("tile", "chan")
    everyone = [(a, b) for a in range(p.tiles) for b in range(p.chans)]

    def flip(value, mask):
        return lax.ppermute(value, "chan", [(b, b ^ mask) for b in range(p.chans)])

    def shift(value, by):
        return lax.ppermute(value, "tile", [(a, (a + by) % p.tiles) for a in range(p.tiles)])

    def send(value, wanted):
        pairs = dict(wanted)
        pairs.update({target: source for source, target in wanted.items()})
        for a, b in everyone:
            if (a, b) not in pairs:
                pairs[a, b] = (a, b ^ 1)
        number = lambda place: place[0] * p.chans + place[1]
        return lax.ppermute(
            value, both, sorted((number(a), number(b)) for a, b in pairs.items())
        )

    def join(values, kernel_shape, after=()):
        return call(
            functools.partial(join_kernel, len(values)),
            shape(kernel_shape, half),
            [*values, *after],
            in_hbm=range(len(values) + len(after)),
            out_hbm=True,
            scratch=[pltpu.SemaphoreType.DMA((len(values),))],
            flops=0,
        )

    def grow(value, over, after=()):
        return join([value, over(value)], (2 * value.shape[0],) + value.shape[1:], after)

    def trade(value, mask):
        return lax.ppermute(value, "tile", [(a, a ^ mask) for a in range(p.tiles)])

    strips = call(
        functools.partial(prepare_kernel, p),
        shape((p.block, p.width), half),
        [fields, diffusivity, usable, b_hidden],
        in_hbm=range(4),
        out_hbm=True,
        scratch=[
            pltpu.VMEM(fields.shape, single),
            pltpu.VMEM(diffusivity.shape, single),
            pltpu.VMEM(usable.shape, jnp.int32),
            pltpu.VMEM(b_hidden.shape, single),
            pltpu.VMEM((p.block, p.width), single),
            pltpu.VMEM((p.block, p.width), half),
            pltpu.SemaphoreType.DMA((5,)),
        ],
        vmem=WHOLE_VMEM_BYTES,
    )
    seen, stages = observed, []
    bit = 1
    while bit < p.tiles:
        if 2 * bit < p.tiles:
            seen = grow(seen, lambda value: trade(value, bit))
        strips = grow(strips, lambda value: trade(value, bit), [seen] if 2 * bit == p.tiles else ())
        stages.append(strips)
        bit *= 2
    bit = p.group
    while bit < p.chans:
        strips = grow(strips, lambda value: flip(value, bit))
        stages.append(strips)
        bit *= 2
    strips = [strips] + [flip(strips, k) for k in range(1, p.group)]

    near = [w_hidden] + [flip(w_hidden, chip * p.group) for chip in range(1, p.chips)]
    near = call(
        functools.partial(stack_kernel, p),
        shape((p.chips * p.deep, p.hidden), half),
        near + [stages[-2]],
        in_hbm=[len(near)],
    )
    weights = [near] + [flip(near, k) for k in range(1, p.group)]

    far_half = p.tiles // 2
    seen = [
        seen,
        send(seen, {(b // p.group ^ far_half, b): (b // p.group, b) for b in range(p.chans)}),
    ]

    reach = p.across + 4
    place, source, cell, *targets = call(
        functools.partial(place_kernel, p),
        [shape((p.rows, 1), jnp.int32)] * 2
        + [shape((3 * reach, 1), jnp.int32)]
        + [shape((p.chips * p.patch, 1), jnp.int32)] * p.group,
        [owners],
        flops=SLACK_FLOPS,
    )
    *parts, slope, kappa = call(
        functools.partial(forward_kernel, p),
        [shape((p.rows // p.steps, p.shard), half)] * p.steps
        + [shape((p.chans, p.rows, p.hidden), single), shape((3 * reach, p.lane), single)],
        [place, source, cell, b_radiance, w_radiance] + strips + weights + seen,
        scratch=[pltpu.VMEM((p.rows, p.hidden * p.chans), half)],
        flops=2 * p.rows * p.hidden * p.chans * (p.features + p.shard),
    )

    pool, held, choices = list(parts), {}, {}
    for j in range(p.steps):
        held[0, j] = choices[0, j] = j
    for step in range(p.steps):
        for since in range(-1, step):
            for j in range(p.steps):
                order = [1 << (j + k) % p.steps for k in range(p.steps)]
                roles = [0] if since < 0 else [
                    order[since] + rest
                    for rest in range(p.chips)
                    if rest & ~sum(order[:since]) == 0
                ]
                wanted = {
                    (a, b): (a, b ^ order[step] * p.group)
                    for a, b in everyone
                    if (b // p.group ^ a) in roles
                }
                source = pool[choices[roles[0], j]]
                for role in roles:
                    choices[role + order[step], j] = len(pool)
                pool.append(send(source, wanted))
    chosen = call(
        functools.partial(choose_kernel, p, choices),
        shape((p.rows, p.shard), half),
        pool,
        in_hbm=range(len(pool)),
        out_hbm=True,
        scratch=[pltpu.SemaphoreType.DMA((p.steps,))],
    )
    depart = [chosen] + [flip(chosen, k) for k in range(1, p.group)]

    partial = call(
        functools.partial(backward_kernel, p),
        [shape((p.chips * p.patch, p.features), half)] * p.group,
        [w_radiance, inv_cov, slope] + depart + weights + targets,
        flops=2 * p.rows * (p.hidden * p.chans * (p.features + p.shard) + inv_cov.size),
    )
    partial = [partial[0]] + [flip(partial[k], k) for k in range(1, p.group)]
    partial = call(
        functools.partial(add_group_kernel, p),
        [shape((p.patch, p.features), half)] * p.chips,
        partial,
    )
    partial = [partial[0]] + [flip(partial[k], k * p.group) for k in range(1, p.chips)]
    partial = call(
        functools.partial(add_chips_kernel, p),
        [shape((p.room, p.features), half)] * p.tiles,
        partial,
    )
    partial = [partial[0]] + [shift(partial[k], k) for k in range(1, p.tiles)]

    edge = 8
    kappa = kappa.reshape(3, reach, p.lane)
    root = jnp.sqrt(
        jnp.concatenate(
            [kappa[0, :, p.along - edge : p.along], kappa[1, :, : p.along], kappa[2, :, :edge]],
            axis=1,
        ).T
    )
    return call(
        functools.partial(diffuse_kernel, p, edge),
        shape(fields.shape, single),
        partial + [root],
        flops=100 * fields.size,
    )


def solution(mesh):
    tiles, chans = mesh.shape["tile"], mesh.shape["chan"]
    by_column = tiles > 1 and chans % tiles == 0 and chans & (chans - 1) == 0 and chans > tiles
    placed = (
        P("chan", "tile", None),
        P("chan", "tile"),
        P(),
        P("tile", "chan"),
        P("tile"),
        P(None, "chan"),
        P("chan"),
        P(None, "chan"),
        P("chan"),
        P("tile", "chan"),
    )
    return jax.shard_map(
        body_by_column if by_column else body_by_owner,
        mesh=mesh,
        in_specs=placed,
        out_specs=P("chan", "tile", None),
        check_vma=False,
    )
```

```python
import functools

import jax
import jax.numpy as jnp
from jax import lax
from jax.experimental import pallas as pl
from jax.experimental.pallas import tpu as pltpu
from jax.sharding import PartitionSpec as P

VMEM_BYTES = 24 * 1024 * 1024
WHOLE_VMEM_BYTES = 63 * 1024 * 1024
SLACK_FLOPS = 10**9
NT_DIMS = (((1,), (1,)), ((), ()))


def padded_2(value, sides, width, wrap):
    for axis, dim in sides:
        devices, length = (lax.axis_size(axis), value.shape[dim])
        up = [(i, (i + 1) % devices) for i in range(devices if wrap else devices - 1)]
        down = [(j, i) for i, j in up]
        last = lax.slice_in_dim(value, length - width, length, axis=dim)
        first = lax.slice_in_dim(value, 0, width, axis=dim)
        before = lax.ppermute(last, axis, up)
        after = lax.ppermute(first, axis, down)
        value = jnp.concatenate([before, value, after], axis=dim)
    return value


def add_rims(values):
    rowwise = padded_2(values, (("chan", 0),), 1, False)
    return padded_2(rowwise, (("tile", 1),), 1, True)


def body_by_owner(
    fields,
    diffusivity,
    owners,
    observed,
    usable,
    w_hidden,
    b_hidden,
    w_radiance,
    b_radiance,
    inv_cov,
):
    tile_count = lax.axis_size("tile")
    chan_count = lax.axis_size("chan")
    tile_index = lax.axis_index("tile")
    chan_index = lax.axis_index("chan")
    slot_count = observed.shape[0]
    capacity = slot_count // tile_count
    cells_across, cells_along, features = fields.shape
    own_cols = cells_across // 4 * (cells_along // 4)
    tile_cols = chan_count * own_cols
    hidden_dev = w_hidden.shape[1]
    owner_table = owners[:, 0].reshape(tile_count, tile_cols)
    owner_hits = (
        owner_table[:, :, None] == jnp.arange(tile_count, dtype=jnp.int32)[None, None, :]
    ).astype(jnp.int32)
    before = jnp.sum((jnp.cumsum(owner_hits, axis=1) - owner_hits) * owner_hits, axis=2)
    tallies = jnp.sum(owner_hits, axis=1)
    slot_of = lax.dynamic_index_in_dim(
        owner_table * capacity + before, tile_index, 0, keepdims=False
    )
    arriving = lax.dynamic_index_in_dim(tallies, tile_index, 1, keepdims=False)
    occupied = (jnp.arange(capacity, dtype=jnp.int32)[None, :] < arriving[:, None]).reshape(
        slot_count
    )
    grouped = fields.reshape(cells_across // 4, 4, cells_along // 4, 4, features)
    columns = (
        (jnp.sum(grouped, axis=(1, 3)) * 0.0625).reshape(own_cols, features).astype(jnp.bfloat16)
    )
    placer = (slot_of[None, :] == jnp.arange(slot_count, dtype=jnp.int32)[:, None]).astype(
        jnp.bfloat16
    )
    outgoing = jnp.dot(
        placer,
        lax.all_gather(columns, "chan", axis=0, tiled=True),
        preferred_element_type=jnp.float32,
    )
    incoming = lax.all_to_all(
        outgoing.astype(jnp.bfloat16), "tile", split_axis=0, concat_axis=0, tiled=True
    )
    preact = lax.dot_general(
        w_hidden, incoming, (((0,), (1,)), ((), ())), preferred_element_type=jnp.float32
    )
    preact = preact + b_hidden[:, None]
    squash = jax.nn.sigmoid(preact)
    active = (preact * squash).astype(jnp.bfloat16)
    radiance = lax.dot_general(
        lax.all_gather(active, "chan", axis=0, tiled=True),
        w_radiance,
        (((0,), (0,)), ((), ())),
        preferred_element_type=jnp.float32,
    )
    radiance = radiance + b_radiance[None, :]
    in_use = usable.astype(jnp.float32) * occupied.astype(jnp.float32)
    departure = ((radiance - observed.astype(jnp.float32)) * in_use[:, None]).astype(jnp.bfloat16)
    cotangent = jnp.dot(
        lax.all_gather(departure, "chan", axis=1, tiled=True),
        lax.all_gather(inv_cov, "tile", axis=0, tiled=True),
        preferred_element_type=jnp.float32,
    )
    cotangent = cotangent.astype(jnp.bfloat16)
    full_sum = lax.psum(
        lax.dot_general(w_radiance, cotangent, NT_DIMS, preferred_element_type=jnp.float32),
        "chan",
    )
    grad_hidden = lax.dynamic_slice_in_dim(full_sum, chan_index * hidden_dev, hidden_dev, 0)
    slope_term = squash * (1.0 + preact * (1.0 - squash))
    grad_pre = (grad_hidden * slope_term).astype(jnp.bfloat16)
    part_grad = lax.dot_general(
        grad_pre, w_hidden, (((0,), (1,)), ((), ())), preferred_element_type=jnp.float32
    )
    returned = lax.all_to_all(part_grad, "tile", split_axis=0, concat_axis=0, tiled=True)
    column_grad = lax.psum_scatter(
        jnp.take(returned, slot_of, axis=0), "chan", scatter_dimension=0, tiled=True
    )
    spread = jnp.repeat(
        column_grad.reshape(cells_across // 4, cells_along // 4, features), 4, axis=0
    )
    adjoint = jnp.repeat(spread, 4, axis=1) * 0.0625
    kappa_root = jnp.sqrt(diffusivity)
    root_rim = add_rims(kappa_root)
    coef_north = (kappa_root * root_rim[2:, 1:-1])[:, :, None]
    coef_south = (kappa_root * root_rim[:-2, 1:-1])[:, :, None]
    coef_east = (kappa_root * root_rim[1:-1, 2:])[:, :, None]
    coef_west = (kappa_root * root_rim[1:-1, :-2])[:, :, None]
    for sweep_index in range(2):
        padded = add_rims(adjoint)
        adjoint = (
            adjoint
            + coef_north * (padded[2:, 1:-1] - adjoint)
            + coef_south * (padded[:-2, 1:-1] - adjoint)
            + coef_east * (padded[1:-1, 2:] - adjoint)
            + coef_west * (padded[1:-1, :-2] - adjoint)
        )
    return adjoint


def up_to(value, multiple):
    return -(-value // multiple) * multiple


def dot(left, right):
    return jnp.dot(left, right, preferred_element_type=jnp.float32)


def dot_nt(left, right):
    return lax.dot_general(left, right, NT_DIMS, preferred_element_type=jnp.float32)


def split_three(value):
    high = value.astype(jnp.bfloat16).astype(jnp.float32)
    middle = (value - high).astype(jnp.bfloat16).astype(jnp.float32)
    return high, middle, value - high - middle


def call(
    kernel, out_shape, args, in_hbm=(), out_hbm=False, scratch=(), flops=0, vmem=VMEM_BYTES
):
    far, near = pl.BlockSpec(memory_space=pl.ANY), pl.BlockSpec(memory_space=pltpu.VMEM)
    bytes_accessed = sum(a.size * a.dtype.itemsize for a in args)
    return pl.pallas_call(
        kernel,
        out_shape=out_shape,
        in_specs=[far if k in in_hbm else near for k in range(len(args))],
        out_specs=jax.tree.map(lambda _: far if out_hbm else near, out_shape),
        scratch_shapes=list(scratch),
        compiler_params=pltpu.CompilerParams(vmem_limit_bytes=vmem),
        cost_estimate=pl.CostEstimate(
            flops=flops, bytes_accessed=bytes_accessed, transcendentals=0
        ),
    )(*args)


class Plan:
    def __init__(self, tiles, chans, fields, owners, observed, w_hidden):
        self.tiles, self.chans = tiles, chans
        self.across, self.along, self.features = fields
        self.own_cols = self.across // 4 * (self.along // 4)
        self.rows = owners[0]
        self.tile_cols = self.rows // tiles
        self.slots = observed[0]
        self.shard = observed[1]
        self.capacity = self.slots // tiles
        self.hidden = w_hidden[1]
        self.group = chans // tiles
        self.chips = chans // self.group
        self.steps = self.chips.bit_length() - 1
        self.lane = up_to(self.along, 128)
        self.flag_at = up_to(self.hidden, 128)
        self.width = max(
            up_to(self.features, 128),
            2 * self.flag_at,
            self.flag_at + up_to(self.slots, 128),
            3 * self.lane,
        )
        self.block = up_to(self.own_cols + 2 + self.across, 16)
        self.per_row = self.own_cols + 2
        self.room = up_to(3 * self.per_row, 16)
        self.patch = 3 * tiles * self.own_cols
        self.deep = up_to(self.features, 16)
        self.strips = self.chips * tiles * self.block

    def order(self, mask):
        return mask % self.group * self.chips + mask // self.group

    def layer(self, refs, k):
        each = self.chans // len(refs)
        at = k % each * self.deep
        return refs[k // each][at : at + self.features, :]

    def mask(self, k):
        return k % self.chips * self.group + k // self.chips


def prepare_kernel(p, *refs):
    ins, out_ref = refs[:4], refs[4]
    fields_ref, diffusivity_ref, usable_ref, bias_ref, flat, packed, sems = refs[5:]
    copies = [
        pltpu.make_async_copy(source, target, sems.at[k])
        for k, (source, target) in enumerate(zip(ins, refs[5:9]))
    ]
    for copy in copies:
        copy.start()
    flat[...] = jnp.zeros(flat.shape, jnp.float32)
    for copy in copies:
        copy.wait()
    shape = (p.own_cols, p.along)
    row = lax.broadcasted_iota(jnp.int32, shape, 0)
    member = row == lax.broadcasted_iota(jnp.int32, shape, 1) // 4
    total = jnp.dot(
        member.astype(jnp.float32),
        fields_ref[0] + fields_ref[1] + fields_ref[2] + fields_ref[3],
        precision=lax.Precision.HIGHEST,
        preferred_element_type=jnp.float32,
    )
    flat[: p.own_cols, : p.features] = total * 0.0625
    at = p.own_cols
    high, middle, low = split_three(bias_ref[...].reshape(1, p.hidden))
    flat[at : at + 1, : p.hidden] = high
    flat[at : at + 1, p.flag_at : p.flag_at + p.hidden] = middle
    flat[at + 1 : at + 2, : p.hidden] = low
    flags = usable_ref[...].reshape(1, p.slots).astype(jnp.float32)
    flat[at + 1 : at + 2, p.flag_at : p.flag_at + p.slots] = flags
    for k, part in enumerate(split_three(diffusivity_ref[...])):
        flat[at + 2 : at + 2 + p.across, k * p.lane : k * p.lane + p.along] = part
    packed[...] = flat[...].astype(jnp.bfloat16)
    copy = pltpu.make_async_copy(packed, out_ref, sems.at[4])
    copy.start()
    copy.wait()


def place_kernel(p, owners_ref, place_ref, source_ref, cell_ref, *target_refs):
    t, c = lax.axis_index("tile"), lax.axis_index("chan")
    owner = owners_ref[...]
    shape = (p.rows, p.rows)
    row = lax.broadcasted_iota(jnp.int32, shape, 0)
    other = lax.broadcasted_iota(jnp.int32, shape, 1)
    across = jnp.sum(jnp.where(row == other, owner, 0), axis=0, keepdims=True)
    first = lax.broadcasted_iota(jnp.int32, owner.shape, 0)
    begin = first // p.tile_cols * p.tile_cols
    same = (owner == across) & (other >= begin) & (other < row)
    rank = jnp.sum(jnp.where(same, 1, 0), axis=1, keepdims=True)
    tile = first // p.tile_cols
    place_ref[...] = (owner ^ t) * p.slots + tile * p.capacity + rank

    def strip(tile, chan):
        other = chan ^ c
        return p.order(other) * p.tiles + (tile ^ t)

    source_ref[...] = (
        strip(tile, first % p.tile_cols // p.own_cols) * p.block + first % p.own_cols
    )

    row = lax.broadcasted_iota(jnp.int32, cell_ref.shape, 0)
    reach = p.across + 4
    tile = (t + row // reach - 1 + p.tiles) % p.tiles
    cell = c * p.across - 2 + row % reach
    inside = (cell >= 0) & (cell < p.chans * p.across)
    cell = jnp.where(inside, cell, 0)
    wanted = strip(tile, cell // p.across) * p.block + p.own_cols + 2 + cell % p.across
    cell_ref[...] = jnp.where(inside, wanted, -1)

    target = lax.broadcasted_iota(jnp.int32, target_refs[0].shape, 0)
    chip, inner = target // p.patch, target % p.patch
    beside, inner = inner // (p.patch // 3) - 1, inner % (p.patch // 3)
    tile, along = inner // p.own_cols, inner % p.own_cols
    for k, target_ref in enumerate(target_refs):
        row = ((chip ^ (c // p.group)) * p.group + (c % p.group ^ k)) + beside
        wanted = tile * p.tile_cols + row * p.own_cols + along
        target_ref[...] = jnp.where((row >= 0) & (row < p.chans), wanted, -1)


def join_kernel(count, *refs):
    ins, out_ref, sems = refs[:count], refs[-2], refs[-1]
    size = out_ref.shape[0] // count
    copies = [
        pltpu.make_async_copy(
            ref, out_ref.at[k] if ref.ndim < out_ref.ndim else out_ref.at[pl.ds(k * size, size)],
            sems.at[k],
        )
        for k, ref in enumerate(ins)
    ]
    for copy in copies:
        copy.start()
    for copy in copies:
        copy.wait()


def stack_kernel(p, count, *refs):
    out_ref, first = refs[-1], 0
    for ref in refs[:count]:
        rows = ref.shape[0]
        out_ref[first : first + rows, :] = ref[...]
        first += up_to(rows, 16)
        fill = up_to(rows, 16) - rows
        if fill:
            out_ref[first - fill : first, :] = jnp.zeros((fill, p.hidden), jnp.bfloat16)


def one_hot(wanted, first, count):
    source = lax.broadcasted_iota(jnp.int32, (wanted.shape[0], count), 1)
    return (source + first == wanted).astype(jnp.bfloat16)


def forward_kernel(p, *refs):
    refs = list(refs)
    take = lambda n: [refs.pop(0) for _ in range(n)]
    place_ref, source_ref, cell_ref, bias_ref, w_radiance_ref = take(5)
    strip_refs, weight_refs, seen_refs = take(p.group), take(2 * p.group), take(2)
    part_refs = take(p.steps)
    slope_ref, kappa_ref, active = refs
    c = lax.axis_index("chan")
    gathered = [ref[...] for ref in strip_refs]
    columns = sum(
        dot(one_hot(source_ref[...], k * p.strips, p.strips), strips)
        for k, strips in enumerate(gathered)
    )
    columns = columns.astype(jnp.bfloat16)[:, : p.features]
    for k in range(p.chans):
        member, chip = k // p.chips, k % p.chips
        at = chip * p.tiles * p.block + p.own_cols
        low = strip_refs[member][at : at + 2, :].astype(jnp.float32)
        bias = (
            low[:1, : p.hidden]
            + low[:1, p.flag_at : p.flag_at + p.hidden]
            + low[1:, : p.hidden]
        )
        preact = dot(columns, p.layer(weight_refs, k)) + bias
        squash = jax.nn.sigmoid(preact)
        slope_ref[k] = squash * (1.0 + preact * (1.0 - squash))
        at = pl.multiple_of((c ^ p.mask(k)) * p.hidden, p.hidden)
        active[:, pl.ds(at, p.hidden)] = (preact * squash).astype(jnp.bfloat16)
    part = p.rows // p.steps
    count = seen_refs[0].shape[0]
    for j, part_ref in enumerate(part_refs):
        at = slice(j * part, (j + 1) * part)
        in_use = jnp.zeros((part, 1), jnp.float32)
        for k in range(p.tiles):
            slot = lax.broadcasted_iota(jnp.int32, (part, p.slots), 1) + k * p.slots
            low = k * p.block + p.own_cols + 1
            flags = strip_refs[0][low : low + 1, p.flag_at : p.flag_at + p.slots]
            flags = jnp.where(place_ref[at, :] == slot, flags.astype(jnp.float32), 0.0)
            in_use = in_use + jnp.sum(flags, axis=1, keepdims=True)
        observed = sum(
            dot(one_hot(place_ref[at, :], k * count, count), ref[...])
            for k, ref in enumerate(seen_refs)
        )
        radiance = dot(active[at, :], w_radiance_ref[...]) + bias_ref[...].reshape(1, p.shard)
        part_ref[...] = ((radiance - observed) * in_use).astype(jnp.bfloat16)
    parts = sum(
        dot(one_hot(cell_ref[...], k * p.strips, p.strips), strips)
        for k, strips in enumerate(gathered)
    )
    kappa_ref[...] = sum(parts[:, k * p.lane : (k + 1) * p.lane] for k in range(3))


def choose_kernel(p, choices, *refs):
    refs, out_ref, sems = refs[:-2], refs[-2], refs[-1]
    size = refs[0].shape[0]
    role = (lax.axis_index("chan") // p.group) ^ lax.axis_index("tile")
    for place in range(p.chips):

        @pl.when(role == place)
        def _():
            copies = [
                pltpu.make_async_copy(
                    refs[choices[place, j]], out_ref.at[pl.ds(j * size, size)], sems.at[j]
                )
                for j in range(p.steps)
            ]
            for copy in copies:
                copy.start()
            for copy in copies:
                copy.wait()


def backward_kernel(p, *refs):
    refs = list(refs)
    take = lambda n: [refs.pop(0) for _ in range(n)]
    w_radiance_ref, inv_cov_ref, slope_ref = take(3)
    depart_refs, weight_refs, target_refs = take(p.group), take(2 * p.group), take(p.group)
    out_refs = refs
    c = lax.axis_index("chan")
    cotangent = None
    for k, ref in enumerate(depart_refs):
        at = pl.multiple_of((c % p.group ^ k) * p.shard, p.shard)
        term = dot(ref[...], inv_cov_ref[pl.ds(at, p.shard), :])
        cotangent = term if cotangent is None else cotangent + term
    cotangent = cotangent.astype(jnp.bfloat16)
    total = jnp.zeros((p.rows, p.features), jnp.float32)
    for k in range(p.chans):
        at = pl.multiple_of((c ^ p.mask(k)) * p.hidden, p.hidden)
        grad_hidden = dot_nt(cotangent, w_radiance_ref[pl.ds(at, p.hidden), :])
        grad_pre = (grad_hidden * slope_ref[k]).astype(jnp.bfloat16)
        total = total + dot_nt(grad_pre, p.layer(weight_refs, k))
    total = total.astype(jnp.bfloat16)
    for target_ref, out_ref in zip(target_refs, out_refs):
        out_ref[...] = dot(one_hot(target_ref[...], 0, p.rows), total).astype(jnp.bfloat16)


def add(refs, at=slice(None)):
    total = refs[0][at, :].astype(jnp.float32)
    for ref in refs[1:]:
        total = total + ref[at, :].astype(jnp.float32)
    return total


def add_group_kernel(p, *refs):
    ins, outs = refs[: p.group], refs[p.group :]
    for k, out_ref in enumerate(outs):
        out_ref[...] = add(ins, slice(k * p.patch, (k + 1) * p.patch)).astype(jnp.bfloat16)


def add_chips_kernel(p, *refs):
    ins, outs = refs[: p.chips], refs[p.chips :]
    total = add(ins).astype(jnp.bfloat16)
    shape = (p.room, p.patch)
    target = lax.broadcasted_iota(jnp.int32, shape, 0)
    source = lax.broadcasted_iota(jnp.int32, shape, 1)
    row, along = target // p.per_row, target % p.per_row - 1
    for k, out_ref in enumerate(outs):
        tile = (lax.axis_index("tile") + k) % p.tiles
        cell = (tile * p.own_cols + along + p.tiles * p.own_cols) % (p.tiles * p.own_cols)
        pick = (source == row * (p.tiles * p.own_cols) + cell) & (row < 3)
        out_ref[...] = dot(pick.astype(jnp.bfloat16), total).astype(jnp.bfloat16)


def diffuse_kernel(p, edge, *refs):
    ins, root_ref, out_ref = refs[: p.tiles], refs[-2], refs[-1]
    total = add(ins) * 0.0625
    length = p.along + 2 * edge
    shape = (length, p.room)
    cell = lax.broadcasted_iota(jnp.int32, shape, 0)
    source = lax.broadcasted_iota(jnp.int32, shape, 1)
    column = (cell - edge + 4) // 4
    spread = []
    for k in range(3):
        pick = (source == column + k * p.per_row) & (column >= 0) & (column < p.per_row)
        spread.append(
            jnp.dot(
                pick.astype(jnp.float32),
                total,
                precision=lax.Precision.HIGHEST,
                preferred_element_type=jnp.float32,
            )
        )
    root = root_ref[...]
    state = [spread[(row + 2) // 4] for row in range(p.across + 4)]
    east_of = functools.partial(pltpu.roll, shift=length - 1, axis=0)
    west_of = functools.partial(pltpu.roll, shift=1, axis=0)
    north = root[:, :-1] * root[:, 1:]
    east, west = root * east_of(root), root * west_of(root)
    for sweep in range(2):
        fresh = list(state)
        for row in range(1 + sweep, p.across + 3 - sweep):
            here = state[row]
            fresh[row] = (
                here
                + north[:, row : row + 1] * (state[row + 1] - here)
                + north[:, row - 1 : row] * (state[row - 1] - here)
                + east[:, row : row + 1] * (east_of(here) - here)
                + west[:, row : row + 1] * (west_of(here) - here)
            )
        state = fresh
    for row in range(p.across):
        out_ref[row] = state[row + 2][edge : edge + p.along, : p.features]


def body_by_column(
    fields,
    diffusivity,
    owners,
    observed,
    usable,
    w_hidden,
    b_hidden,
    w_radiance,
    b_radiance,
    inv_cov,
):
    p = Plan(
        lax.axis_size("tile"),
        lax.axis_size("chan"),
        fields.shape,
        owners.shape,
        observed.shape,
        w_hidden.shape,
    )
    half, single = jnp.bfloat16, jnp.float32
    shape = jax.ShapeDtypeStruct
    both = ("tile", "chan")
    everyone = [(a, b) for a in range(p.tiles) for b in range(p.chans)]

    def flip(value, mask):
        return lax.ppermute(value, "chan", [(b, b ^ mask) for b in range(p.chans)])

    def shift(value, by):
        return lax.ppermute(value, "tile", [(a, (a + by) % p.tiles) for a in range(p.tiles)])

    def send(value, wanted):
        pairs = dict(wanted)
        pairs.update({target: source for source, target in wanted.items()})
        for a, b in everyone:
            if (a, b) not in pairs:
                pairs[a, b] = (a, b ^ 1)
        number = lambda place: place[0] * p.chans + place[1]
        return lax.ppermute(
            value, both, sorted((number(a), number(b)) for a, b in pairs.items())
        )

    def join(values, kernel_shape, after=()):
        return call(
            functools.partial(join_kernel, len(values)),
            shape(kernel_shape, half),
            [*values, *after],
            in_hbm=range(len(values) + len(after)),
            out_hbm=True,
            scratch=[pltpu.SemaphoreType.DMA((len(values),))],
            flops=0,
        )

    def trade(value, mask):
        return lax.ppermute(value, "tile", [(a, a ^ mask) for a in range(p.tiles)])

    strips = call(
        functools.partial(prepare_kernel, p),
        shape((p.block, p.width), half),
        [fields, diffusivity, usable, b_hidden],
        in_hbm=range(4),
        out_hbm=True,
        scratch=[
            pltpu.VMEM(fields.shape, single),
            pltpu.VMEM(diffusivity.shape, single),
            pltpu.VMEM(usable.shape, jnp.int32),
            pltpu.VMEM(b_hidden.shape, single),
            pltpu.VMEM((p.block, p.width), single),
            pltpu.VMEM((p.block, p.width), half),
            pltpu.SemaphoreType.DMA((5,)),
        ],
        vmem=WHOLE_VMEM_BYTES,
    )
    strips, w_hidden, observed = lax.optimization_barrier((strips, w_hidden, observed))

    seen, bit = observed, 1
    while 2 * bit < p.tiles:
        seen = join([seen, trade(seen, bit)], (2 * seen.shape[0], p.shard))
        bit *= 2
    seen = [
        seen,
        send(seen, {(b // p.group ^ bit, b): (b // p.group, b) for b in range(p.chans)}),
    ]

    strips = [strips] + [trade(strips, k) for k in range(1, p.tiles)]
    strips = join(strips, (p.tiles * p.block, p.width), [seen[0]])

    near, count, bit = w_hidden, 1, p.group
    while 2 * bit < p.chans:
        near = call(
            functools.partial(stack_kernel, p, 2),
            shape((2 * count * p.deep, p.hidden), half),
            [near, flip(near, bit), strips],
            in_hbm=[2],
        )
        count, bit = 2 * count, 2 * bit
    near = [near, flip(near, bit)]
    strips = [strips] + [flip(strips, k * p.group) for k in range(1, p.chips)]
    strips = join(strips, (p.strips, p.width))
    strips, seen, *near = lax.optimization_barrier((strips, seen, *near))
    strips = [strips] + [flip(strips, k) for k in range(1, p.group)]
    weights = near + [flip(value, k) for k in range(1, p.group) for value in near]

    reach = p.across + 4
    place, source, cell, *targets = call(
        functools.partial(place_kernel, p),
        [shape((p.rows, 1), jnp.int32)] * 2
        + [shape((3 * reach, 1), jnp.int32)]
        + [shape((p.chips * p.patch, 1), jnp.int32)] * p.group,
        [owners],
        flops=SLACK_FLOPS,
    )
    *parts, slope, kappa = call(
        functools.partial(forward_kernel, p),
        [shape((p.rows // p.steps, p.shard), half)] * p.steps
        + [shape((p.chans, p.rows, p.hidden), single), shape((3 * reach, p.lane), single)],
        [place, source, cell, b_radiance, w_radiance] + strips + weights + seen,
        scratch=[pltpu.VMEM((p.rows, p.hidden * p.chans), half)],
        flops=2 * p.rows * p.hidden * p.chans * (p.features + p.shard),
    )

    pool, held, choices = list(parts), {}, {}
    for j in range(p.steps):
        held[0, j] = choices[0, j] = j
    for step in range(p.steps):
        for since in range(-1, step):
            for j in range(p.steps):
                order = [1 << (j + k) % p.steps for k in range(p.steps)]
                roles = [0] if since < 0 else [
                    order[since] + rest
                    for rest in range(p.chips)
                    if rest & ~sum(order[:since]) == 0
                ]
                wanted = {
                    (a, b): (a, b ^ order[step] * p.group)
                    for a, b in everyone
                    if (b // p.group ^ a) in roles
                }
                source = pool[choices[roles[0], j]]
                for role in roles:
                    choices[role + order[step], j] = len(pool)
                pool.append(send(source, wanted))
    chosen = call(
        functools.partial(choose_kernel, p, choices),
        shape((p.rows, p.shard), half),
        pool,
        in_hbm=range(len(pool)),
        out_hbm=True,
        scratch=[pltpu.SemaphoreType.DMA((p.steps,))],
    )
    depart = [chosen] + [flip(chosen, k) for k in range(1, p.group)]

    partial = call(
        functools.partial(backward_kernel, p),
        [shape((p.chips * p.patch, p.features), half)] * p.group,
        [w_radiance, inv_cov, slope] + depart + weights + targets,
        flops=2 * p.rows * (p.hidden * p.chans * (p.features + p.shard) + inv_cov.size),
    )
    partial = [partial[0]] + [flip(partial[k], k) for k in range(1, p.group)]
    partial = call(
        functools.partial(add_group_kernel, p),
        [shape((p.patch, p.features), half)] * p.chips,
        partial,
    )
    partial = [partial[0]] + [flip(partial[k], k * p.group) for k in range(1, p.chips)]
    partial = call(
        functools.partial(add_chips_kernel, p),
        [shape((p.room, p.features), half)] * p.tiles,
        partial,
    )
    partial = [partial[0]] + [shift(partial[k], k) for k in range(1, p.tiles)]

    edge = 8
    kappa = kappa.reshape(3, reach, p.lane)
    root = jnp.sqrt(
        jnp.concatenate(
            [kappa[0, :, p.along - edge : p.along], kappa[1, :, : p.along], kappa[2, :, :edge]],
            axis=1,
        ).T
    )
    return call(
        functools.partial(diffuse_kernel, p, edge),
        shape(fields.shape, single),
        partial + [root],
        flops=100 * fields.size,
    )


def solution(mesh):
    tiles, chans = mesh.shape["tile"], mesh.shape["chan"]
    by_column = tiles > 1 and chans % tiles == 0 and chans & (chans - 1) == 0 and chans > tiles
    placed = (
        P("chan", "tile", None),
        P("chan", "tile"),
        P(),
        P("tile", "chan"),
        P("tile"),
        P(None, "chan"),
        P("chan"),
        P(None, "chan"),
        P("chan"),
        P("tile", "chan"),
    )
    return jax.shard_map(
        body_by_column if by_column else body_by_owner,
        mesh=mesh,
        in_specs=placed,
        out_specs=P("chan", "tile", None),
        check_vma=False,
    )
```

```python
import functools

import jax
import jax.numpy as jnp
from jax import lax
from jax.experimental import pallas as pl
from jax.experimental.pallas import tpu as pltpu
from jax.sharding import PartitionSpec as P

VMEM_BYTES = 24 * 1024 * 1024
WHOLE_VMEM_BYTES = 63 * 1024 * 1024
SLACK_FLOPS = 10**9
NT_DIMS = (((1,), (1,)), ((), ()))


def padded_2(value, sides, width, wrap):
    for axis, dim in sides:
        devices, length = (lax.axis_size(axis), value.shape[dim])
        up = [(i, (i + 1) % devices) for i in range(devices if wrap else devices - 1)]
        down = [(j, i) for i, j in up]
        last = lax.slice_in_dim(value, length - width, length, axis=dim)
        first = lax.slice_in_dim(value, 0, width, axis=dim)
        before = lax.ppermute(last, axis, up)
        after = lax.ppermute(first, axis, down)
        value = jnp.concatenate([before, value, after], axis=dim)
    return value


def add_rims(values):
    rowwise = padded_2(values, (("chan", 0),), 1, False)
    return padded_2(rowwise, (("tile", 1),), 1, True)


def body_by_owner(
    fields,
    diffusivity,
    owners,
    observed,
    usable,
    w_hidden,
    b_hidden,
    w_radiance,
    b_radiance,
    inv_cov,
):
    tile_count = lax.axis_size("tile")
    chan_count = lax.axis_size("chan")
    tile_index = lax.axis_index("tile")
    chan_index = lax.axis_index("chan")
    slot_count = observed.shape[0]
    capacity = slot_count // tile_count
    cells_across, cells_along, features = fields.shape
    own_cols = cells_across // 4 * (cells_along // 4)
    tile_cols = chan_count * own_cols
    hidden_dev = w_hidden.shape[1]
    owner_table = owners[:, 0].reshape(tile_count, tile_cols)
    owner_hits = (
        owner_table[:, :, None] == jnp.arange(tile_count, dtype=jnp.int32)[None, None, :]
    ).astype(jnp.int32)
    before = jnp.sum((jnp.cumsum(owner_hits, axis=1) - owner_hits) * owner_hits, axis=2)
    tallies = jnp.sum(owner_hits, axis=1)
    slot_of = lax.dynamic_index_in_dim(
        owner_table * capacity + before, tile_index, 0, keepdims=False
    )
    arriving = lax.dynamic_index_in_dim(tallies, tile_index, 1, keepdims=False)
    occupied = (jnp.arange(capacity, dtype=jnp.int32)[None, :] < arriving[:, None]).reshape(
        slot_count
    )
    grouped = fields.reshape(cells_across // 4, 4, cells_along // 4, 4, features)
    columns = (
        (jnp.sum(grouped, axis=(1, 3)) * 0.0625).reshape(own_cols, features).astype(jnp.bfloat16)
    )
    placer = (slot_of[None, :] == jnp.arange(slot_count, dtype=jnp.int32)[:, None]).astype(
        jnp.bfloat16
    )
    outgoing = jnp.dot(
        placer,
        lax.all_gather(columns, "chan", axis=0, tiled=True),
        preferred_element_type=jnp.float32,
    )
    incoming = lax.all_to_all(
        outgoing.astype(jnp.bfloat16), "tile", split_axis=0, concat_axis=0, tiled=True
    )
    preact = lax.dot_general(
        w_hidden, incoming, (((0,), (1,)), ((), ())), preferred_element_type=jnp.float32
    )
    preact = preact + b_hidden[:, None]
    squash = jax.nn.sigmoid(preact)
    active = (preact * squash).astype(jnp.bfloat16)
    radiance = lax.dot_general(
        lax.all_gather(active, "chan", axis=0, tiled=True),
        w_radiance,
        (((0,), (0,)), ((), ())),
        preferred_element_type=jnp.float32,
    )
    radiance = radiance + b_radiance[None, :]
    in_use = usable.astype(jnp.float32) * occupied.astype(jnp.float32)
    departure = ((radiance - observed.astype(jnp.float32)) * in_use[:, None]).astype(jnp.bfloat16)
    cotangent = jnp.dot(
        lax.all_gather(departure, "chan", axis=1, tiled=True),
        lax.all_gather(inv_cov, "tile", axis=0, tiled=True),
        preferred_element_type=jnp.float32,
    )
    cotangent = cotangent.astype(jnp.bfloat16)
    full_sum = lax.psum(
        lax.dot_general(w_radiance, cotangent, NT_DIMS, preferred_element_type=jnp.float32),
        "chan",
    )
    grad_hidden = lax.dynamic_slice_in_dim(full_sum, chan_index * hidden_dev, hidden_dev, 0)
    slope_term = squash * (1.0 + preact * (1.0 - squash))
    grad_pre = (grad_hidden * slope_term).astype(jnp.bfloat16)
    part_grad = lax.dot_general(
        grad_pre, w_hidden, (((0,), (1,)), ((), ())), preferred_element_type=jnp.float32
    )
    returned = lax.all_to_all(part_grad, "tile", split_axis=0, concat_axis=0, tiled=True)
    column_grad = lax.psum_scatter(
        jnp.take(returned, slot_of, axis=0), "chan", scatter_dimension=0, tiled=True
    )
    spread = jnp.repeat(
        column_grad.reshape(cells_across // 4, cells_along // 4, features), 4, axis=0
    )
    adjoint = jnp.repeat(spread, 4, axis=1) * 0.0625
    kappa_root = jnp.sqrt(diffusivity)
    root_rim = add_rims(kappa_root)
    coef_north = (kappa_root * root_rim[2:, 1:-1])[:, :, None]
    coef_south = (kappa_root * root_rim[:-2, 1:-1])[:, :, None]
    coef_east = (kappa_root * root_rim[1:-1, 2:])[:, :, None]
    coef_west = (kappa_root * root_rim[1:-1, :-2])[:, :, None]
    for sweep_index in range(2):
        padded = add_rims(adjoint)
        adjoint = (
            adjoint
            + coef_north * (padded[2:, 1:-1] - adjoint)
            + coef_south * (padded[:-2, 1:-1] - adjoint)
            + coef_east * (padded[1:-1, 2:] - adjoint)
            + coef_west * (padded[1:-1, :-2] - adjoint)
        )
    return adjoint


def up_to(value, multiple):
    return -(-value // multiple) * multiple


def dot(left, right):
    return jnp.dot(left, right, preferred_element_type=jnp.float32)


def dot_nt(left, right):
    return lax.dot_general(left, right, NT_DIMS, preferred_element_type=jnp.float32)


def split_three(value):
    high = value.astype(jnp.bfloat16).astype(jnp.float32)
    middle = (value - high).astype(jnp.bfloat16).astype(jnp.float32)
    return high, middle, value - high - middle


def call(
    kernel, out_shape, args, in_hbm=(), out_hbm=False, scratch=(), flops=0, vmem=VMEM_BYTES
):
    far, near = pl.BlockSpec(memory_space=pl.ANY), pl.BlockSpec(memory_space=pltpu.VMEM)
    bytes_accessed = sum(a.size * a.dtype.itemsize for a in args)
    return pl.pallas_call(
        kernel,
        out_shape=out_shape,
        in_specs=[far if k in in_hbm else near for k in range(len(args))],
        out_specs=jax.tree.map(lambda _: far if out_hbm else near, out_shape),
        scratch_shapes=list(scratch),
        compiler_params=pltpu.CompilerParams(vmem_limit_bytes=vmem),
        cost_estimate=pl.CostEstimate(
            flops=flops, bytes_accessed=bytes_accessed, transcendentals=0
        ),
    )(*args)


class Plan:
    def __init__(self, tiles, chans, fields, owners, observed, w_hidden):
        self.tiles, self.chans = tiles, chans
        self.across, self.along, self.features = fields
        self.own_cols = self.across // 4 * (self.along // 4)
        self.rows = owners[0]
        self.tile_cols = self.rows // tiles
        self.slots = observed[0]
        self.shard = observed[1]
        self.capacity = self.slots // tiles
        self.hidden = w_hidden[1]
        self.group = chans // tiles
        self.chips = chans // self.group
        self.steps = self.chips.bit_length() - 1
        self.lane = up_to(self.along, 128)
        self.flag_at = up_to(self.hidden, 128)
        self.width = max(
            up_to(self.features, 128),
            2 * self.flag_at,
            self.flag_at + up_to(self.slots, 128),
            3 * self.lane,
        )
        self.block = up_to(self.own_cols + 2 + self.across, 16)
        self.per_row = self.own_cols + 2
        self.room = up_to(3 * self.per_row, 16)
        self.patch = 3 * tiles * self.own_cols
        self.deep = up_to(self.features, 16)
        self.strips = self.chips * tiles * self.block

    def order(self, mask):
        return mask % self.group * self.chips + mask // self.group

    def layer(self, refs, k):
        at = k % self.chips * self.deep
        return refs[k // self.chips][at : at + self.features, :]

    def mask(self, k):
        return k % self.chips * self.group + k // self.chips


def prepare_kernel(p, *refs):
    ins, out_ref = refs[:4], refs[4]
    fields_ref, diffusivity_ref, usable_ref, bias_ref, flat, packed, sems = refs[5:]
    copies = [
        pltpu.make_async_copy(source, target, sems.at[k])
        for k, (source, target) in enumerate(zip(ins, refs[5:9]))
    ]
    for copy in copies:
        copy.start()
    flat[...] = jnp.zeros(flat.shape, jnp.float32)
    for copy in copies:
        copy.wait()
    shape = (p.own_cols, p.along)
    row = lax.broadcasted_iota(jnp.int32, shape, 0)
    member = row == lax.broadcasted_iota(jnp.int32, shape, 1) // 4
    total = jnp.dot(
        member.astype(jnp.float32),
        fields_ref[0] + fields_ref[1] + fields_ref[2] + fields_ref[3],
        precision=lax.Precision.HIGHEST,
        preferred_element_type=jnp.float32,
    )
    flat[: p.own_cols, : p.features] = total * 0.0625
    at = p.own_cols
    high, middle, low = split_three(bias_ref[...].reshape(1, p.hidden))
    flat[at : at + 1, : p.hidden] = high
    flat[at : at + 1, p.flag_at : p.flag_at + p.hidden] = middle
    flat[at + 1 : at + 2, : p.hidden] = low
    flags = usable_ref[...].reshape(1, p.slots).astype(jnp.float32)
    flat[at + 1 : at + 2, p.flag_at : p.flag_at + p.slots] = flags
    for k, part in enumerate(split_three(diffusivity_ref[...])):
        flat[at + 2 : at + 2 + p.across, k * p.lane : k * p.lane + p.along] = part
    packed[...] = flat[...].astype(jnp.bfloat16)
    copy = pltpu.make_async_copy(packed, out_ref, sems.at[4])
    copy.start()
    copy.wait()


def place_kernel(p, owners_ref, place_ref, source_ref, cell_ref, *target_refs):
    t, c = lax.axis_index("tile"), lax.axis_index("chan")
    owner = owners_ref[...]
    shape = (p.rows, p.rows)
    row = lax.broadcasted_iota(jnp.int32, shape, 0)
    other = lax.broadcasted_iota(jnp.int32, shape, 1)
    across = jnp.sum(jnp.where(row == other, owner, 0), axis=0, keepdims=True)
    first = lax.broadcasted_iota(jnp.int32, owner.shape, 0)
    begin = first // p.tile_cols * p.tile_cols
    same = (owner == across) & (other >= begin) & (other < row)
    rank = jnp.sum(jnp.where(same, 1, 0), axis=1, keepdims=True)
    tile = first // p.tile_cols
    place_ref[...] = (owner ^ t) * p.slots + tile * p.capacity + rank

    def strip(tile, chan):
        other = chan ^ c
        return p.order(other) * p.tiles + (tile ^ t)

    source_ref[...] = (
        strip(tile, first % p.tile_cols // p.own_cols) * p.block + first % p.own_cols
    )

    row = lax.broadcasted_iota(jnp.int32, cell_ref.shape, 0)
    reach = p.across + 4
    tile = (t + row // reach - 1 + p.tiles) % p.tiles
    cell = c * p.across - 2 + row % reach
    inside = (cell >= 0) & (cell < p.chans * p.across)
    cell = jnp.where(inside, cell, 0)
    wanted = strip(tile, cell // p.across) * p.block + p.own_cols + 2 + cell % p.across
    cell_ref[...] = jnp.where(inside, wanted, -1)

    target = lax.broadcasted_iota(jnp.int32, target_refs[0].shape, 0)
    chip, inner = target // p.patch, target % p.patch
    beside, inner = inner // (p.patch // 3) - 1, inner % (p.patch // 3)
    tile, along = inner // p.own_cols, inner % p.own_cols
    for k, target_ref in enumerate(target_refs):
        row = ((chip ^ (c // p.group)) * p.group + (c % p.group ^ k)) + beside
        wanted = tile * p.tile_cols + row * p.own_cols + along
        target_ref[...] = jnp.where((row >= 0) & (row < p.chans), wanted, -1)


def join_kernel(count, *refs):
    ins, out_ref, sems = refs[:count], refs[-2], refs[-1]
    size = out_ref.shape[0] // count
    copies = [
        pltpu.make_async_copy(
            ref, out_ref.at[k] if ref.ndim < out_ref.ndim else out_ref.at[pl.ds(k * size, size)],
            sems.at[k],
        )
        for k, ref in enumerate(ins)
    ]
    for copy in copies:
        copy.start()
    for copy in copies:
        copy.wait()


def stack_kernel(p, *refs):
    for k, ref in enumerate(refs[: p.chips]):
        refs[-1][k * p.deep : k * p.deep + p.features, :] = ref[...]
        refs[-1][k * p.deep + p.features : (k + 1) * p.deep, :] = jnp.zeros(
            (p.deep - p.features, p.hidden), jnp.bfloat16
        )


def one_hot(wanted, first, count):
    source = lax.broadcasted_iota(jnp.int32, (wanted.shape[0], count), 1)
    return (source + first == wanted).astype(jnp.bfloat16)


def forward_kernel(p, *refs):
    refs = list(refs)
    take = lambda n: [refs.pop(0) for _ in range(n)]
    place_ref, source_ref, cell_ref, bias_ref, w_radiance_ref = take(5)
    strip_refs, weight_refs, seen_refs = take(p.group), take(p.group), take(2)
    part_refs = take(p.steps)
    slope_ref, kappa_ref, active = refs
    c = lax.axis_index("chan")
    gathered = [ref[...] for ref in strip_refs]
    columns = sum(
        dot(one_hot(source_ref[...], k * p.strips, p.strips), strips)
        for k, strips in enumerate(gathered)
    )
    columns = columns.astype(jnp.bfloat16)[:, : p.features]
    for k in range(p.chans):
        member, chip = k // p.chips, k % p.chips
        at = chip * p.tiles * p.block + p.own_cols
        low = strip_refs[member][at : at + 2, :].astype(jnp.float32)
        bias = (
            low[:1, : p.hidden]
            + low[:1, p.flag_at : p.flag_at + p.hidden]
            + low[1:, : p.hidden]
        )
        preact = dot(columns, p.layer(weight_refs, k)) + bias
        squash = jax.nn.sigmoid(preact)
        slope_ref[k] = squash * (1.0 + preact * (1.0 - squash))
        at = pl.multiple_of((c ^ p.mask(k)) * p.hidden, p.hidden)
        active[:, pl.ds(at, p.hidden)] = (preact * squash).astype(jnp.bfloat16)
    part = p.rows // p.steps
    count = seen_refs[0].shape[0]
    for j, part_ref in enumerate(part_refs):
        at = slice(j * part, (j + 1) * part)
        in_use = jnp.zeros((part, 1), jnp.float32)
        for k in range(p.tiles):
            slot = lax.broadcasted_iota(jnp.int32, (part, p.slots), 1) + k * p.slots
            low = k * p.block + p.own_cols + 1
            flags = strip_refs[0][low : low + 1, p.flag_at : p.flag_at + p.slots]
            flags = jnp.where(place_ref[at, :] == slot, flags.astype(jnp.float32), 0.0)
            in_use = in_use + jnp.sum(flags, axis=1, keepdims=True)
        observed = sum(
            dot(one_hot(place_ref[at, :], k * count, count), ref[...])
            for k, ref in enumerate(seen_refs)
        )
        radiance = dot(active[at, :], w_radiance_ref[...]) + bias_ref[...].reshape(1, p.shard)
        part_ref[...] = ((radiance - observed) * in_use).astype(jnp.bfloat16)
    parts = sum(
        dot(one_hot(cell_ref[...], k * p.strips, p.strips), strips)
        for k, strips in enumerate(gathered)
    )
    kappa_ref[...] = sum(parts[:, k * p.lane : (k + 1) * p.lane] for k in range(3))


def choose_kernel(p, choices, *refs):
    refs, out_ref, sems = refs[:-2], refs[-2], refs[-1]
    size = refs[0].shape[0]
    role = (lax.axis_index("chan") // p.group) ^ lax.axis_index("tile")
    for place in range(p.chips):

        @pl.when(role == place)
        def _():
            copies = [
                pltpu.make_async_copy(
                    refs[choices[place, j]], out_ref.at[pl.ds(j * size, size)], sems.at[j]
                )
                for j in range(p.steps)
            ]
            for copy in copies:
                copy.start()
            for copy in copies:
                copy.wait()


def backward_kernel(p, *refs):
    refs = list(refs)
    take = lambda n: [refs.pop(0) for _ in range(n)]
    w_radiance_ref, inv_cov_ref, slope_ref = take(3)
    depart_refs, weight_refs, target_refs = take(p.group), take(p.group), take(p.group)
    out_refs = refs
    c = lax.axis_index("chan")
    cotangent = None
    for k, ref in enumerate(depart_refs):
        at = pl.multiple_of((c % p.group ^ k) * p.shard, p.shard)
        term = dot(ref[...], inv_cov_ref[pl.ds(at, p.shard), :])
        cotangent = term if cotangent is None else cotangent + term
    cotangent = cotangent.astype(jnp.bfloat16)
    total = jnp.zeros((p.rows, p.features), jnp.float32)
    for k in range(p.chans):
        at = pl.multiple_of((c ^ p.mask(k)) * p.hidden, p.hidden)
        grad_hidden = dot_nt(cotangent, w_radiance_ref[pl.ds(at, p.hidden), :])
        grad_pre = (grad_hidden * slope_ref[k]).astype(jnp.bfloat16)
        total = total + dot_nt(grad_pre, p.layer(weight_refs, k))
    total = total.astype(jnp.bfloat16)
    for target_ref, out_ref in zip(target_refs, out_refs):
        out_ref[...] = dot(one_hot(target_ref[...], 0, p.rows), total).astype(jnp.bfloat16)


def add(refs, at=slice(None)):
    total = refs[0][at, :].astype(jnp.float32)
    for ref in refs[1:]:
        total = total + ref[at, :].astype(jnp.float32)
    return total


def add_group_kernel(p, *refs):
    ins, outs = refs[: p.group], refs[p.group :]
    for k, out_ref in enumerate(outs):
        out_ref[...] = add(ins, slice(k * p.patch, (k + 1) * p.patch)).astype(jnp.bfloat16)


def add_chips_kernel(p, *refs):
    ins, outs = refs[: p.chips], refs[p.chips :]
    total = add(ins).astype(jnp.bfloat16)
    shape = (p.room, p.patch)
    target = lax.broadcasted_iota(jnp.int32, shape, 0)
    source = lax.broadcasted_iota(jnp.int32, shape, 1)
    row, along = target // p.per_row, target % p.per_row - 1
    for k, out_ref in enumerate(outs):
        tile = (lax.axis_index("tile") + k) % p.tiles
        cell = (tile * p.own_cols + along + p.tiles * p.own_cols) % (p.tiles * p.own_cols)
        pick = (source == row * (p.tiles * p.own_cols) + cell) & (row < 3)
        out_ref[...] = dot(pick.astype(jnp.bfloat16), total).astype(jnp.bfloat16)


def diffuse_kernel(p, edge, *refs):
    ins, root_ref, out_ref = refs[: p.tiles], refs[-2], refs[-1]
    total = add(ins) * 0.0625
    length = p.along + 2 * edge
    shape = (length, p.room)
    cell = lax.broadcasted_iota(jnp.int32, shape, 0)
    source = lax.broadcasted_iota(jnp.int32, shape, 1)
    column = (cell - edge + 4) // 4
    spread = []
    for k in range(3):
        pick = (source == column + k * p.per_row) & (column >= 0) & (column < p.per_row)
        spread.append(
            jnp.dot(
                pick.astype(jnp.float32),
                total,
                precision=lax.Precision.HIGHEST,
                preferred_element_type=jnp.float32,
            )
        )
    root = root_ref[...]
    state = [spread[(row + 2) // 4] for row in range(p.across + 4)]
    east_of = functools.partial(pltpu.roll, shift=length - 1, axis=0)
    west_of = functools.partial(pltpu.roll, shift=1, axis=0)
    north = root[:, :-1] * root[:, 1:]
    east, west = root * east_of(root), root * west_of(root)
    for sweep in range(2):
        fresh = list(state)
        for row in range(1 + sweep, p.across + 3 - sweep):
            here = state[row]
            fresh[row] = (
                here
                + north[:, row : row + 1] * (state[row + 1] - here)
                + north[:, row - 1 : row] * (state[row - 1] - here)
                + east[:, row : row + 1] * (east_of(here) - here)
                + west[:, row : row + 1] * (west_of(here) - here)
            )
        state = fresh
    for row in range(p.across):
        out_ref[row] = state[row + 2][edge : edge + p.along, : p.features]


def body_by_column(
    fields,
    diffusivity,
    owners,
    observed,
    usable,
    w_hidden,
    b_hidden,
    w_radiance,
    b_radiance,
    inv_cov,
):
    p = Plan(
        lax.axis_size("tile"),
        lax.axis_size("chan"),
        fields.shape,
        owners.shape,
        observed.shape,
        w_hidden.shape,
    )
    half, single = jnp.bfloat16, jnp.float32
    shape = jax.ShapeDtypeStruct
    both = ("tile", "chan")
    everyone = [(a, b) for a in range(p.tiles) for b in range(p.chans)]

    def flip(value, mask):
        return lax.ppermute(value, "chan", [(b, b ^ mask) for b in range(p.chans)])

    def shift(value, by):
        return lax.ppermute(value, "tile", [(a, (a + by) % p.tiles) for a in range(p.tiles)])

    def send(value, wanted):
        pairs = dict(wanted)
        pairs.update({target: source for source, target in wanted.items()})
        for a, b in everyone:
            if (a, b) not in pairs:
                pairs[a, b] = (a, b ^ 1)
        number = lambda place: place[0] * p.chans + place[1]
        return lax.ppermute(
            value, both, sorted((number(a), number(b)) for a, b in pairs.items())
        )

    def join(values, kernel_shape, after=()):
        return call(
            functools.partial(join_kernel, len(values)),
            shape(kernel_shape, half),
            [*values, *after],
            in_hbm=range(len(values) + len(after)),
            out_hbm=True,
            scratch=[pltpu.SemaphoreType.DMA((len(values),))],
            flops=0,
        )

    def grow(value, over, after=()):
        return join([value, over(value)], (2 * value.shape[0],) + value.shape[1:], after)

    def trade(value, mask):
        return lax.ppermute(value, "tile", [(a, a ^ mask) for a in range(p.tiles)])

    strips = call(
        functools.partial(prepare_kernel, p),
        shape((p.block, p.width), half),
        [fields, diffusivity, usable, b_hidden],
        in_hbm=range(4),
        out_hbm=True,
        scratch=[
            pltpu.VMEM(fields.shape, single),
            pltpu.VMEM(diffusivity.shape, single),
            pltpu.VMEM(usable.shape, jnp.int32),
            pltpu.VMEM(b_hidden.shape, single),
            pltpu.VMEM((p.block, p.width), single),
            pltpu.VMEM((p.block, p.width), half),
            pltpu.SemaphoreType.DMA((5,)),
        ],
        vmem=WHOLE_VMEM_BYTES,
    )
    seen, stages = observed, []
    bit = 1
    while bit < p.tiles:
        if 2 * bit < p.tiles:
            seen = grow(seen, lambda value: trade(value, bit))
        strips = grow(strips, lambda value: trade(value, bit), [seen] if 2 * bit == p.tiles else ())
        stages.append(strips)
        bit *= 2
    strips = join(
        [strips] + [flip(strips, k * p.group) for k in range(1, p.chips)], (p.strips, p.width)
    )
    strips = [strips] + [flip(strips, k) for k in range(1, p.group)]

    near = [w_hidden] + [flip(w_hidden, chip * p.group) for chip in range(1, p.chips)]
    near = call(
        functools.partial(stack_kernel, p),
        shape((p.chips * p.deep, p.hidden), half),
        near + [stages[-1]],
        in_hbm=[len(near)],
    )
    weights = [near] + [flip(near, k) for k in range(1, p.group)]

    far_half = p.tiles // 2
    seen = [
        seen,
        send(seen, {(b // p.group ^ far_half, b): (b // p.group, b) for b in range(p.chans)}),
    ]

    reach = p.across + 4
    place, source, cell, *targets = call(
        functools.partial(place_kernel, p),
        [shape((p.rows, 1), jnp.int32)] * 2
        + [shape((3 * reach, 1), jnp.int32)]
        + [shape((p.chips * p.patch, 1), jnp.int32)] * p.group,
        [owners],
        flops=SLACK_FLOPS,
    )
    *parts, slope, kappa = call(
        functools.partial(forward_kernel, p),
        [shape((p.rows // p.steps, p.shard), half)] * p.steps
        + [shape((p.chans, p.rows, p.hidden), single), shape((3 * reach, p.lane), single)],
        [place, source, cell, b_radiance, w_radiance] + strips + weights + seen,
        scratch=[pltpu.VMEM((p.rows, p.hidden * p.chans), half)],
        flops=2 * p.rows * p.hidden * p.chans * (p.features + p.shard),
    )

    pool, held, choices = list(parts), {}, {}
    for j in range(p.steps):
        held[0, j] = choices[0, j] = j
    for step in range(p.steps):
        for since in range(-1, step):
            for j in range(p.steps):
                order = [1 << (j + k) % p.steps for k in range(p.steps)]
                roles = [0] if since < 0 else [
                    order[since] + rest
                    for rest in range(p.chips)
                    if rest & ~sum(order[:since]) == 0
                ]
                wanted = {
                    (a, b): (a, b ^ order[step] * p.group)
                    for a, b in everyone
                    if (b // p.group ^ a) in roles
                }
                source = pool[choices[roles[0], j]]
                for role in roles:
                    choices[role + order[step], j] = len(pool)
                pool.append(send(source, wanted))
    chosen = call(
        functools.partial(choose_kernel, p, choices),
        shape((p.rows, p.shard), half),
        pool,
        in_hbm=range(len(pool)),
        out_hbm=True,
        scratch=[pltpu.SemaphoreType.DMA((p.steps,))],
    )
    depart = [chosen] + [flip(chosen, k) for k in range(1, p.group)]

    partial = call(
        functools.partial(backward_kernel, p),
        [shape((p.chips * p.patch, p.features), half)] * p.group,
        [w_radiance, inv_cov, slope] + depart + weights + targets,
        flops=2 * p.rows * (p.hidden * p.chans * (p.features + p.shard) + inv_cov.size),
    )
    partial = [partial[0]] + [flip(partial[k], k) for k in range(1, p.group)]
    partial = call(
        functools.partial(add_group_kernel, p),
        [shape((p.patch, p.features), half)] * p.chips,
        partial,
    )
    partial = [partial[0]] + [flip(partial[k], k * p.group) for k in range(1, p.chips)]
    partial = call(
        functools.partial(add_chips_kernel, p),
        [shape((p.room, p.features), half)] * p.tiles,
        partial,
    )
    partial = [partial[0]] + [shift(partial[k], k) for k in range(1, p.tiles)]

    edge = 8
    kappa = kappa.reshape(3, reach, p.lane)
    root = jnp.sqrt(
        jnp.concatenate(
            [kappa[0, :, p.along - edge : p.along], kappa[1, :, : p.along], kappa[2, :, :edge]],
            axis=1,
        ).T
    )
    return call(
        functools.partial(diffuse_kernel, p, edge),
        shape(fields.shape, single),
        partial + [root],
        flops=100 * fields.size,
    )


def solution(mesh):
    tiles, chans = mesh.shape["tile"], mesh.shape["chan"]
    by_column = tiles > 1 and chans % tiles == 0 and chans & (chans - 1) == 0 and chans > tiles
    placed = (
        P("chan", "tile", None),
        P("chan", "tile"),
        P(),
        P("tile", "chan"),
        P("tile"),
        P(None, "chan"),
        P("chan"),
        P(None, "chan"),
        P("chan"),
        P("tile", "chan"),
    )
    return jax.shard_map(
        body_by_column if by_column else body_by_owner,
        mesh=mesh,
        in_specs=placed,
        out_specs=P("chan", "tile", None),
        check_vma=False,
    )
```

```python
import functools

import jax
import jax.numpy as jnp
from jax import lax
from jax.experimental import pallas as pl
from jax.experimental.pallas import tpu as pltpu
from jax.sharding import PartitionSpec as P

VMEM_BYTES = 24 * 1024 * 1024
WHOLE_VMEM_BYTES = 63 * 1024 * 1024
SLACK_FLOPS = 2 * 10**9
NT_DIMS = (((1,), (1,)), ((), ()))


def padded_2(value, sides, width, wrap):
    for axis, dim in sides:
        devices, length = (lax.axis_size(axis), value.shape[dim])
        up = [(i, (i + 1) % devices) for i in range(devices if wrap else devices - 1)]
        down = [(j, i) for i, j in up]
        last = lax.slice_in_dim(value, length - width, length, axis=dim)
        first = lax.slice_in_dim(value, 0, width, axis=dim)
        before = lax.ppermute(last, axis, up)
        after = lax.ppermute(first, axis, down)
        value = jnp.concatenate([before, value, after], axis=dim)
    return value


def add_rims(values):
    rowwise = padded_2(values, (("chan", 0),), 1, False)
    return padded_2(rowwise, (("tile", 1),), 1, True)


def body_by_owner(
    fields,
    diffusivity,
    owners,
    observed,
    usable,
    w_hidden,
    b_hidden,
    w_radiance,
    b_radiance,
    inv_cov,
):
    tile_count = lax.axis_size("tile")
    chan_count = lax.axis_size("chan")
    tile_index = lax.axis_index("tile")
    chan_index = lax.axis_index("chan")
    slot_count = observed.shape[0]
    capacity = slot_count // tile_count
    cells_across, cells_along, features = fields.shape
    own_cols = cells_across // 4 * (cells_along // 4)
    tile_cols = chan_count * own_cols
    hidden_dev = w_hidden.shape[1]
    owner_table = owners[:, 0].reshape(tile_count, tile_cols)
    owner_hits = (
        owner_table[:, :, None] == jnp.arange(tile_count, dtype=jnp.int32)[None, None, :]
    ).astype(jnp.int32)
    before = jnp.sum((jnp.cumsum(owner_hits, axis=1) - owner_hits) * owner_hits, axis=2)
    tallies = jnp.sum(owner_hits, axis=1)
    slot_of = lax.dynamic_index_in_dim(
        owner_table * capacity + before, tile_index, 0, keepdims=False
    )
    arriving = lax.dynamic_index_in_dim(tallies, tile_index, 1, keepdims=False)
    occupied = (jnp.arange(capacity, dtype=jnp.int32)[None, :] < arriving[:, None]).reshape(
        slot_count
    )
    grouped = fields.reshape(cells_across // 4, 4, cells_along // 4, 4, features)
    columns = (
        (jnp.sum(grouped, axis=(1, 3)) * 0.0625).reshape(own_cols, features).astype(jnp.bfloat16)
    )
    placer = (slot_of[None, :] == jnp.arange(slot_count, dtype=jnp.int32)[:, None]).astype(
        jnp.bfloat16
    )
    outgoing = jnp.dot(
        placer,
        lax.all_gather(columns, "chan", axis=0, tiled=True),
        preferred_element_type=jnp.float32,
    )
    incoming = lax.all_to_all(
        outgoing.astype(jnp.bfloat16), "tile", split_axis=0, concat_axis=0, tiled=True
    )
    preact = lax.dot_general(
        w_hidden, incoming, (((0,), (1,)), ((), ())), preferred_element_type=jnp.float32
    )
    preact = preact + b_hidden[:, None]
    squash = jax.nn.sigmoid(preact)
    active = (preact * squash).astype(jnp.bfloat16)
    radiance = lax.dot_general(
        lax.all_gather(active, "chan", axis=0, tiled=True),
        w_radiance,
        (((0,), (0,)), ((), ())),
        preferred_element_type=jnp.float32,
    )
    radiance = radiance + b_radiance[None, :]
    in_use = usable.astype(jnp.float32) * occupied.astype(jnp.float32)
    departure = ((radiance - observed.astype(jnp.float32)) * in_use[:, None]).astype(jnp.bfloat16)
    cotangent = jnp.dot(
        lax.all_gather(departure, "chan", axis=1, tiled=True),
        lax.all_gather(inv_cov, "tile", axis=0, tiled=True),
        preferred_element_type=jnp.float32,
    )
    cotangent = cotangent.astype(jnp.bfloat16)
    full_sum = lax.psum(
        lax.dot_general(w_radiance, cotangent, NT_DIMS, preferred_element_type=jnp.float32),
        "chan",
    )
    grad_hidden = lax.dynamic_slice_in_dim(full_sum, chan_index * hidden_dev, hidden_dev, 0)
    slope_term = squash * (1.0 + preact * (1.0 - squash))
    grad_pre = (grad_hidden * slope_term).astype(jnp.bfloat16)
    part_grad = lax.dot_general(
        grad_pre, w_hidden, (((0,), (1,)), ((), ())), preferred_element_type=jnp.float32
    )
    returned = lax.all_to_all(part_grad, "tile", split_axis=0, concat_axis=0, tiled=True)
    column_grad = lax.psum_scatter(
        jnp.take(returned, slot_of, axis=0), "chan", scatter_dimension=0, tiled=True
    )
    spread = jnp.repeat(
        column_grad.reshape(cells_across // 4, cells_along // 4, features), 4, axis=0
    )
    adjoint = jnp.repeat(spread, 4, axis=1) * 0.0625
    kappa_root = jnp.sqrt(diffusivity)
    root_rim = add_rims(kappa_root)
    coef_north = (kappa_root * root_rim[2:, 1:-1])[:, :, None]
    coef_south = (kappa_root * root_rim[:-2, 1:-1])[:, :, None]
    coef_east = (kappa_root * root_rim[1:-1, 2:])[:, :, None]
    coef_west = (kappa_root * root_rim[1:-1, :-2])[:, :, None]
    for sweep_index in range(2):
        padded = add_rims(adjoint)
        adjoint = (
            adjoint
            + coef_north * (padded[2:, 1:-1] - adjoint)
            + coef_south * (padded[:-2, 1:-1] - adjoint)
            + coef_east * (padded[1:-1, 2:] - adjoint)
            + coef_west * (padded[1:-1, :-2] - adjoint)
        )
    return adjoint


def up_to(value, multiple):
    return -(-value // multiple) * multiple


def dot(left, right):
    return jnp.dot(left, right, preferred_element_type=jnp.float32)


def dot_nt(left, right):
    return lax.dot_general(left, right, NT_DIMS, preferred_element_type=jnp.float32)


def split_three(value):
    high = value.astype(jnp.bfloat16).astype(jnp.float32)
    middle = (value - high).astype(jnp.bfloat16).astype(jnp.float32)
    return high, middle, value - high - middle


def call(
    kernel, out_shape, args, in_hbm=(), out_hbm=False, scratch=(), flops=0, vmem=VMEM_BYTES
):
    far, near = pl.BlockSpec(memory_space=pl.ANY), pl.BlockSpec(memory_space=pltpu.VMEM)
    bytes_accessed = sum(a.size * a.dtype.itemsize for a in args)
    return pl.pallas_call(
        kernel,
        out_shape=out_shape,
        in_specs=[far if k in in_hbm else near for k in range(len(args))],
        out_specs=jax.tree.map(lambda _: far if out_hbm else near, out_shape),
        scratch_shapes=list(scratch),
        compiler_params=pltpu.CompilerParams(vmem_limit_bytes=vmem),
        cost_estimate=pl.CostEstimate(
            flops=flops, bytes_accessed=bytes_accessed, transcendentals=0
        ),
    )(*args)


class Plan:
    def __init__(self, tiles, chans, fields, owners, observed, w_hidden):
        self.tiles, self.chans = tiles, chans
        self.across, self.along, self.features = fields
        self.own_cols = self.across // 4 * (self.along // 4)
        self.rows = owners[0]
        self.tile_cols = self.rows // tiles
        self.slots = observed[0]
        self.shard = observed[1]
        self.capacity = self.slots // tiles
        self.hidden = w_hidden[1]
        self.group = chans // tiles
        self.chips = chans // self.group
        self.steps = self.chips.bit_length() - 1
        self.lane = up_to(self.along, 128)
        self.flag_at = up_to(self.hidden, 128)
        self.width = max(
            up_to(self.features, 128),
            2 * self.flag_at,
            self.flag_at + up_to(self.slots, 128),
            3 * self.lane,
        )
        self.block = up_to(self.own_cols + 2 + self.across, 16)
        self.per_row = self.own_cols + 2
        self.room = up_to(3 * self.per_row, 16)
        self.patch = 3 * tiles * self.own_cols
        self.deep = up_to(self.features, 16)
        self.strips = self.chips * tiles * self.block

    def order(self, mask):
        return mask % self.group * self.chips + mask // self.group

    def layer(self, refs, k):
        at = k % self.chips * self.deep
        return refs[k // self.chips][at : at + self.features, :]

    def mask(self, k):
        return k % self.chips * self.group + k // self.chips


def prepare_kernel(p, *refs):
    ins, out_ref = refs[:4], refs[4]
    fields_ref, diffusivity_ref, usable_ref, bias_ref, flat, packed, sems = refs[5:]
    copies = [
        pltpu.make_async_copy(source, target, sems.at[k])
        for k, (source, target) in enumerate(zip(ins, refs[5:9]))
    ]
    for copy in copies:
        copy.start()
    flat[...] = jnp.zeros(flat.shape, jnp.float32)
    for copy in copies:
        copy.wait()
    shape = (p.own_cols, p.along)
    row = lax.broadcasted_iota(jnp.int32, shape, 0)
    member = row == lax.broadcasted_iota(jnp.int32, shape, 1) // 4
    total = jnp.dot(
        member.astype(jnp.float32),
        fields_ref[0] + fields_ref[1] + fields_ref[2] + fields_ref[3],
        precision=lax.Precision.HIGHEST,
        preferred_element_type=jnp.float32,
    )
    flat[: p.own_cols, : p.features] = total * 0.0625
    at = p.own_cols
    high, middle, low = split_three(bias_ref[...].reshape(1, p.hidden))
    flat[at : at + 1, : p.hidden] = high
    flat[at : at + 1, p.flag_at : p.flag_at + p.hidden] = middle
    flat[at + 1 : at + 2, : p.hidden] = low
    flags = usable_ref[...].reshape(1, p.slots).astype(jnp.float32)
    flat[at + 1 : at + 2, p.flag_at : p.flag_at + p.slots] = flags
    for k, part in enumerate(split_three(diffusivity_ref[...])):
        flat[at + 2 : at + 2 + p.across, k * p.lane : k * p.lane + p.along] = part
    packed[...] = flat[...].astype(jnp.bfloat16)
    copy = pltpu.make_async_copy(packed, out_ref, sems.at[4])
    copy.start()
    copy.wait()


def place_kernel(p, owners_ref, place_ref, source_ref, cell_ref, *target_refs):
    t, c = lax.axis_index("tile"), lax.axis_index("chan")
    across = owners_ref[...]
    shape = (p.rows, p.rows)
    row = lax.broadcasted_iota(jnp.int32, shape, 0)
    other = lax.broadcasted_iota(jnp.int32, shape, 1)
    owner = jnp.sum(jnp.where(row == other, across, 0), axis=1, keepdims=True)
    first = lax.broadcasted_iota(jnp.int32, owner.shape, 0)
    begin = first // p.tile_cols * p.tile_cols
    same = (owner == across) & (other >= begin) & (other < row)
    rank = jnp.sum(jnp.where(same, 1, 0), axis=1, keepdims=True)
    tile = first // p.tile_cols
    place_ref[...] = (owner ^ t) * p.slots + tile * p.capacity + rank

    def strip(tile, chan):
        other = chan ^ c
        return p.order(other) * p.tiles + (tile ^ t)

    source_ref[...] = (
        strip(tile, first % p.tile_cols // p.own_cols) * p.block + first % p.own_cols
    )

    row = lax.broadcasted_iota(jnp.int32, cell_ref.shape, 0)
    reach = p.across + 4
    tile = (t + row // reach - 1 + p.tiles) % p.tiles
    cell = c * p.across - 2 + row % reach
    inside = (cell >= 0) & (cell < p.chans * p.across)
    cell = jnp.where(inside, cell, 0)
    wanted = strip(tile, cell // p.across) * p.block + p.own_cols + 2 + cell % p.across
    cell_ref[...] = jnp.where(inside, wanted, -1)

    target = lax.broadcasted_iota(jnp.int32, target_refs[0].shape, 0)
    chip, inner = target // p.patch, target % p.patch
    beside, inner = inner // (p.patch // 3) - 1, inner % (p.patch // 3)
    tile, along = inner // p.own_cols, inner % p.own_cols
    for k, target_ref in enumerate(target_refs):
        row = ((chip ^ (c // p.group)) * p.group + (c % p.group ^ k)) + beside
        wanted = tile * p.tile_cols + row * p.own_cols + along
        target_ref[...] = jnp.where((row >= 0) & (row < p.chans), wanted, -1)


def join_kernel(count, *refs):
    ins, out_ref, sems = refs[:count], refs[-2], refs[-1]
    size = out_ref.shape[0] // count
    copies = [
        pltpu.make_async_copy(
            ref, out_ref.at[k] if ref.ndim < out_ref.ndim else out_ref.at[pl.ds(k * size, size)],
            sems.at[k],
        )
        for k, ref in enumerate(ins)
    ]
    for copy in copies:
        copy.start()
    for copy in copies:
        copy.wait()


def stack_kernel(p, *refs):
    for k, ref in enumerate(refs[: p.chips]):
        refs[-1][k * p.deep : k * p.deep + p.features, :] = ref[...]
        refs[-1][k * p.deep + p.features : (k + 1) * p.deep, :] = jnp.zeros(
            (p.deep - p.features, p.hidden), jnp.bfloat16
        )


def one_hot(wanted, first, count):
    source = lax.broadcasted_iota(jnp.int32, (wanted.shape[0], count), 1)
    return (source + first == wanted).astype(jnp.bfloat16)


def forward_kernel(p, *refs):
    refs = list(refs)
    take = lambda n: [refs.pop(0) for _ in range(n)]
    place_ref, source_ref, cell_ref, bias_ref, w_radiance_ref = take(5)
    strip_refs, weight_refs, seen_refs = take(p.group), take(p.group), take(2)
    part_refs = take(p.steps)
    slope_ref, kappa_ref, active = refs
    c = lax.axis_index("chan")
    gathered = [ref[...] for ref in strip_refs]
    columns = sum(
        dot(one_hot(source_ref[...], k * p.strips, p.strips), strips)
        for k, strips in enumerate(gathered)
    )
    columns = columns.astype(jnp.bfloat16)[:, : p.features]
    for k in range(p.chans):
        member, chip = k // p.chips, k % p.chips
        at = chip * p.tiles * p.block + p.own_cols
        low = strip_refs[member][at : at + 2, :].astype(jnp.float32)
        bias = (
            low[:1, : p.hidden]
            + low[:1, p.flag_at : p.flag_at + p.hidden]
            + low[1:, : p.hidden]
        )
        preact = dot(columns, p.layer(weight_refs, k)) + bias
        squash = jax.nn.sigmoid(preact)
        slope_ref[k] = squash * (1.0 + preact * (1.0 - squash))
        at = pl.multiple_of((c ^ p.mask(k)) * p.hidden, p.hidden)
        active[:, pl.ds(at, p.hidden)] = (preact * squash).astype(jnp.bfloat16)
    part = p.rows // p.steps
    count = seen_refs[0].shape[0]
    for j, part_ref in enumerate(part_refs):
        at = slice(j * part, (j + 1) * part)
        in_use = jnp.zeros((part, 1), jnp.float32)
        for k in range(p.tiles):
            slot = lax.broadcasted_iota(jnp.int32, (part, p.slots), 1) + k * p.slots
            low = k * p.block + p.own_cols + 1
            flags = strip_refs[0][low : low + 1, p.flag_at : p.flag_at + p.slots]
            flags = jnp.where(place_ref[at, :] == slot, flags.astype(jnp.float32), 0.0)
            in_use = in_use + jnp.sum(flags, axis=1, keepdims=True)
        observed = sum(
            dot(one_hot(place_ref[at, :], k * count, count), ref[...])
            for k, ref in enumerate(seen_refs)
        )
        radiance = dot(active[at, :], w_radiance_ref[...]) + bias_ref[...].reshape(1, p.shard)
        part_ref[...] = ((radiance - observed) * in_use).astype(jnp.bfloat16)
    parts = sum(
        dot(one_hot(cell_ref[...], k * p.strips, p.strips), strips)
        for k, strips in enumerate(gathered)
    )
    kappa_ref[...] = sum(parts[:, k * p.lane : (k + 1) * p.lane] for k in range(3))


def choose_kernel(p, choices, *refs):
    refs, out_ref, sems = refs[:-2], refs[-2], refs[-1]
    size = refs[0].shape[0]
    role = (lax.axis_index("chan") // p.group) ^ lax.axis_index("tile")
    for place in range(p.chips):

        @pl.when(role == place)
        def _():
            copies = [
                pltpu.make_async_copy(
                    refs[choices[place, j]], out_ref.at[pl.ds(j * size, size)], sems.at[j]
                )
                for j in range(p.steps)
            ]
            for copy in copies:
                copy.start()
            for copy in copies:
                copy.wait()


def backward_kernel(p, *refs):
    refs = list(refs)
    take = lambda n: [refs.pop(0) for _ in range(n)]
    w_radiance_ref, inv_cov_ref, slope_ref = take(3)
    depart_refs, weight_refs, target_refs = take(p.group), take(p.group), take(p.group)
    out_refs = refs
    c = lax.axis_index("chan")
    cotangent = None
    for k, ref in enumerate(depart_refs):
        at = pl.multiple_of((c % p.group ^ k) * p.shard, p.shard)
        term = dot(ref[...], inv_cov_ref[pl.ds(at, p.shard), :])
        cotangent = term if cotangent is None else cotangent + term
    cotangent = cotangent.astype(jnp.bfloat16)
    total = jnp.zeros((p.rows, p.features), jnp.float32)
    for k in range(p.chans):
        at = pl.multiple_of((c ^ p.mask(k)) * p.hidden, p.hidden)
        grad_hidden = dot_nt(cotangent, w_radiance_ref[pl.ds(at, p.hidden), :])
        grad_pre = (grad_hidden * slope_ref[k]).astype(jnp.bfloat16)
        total = total + dot_nt(grad_pre, p.layer(weight_refs, k))
    total = total.astype(jnp.bfloat16)
    for target_ref, out_ref in zip(target_refs, out_refs):
        out_ref[...] = dot(one_hot(target_ref[...], 0, p.rows), total).astype(jnp.bfloat16)


def add(refs, at=slice(None)):
    total = refs[0][at, :].astype(jnp.float32)
    for ref in refs[1:]:
        total = total + ref[at, :].astype(jnp.float32)
    return total


def add_group_kernel(p, *refs):
    ins, outs = refs[: p.group], refs[p.group :]
    for k, out_ref in enumerate(outs):
        out_ref[...] = add(ins, slice(k * p.patch, (k + 1) * p.patch)).astype(jnp.bfloat16)


def add_chips_kernel(p, *refs):
    ins, outs = refs[: p.chips], refs[p.chips :]
    total = add(ins).astype(jnp.bfloat16)
    shape = (p.room, p.patch)
    target = lax.broadcasted_iota(jnp.int32, shape, 0)
    source = lax.broadcasted_iota(jnp.int32, shape, 1)
    row, along = target // p.per_row, target % p.per_row - 1
    for k, out_ref in enumerate(outs):
        tile = (lax.axis_index("tile") + k) % p.tiles
        cell = (tile * p.own_cols + along + p.tiles * p.own_cols) % (p.tiles * p.own_cols)
        pick = (source == row * (p.tiles * p.own_cols) + cell) & (row < 3)
        out_ref[...] = dot(pick.astype(jnp.bfloat16), total).astype(jnp.bfloat16)


def diffuse_kernel(p, edge, *refs):
    ins, root_ref, out_ref = refs[: p.tiles], refs[-2], refs[-1]
    total = add(ins) * 0.0625
    length = p.along + 2 * edge
    shape = (length, p.room)
    cell = lax.broadcasted_iota(jnp.int32, shape, 0)
    source = lax.broadcasted_iota(jnp.int32, shape, 1)
    column = (cell - edge + 4) // 4
    spread = []
    for k in range(3):
        pick = (source == column + k * p.per_row) & (column >= 0) & (column < p.per_row)
        spread.append(
            jnp.dot(
                pick.astype(jnp.float32),
                total,
                precision=lax.Precision.HIGHEST,
                preferred_element_type=jnp.float32,
            )
        )
    root = root_ref[...]
    state = [spread[(row + 2) // 4] for row in range(p.across + 4)]
    east_of = functools.partial(pltpu.roll, shift=length - 1, axis=0)
    west_of = functools.partial(pltpu.roll, shift=1, axis=0)
    north = root[:, :-1] * root[:, 1:]
    east, west = root * east_of(root), root * west_of(root)
    for sweep in range(2):
        fresh = list(state)
        for row in range(1 + sweep, p.across + 3 - sweep):
            here = state[row]
            fresh[row] = (
                here
                + north[:, row : row + 1] * (state[row + 1] - here)
                + north[:, row - 1 : row] * (state[row - 1] - here)
                + east[:, row : row + 1] * (east_of(here) - here)
                + west[:, row : row + 1] * (west_of(here) - here)
            )
        state = fresh
    for row in range(p.across):
        out_ref[row] = state[row + 2][edge : edge + p.along, : p.features]


def body_by_column(
    fields,
    diffusivity,
    owners,
    observed,
    usable,
    w_hidden,
    b_hidden,
    w_radiance,
    b_radiance,
    inv_cov,
):
    p = Plan(
        lax.axis_size("tile"),
        lax.axis_size("chan"),
        fields.shape,
        owners.shape,
        observed.shape,
        w_hidden.shape,
    )
    half, single = jnp.bfloat16, jnp.float32
    shape = jax.ShapeDtypeStruct
    both = ("tile", "chan")
    everyone = [(a, b) for a in range(p.tiles) for b in range(p.chans)]

    def flip(value, mask):
        return lax.ppermute(value, "chan", [(b, b ^ mask) for b in range(p.chans)])

    def shift(value, by):
        return lax.ppermute(value, "tile", [(a, (a + by) % p.tiles) for a in range(p.tiles)])

    def send(value, wanted):
        pairs = dict(wanted)
        pairs.update({target: source for source, target in wanted.items()})
        for a, b in everyone:
            if (a, b) not in pairs:
                pairs[a, b] = (a, b ^ 1)
        number = lambda place: place[0] * p.chans + place[1]
        return lax.ppermute(
            value, both, sorted((number(a), number(b)) for a, b in pairs.items())
        )

    def join(values, kernel_shape, after=()):
        return call(
            functools.partial(join_kernel, len(values)),
            shape(kernel_shape, half),
            [*values, *after],
            in_hbm=range(len(values) + len(after)),
            out_hbm=True,
            scratch=[pltpu.SemaphoreType.DMA((len(values),))],
            flops=0,
        )

    def grow(value, over, after=()):
        return join([value, over(value)], (2 * value.shape[0],) + value.shape[1:], after)

    def trade(value, mask):
        return lax.ppermute(value, "tile", [(a, a ^ mask) for a in range(p.tiles)])

    strips = call(
        functools.partial(prepare_kernel, p),
        shape((p.block, p.width), half),
        [fields, diffusivity, usable, b_hidden],
        in_hbm=range(4),
        out_hbm=True,
        scratch=[
            pltpu.VMEM(fields.shape, single),
            pltpu.VMEM(diffusivity.shape, single),
            pltpu.VMEM(usable.shape, jnp.int32),
            pltpu.VMEM(b_hidden.shape, single),
            pltpu.VMEM((p.block, p.width), single),
            pltpu.VMEM((p.block, p.width), half),
            pltpu.SemaphoreType.DMA((5,)),
        ],
        vmem=WHOLE_VMEM_BYTES,
    )
    seen, stages = observed, []
    bit = 1
    while bit < p.tiles:
        if 2 * bit < p.tiles:
            seen = grow(seen, lambda value: trade(value, bit))
        strips = grow(strips, lambda value: trade(value, bit), [seen] if 2 * bit == p.tiles else ())
        stages.append(strips)
        bit *= 2
    strips = join(
        [strips] + [flip(strips, k * p.group) for k in range(1, p.chips)], (p.strips, p.width)
    )
    strips = [strips] + [flip(strips, k) for k in range(1, p.group)]

    near = [w_hidden] + [flip(w_hidden, chip * p.group) for chip in range(1, p.chips)]
    near = call(
        functools.partial(stack_kernel, p),
        shape((p.chips * p.deep, p.hidden), half),
        near + [stages[-1]],
        in_hbm=[len(near)],
    )
    weights = [near] + [flip(near, k) for k in range(1, p.group)]

    far_half = p.tiles // 2
    seen = [
        seen,
        send(seen, {(b // p.group ^ far_half, b): (b // p.group, b) for b in range(p.chans)}),
    ]

    reach = p.across + 4
    place, source, cell, *targets = call(
        functools.partial(place_kernel, p),
        [shape((p.rows, 1), jnp.int32)] * 2
        + [shape((3 * reach, 1), jnp.int32)]
        + [shape((p.chips * p.patch, 1), jnp.int32)] * p.group,
        [owners.reshape(1, p.rows)],
        flops=SLACK_FLOPS,
    )
    *parts, slope, kappa = call(
        functools.partial(forward_kernel, p),
        [shape((p.rows // p.steps, p.shard), half)] * p.steps
        + [shape((p.chans, p.rows, p.hidden), single), shape((3 * reach, p.lane), single)],
        [place, source, cell, b_radiance, w_radiance] + strips + weights + seen,
        scratch=[pltpu.VMEM((p.rows, p.hidden * p.chans), half)],
        flops=2 * p.rows * p.hidden * p.chans * (p.features + p.shard),
    )

    pool, held, choices = list(parts), {}, {}
    for j in range(p.steps):
        held[0, j] = choices[0, j] = j
    for step in range(p.steps):
        for since in range(-1, step):
            for j in range(p.steps):
                order = [1 << (j + k) % p.steps for k in range(p.steps)]
                roles = [0] if since < 0 else [
                    order[since] + rest
                    for rest in range(p.chips)
                    if rest & ~sum(order[:since]) == 0
                ]
                wanted = {
                    (a, b): (a, b ^ order[step] * p.group)
                    for a, b in everyone
                    if (b // p.group ^ a) in roles
                }
                source = pool[choices[roles[0], j]]
                for role in roles:
                    choices[role + order[step], j] = len(pool)
                pool.append(send(source, wanted))
    chosen = call(
        functools.partial(choose_kernel, p, choices),
        shape((p.rows, p.shard), half),
        pool,
        in_hbm=range(len(pool)),
        out_hbm=True,
        scratch=[pltpu.SemaphoreType.DMA((p.steps,))],
    )
    depart = [chosen] + [flip(chosen, k) for k in range(1, p.group)]

    partial = call(
        functools.partial(backward_kernel, p),
        [shape((p.chips * p.patch, p.features), half)] * p.group,
        [w_radiance, inv_cov, slope] + depart + weights + targets,
        flops=2 * p.rows * (p.hidden * p.chans * (p.features + p.shard) + inv_cov.size),
    )
    partial = [partial[0]] + [flip(partial[k], k) for k in range(1, p.group)]
    partial = call(
        functools.partial(add_group_kernel, p),
        [shape((p.patch, p.features), half)] * p.chips,
        partial,
    )
    partial = [partial[0]] + [flip(partial[k], k * p.group) for k in range(1, p.chips)]
    partial = call(
        functools.partial(add_chips_kernel, p),
        [shape((p.room, p.features), half)] * p.tiles,
        partial,
    )
    partial = [partial[0]] + [shift(partial[k], k) for k in range(1, p.tiles)]

    edge = 8
    kappa = kappa.reshape(3, reach, p.lane)
    root = jnp.sqrt(
        jnp.concatenate(
            [kappa[0, :, p.along - edge : p.along], kappa[1, :, : p.along], kappa[2, :, :edge]],
            axis=1,
        ).T
    )
    return call(
        functools.partial(diffuse_kernel, p, edge),
        shape(fields.shape, single),
        partial + [root],
        flops=100 * fields.size,
    )


def solution(mesh):
    tiles, chans = mesh.shape["tile"], mesh.shape["chan"]
    by_column = tiles > 1 and chans % tiles == 0 and chans & (chans - 1) == 0 and chans > tiles
    placed = (
        P("chan", "tile", None),
        P("chan", "tile"),
        P(),
        P("tile", "chan"),
        P("tile"),
        P(None, "chan"),
        P("chan"),
        P(None, "chan"),
        P("chan"),
        P("tile", "chan"),
    )
    return jax.shard_map(
        body_by_column if by_column else body_by_owner,
        mesh=mesh,
        in_specs=placed,
        out_specs=P("chan", "tile", None),
        check_vma=False,
    )
```

```python
import functools

import jax
import jax.numpy as jnp
from jax import lax
from jax.experimental import pallas as pl
from jax.experimental.pallas import tpu as pltpu
from jax.sharding import PartitionSpec as P

VMEM_BYTES = 24 * 1024 * 1024
WHOLE_VMEM_BYTES = 63 * 1024 * 1024
SLACK_FLOPS = 2 * 10**9
NT_DIMS = (((1,), (1,)), ((), ()))


def padded_2(value, sides, width, wrap):
    for axis, dim in sides:
        devices, length = (lax.axis_size(axis), value.shape[dim])
        up = [(i, (i + 1) % devices) for i in range(devices if wrap else devices - 1)]
        down = [(j, i) for i, j in up]
        last = lax.slice_in_dim(value, length - width, length, axis=dim)
        first = lax.slice_in_dim(value, 0, width, axis=dim)
        before = lax.ppermute(last, axis, up)
        after = lax.ppermute(first, axis, down)
        value = jnp.concatenate([before, value, after], axis=dim)
    return value


def add_rims(values):
    rowwise = padded_2(values, (("chan", 0),), 1, False)
    return padded_2(rowwise, (("tile", 1),), 1, True)


def body_by_owner(
    fields,
    diffusivity,
    owners,
    observed,
    usable,
    w_hidden,
    b_hidden,
    w_radiance,
    b_radiance,
    inv_cov,
):
    tile_count = lax.axis_size("tile")
    chan_count = lax.axis_size("chan")
    tile_index = lax.axis_index("tile")
    chan_index = lax.axis_index("chan")
    slot_count = observed.shape[0]
    capacity = slot_count // tile_count
    cells_across, cells_along, features = fields.shape
    own_cols = cells_across // 4 * (cells_along // 4)
    tile_cols = chan_count * own_cols
    hidden_dev = w_hidden.shape[1]
    owner_table = owners[:, 0].reshape(tile_count, tile_cols)
    owner_hits = (
        owner_table[:, :, None] == jnp.arange(tile_count, dtype=jnp.int32)[None, None, :]
    ).astype(jnp.int32)
    before = jnp.sum((jnp.cumsum(owner_hits, axis=1) - owner_hits) * owner_hits, axis=2)
    tallies = jnp.sum(owner_hits, axis=1)
    slot_of = lax.dynamic_index_in_dim(
        owner_table * capacity + before, tile_index, 0, keepdims=False
    )
    arriving = lax.dynamic_index_in_dim(tallies, tile_index, 1, keepdims=False)
    occupied = (jnp.arange(capacity, dtype=jnp.int32)[None, :] < arriving[:, None]).reshape(
        slot_count
    )
    grouped = fields.reshape(cells_across // 4, 4, cells_along // 4, 4, features)
    columns = (
        (jnp.sum(grouped, axis=(1, 3)) * 0.0625).reshape(own_cols, features).astype(jnp.bfloat16)
    )
    placer = (slot_of[None, :] == jnp.arange(slot_count, dtype=jnp.int32)[:, None]).astype(
        jnp.bfloat16
    )
    outgoing = jnp.dot(
        placer,
        lax.all_gather(columns, "chan", axis=0, tiled=True),
        preferred_element_type=jnp.float32,
    )
    incoming = lax.all_to_all(
        outgoing.astype(jnp.bfloat16), "tile", split_axis=0, concat_axis=0, tiled=True
    )
    preact = lax.dot_general(
        w_hidden, incoming, (((0,), (1,)), ((), ())), preferred_element_type=jnp.float32
    )
    preact = preact + b_hidden[:, None]
    squash = jax.nn.sigmoid(preact)
    active = (preact * squash).astype(jnp.bfloat16)
    radiance = lax.dot_general(
        lax.all_gather(active, "chan", axis=0, tiled=True),
        w_radiance,
        (((0,), (0,)), ((), ())),
        preferred_element_type=jnp.float32,
    )
    radiance = radiance + b_radiance[None, :]
    in_use = usable.astype(jnp.float32) * occupied.astype(jnp.float32)
    departure = ((radiance - observed.astype(jnp.float32)) * in_use[:, None]).astype(jnp.bfloat16)
    cotangent = jnp.dot(
        lax.all_gather(departure, "chan", axis=1, tiled=True),
        lax.all_gather(inv_cov, "tile", axis=0, tiled=True),
        preferred_element_type=jnp.float32,
    )
    cotangent = cotangent.astype(jnp.bfloat16)
    full_sum = lax.psum(
        lax.dot_general(w_radiance, cotangent, NT_DIMS, preferred_element_type=jnp.float32),
        "chan",
    )
    grad_hidden = lax.dynamic_slice_in_dim(full_sum, chan_index * hidden_dev, hidden_dev, 0)
    slope_term = squash * (1.0 + preact * (1.0 - squash))
    grad_pre = (grad_hidden * slope_term).astype(jnp.bfloat16)
    part_grad = lax.dot_general(
        grad_pre, w_hidden, (((0,), (1,)), ((), ())), preferred_element_type=jnp.float32
    )
    returned = lax.all_to_all(part_grad, "tile", split_axis=0, concat_axis=0, tiled=True)
    column_grad = lax.psum_scatter(
        jnp.take(returned, slot_of, axis=0), "chan", scatter_dimension=0, tiled=True
    )
    spread = jnp.repeat(
        column_grad.reshape(cells_across // 4, cells_along // 4, features), 4, axis=0
    )
    adjoint = jnp.repeat(spread, 4, axis=1) * 0.0625
    kappa_root = jnp.sqrt(diffusivity)
    root_rim = add_rims(kappa_root)
    coef_north = (kappa_root * root_rim[2:, 1:-1])[:, :, None]
    coef_south = (kappa_root * root_rim[:-2, 1:-1])[:, :, None]
    coef_east = (kappa_root * root_rim[1:-1, 2:])[:, :, None]
    coef_west = (kappa_root * root_rim[1:-1, :-2])[:, :, None]
    for sweep_index in range(2):
        padded = add_rims(adjoint)
        adjoint = (
            adjoint
            + coef_north * (padded[2:, 1:-1] - adjoint)
            + coef_south * (padded[:-2, 1:-1] - adjoint)
            + coef_east * (padded[1:-1, 2:] - adjoint)
            + coef_west * (padded[1:-1, :-2] - adjoint)
        )
    return adjoint


def up_to(value, multiple):
    return -(-value // multiple) * multiple


def dot(left, right):
    return jnp.dot(left, right, preferred_element_type=jnp.float32)


def dot_nt(left, right):
    return lax.dot_general(left, right, NT_DIMS, preferred_element_type=jnp.float32)


def split_three(value):
    high = value.astype(jnp.bfloat16).astype(jnp.float32)
    middle = (value - high).astype(jnp.bfloat16).astype(jnp.float32)
    return high, middle, value - high - middle


def call(
    kernel, out_shape, args, in_hbm=(), out_hbm=False, scratch=(), flops=0, vmem=VMEM_BYTES
):
    far, near = pl.BlockSpec(memory_space=pl.ANY), pl.BlockSpec(memory_space=pltpu.VMEM)
    bytes_accessed = sum(a.size * a.dtype.itemsize for a in args)
    return pl.pallas_call(
        kernel,
        out_shape=out_shape,
        in_specs=[far if k in in_hbm else near for k in range(len(args))],
        out_specs=jax.tree.map(lambda _: far if out_hbm else near, out_shape),
        scratch_shapes=list(scratch),
        compiler_params=pltpu.CompilerParams(vmem_limit_bytes=vmem),
        cost_estimate=pl.CostEstimate(
            flops=flops, bytes_accessed=bytes_accessed, transcendentals=0
        ),
    )(*args)


class Plan:
    def __init__(self, tiles, chans, fields, owners, observed, w_hidden):
        self.tiles, self.chans = tiles, chans
        self.across, self.along, self.features = fields
        self.own_cols = self.across // 4 * (self.along // 4)
        self.rows = owners[0]
        self.tile_cols = self.rows // tiles
        self.slots = observed[0]
        self.shard = observed[1]
        self.capacity = self.slots // tiles
        self.hidden = w_hidden[1]
        self.group = chans // tiles
        self.chips = chans // self.group
        self.steps = self.chips.bit_length() - 1
        self.lane = up_to(self.along, 128)
        self.flag_at = up_to(self.hidden, 128)
        self.width = max(
            up_to(self.features, 128),
            2 * self.flag_at,
            self.flag_at + up_to(self.slots, 128),
            3 * self.lane,
        )
        self.block = up_to(self.own_cols + 2 + self.across, 16)
        self.per_row = self.own_cols + 2
        self.rows_each = chans // self.group
        self.around = (self.group + 2) * self.per_row
        self.deep = up_to(self.features, 16)
        self.strips = self.chips * tiles * self.block

    def order(self, mask):
        return mask % self.group * self.chips + mask // self.group

    def layer(self, refs, k):
        at = k % self.chips * self.deep
        return refs[k // self.chips][at : at + self.features, :]

    def mask(self, k):
        return k % self.chips * self.group + k // self.chips


def prepare_kernel(p, *refs):
    ins, out_ref = refs[:4], refs[4]
    fields_ref, diffusivity_ref, usable_ref, bias_ref, flat, packed, sems = refs[5:]
    copies = [
        pltpu.make_async_copy(source, target, sems.at[k])
        for k, (source, target) in enumerate(zip(ins, refs[5:9]))
    ]
    for copy in copies:
        copy.start()
    flat[...] = jnp.zeros(flat.shape, jnp.float32)
    for copy in copies:
        copy.wait()
    shape = (p.own_cols, p.along)
    row = lax.broadcasted_iota(jnp.int32, shape, 0)
    member = row == lax.broadcasted_iota(jnp.int32, shape, 1) // 4
    total = jnp.dot(
        member.astype(jnp.float32),
        fields_ref[0] + fields_ref[1] + fields_ref[2] + fields_ref[3],
        precision=lax.Precision.HIGHEST,
        preferred_element_type=jnp.float32,
    )
    flat[: p.own_cols, : p.features] = total * 0.0625
    at = p.own_cols
    high, middle, low = split_three(bias_ref[...].reshape(1, p.hidden))
    flat[at : at + 1, : p.hidden] = high
    flat[at : at + 1, p.flag_at : p.flag_at + p.hidden] = middle
    flat[at + 1 : at + 2, : p.hidden] = low
    flags = usable_ref[...].reshape(1, p.slots).astype(jnp.float32)
    flat[at + 1 : at + 2, p.flag_at : p.flag_at + p.slots] = flags
    for k, part in enumerate(split_three(diffusivity_ref[...])):
        flat[at + 2 : at + 2 + p.across, k * p.lane : k * p.lane + p.along] = part
    packed[...] = flat[...].astype(jnp.bfloat16)
    copy = pltpu.make_async_copy(packed, out_ref, sems.at[4])
    copy.start()
    copy.wait()


def place_kernel(p, owners_ref, place_ref, source_ref, cell_ref, *target_refs):
    t, c = lax.axis_index("tile"), lax.axis_index("chan")
    across = owners_ref[...]
    shape = (p.rows, p.rows)
    row = lax.broadcasted_iota(jnp.int32, shape, 0)
    other = lax.broadcasted_iota(jnp.int32, shape, 1)
    owner = jnp.sum(jnp.where(row == other, across, 0), axis=1, keepdims=True)
    first = lax.broadcasted_iota(jnp.int32, owner.shape, 0)
    begin = first // p.tile_cols * p.tile_cols
    same = (owner == across) & (other >= begin) & (other < row)
    rank = jnp.sum(jnp.where(same, 1, 0), axis=1, keepdims=True)
    tile = first // p.tile_cols
    place_ref[...] = (owner ^ t) * p.slots + tile * p.capacity + rank

    def strip(tile, chan):
        other = chan ^ c
        return p.order(other) * p.tiles + (tile ^ t)

    source_ref[...] = (
        strip(tile, first % p.tile_cols // p.own_cols) * p.block + first % p.own_cols
    )

    row = lax.broadcasted_iota(jnp.int32, cell_ref.shape, 0)
    reach = p.across + 4
    tile = (t + row // reach - 1 + p.tiles) % p.tiles
    cell = c * p.across - 2 + row % reach
    inside = (cell >= 0) & (cell < p.chans * p.across)
    cell = jnp.where(inside, cell, 0)
    wanted = strip(tile, cell // p.across) * p.block + p.own_cols + 2 + cell % p.across
    cell_ref[...] = jnp.where(inside, wanted, -1)

    each = p.rows_each * p.own_cols
    target = lax.broadcasted_iota(jnp.int32, target_refs[0].shape, 0)
    for k, target_ref in enumerate(target_refs):
        first = (c % p.group ^ k) * each
        target_ref[...] = target // each * p.tile_cols + first + target % each


def join_kernel(count, *refs):
    ins, out_ref, sems = refs[:count], refs[-2], refs[-1]
    size = out_ref.shape[0] // count
    copies = [
        pltpu.make_async_copy(
            ref, out_ref.at[k] if ref.ndim < out_ref.ndim else out_ref.at[pl.ds(k * size, size)],
            sems.at[k],
        )
        for k, ref in enumerate(ins)
    ]
    for copy in copies:
        copy.start()
    for copy in copies:
        copy.wait()


def stack_kernel(p, *refs):
    for k, ref in enumerate(refs[: p.chips]):
        refs[-1][k * p.deep : k * p.deep + p.features, :] = ref[...]
        refs[-1][k * p.deep + p.features : (k + 1) * p.deep, :] = jnp.zeros(
            (p.deep - p.features, p.hidden), jnp.bfloat16
        )


def one_hot(wanted, first, count):
    source = lax.broadcasted_iota(jnp.int32, (wanted.shape[0], count), 1)
    return (source + first == wanted).astype(jnp.bfloat16)


def forward_kernel(p, *refs):
    refs = list(refs)
    take = lambda n: [refs.pop(0) for _ in range(n)]
    place_ref, source_ref, cell_ref, bias_ref, w_radiance_ref = take(5)
    strip_refs, weight_refs, seen_refs = take(p.group), take(p.group), take(2)
    part_refs = take(p.steps)
    preact_ref, kappa_ref, active = refs
    c = lax.axis_index("chan")
    gathered = [ref[...] for ref in strip_refs]
    columns = sum(
        dot(one_hot(source_ref[...], k * p.strips, p.strips), strips)
        for k, strips in enumerate(gathered)
    )
    columns = columns.astype(jnp.bfloat16)[:, : p.features]
    for k in range(p.chans):
        member, chip = k // p.chips, k % p.chips
        at = chip * p.tiles * p.block + p.own_cols
        low = strip_refs[member][at : at + 2, :].astype(jnp.float32)
        bias = (
            low[:1, : p.hidden]
            + low[:1, p.flag_at : p.flag_at + p.hidden]
            + low[1:, : p.hidden]
        )
        preact = dot(columns, p.layer(weight_refs, k)) + bias
        preact_ref[k] = preact
        at = pl.multiple_of((c ^ p.mask(k)) * p.hidden, p.hidden)
        active[:, pl.ds(at, p.hidden)] = (preact * jax.nn.sigmoid(preact)).astype(jnp.bfloat16)
    part = p.rows // p.steps
    count = seen_refs[0].shape[0]
    for j, part_ref in enumerate(part_refs):
        at = slice(j * part, (j + 1) * part)
        in_use = jnp.zeros((part, 1), jnp.float32)
        for k in range(p.tiles):
            slot = lax.broadcasted_iota(jnp.int32, (part, p.slots), 1) + k * p.slots
            low = k * p.block + p.own_cols + 1
            flags = strip_refs[0][low : low + 1, p.flag_at : p.flag_at + p.slots]
            flags = jnp.where(place_ref[at, :] == slot, flags.astype(jnp.float32), 0.0)
            in_use = in_use + jnp.sum(flags, axis=1, keepdims=True)
        observed = sum(
            dot(one_hot(place_ref[at, :], k * count, count), ref[...])
            for k, ref in enumerate(seen_refs)
        )
        radiance = dot(active[at, :], w_radiance_ref[...]) + bias_ref[...].reshape(1, p.shard)
        part_ref[...] = ((radiance - observed) * in_use).astype(jnp.bfloat16)
    parts = sum(
        dot(one_hot(cell_ref[...], k * p.strips, p.strips), strips)
        for k, strips in enumerate(gathered)
    )
    kappa_ref[...] = sum(parts[:, k * p.lane : (k + 1) * p.lane] for k in range(3))


def slope_kernel(preact_ref, slope_ref):
    for k in range(preact_ref.shape[0]):
        preact = preact_ref[k]
        squash = jax.nn.sigmoid(preact)
        slope_ref[k] = (squash * (1.0 + preact * (1.0 - squash))).T


def choose_kernel(p, choices, *refs):
    refs, out_ref, sems = refs[:-3], refs[-2], refs[-1]
    size = refs[0].shape[0]
    role = (lax.axis_index("chan") // p.group) ^ lax.axis_index("tile")
    for place in range(p.chips):

        @pl.when(role == place)
        def _():
            copies = [
                pltpu.make_async_copy(
                    refs[choices[place, j]], out_ref.at[pl.ds(j * size, size)], sems.at[j]
                )
                for j in range(p.steps)
            ]
            for copy in copies:
                copy.start()
            for copy in copies:
                copy.wait()


def backward_kernel(p, *refs):
    refs = list(refs)
    take = lambda n: [refs.pop(0) for _ in range(n)]
    w_radiance_ref, inv_cov_ref, slope_ref = take(3)
    depart_refs, weight_refs, target_refs = take(p.group), take(p.group), take(p.group)
    out_refs = refs
    c = lax.axis_index("chan")
    cotangent = None
    for k, ref in enumerate(depart_refs):
        at = pl.multiple_of((c % p.group ^ k) * p.shard, p.shard)
        term = dot(ref[...], inv_cov_ref[pl.ds(at, p.shard), :])
        cotangent = term if cotangent is None else cotangent + term
    cotangent = cotangent.T.astype(jnp.bfloat16)
    total = jnp.zeros((p.features, p.rows), jnp.float32)
    for k in range(p.chans):
        at = pl.multiple_of((c ^ p.mask(k)) * p.hidden, p.hidden)
        grad_hidden = dot(w_radiance_ref[pl.ds(at, p.hidden), :], cotangent)
        grad_pre = (grad_hidden * slope_ref[k]).astype(jnp.bfloat16)
        total = total + dot(p.layer(weight_refs, k), grad_pre)
    total = total.astype(jnp.bfloat16)
    for target_ref, out_ref in zip(target_refs, out_refs):
        out_ref[...] = dot_nt(one_hot(target_ref[...], 0, p.rows), total).astype(jnp.bfloat16)


def add(refs):
    total = refs[0][...].astype(jnp.float32)
    for ref in refs[1:]:
        total = total + ref[...].astype(jnp.float32)
    return total


def rows_and_cells(p, count):
    target = lax.broadcasted_iota(jnp.int32, (count, 1), 0)
    return target // p.per_row, target % p.per_row - 1


def add_group_kernel(p, *refs):
    ins, outs = refs[: p.group], refs[p.group :]
    total = add(ins).astype(jnp.bfloat16)
    row, along = rows_and_cells(p, outs[0].shape[0])
    for k, out_ref in enumerate(outs):
        tile = (lax.axis_index("tile") + k) % p.tiles
        cell = (tile * p.own_cols + along + p.tiles * p.own_cols) % (p.tiles * p.own_cols)
        wanted = (cell // p.own_cols * p.rows_each + row) * p.own_cols + cell % p.own_cols
        out_ref[...] = dot(one_hot(wanted, 0, total.shape[0]), total).astype(jnp.bfloat16)


def add_tiles_kernel(p, *refs):
    ins, outs = refs[: p.tiles], refs[p.tiles :]
    total = add(ins).astype(jnp.bfloat16)
    row, along = rows_and_cells(p, p.around)
    c = lax.axis_index("chan")
    for k, out_ref in enumerate(outs):
        held = ((c // p.group) ^ k) * p.group - 1 + row - c % p.group * p.rows_each
        wanted = jnp.where(
            (held >= 0) & (held < p.rows_each), held * p.per_row + along + 1, -1
        )
        out_ref[...] = dot(one_hot(wanted, 0, total.shape[0]), total).astype(jnp.bfloat16)


def add_chips_kernel(*refs):
    refs[-1][...] = add(refs[:-1])


def diffuse_kernel(p, edge, *refs):
    ins, root_ref, out_ref = refs[: p.group], refs[-2], refs[-1]
    total = add(ins) * 0.0625
    length = p.along + 2 * edge
    shape = (length, p.around)
    cell = lax.broadcasted_iota(jnp.int32, shape, 0)
    source = lax.broadcasted_iota(jnp.int32, shape, 1)
    column = (cell - edge + 4) // 4
    spread = []
    for k in range(3):
        row = lax.axis_index("chan") % p.group + k
        pick = (source == column + row * p.per_row) & (column >= 0) & (column < p.per_row)
        spread.append(
            jnp.dot(
                pick.astype(jnp.float32),
                total,
                precision=lax.Precision.HIGHEST,
                preferred_element_type=jnp.float32,
            )
        )
    root = root_ref[...]
    state = [spread[(row + 2) // 4] for row in range(p.across + 4)]
    east_of = functools.partial(pltpu.roll, shift=length - 1, axis=0)
    west_of = functools.partial(pltpu.roll, shift=1, axis=0)
    north = root[:, :-1] * root[:, 1:]
    east, west = root * east_of(root), root * west_of(root)
    for sweep in range(2):
        fresh = list(state)
        for row in range(1 + sweep, p.across + 3 - sweep):
            here = state[row]
            fresh[row] = (
                here
                + north[:, row : row + 1] * (state[row + 1] - here)
                + north[:, row - 1 : row] * (state[row - 1] - here)
                + east[:, row : row + 1] * (east_of(here) - here)
                + west[:, row : row + 1] * (west_of(here) - here)
            )
        state = fresh
    for row in range(p.across):
        out_ref[row] = state[row + 2][edge : edge + p.along, : p.features]


def body_by_column(
    fields,
    diffusivity,
    owners,
    observed,
    usable,
    w_hidden,
    b_hidden,
    w_radiance,
    b_radiance,
    inv_cov,
):
    p = Plan(
        lax.axis_size("tile"),
        lax.axis_size("chan"),
        fields.shape,
        owners.shape,
        observed.shape,
        w_hidden.shape,
    )
    half, single = jnp.bfloat16, jnp.float32
    shape = jax.ShapeDtypeStruct
    both = ("tile", "chan")
    everyone = [(a, b) for a in range(p.tiles) for b in range(p.chans)]

    def flip(value, mask):
        return lax.ppermute(value, "chan", [(b, b ^ mask) for b in range(p.chans)])

    def shift(value, by):
        return lax.ppermute(value, "tile", [(a, (a + by) % p.tiles) for a in range(p.tiles)])

    def send(value, wanted):
        pairs = dict(wanted)
        pairs.update({target: source for source, target in wanted.items()})
        for a, b in everyone:
            if (a, b) not in pairs:
                pairs[a, b] = (a, b ^ 1)
        number = lambda place: place[0] * p.chans + place[1]
        return lax.ppermute(
            value, both, sorted((number(a), number(b)) for a, b in pairs.items())
        )

    def join(values, kernel_shape, after=()):
        return call(
            functools.partial(join_kernel, len(values)),
            shape(kernel_shape, half),
            [*values, *after],
            in_hbm=range(len(values) + len(after)),
            out_hbm=True,
            scratch=[pltpu.SemaphoreType.DMA((len(values),))],
            flops=0,
        )

    def grow(value, over, after=()):
        return join([value, over(value)], (2 * value.shape[0],) + value.shape[1:], after)

    def trade(value, mask):
        return lax.ppermute(value, "tile", [(a, a ^ mask) for a in range(p.tiles)])

    strips = call(
        functools.partial(prepare_kernel, p),
        shape((p.block, p.width), half),
        [fields, diffusivity, usable, b_hidden],
        in_hbm=range(4),
        out_hbm=True,
        scratch=[
            pltpu.VMEM(fields.shape, single),
            pltpu.VMEM(diffusivity.shape, single),
            pltpu.VMEM(usable.shape, jnp.int32),
            pltpu.VMEM(b_hidden.shape, single),
            pltpu.VMEM((p.block, p.width), single),
            pltpu.VMEM((p.block, p.width), half),
            pltpu.SemaphoreType.DMA((5,)),
        ],
        vmem=WHOLE_VMEM_BYTES,
    )
    seen, stages = observed, []
    bit = 1
    while bit < p.tiles:
        if 2 * bit < p.tiles:
            seen = grow(seen, lambda value: trade(value, bit))
        strips = grow(strips, lambda value: trade(value, bit), [seen] if bit == 1 else ())
        stages.append(strips)
        bit *= 2
    strips = join(
        [strips] + [flip(strips, k * p.group) for k in range(1, p.chips)], (p.strips, p.width)
    )
    strips = [strips] + [flip(strips, k) for k in range(1, p.group)]

    near = [w_hidden] + [flip(w_hidden, chip * p.group) for chip in range(1, p.chips)]
    near = call(
        functools.partial(stack_kernel, p),
        shape((p.chips * p.deep, p.hidden), half),
        near + [stages[-1]],
        in_hbm=[len(near)],
    )
    weights = [near] + [flip(near, k) for k in range(1, p.group)]

    far_half = p.tiles // 2
    seen = [
        seen,
        send(seen, {(b // p.group ^ far_half, b): (b // p.group, b) for b in range(p.chans)}),
    ]

    reach = p.across + 4
    place, source, cell, *targets = call(
        functools.partial(place_kernel, p),
        [shape((p.rows, 1), jnp.int32)] * 2
        + [shape((3 * reach, 1), jnp.int32)]
        + [shape((p.rows // p.group, 1), jnp.int32)] * p.group,
        [owners.reshape(1, p.rows)],
        flops=SLACK_FLOPS,
    )
    *parts, preact, kappa = call(
        functools.partial(forward_kernel, p),
        [shape((p.rows // p.steps, p.shard), half)] * p.steps
        + [shape((p.chans, p.rows, p.hidden), single), shape((3 * reach, p.lane), single)],
        [place, source, cell, b_radiance, w_radiance] + strips + weights + seen,
        scratch=[pltpu.VMEM((p.rows, p.hidden * p.chans), half)],
        flops=2 * p.rows * p.hidden * p.chans * (p.features + p.shard),
    )

    slope = call(
        slope_kernel,
        shape((p.chans, p.hidden, p.rows), single),
        [preact],
        flops=40 * preact.size,
    )

    pool, held, choices = list(parts), {}, {}
    for j in range(p.steps):
        held[0, j] = choices[0, j] = j
    for step in range(p.steps):
        for since in range(-1, step):
            for j in range(p.steps):
                order = [1 << (j + k) % p.steps for k in range(p.steps)]
                roles = [0] if since < 0 else [
                    order[since] + rest
                    for rest in range(p.chips)
                    if rest & ~sum(order[:since]) == 0
                ]
                wanted = {
                    (a, b): (a, b ^ order[step] * p.group)
                    for a, b in everyone
                    if (b // p.group ^ a) in roles
                }
                source = pool[choices[roles[0], j]]
                for role in roles:
                    choices[role + order[step], j] = len(pool)
                pool.append(send(source, wanted))
    chosen = call(
        functools.partial(choose_kernel, p, choices),
        shape((p.rows, p.shard), half),
        pool + [slope],
        in_hbm=range(len(pool) + 1),
        out_hbm=True,
        scratch=[pltpu.SemaphoreType.DMA((p.steps,))],
    )
    depart = [chosen] + [flip(chosen, k) for k in range(1, p.group)]

    partial = call(
        functools.partial(backward_kernel, p),
        [shape((p.rows // p.group, p.features), half)] * p.group,
        [w_radiance, inv_cov, slope] + depart + weights + targets,
        flops=2 * p.rows * (p.hidden * p.chans * (p.features + p.shard) + inv_cov.size),
    )
    partial = [partial[0]] + [flip(partial[k], k) for k in range(1, p.group)]
    partial = call(
        functools.partial(add_group_kernel, p),
        [shape((p.rows_each * p.per_row, p.features), half)] * p.tiles,
        partial,
    )
    partial = [partial[0]] + [shift(partial[k], k) for k in range(1, p.tiles)]
    partial = call(
        functools.partial(add_tiles_kernel, p),
        [shape((p.around, p.features), half)] * p.chips,
        partial,
    )
    partial = [partial[0]] + [flip(partial[k], k * p.group) for k in range(1, p.chips)]
    partial = call(add_chips_kernel, shape((p.around, p.features), single), partial)
    partial = [partial] + [flip(partial, k) for k in range(1, p.group)]

    edge = 8
    kappa = kappa.reshape(3, reach, p.lane)
    root = jnp.sqrt(
        jnp.concatenate(
            [kappa[0, :, p.along - edge : p.along], kappa[1, :, : p.along], kappa[2, :, :edge]],
            axis=1,
        ).T
    )
    return call(
        functools.partial(diffuse_kernel, p, edge),
        shape(fields.shape, single),
        partial + [root],
        flops=100 * fields.size,
    )


def solution(mesh):
    tiles, chans = mesh.shape["tile"], mesh.shape["chan"]
    by_column = tiles > 1 and chans % tiles == 0 and chans & (chans - 1) == 0 and chans > tiles
    placed = (
        P("chan", "tile", None),
        P("chan", "tile"),
        P(),
        P("tile", "chan"),
        P("tile"),
        P(None, "chan"),
        P("chan"),
        P(None, "chan"),
        P("chan"),
        P("tile", "chan"),
    )
    return jax.shard_map(
        body_by_column if by_column else body_by_owner,
        mesh=mesh,
        in_specs=placed,
        out_specs=P("chan", "tile", None),
        check_vma=False,
    )
```

```python
import functools

import jax
import jax.numpy as jnp
from jax import lax
from jax.experimental import pallas as pl
from jax.experimental.pallas import tpu as pltpu
from jax.sharding import PartitionSpec as P

VMEM_BYTES = 24 * 1024 * 1024
WHOLE_VMEM_BYTES = 63 * 1024 * 1024
SLACK_FLOPS = 2 * 10**9
NT_DIMS = (((1,), (1,)), ((), ()))


def padded_2(value, sides, width, wrap):
    for axis, dim in sides:
        devices, length = (lax.axis_size(axis), value.shape[dim])
        up = [(i, (i + 1) % devices) for i in range(devices if wrap else devices - 1)]
        down = [(j, i) for i, j in up]
        last = lax.slice_in_dim(value, length - width, length, axis=dim)
        first = lax.slice_in_dim(value, 0, width, axis=dim)
        before = lax.ppermute(last, axis, up)
        after = lax.ppermute(first, axis, down)
        value = jnp.concatenate([before, value, after], axis=dim)
    return value


def add_rims(values):
    rowwise = padded_2(values, (("chan", 0),), 1, False)
    return padded_2(rowwise, (("tile", 1),), 1, True)


def body_by_owner(
    fields,
    diffusivity,
    owners,
    observed,
    usable,
    w_hidden,
    b_hidden,
    w_radiance,
    b_radiance,
    inv_cov,
):
    tile_count = lax.axis_size("tile")
    chan_count = lax.axis_size("chan")
    tile_index = lax.axis_index("tile")
    chan_index = lax.axis_index("chan")
    slot_count = observed.shape[0]
    capacity = slot_count // tile_count
    cells_across, cells_along, features = fields.shape
    own_cols = cells_across // 4 * (cells_along // 4)
    tile_cols = chan_count * own_cols
    hidden_dev = w_hidden.shape[1]
    owner_table = owners[:, 0].reshape(tile_count, tile_cols)
    owner_hits = (
        owner_table[:, :, None] == jnp.arange(tile_count, dtype=jnp.int32)[None, None, :]
    ).astype(jnp.int32)
    before = jnp.sum((jnp.cumsum(owner_hits, axis=1) - owner_hits) * owner_hits, axis=2)
    tallies = jnp.sum(owner_hits, axis=1)
    slot_of = lax.dynamic_index_in_dim(
        owner_table * capacity + before, tile_index, 0, keepdims=False
    )
    arriving = lax.dynamic_index_in_dim(tallies, tile_index, 1, keepdims=False)
    occupied = (jnp.arange(capacity, dtype=jnp.int32)[None, :] < arriving[:, None]).reshape(
        slot_count
    )
    grouped = fields.reshape(cells_across // 4, 4, cells_along // 4, 4, features)
    columns = (
        (jnp.sum(grouped, axis=(1, 3)) * 0.0625).reshape(own_cols, features).astype(jnp.bfloat16)
    )
    placer = (slot_of[None, :] == jnp.arange(slot_count, dtype=jnp.int32)[:, None]).astype(
        jnp.bfloat16
    )
    outgoing = jnp.dot(
        placer,
        lax.all_gather(columns, "chan", axis=0, tiled=True),
        preferred_element_type=jnp.float32,
    )
    incoming = lax.all_to_all(
        outgoing.astype(jnp.bfloat16), "tile", split_axis=0, concat_axis=0, tiled=True
    )
    preact = lax.dot_general(
        w_hidden, incoming, (((0,), (1,)), ((), ())), preferred_element_type=jnp.float32
    )
    preact = preact + b_hidden[:, None]
    squash = jax.nn.sigmoid(preact)
    active = (preact * squash).astype(jnp.bfloat16)
    radiance = lax.dot_general(
        lax.all_gather(active, "chan", axis=0, tiled=True),
        w_radiance,
        (((0,), (0,)), ((), ())),
        preferred_element_type=jnp.float32,
    )
    radiance = radiance + b_radiance[None, :]
    in_use = usable.astype(jnp.float32) * occupied.astype(jnp.float32)
    departure = ((radiance - observed.astype(jnp.float32)) * in_use[:, None]).astype(jnp.bfloat16)
    cotangent = jnp.dot(
        lax.all_gather(departure, "chan", axis=1, tiled=True),
        lax.all_gather(inv_cov, "tile", axis=0, tiled=True),
        preferred_element_type=jnp.float32,
    )
    cotangent = cotangent.astype(jnp.bfloat16)
    full_sum = lax.psum(
        lax.dot_general(w_radiance, cotangent, NT_DIMS, preferred_element_type=jnp.float32),
        "chan",
    )
    grad_hidden = lax.dynamic_slice_in_dim(full_sum, chan_index * hidden_dev, hidden_dev, 0)
    slope_term = squash * (1.0 + preact * (1.0 - squash))
    grad_pre = (grad_hidden * slope_term).astype(jnp.bfloat16)
    part_grad = lax.dot_general(
        grad_pre, w_hidden, (((0,), (1,)), ((), ())), preferred_element_type=jnp.float32
    )
    returned = lax.all_to_all(part_grad, "tile", split_axis=0, concat_axis=0, tiled=True)
    column_grad = lax.psum_scatter(
        jnp.take(returned, slot_of, axis=0), "chan", scatter_dimension=0, tiled=True
    )
    spread = jnp.repeat(
        column_grad.reshape(cells_across // 4, cells_along // 4, features), 4, axis=0
    )
    adjoint = jnp.repeat(spread, 4, axis=1) * 0.0625
    kappa_root = jnp.sqrt(diffusivity)
    root_rim = add_rims(kappa_root)
    coef_north = (kappa_root * root_rim[2:, 1:-1])[:, :, None]
    coef_south = (kappa_root * root_rim[:-2, 1:-1])[:, :, None]
    coef_east = (kappa_root * root_rim[1:-1, 2:])[:, :, None]
    coef_west = (kappa_root * root_rim[1:-1, :-2])[:, :, None]
    for sweep_index in range(2):
        padded = add_rims(adjoint)
        adjoint = (
            adjoint
            + coef_north * (padded[2:, 1:-1] - adjoint)
            + coef_south * (padded[:-2, 1:-1] - adjoint)
            + coef_east * (padded[1:-1, 2:] - adjoint)
            + coef_west * (padded[1:-1, :-2] - adjoint)
        )
    return adjoint


def up_to(value, multiple):
    return -(-value // multiple) * multiple


def dot(left, right):
    return jnp.dot(left, right, preferred_element_type=jnp.float32)


def dot_nt(left, right):
    return lax.dot_general(left, right, NT_DIMS, preferred_element_type=jnp.float32)


def split_three(value):
    high = value.astype(jnp.bfloat16).astype(jnp.float32)
    middle = (value - high).astype(jnp.bfloat16).astype(jnp.float32)
    return high, middle, value - high - middle


def call(
    kernel, out_shape, args, in_hbm=(), out_hbm=False, scratch=(), flops=0, vmem=VMEM_BYTES
):
    far, near = pl.BlockSpec(memory_space=pl.ANY), pl.BlockSpec(memory_space=pltpu.VMEM)
    bytes_accessed = sum(a.size * a.dtype.itemsize for a in args)
    return pl.pallas_call(
        kernel,
        out_shape=out_shape,
        in_specs=[far if k in in_hbm else near for k in range(len(args))],
        out_specs=jax.tree.map(lambda _: far if out_hbm else near, out_shape),
        scratch_shapes=list(scratch),
        compiler_params=pltpu.CompilerParams(vmem_limit_bytes=vmem),
        cost_estimate=pl.CostEstimate(
            flops=flops, bytes_accessed=bytes_accessed, transcendentals=0
        ),
    )(*args)


class Plan:
    def __init__(self, tiles, chans, fields, owners, observed, w_hidden):
        self.tiles, self.chans = tiles, chans
        self.across, self.along, self.features = fields
        self.own_cols = self.across // 4 * (self.along // 4)
        self.rows = owners[0]
        self.tile_cols = self.rows // tiles
        self.slots = observed[0]
        self.shard = observed[1]
        self.capacity = self.slots // tiles
        self.hidden = w_hidden[1]
        self.group = chans // tiles
        self.chips = chans // self.group
        self.steps = self.chips.bit_length() - 1
        self.lane = up_to(self.along, 128)
        self.flag_at = up_to(self.hidden, 128)
        self.width = max(
            up_to(self.features, 128),
            2 * self.flag_at,
            self.flag_at + up_to(self.slots, 128),
            3 * self.lane,
        )
        self.block = up_to(self.own_cols + 2 + self.across, 16)
        self.per_row = self.own_cols + 2
        self.rows_each = chans // self.group
        self.around = (self.group + 2) * self.per_row
        self.deep = up_to(self.features, 16)
        self.strips = self.chips * tiles * self.block

    def order(self, mask):
        return mask % self.group * self.chips + mask // self.group

    def layer(self, refs, k):
        at = k % self.chips * self.deep
        return refs[k // self.chips][at : at + self.features, :]

    def mask(self, k):
        return k % self.chips * self.group + k // self.chips


def prepare_kernel(p, *refs):
    ins, out_ref = refs[:4], refs[4]
    fields_ref, diffusivity_ref, usable_ref, bias_ref, flat, packed, sems = refs[5:]
    copies = [
        pltpu.make_async_copy(source, target, sems.at[k])
        for k, (source, target) in enumerate(zip(ins, refs[5:9]))
    ]
    for copy in copies:
        copy.start()
    flat[...] = jnp.zeros(flat.shape, jnp.float32)
    for copy in copies:
        copy.wait()
    shape = (p.own_cols, p.along)
    row = lax.broadcasted_iota(jnp.int32, shape, 0)
    member = row == lax.broadcasted_iota(jnp.int32, shape, 1) // 4
    total = jnp.dot(
        member.astype(jnp.float32),
        fields_ref[0] + fields_ref[1] + fields_ref[2] + fields_ref[3],
        precision=lax.Precision.HIGHEST,
        preferred_element_type=jnp.float32,
    )
    flat[: p.own_cols, : p.features] = total * 0.0625
    at = p.own_cols
    high, middle, low = split_three(bias_ref[...].reshape(1, p.hidden))
    flat[at : at + 1, : p.hidden] = high
    flat[at : at + 1, p.flag_at : p.flag_at + p.hidden] = middle
    flat[at + 1 : at + 2, : p.hidden] = low
    flags = usable_ref[...].reshape(1, p.slots).astype(jnp.float32)
    flat[at + 1 : at + 2, p.flag_at : p.flag_at + p.slots] = flags
    for k, part in enumerate(split_three(diffusivity_ref[...])):
        flat[at + 2 : at + 2 + p.across, k * p.lane : k * p.lane + p.along] = part
    packed[...] = flat[...].astype(jnp.bfloat16)
    copy = pltpu.make_async_copy(packed, out_ref, sems.at[4])
    copy.start()
    copy.wait()


def place_kernel(p, owners_ref, place_ref, source_ref, cell_ref, *target_refs):
    t, c = lax.axis_index("tile"), lax.axis_index("chan")
    across = owners_ref[...]
    shape = (p.rows, p.rows)
    row = lax.broadcasted_iota(jnp.int32, shape, 0)
    other = lax.broadcasted_iota(jnp.int32, shape, 1)
    owner = jnp.sum(jnp.where(row == other, across, 0), axis=1, keepdims=True)
    first = lax.broadcasted_iota(jnp.int32, owner.shape, 0)
    begin = first // p.tile_cols * p.tile_cols
    same = (owner == across) & (other >= begin) & (other < row)
    rank = jnp.sum(jnp.where(same, 1, 0), axis=1, keepdims=True)
    tile = first // p.tile_cols
    place_ref[...] = (owner ^ t) * p.slots + tile * p.capacity + rank

    def strip(tile, chan):
        other = chan ^ c
        return p.order(other) * p.tiles + (tile ^ t)

    source_ref[...] = (
        strip(tile, first % p.tile_cols // p.own_cols) * p.block + first % p.own_cols
    )

    row = lax.broadcasted_iota(jnp.int32, cell_ref.shape, 0)
    reach = p.across + 4
    tile = (t + row // reach - 1 + p.tiles) % p.tiles
    cell = c * p.across - 2 + row % reach
    inside = (cell >= 0) & (cell < p.chans * p.across)
    cell = jnp.where(inside, cell, 0)
    wanted = strip(tile, cell // p.across) * p.block + p.own_cols + 2 + cell % p.across
    cell_ref[...] = jnp.where(inside, wanted, -1)

    each = p.rows_each * p.own_cols
    target = lax.broadcasted_iota(jnp.int32, target_refs[0].shape, 0)
    for k, target_ref in enumerate(target_refs):
        first = (c % p.group ^ k) * each
        target_ref[...] = target // each * p.tile_cols + first + target % each


def join_kernel(count, *refs):
    ins, out_ref, sems = refs[:count], refs[-2], refs[-1]
    size = out_ref.shape[0] // count
    copies = [
        pltpu.make_async_copy(
            ref, out_ref.at[k] if ref.ndim < out_ref.ndim else out_ref.at[pl.ds(k * size, size)],
            sems.at[k],
        )
        for k, ref in enumerate(ins)
    ]
    for copy in copies:
        copy.start()
    for copy in copies:
        copy.wait()


def stack_kernel(p, *refs):
    for k, ref in enumerate(refs[: p.chips]):
        refs[-1][k * p.deep : k * p.deep + p.features, :] = ref[...]
        refs[-1][k * p.deep + p.features : (k + 1) * p.deep, :] = jnp.zeros(
            (p.deep - p.features, p.hidden), jnp.bfloat16
        )


def one_hot(wanted, first, count):
    source = lax.broadcasted_iota(jnp.int32, (wanted.shape[0], count), 1)
    return (source + first == wanted).astype(jnp.bfloat16)


def forward_kernel(p, *refs):
    refs = list(refs)
    take = lambda n: [refs.pop(0) for _ in range(n)]
    place_ref, source_ref, cell_ref, bias_ref, w_radiance_ref = take(5)
    strip_refs, weight_refs, seen_refs = take(p.group), take(p.group), take(p.tiles)
    part_refs = take(p.steps)
    preact_ref, kappa_ref, active = refs
    c = lax.axis_index("chan")
    gathered = [ref[...] for ref in strip_refs]
    columns = sum(
        dot(one_hot(source_ref[...], k * p.strips, p.strips), strips)
        for k, strips in enumerate(gathered)
    )
    columns = columns.astype(jnp.bfloat16)[:, : p.features]
    for k in range(p.chans):
        member, chip = k // p.chips, k % p.chips
        at = chip * p.tiles * p.block + p.own_cols
        low = strip_refs[member][at : at + 2, :].astype(jnp.float32)
        bias = (
            low[:1, : p.hidden]
            + low[:1, p.flag_at : p.flag_at + p.hidden]
            + low[1:, : p.hidden]
        )
        preact = dot(columns, p.layer(weight_refs, k)) + bias
        preact_ref[k] = preact
        at = pl.multiple_of((c ^ p.mask(k)) * p.hidden, p.hidden)
        active[:, pl.ds(at, p.hidden)] = (preact * jax.nn.sigmoid(preact)).astype(jnp.bfloat16)
    part = p.rows // p.steps
    count = seen_refs[0].shape[0]
    for j, part_ref in enumerate(part_refs):
        at = slice(j * part, (j + 1) * part)
        in_use = jnp.zeros((part, 1), jnp.float32)
        for k in range(p.tiles):
            slot = lax.broadcasted_iota(jnp.int32, (part, p.slots), 1) + k * p.slots
            low = k * p.block + p.own_cols + 1
            flags = strip_refs[0][low : low + 1, p.flag_at : p.flag_at + p.slots]
            flags = jnp.where(place_ref[at, :] == slot, flags.astype(jnp.float32), 0.0)
            in_use = in_use + jnp.sum(flags, axis=1, keepdims=True)
        observed = sum(
            dot(one_hot(place_ref[at, :], k * count, count), ref[...])
            for k, ref in enumerate(seen_refs)
        )
        radiance = dot(active[at, :], w_radiance_ref[...]) + bias_ref[...].reshape(1, p.shard)
        part_ref[...] = ((radiance - observed) * in_use).astype(jnp.bfloat16)
    parts = sum(
        dot(one_hot(cell_ref[...], k * p.strips, p.strips), strips)
        for k, strips in enumerate(gathered)
    )
    kappa_ref[...] = sum(parts[:, k * p.lane : (k + 1) * p.lane] for k in range(3))


def slope_kernel(preact_ref, slope_ref):
    for k in range(preact_ref.shape[0]):
        preact = preact_ref[k]
        squash = jax.nn.sigmoid(preact)
        slope_ref[k] = (squash * (1.0 + preact * (1.0 - squash))).T


def choose_kernel(p, early, count, *refs):
    refs, out_ref, sems = refs[: 2 * count], refs[-2], refs[-1]
    size = out_ref.shape[0] // count
    role = (lax.axis_index("chan") // p.group) ^ lax.axis_index("tile")
    for j in range(count):
        held = (role & ~early[j]) == 0
        for ref, wanted in ((refs[2 * j], held), (refs[2 * j + 1], ~held)):

            @pl.when(wanted)
            def _():
                pltpu.make_async_copy(ref, out_ref.at[pl.ds(j * size, size)], sems.at[j]).start()

    for j in range(count):
        pltpu.make_async_copy(
            refs[2 * j], out_ref.at[pl.ds(j * size, size)], sems.at[j]
        ).wait()


def backward_kernel(p, *refs):
    refs = list(refs)
    take = lambda n: [refs.pop(0) for _ in range(n)]
    w_radiance_ref, inv_cov_ref, slope_ref = take(3)
    depart_refs, weight_refs, target_refs = take(p.group), take(p.group), take(p.group)
    out_refs = refs
    c = lax.axis_index("chan")
    cotangent = None
    for k, ref in enumerate(depart_refs):
        at = pl.multiple_of((c % p.group ^ k) * p.shard, p.shard)
        term = dot(ref[...], inv_cov_ref[pl.ds(at, p.shard), :])
        cotangent = term if cotangent is None else cotangent + term
    cotangent = cotangent.T.astype(jnp.bfloat16)
    total = jnp.zeros((p.features, p.rows), jnp.float32)
    for k in range(p.chans):
        at = pl.multiple_of((c ^ p.mask(k)) * p.hidden, p.hidden)
        grad_hidden = dot(w_radiance_ref[pl.ds(at, p.hidden), :], cotangent)
        grad_pre = (grad_hidden * slope_ref[k]).astype(jnp.bfloat16)
        total = total + dot(p.layer(weight_refs, k), grad_pre)
    total = total.astype(jnp.bfloat16)
    for target_ref, out_ref in zip(target_refs, out_refs):
        out_ref[...] = dot_nt(one_hot(target_ref[...], 0, p.rows), total).astype(jnp.bfloat16)


def add(refs):
    total = refs[0][...].astype(jnp.float32)
    for ref in refs[1:]:
        total = total + ref[...].astype(jnp.float32)
    return total


def rows_and_cells(p, count):
    target = lax.broadcasted_iota(jnp.int32, (count, 1), 0)
    return target // p.per_row, target % p.per_row - 1


def add_group_kernel(p, *refs):
    ins, outs = refs[: p.group], refs[p.group :]
    total = add(ins).astype(jnp.bfloat16)
    row, along = rows_and_cells(p, outs[0].shape[0])
    for k, out_ref in enumerate(outs):
        tile = lax.axis_index("tile") ^ k
        cell = (tile * p.own_cols + along + p.tiles * p.own_cols) % (p.tiles * p.own_cols)
        wanted = (cell // p.own_cols * p.rows_each + row) * p.own_cols + cell % p.own_cols
        out_ref[...] = dot(one_hot(wanted, 0, total.shape[0]), total).astype(jnp.bfloat16)


def add_tiles_kernel(p, *refs):
    ins, outs = refs[: p.tiles], refs[p.tiles :]
    total = add(ins).astype(jnp.bfloat16)
    row, along = rows_and_cells(p, p.around)
    c = lax.axis_index("chan")
    for k, out_ref in enumerate(outs):
        held = ((c // p.group) ^ k) * p.group - 1 + row - c % p.group * p.rows_each
        wanted = jnp.where(
            (held >= 0) & (held < p.rows_each), held * p.per_row + along + 1, -1
        )
        out_ref[...] = dot(one_hot(wanted, 0, total.shape[0]), total).astype(jnp.bfloat16)


def add_chips_kernel(*refs):
    refs[-1][...] = add(refs[:-1])


def diffuse_kernel(p, edge, *refs):
    ins, root_ref, out_ref = refs[: p.group], refs[-2], refs[-1]
    total = add(ins) * 0.0625
    length = p.along + 2 * edge
    shape = (length, p.around)
    cell = lax.broadcasted_iota(jnp.int32, shape, 0)
    source = lax.broadcasted_iota(jnp.int32, shape, 1)
    column = (cell - edge + 4) // 4
    spread = []
    for k in range(3):
        row = lax.axis_index("chan") % p.group + k
        pick = (source == column + row * p.per_row) & (column >= 0) & (column < p.per_row)
        spread.append(
            jnp.dot(
                pick.astype(jnp.float32),
                total,
                precision=lax.Precision.HIGHEST,
                preferred_element_type=jnp.float32,
            )
        )
    root = root_ref[...]
    state = [spread[(row + 2) // 4] for row in range(p.across + 4)]
    east_of = functools.partial(pltpu.roll, shift=length - 1, axis=0)
    west_of = functools.partial(pltpu.roll, shift=1, axis=0)
    north = root[:, :-1] * root[:, 1:]
    east, west = root * east_of(root), root * west_of(root)
    for sweep in range(2):
        fresh = list(state)
        for row in range(1 + sweep, p.across + 3 - sweep):
            here = state[row]
            fresh[row] = (
                here
                + north[:, row : row + 1] * (state[row + 1] - here)
                + north[:, row - 1 : row] * (state[row - 1] - here)
                + east[:, row : row + 1] * (east_of(here) - here)
                + west[:, row : row + 1] * (west_of(here) - here)
            )
        state = fresh
    for row in range(p.across):
        out_ref[row] = state[row + 2][edge : edge + p.along, : p.features]


def body_by_column(
    fields,
    diffusivity,
    owners,
    observed,
    usable,
    w_hidden,
    b_hidden,
    w_radiance,
    b_radiance,
    inv_cov,
):
    p = Plan(
        lax.axis_size("tile"),
        lax.axis_size("chan"),
        fields.shape,
        owners.shape,
        observed.shape,
        w_hidden.shape,
    )
    half, single = jnp.bfloat16, jnp.float32
    shape = jax.ShapeDtypeStruct
    both = ("tile", "chan")
    everyone = [(a, b) for a in range(p.tiles) for b in range(p.chans)]

    def flip(value, mask):
        return lax.ppermute(value, "chan", [(b, b ^ mask) for b in range(p.chans)])

    def trade(value, mask):
        return lax.ppermute(value, "tile", [(a, a ^ mask) for a in range(p.tiles)])

    def send(value, wanted):
        pairs = dict(wanted)
        pairs.update({target: source for source, target in wanted.items()})
        for a, b in everyone:
            if (a, b) not in pairs:
                pairs[a, b] = (a, b ^ 1)
        number = lambda place: place[0] * p.chans + place[1]
        return lax.ppermute(
            value, both, sorted((number(a), number(b)) for a, b in pairs.items())
        )

    def join(values, kernel_shape, after=()):
        return call(
            functools.partial(join_kernel, len(values)),
            shape(kernel_shape, half),
            [*values, *after],
            in_hbm=range(len(values) + len(after)),
            out_hbm=True,
            scratch=[pltpu.SemaphoreType.DMA((len(values),))],
            flops=0,
        )

    strips = call(
        functools.partial(prepare_kernel, p),
        shape((p.block, p.width), half),
        [fields, diffusivity, usable, b_hidden],
        in_hbm=range(4),
        out_hbm=True,
        scratch=[
            pltpu.VMEM(fields.shape, single),
            pltpu.VMEM(diffusivity.shape, single),
            pltpu.VMEM(usable.shape, jnp.int32),
            pltpu.VMEM(b_hidden.shape, single),
            pltpu.VMEM((p.block, p.width), single),
            pltpu.VMEM((p.block, p.width), half),
            pltpu.SemaphoreType.DMA((5,)),
        ],
        vmem=WHOLE_VMEM_BYTES,
    )
    _, layer, held = lax.optimization_barrier((strips, w_hidden, observed))
    held, bit = [held], 1
    while 2 * bit < p.tiles:
        held += [trade(value, bit) for value in held]
        bit *= 2
    wanted = {(b // p.group ^ bit, b): (b // p.group, b) for b in range(p.chans)}
    far = [send(value, wanted) for value in held]
    seen = [observed] + held[1:] + far

    near = [w_hidden] + [flip(layer, chip * p.group) for chip in range(1, p.chips - 1)]
    bit, before = 1, held[1:] + far[:1]
    while bit < p.tiles:
        strips = join(
            [strips, trade(strips, bit)], (2 * strips.shape[0], p.width), before
        )
        if bit == 1:
            _, layer = lax.optimization_barrier((strips, layer))
            near.append(flip(layer, (p.chips - 1) * p.group))
        bit, before = 2 * bit, ()

    near = call(
        functools.partial(stack_kernel, p),
        shape((p.chips * p.deep, p.hidden), half),
        near + [strips],
        in_hbm=[len(near)],
    )
    weights = [near] + [flip(near, k) for k in range(1, p.group)]
    strips = join(
        [strips] + [flip(strips, k * p.group) for k in range(1, p.chips)],
        (p.strips, p.width),
        far[1:],
    )
    strips = [strips] + [flip(strips, k) for k in range(1, p.group)]

    reach = p.across + 4
    place, source, cell, *targets = call(
        functools.partial(place_kernel, p),
        [shape((p.rows, 1), jnp.int32)] * 2
        + [shape((3 * reach, 1), jnp.int32)]
        + [shape((p.rows // p.group, 1), jnp.int32)] * p.group,
        [owners.reshape(1, p.rows)],
        flops=SLACK_FLOPS,
    )
    *parts, preact, kappa = call(
        functools.partial(forward_kernel, p),
        [shape((p.rows // p.steps, p.shard), half)] * p.steps
        + [shape((p.chans, p.rows, p.hidden), single), shape((3 * reach, p.lane), single)],
        [place, source, cell, b_radiance, w_radiance] + strips + weights + seen,
        scratch=[pltpu.VMEM((p.rows, p.hidden * p.chans), half)],
        flops=2 * p.rows * p.hidden * p.chans * (p.features + p.shard),
    )

    slope = call(
        slope_kernel,
        shape((p.chans, p.hidden, p.rows), single),
        [preact],
        flops=40 * preact.size,
    )

    def choose(pairs, early, after=()):
        values = [value for pair in pairs for value in pair]
        return call(
            functools.partial(choose_kernel, p, early, len(pairs)),
            shape((len(pairs) * values[0].shape[0], p.shard), half),
            [*values, *after],
            in_hbm=range(len(values) + len(after)),
            out_hbm=True,
            scratch=[pltpu.SemaphoreType.DMA((len(pairs),))],
        )

    held = [(part, None, 0) for part in parts]
    for step in range(p.steps):
        for j, (part, arrived, early) in enumerate(held):
            bit = 1 << (j + step) % p.steps
            if arrived is not None:
                reached = early | 1 << (j + step - 1) % p.steps
                part, early = choose([(part, arrived)], [early]), reached
            wanted = {
                (a, b): (a, b ^ bit * p.group)
                for a, b in everyone
                if (b // p.group ^ a) & ~early == 0
            }
            held[j] = part, send(part, wanted), early
    chosen = choose([pair[:2] for pair in held], [pair[2] for pair in held], [slope])
    depart = [chosen] + [flip(chosen, k) for k in range(1, p.group)]

    partial = call(
        functools.partial(backward_kernel, p),
        [shape((p.rows // p.group, p.features), half)] * p.group,
        [w_radiance, inv_cov, slope] + depart + weights + targets,
        flops=2 * p.rows * (p.hidden * p.chans * (p.features + p.shard) + inv_cov.size),
    )
    partial = [partial[0]] + [flip(partial[k], k) for k in range(1, p.group)]
    partial = call(
        functools.partial(add_group_kernel, p),
        [shape((p.rows_each * p.per_row, p.features), half)] * p.tiles,
        partial,
    )
    partial = [partial[0]] + [trade(partial[k], k) for k in range(1, p.tiles)]
    partial = call(
        functools.partial(add_tiles_kernel, p),
        [shape((p.around, p.features), half)] * p.chips,
        partial,
    )
    partial = [partial[0]] + [flip(partial[k], k * p.group) for k in range(1, p.chips)]
    partial = call(add_chips_kernel, shape((p.around, p.features), single), partial)
    partial = [partial] + [flip(partial, k) for k in range(1, p.group)]

    edge = 8
    kappa = kappa.reshape(3, reach, p.lane)
    root = jnp.sqrt(
        jnp.concatenate(
            [kappa[0, :, p.along - edge : p.along], kappa[1, :, : p.along], kappa[2, :, :edge]],
            axis=1,
        ).T
    )
    return call(
        functools.partial(diffuse_kernel, p, edge),
        shape(fields.shape, single),
        partial + [root],
        flops=100 * fields.size,
    )


def solution(mesh):
    tiles, chans = mesh.shape["tile"], mesh.shape["chan"]
    by_column = tiles > 1 and chans % tiles == 0 and chans & (chans - 1) == 0 and chans > tiles
    placed = (
        P("chan", "tile", None),
        P("chan", "tile"),
        P(),
        P("tile", "chan"),
        P("tile"),
        P(None, "chan"),
        P("chan"),
        P(None, "chan"),
        P("chan"),
        P("tile", "chan"),
    )
    return jax.shard_map(
        body_by_column if by_column else body_by_owner,
        mesh=mesh,
        in_specs=placed,
        out_specs=P("chan", "tile", None),
        check_vma=False,
    )
```

```python
import functools

import jax
import jax.numpy as jnp
from jax import lax
from jax.experimental import pallas as pl
from jax.experimental.pallas import tpu as pltpu
from jax.sharding import PartitionSpec as P

VMEM_BYTES = 24 * 1024 * 1024
WHOLE_VMEM_BYTES = 63 * 1024 * 1024
SLACK_FLOPS = 2 * 10**9
NT_DIMS = (((1,), (1,)), ((), ()))


def padded_2(value, sides, width, wrap):
    for axis, dim in sides:
        devices, length = (lax.axis_size(axis), value.shape[dim])
        up = [(i, (i + 1) % devices) for i in range(devices if wrap else devices - 1)]
        down = [(j, i) for i, j in up]
        last = lax.slice_in_dim(value, length - width, length, axis=dim)
        first = lax.slice_in_dim(value, 0, width, axis=dim)
        before = lax.ppermute(last, axis, up)
        after = lax.ppermute(first, axis, down)
        value = jnp.concatenate([before, value, after], axis=dim)
    return value


def add_rims(values):
    rowwise = padded_2(values, (("chan", 0),), 1, False)
    return padded_2(rowwise, (("tile", 1),), 1, True)


def body_by_owner(
    fields,
    diffusivity,
    owners,
    observed,
    usable,
    w_hidden,
    b_hidden,
    w_radiance,
    b_radiance,
    inv_cov,
):
    tile_count = lax.axis_size("tile")
    chan_count = lax.axis_size("chan")
    tile_index = lax.axis_index("tile")
    chan_index = lax.axis_index("chan")
    slot_count = observed.shape[0]
    capacity = slot_count // tile_count
    cells_across, cells_along, features = fields.shape
    own_cols = cells_across // 4 * (cells_along // 4)
    tile_cols = chan_count * own_cols
    hidden_dev = w_hidden.shape[1]
    owner_table = owners[:, 0].reshape(tile_count, tile_cols)
    owner_hits = (
        owner_table[:, :, None] == jnp.arange(tile_count, dtype=jnp.int32)[None, None, :]
    ).astype(jnp.int32)
    before = jnp.sum((jnp.cumsum(owner_hits, axis=1) - owner_hits) * owner_hits, axis=2)
    tallies = jnp.sum(owner_hits, axis=1)
    slot_of = lax.dynamic_index_in_dim(
        owner_table * capacity + before, tile_index, 0, keepdims=False
    )
    arriving = lax.dynamic_index_in_dim(tallies, tile_index, 1, keepdims=False)
    occupied = (jnp.arange(capacity, dtype=jnp.int32)[None, :] < arriving[:, None]).reshape(
        slot_count
    )
    grouped = fields.reshape(cells_across // 4, 4, cells_along // 4, 4, features)
    columns = (
        (jnp.sum(grouped, axis=(1, 3)) * 0.0625).reshape(own_cols, features).astype(jnp.bfloat16)
    )
    placer = (slot_of[None, :] == jnp.arange(slot_count, dtype=jnp.int32)[:, None]).astype(
        jnp.bfloat16
    )
    outgoing = jnp.dot(
        placer,
        lax.all_gather(columns, "chan", axis=0, tiled=True),
        preferred_element_type=jnp.float32,
    )
    incoming = lax.all_to_all(
        outgoing.astype(jnp.bfloat16), "tile", split_axis=0, concat_axis=0, tiled=True
    )
    preact = lax.dot_general(
        w_hidden, incoming, (((0,), (1,)), ((), ())), preferred_element_type=jnp.float32
    )
    preact = preact + b_hidden[:, None]
    squash = jax.nn.sigmoid(preact)
    active = (preact * squash).astype(jnp.bfloat16)
    radiance = lax.dot_general(
        lax.all_gather(active, "chan", axis=0, tiled=True),
        w_radiance,
        (((0,), (0,)), ((), ())),
        preferred_element_type=jnp.float32,
    )
    radiance = radiance + b_radiance[None, :]
    in_use = usable.astype(jnp.float32) * occupied.astype(jnp.float32)
    departure = ((radiance - observed.astype(jnp.float32)) * in_use[:, None]).astype(jnp.bfloat16)
    cotangent = jnp.dot(
        lax.all_gather(departure, "chan", axis=1, tiled=True),
        lax.all_gather(inv_cov, "tile", axis=0, tiled=True),
        preferred_element_type=jnp.float32,
    )
    cotangent = cotangent.astype(jnp.bfloat16)
    full_sum = lax.psum(
        lax.dot_general(w_radiance, cotangent, NT_DIMS, preferred_element_type=jnp.float32),
        "chan",
    )
    grad_hidden = lax.dynamic_slice_in_dim(full_sum, chan_index * hidden_dev, hidden_dev, 0)
    slope_term = squash * (1.0 + preact * (1.0 - squash))
    grad_pre = (grad_hidden * slope_term).astype(jnp.bfloat16)
    part_grad = lax.dot_general(
        grad_pre, w_hidden, (((0,), (1,)), ((), ())), preferred_element_type=jnp.float32
    )
    returned = lax.all_to_all(part_grad, "tile", split_axis=0, concat_axis=0, tiled=True)
    column_grad = lax.psum_scatter(
        jnp.take(returned, slot_of, axis=0), "chan", scatter_dimension=0, tiled=True
    )
    spread = jnp.repeat(
        column_grad.reshape(cells_across // 4, cells_along // 4, features), 4, axis=0
    )
    adjoint = jnp.repeat(spread, 4, axis=1) * 0.0625
    kappa_root = jnp.sqrt(diffusivity)
    root_rim = add_rims(kappa_root)
    coef_north = (kappa_root * root_rim[2:, 1:-1])[:, :, None]
    coef_south = (kappa_root * root_rim[:-2, 1:-1])[:, :, None]
    coef_east = (kappa_root * root_rim[1:-1, 2:])[:, :, None]
    coef_west = (kappa_root * root_rim[1:-1, :-2])[:, :, None]
    for sweep_index in range(2):
        padded = add_rims(adjoint)
        adjoint = (
            adjoint
            + coef_north * (padded[2:, 1:-1] - adjoint)
            + coef_south * (padded[:-2, 1:-1] - adjoint)
            + coef_east * (padded[1:-1, 2:] - adjoint)
            + coef_west * (padded[1:-1, :-2] - adjoint)
        )
    return adjoint


def up_to(value, multiple):
    return -(-value // multiple) * multiple


def dot(left, right):
    return jnp.dot(left, right, preferred_element_type=jnp.float32)


def dot_nt(left, right):
    return lax.dot_general(left, right, NT_DIMS, preferred_element_type=jnp.float32)


def split_three(value):
    high = value.astype(jnp.bfloat16).astype(jnp.float32)
    middle = (value - high).astype(jnp.bfloat16).astype(jnp.float32)
    return high, middle, value - high - middle


def call(
    kernel, out_shape, args, in_hbm=(), out_hbm=False, scratch=(), flops=0, vmem=VMEM_BYTES
):
    far, near = pl.BlockSpec(memory_space=pl.ANY), pl.BlockSpec(memory_space=pltpu.VMEM)
    bytes_accessed = sum(a.size * a.dtype.itemsize for a in args)
    return pl.pallas_call(
        kernel,
        out_shape=out_shape,
        in_specs=[far if k in in_hbm else near for k in range(len(args))],
        out_specs=jax.tree.map(lambda _: far if out_hbm else near, out_shape),
        scratch_shapes=list(scratch),
        compiler_params=pltpu.CompilerParams(vmem_limit_bytes=vmem),
        cost_estimate=pl.CostEstimate(
            flops=flops, bytes_accessed=bytes_accessed, transcendentals=0
        ),
    )(*args)


class Plan:
    def __init__(self, tiles, chans, fields, owners, observed, w_hidden):
        self.tiles, self.chans = tiles, chans
        self.across, self.along, self.features = fields
        self.own_cols = self.across // 4 * (self.along // 4)
        self.rows = owners[0]
        self.tile_cols = self.rows // tiles
        self.slots = observed[0]
        self.shard = observed[1]
        self.capacity = self.slots // tiles
        self.hidden = w_hidden[1]
        self.group = chans // tiles
        self.chips = chans // self.group
        self.steps = self.chips.bit_length() - 1
        self.lane = up_to(self.along, 128)
        self.flag_at = up_to(self.hidden, 128)
        self.width = max(
            up_to(self.features, 128),
            2 * self.flag_at,
            self.flag_at + up_to(self.slots, 128),
            3 * self.lane,
        )
        self.block = up_to(self.own_cols + 2 + self.across, 16)
        self.per_row = self.own_cols + 2
        self.rows_each = chans // self.group
        self.around = (self.group + 2) * self.per_row
        self.deep = up_to(self.features, 16)
        self.strips = self.chips * tiles * self.block

    def order(self, mask):
        return mask % self.group * self.chips + mask // self.group

    def layer(self, refs, k):
        at = k % self.chips * self.deep
        return refs[k // self.chips][at : at + self.features, :]

    def mask(self, k):
        return k % self.chips * self.group + k // self.chips


def prepare_kernel(p, *refs):
    ins, out_ref = refs[:4], refs[4]
    fields_ref, diffusivity_ref, usable_ref, bias_ref, flat, packed, sems = refs[5:]
    copies = [
        pltpu.make_async_copy(source, target, sems.at[k])
        for k, (source, target) in enumerate(zip(ins, refs[5:9]))
    ]
    for copy in copies:
        copy.start()
    flat[...] = jnp.zeros(flat.shape, jnp.float32)
    for copy in copies:
        copy.wait()
    shape = (p.own_cols, p.along)
    row = lax.broadcasted_iota(jnp.int32, shape, 0)
    member = row == lax.broadcasted_iota(jnp.int32, shape, 1) // 4
    total = jnp.dot(
        member.astype(jnp.float32),
        fields_ref[0] + fields_ref[1] + fields_ref[2] + fields_ref[3],
        precision=lax.Precision.HIGHEST,
        preferred_element_type=jnp.float32,
    )
    flat[: p.own_cols, : p.features] = total * 0.0625
    at = p.own_cols
    high, middle, low = split_three(bias_ref[...].reshape(1, p.hidden))
    flat[at : at + 1, : p.hidden] = high
    flat[at : at + 1, p.flag_at : p.flag_at + p.hidden] = middle
    flat[at + 1 : at + 2, : p.hidden] = low
    flags = usable_ref[...].reshape(1, p.slots).astype(jnp.float32)
    flat[at + 1 : at + 2, p.flag_at : p.flag_at + p.slots] = flags
    for k, part in enumerate(split_three(diffusivity_ref[...])):
        flat[at + 2 : at + 2 + p.across, k * p.lane : k * p.lane + p.along] = part
    packed[...] = flat[...].astype(jnp.bfloat16)
    copy = pltpu.make_async_copy(packed, out_ref, sems.at[4])
    copy.start()
    copy.wait()


def place_kernel(p, owners_ref, place_ref, source_ref, cell_ref, *target_refs):
    t, c = lax.axis_index("tile"), lax.axis_index("chan")
    across = owners_ref[...]
    shape = (p.rows, p.rows)
    row = lax.broadcasted_iota(jnp.int32, shape, 0)
    other = lax.broadcasted_iota(jnp.int32, shape, 1)
    owner = jnp.sum(jnp.where(row == other, across, 0), axis=1, keepdims=True)
    first = lax.broadcasted_iota(jnp.int32, owner.shape, 0)
    begin = first // p.tile_cols * p.tile_cols
    same = (owner == across) & (other >= begin) & (other < row)
    rank = jnp.sum(jnp.where(same, 1, 0), axis=1, keepdims=True)
    tile = first // p.tile_cols
    place_ref[...] = (owner ^ t) * p.slots + tile * p.capacity + rank

    def strip(tile, chan):
        other = chan ^ c
        return p.order(other) * p.tiles + (tile ^ t)

    source_ref[...] = (
        strip(tile, first % p.tile_cols // p.own_cols) * p.block + first % p.own_cols
    )

    row = lax.broadcasted_iota(jnp.int32, cell_ref.shape, 0)
    reach = p.across + 4
    tile = (t + row // reach - 1 + p.tiles) % p.tiles
    cell = c * p.across - 2 + row % reach
    inside = (cell >= 0) & (cell < p.chans * p.across)
    cell = jnp.where(inside, cell, 0)
    wanted = strip(tile, cell // p.across) * p.block + p.own_cols + 2 + cell % p.across
    cell_ref[...] = jnp.where(inside, wanted, -1)

    each = p.rows_each * p.own_cols
    target = lax.broadcasted_iota(jnp.int32, target_refs[0].shape, 0)
    for k, target_ref in enumerate(target_refs):
        first = (c % p.group ^ k) * each
        target_ref[...] = target // each * p.tile_cols + first + target % each


def join_kernel(count, *refs):
    ins, out_ref, sems = refs[:count], refs[-2], refs[-1]
    size = out_ref.shape[0] // count
    copies = [
        pltpu.make_async_copy(
            ref, out_ref.at[k] if ref.ndim < out_ref.ndim else out_ref.at[pl.ds(k * size, size)],
            sems.at[k],
        )
        for k, ref in enumerate(ins)
    ]
    for copy in copies:
        copy.start()
    for copy in copies:
        copy.wait()


def stack_kernel(p, *refs):
    for k, ref in enumerate(refs[: p.chips]):
        refs[-1][k * p.deep : k * p.deep + p.features, :] = ref[...]
        refs[-1][k * p.deep + p.features : (k + 1) * p.deep, :] = jnp.zeros(
            (p.deep - p.features, p.hidden), jnp.bfloat16
        )


def one_hot(wanted, first, count):
    source = lax.broadcasted_iota(jnp.int32, (wanted.shape[0], count), 1)
    return (source + first == wanted).astype(jnp.bfloat16)


def forward_kernel(p, *refs):
    refs = list(refs)
    take = lambda n: [refs.pop(0) for _ in range(n)]
    place_ref, source_ref, cell_ref, bias_ref, w_radiance_ref = take(5)
    strip_refs, weight_refs, seen_refs = take(p.group), take(p.group), take(p.tiles)
    part_refs = take(p.steps)
    preact_ref, kappa_ref, active = refs
    c = lax.axis_index("chan")
    gathered = [ref[...] for ref in strip_refs]
    columns = sum(
        dot(one_hot(source_ref[...], k * p.strips, p.strips), strips)
        for k, strips in enumerate(gathered)
    )
    columns = columns.astype(jnp.bfloat16)[:, : p.features]
    for k in range(p.chans):
        member, chip = k // p.chips, k % p.chips
        at = chip * p.tiles * p.block + p.own_cols
        low = strip_refs[member][at : at + 2, :].astype(jnp.float32)
        bias = (
            low[:1, : p.hidden]
            + low[:1, p.flag_at : p.flag_at + p.hidden]
            + low[1:, : p.hidden]
        )
        preact = dot(columns, p.layer(weight_refs, k)) + bias
        preact_ref[k] = preact
        at = pl.multiple_of((c ^ p.mask(k)) * p.hidden, p.hidden)
        active[:, pl.ds(at, p.hidden)] = (preact * jax.nn.sigmoid(preact)).astype(jnp.bfloat16)
    part = p.rows // p.steps
    count = seen_refs[0].shape[0]
    for j, part_ref in enumerate(part_refs):
        at = slice(j * part, (j + 1) * part)
        in_use = jnp.zeros((part, 1), jnp.float32)
        for k in range(p.tiles):
            slot = lax.broadcasted_iota(jnp.int32, (part, p.slots), 1) + k * p.slots
            low = k * p.block + p.own_cols + 1
            flags = strip_refs[0][low : low + 1, p.flag_at : p.flag_at + p.slots]
            flags = jnp.where(place_ref[at, :] == slot, flags.astype(jnp.float32), 0.0)
            in_use = in_use + jnp.sum(flags, axis=1, keepdims=True)
        observed = sum(
            dot(one_hot(place_ref[at, :], k * count, count), ref[...])
            for k, ref in enumerate(seen_refs)
        )
        radiance = dot(active[at, :], w_radiance_ref[...]) + bias_ref[...].reshape(1, p.shard)
        part_ref[...] = ((radiance - observed) * in_use).astype(jnp.bfloat16)
    parts = sum(
        dot(one_hot(cell_ref[...], k * p.strips, p.strips), strips)
        for k, strips in enumerate(gathered)
    )
    kappa_ref[...] = sum(parts[:, k * p.lane : (k + 1) * p.lane] for k in range(3))


def slope_kernel(preact_ref, slope_ref):
    for k in range(preact_ref.shape[0]):
        preact = preact_ref[k]
        squash = jax.nn.sigmoid(preact)
        slope_ref[k] = (squash * (1.0 + preact * (1.0 - squash))).T


def choose_kernel(p, choices, *refs):
    refs, out_ref, sems = refs[:-3], refs[-2], refs[-1]
    size = refs[0].shape[0]
    role = (lax.axis_index("chan") // p.group) ^ lax.axis_index("tile")
    for place in range(p.chips):

        @pl.when(role == place)
        def _():
            copies = [
                pltpu.make_async_copy(
                    refs[choices[place, j]], out_ref.at[pl.ds(j * size, size)], sems.at[j]
                )
                for j in range(p.steps)
            ]
            for copy in copies:
                copy.start()
            for copy in copies:
                copy.wait()


def backward_kernel(p, *refs):
    refs = list(refs)
    take = lambda n: [refs.pop(0) for _ in range(n)]
    w_radiance_ref, inv_cov_ref, slope_ref = take(3)
    depart_refs, weight_refs, target_refs = take(p.group), take(p.group), take(p.group)
    out_refs = refs
    c = lax.axis_index("chan")
    cotangent = None
    for k, ref in enumerate(depart_refs):
        at = pl.multiple_of((c % p.group ^ k) * p.shard, p.shard)
        term = dot(ref[...], inv_cov_ref[pl.ds(at, p.shard), :])
        cotangent = term if cotangent is None else cotangent + term
    cotangent = cotangent.T.astype(jnp.bfloat16)
    total = jnp.zeros((p.features, p.rows), jnp.float32)
    for k in range(p.chans):
        at = pl.multiple_of((c ^ p.mask(k)) * p.hidden, p.hidden)
        grad_hidden = dot(w_radiance_ref[pl.ds(at, p.hidden), :], cotangent)
        grad_pre = (grad_hidden * slope_ref[k]).astype(jnp.bfloat16)
        total = total + dot(p.layer(weight_refs, k), grad_pre)
    total = total.astype(jnp.bfloat16)
    for target_ref, out_ref in zip(target_refs, out_refs):
        out_ref[...] = dot_nt(one_hot(target_ref[...], 0, p.rows), total).astype(jnp.bfloat16)


def add(refs):
    total = refs[0][...].astype(jnp.float32)
    for ref in refs[1:]:
        total = total + ref[...].astype(jnp.float32)
    return total


def rows_and_cells(p, count):
    target = lax.broadcasted_iota(jnp.int32, (count, 1), 0)
    return target // p.per_row, target % p.per_row - 1


def add_group_kernel(p, *refs):
    ins, outs = refs[: p.group], refs[p.group :]
    total = add(ins).astype(jnp.bfloat16)
    row, along = rows_and_cells(p, outs[0].shape[0])
    for k, out_ref in enumerate(outs):
        tile = lax.axis_index("tile") ^ k
        cell = (tile * p.own_cols + along + p.tiles * p.own_cols) % (p.tiles * p.own_cols)
        wanted = (cell // p.own_cols * p.rows_each + row) * p.own_cols + cell % p.own_cols
        out_ref[...] = dot(one_hot(wanted, 0, total.shape[0]), total).astype(jnp.bfloat16)


def add_tiles_kernel(p, *refs):
    ins, outs = refs[: p.tiles], refs[p.tiles :]
    total = add(ins).astype(jnp.bfloat16)
    row, along = rows_and_cells(p, p.around)
    c = lax.axis_index("chan")
    for k, out_ref in enumerate(outs):
        held = ((c // p.group) ^ k) * p.group - 1 + row - c % p.group * p.rows_each
        wanted = jnp.where(
            (held >= 0) & (held < p.rows_each), held * p.per_row + along + 1, -1
        )
        out_ref[...] = dot(one_hot(wanted, 0, total.shape[0]), total).astype(jnp.bfloat16)


def add_chips_kernel(*refs):
    refs[-1][...] = add(refs[:-1])


def diffuse_kernel(p, edge, *refs):
    ins, root_ref, out_ref = refs[: p.group], refs[-2], refs[-1]
    total = add(ins) * 0.0625
    length = p.along + 2 * edge
    shape = (length, p.around)
    cell = lax.broadcasted_iota(jnp.int32, shape, 0)
    source = lax.broadcasted_iota(jnp.int32, shape, 1)
    column = (cell - edge + 4) // 4
    spread = []
    for k in range(3):
        row = lax.axis_index("chan") % p.group + k
        pick = (source == column + row * p.per_row) & (column >= 0) & (column < p.per_row)
        spread.append(
            jnp.dot(
                pick.astype(jnp.float32),
                total,
                precision=lax.Precision.HIGHEST,
                preferred_element_type=jnp.float32,
            )
        )
    root = root_ref[...]
    state = [spread[(row + 2) // 4] for row in range(p.across + 4)]
    east_of = functools.partial(pltpu.roll, shift=length - 1, axis=0)
    west_of = functools.partial(pltpu.roll, shift=1, axis=0)
    north = root[:, :-1] * root[:, 1:]
    east, west = root * east_of(root), root * west_of(root)
    for sweep in range(2):
        fresh = list(state)
        for row in range(1 + sweep, p.across + 3 - sweep):
            here = state[row]
            fresh[row] = (
                here
                + north[:, row : row + 1] * (state[row + 1] - here)
                + north[:, row - 1 : row] * (state[row - 1] - here)
                + east[:, row : row + 1] * (east_of(here) - here)
                + west[:, row : row + 1] * (west_of(here) - here)
            )
        state = fresh
    for row in range(p.across):
        out_ref[row] = state[row + 2][edge : edge + p.along, : p.features]


def body_by_column(
    fields,
    diffusivity,
    owners,
    observed,
    usable,
    w_hidden,
    b_hidden,
    w_radiance,
    b_radiance,
    inv_cov,
):
    p = Plan(
        lax.axis_size("tile"),
        lax.axis_size("chan"),
        fields.shape,
        owners.shape,
        observed.shape,
        w_hidden.shape,
    )
    half, single = jnp.bfloat16, jnp.float32
    shape = jax.ShapeDtypeStruct
    both = ("tile", "chan")
    everyone = [(a, b) for a in range(p.tiles) for b in range(p.chans)]

    def flip(value, mask):
        return lax.ppermute(value, "chan", [(b, b ^ mask) for b in range(p.chans)])

    def trade(value, mask):
        return lax.ppermute(value, "tile", [(a, a ^ mask) for a in range(p.tiles)])

    def send(value, wanted):
        pairs = dict(wanted)
        pairs.update({target: source for source, target in wanted.items()})
        for a, b in everyone:
            if (a, b) not in pairs:
                pairs[a, b] = (a, b ^ 1)
        number = lambda place: place[0] * p.chans + place[1]
        return lax.ppermute(
            value, both, sorted((number(a), number(b)) for a, b in pairs.items())
        )

    def join(values, kernel_shape, after=()):
        return call(
            functools.partial(join_kernel, len(values)),
            shape(kernel_shape, half),
            [*values, *after],
            in_hbm=range(len(values) + len(after)),
            out_hbm=True,
            scratch=[pltpu.SemaphoreType.DMA((len(values),))],
            flops=0,
        )

    strips = call(
        functools.partial(prepare_kernel, p),
        shape((p.block, p.width), half),
        [fields, diffusivity, usable, b_hidden],
        in_hbm=range(4),
        out_hbm=True,
        scratch=[
            pltpu.VMEM(fields.shape, single),
            pltpu.VMEM(diffusivity.shape, single),
            pltpu.VMEM(usable.shape, jnp.int32),
            pltpu.VMEM(b_hidden.shape, single),
            pltpu.VMEM((p.block, p.width), single),
            pltpu.VMEM((p.block, p.width), half),
            pltpu.SemaphoreType.DMA((5,)),
        ],
        vmem=WHOLE_VMEM_BYTES,
    )
    near = [w_hidden] + [flip(w_hidden, chip * p.group) for chip in range(1, p.chips)]
    strips = [strips] + [trade(strips, k) for k in range(1, p.tiles)]
    strips = join(strips, (p.tiles * p.block, p.width), near[1:])
    near = call(
        functools.partial(stack_kernel, p),
        shape((p.chips * p.deep, p.hidden), half),
        near + [strips],
        in_hbm=[len(near)],
    )
    weights = [near] + [flip(near, k) for k in range(1, p.group)]

    _, leaving = lax.optimization_barrier((strips, observed))
    seen = [observed] + [
        send(leaving, {(b // p.group ^ k, b): (b // p.group, b) for b in range(p.chans)})
        for k in range(1, p.tiles)
    ]
    strips = join(
        [strips] + [flip(strips, k * p.group) for k in range(1, p.chips)],
        (p.strips, p.width),
        weights[1:] + seen[1:],
    )
    strips = [strips] + [flip(strips, k) for k in range(1, p.group)]

    reach = p.across + 4
    place, source, cell, *targets = call(
        functools.partial(place_kernel, p),
        [shape((p.rows, 1), jnp.int32)] * 2
        + [shape((3 * reach, 1), jnp.int32)]
        + [shape((p.rows // p.group, 1), jnp.int32)] * p.group,
        [owners.reshape(1, p.rows)],
        flops=SLACK_FLOPS,
    )
    *parts, preact, kappa = call(
        functools.partial(forward_kernel, p),
        [shape((p.rows // p.steps, p.shard), half)] * p.steps
        + [shape((p.chans, p.rows, p.hidden), single), shape((3 * reach, p.lane), single)],
        [place, source, cell, b_radiance, w_radiance] + strips + weights + seen,
        scratch=[pltpu.VMEM((p.rows, p.hidden * p.chans), half)],
        flops=2 * p.rows * p.hidden * p.chans * (p.features + p.shard),
    )

    slope = call(
        slope_kernel,
        shape((p.chans, p.hidden, p.rows), single),
        [preact],
        flops=40 * preact.size,
    )

    pool, held, choices = list(parts), {}, {}
    for j in range(p.steps):
        held[0, j] = choices[0, j] = j
    for step in range(p.steps):
        for since in range(-1, step):
            for j in range(p.steps):
                order = [1 << (j + k) % p.steps for k in range(p.steps)]
                roles = [0] if since < 0 else [
                    order[since] + rest
                    for rest in range(p.chips)
                    if rest & ~sum(order[:since]) == 0
                ]
                wanted = {
                    (a, b): (a, b ^ order[step] * p.group)
                    for a, b in everyone
                    if (b // p.group ^ a) in roles
                }
                source = pool[choices[roles[0], j]]
                for role in roles:
                    choices[role + order[step], j] = len(pool)
                pool.append(send(source, wanted))
    chosen = call(
        functools.partial(choose_kernel, p, choices),
        shape((p.rows, p.shard), half),
        pool + [slope],
        in_hbm=range(len(pool) + 1),
        out_hbm=True,
        scratch=[pltpu.SemaphoreType.DMA((p.steps,))],
    )
    depart = [chosen] + [flip(chosen, k) for k in range(1, p.group)]

    partial = call(
        functools.partial(backward_kernel, p),
        [shape((p.rows // p.group, p.features), half)] * p.group,
        [w_radiance, inv_cov, slope] + depart + weights + targets,
        flops=2 * p.rows * (p.hidden * p.chans * (p.features + p.shard) + inv_cov.size),
    )
    partial = [partial[0]] + [flip(partial[k], k) for k in range(1, p.group)]
    partial = call(
        functools.partial(add_group_kernel, p),
        [shape((p.rows_each * p.per_row, p.features), half)] * p.tiles,
        partial,
    )
    partial = [partial[0]] + [trade(partial[k], k) for k in range(1, p.tiles)]
    partial = call(
        functools.partial(add_tiles_kernel, p),
        [shape((p.around, p.features), half)] * p.chips,
        partial,
    )
    partial = [partial[0]] + [flip(partial[k], k * p.group) for k in range(1, p.chips)]
    partial = call(add_chips_kernel, shape((p.around, p.features), single), partial)
    partial = [partial] + [flip(partial, k) for k in range(1, p.group)]

    edge = 8
    kappa = kappa.reshape(3, reach, p.lane)
    root = jnp.sqrt(
        jnp.concatenate(
            [kappa[0, :, p.along - edge : p.along], kappa[1, :, : p.along], kappa[2, :, :edge]],
            axis=1,
        ).T
    )
    return call(
        functools.partial(diffuse_kernel, p, edge),
        shape(fields.shape, single),
        partial + [root],
        flops=100 * fields.size,
    )


def solution(mesh):
    tiles, chans = mesh.shape["tile"], mesh.shape["chan"]
    by_column = tiles > 1 and chans % tiles == 0 and chans & (chans - 1) == 0 and chans > tiles
    placed = (
        P("chan", "tile", None),
        P("chan", "tile"),
        P(),
        P("tile", "chan"),
        P("tile"),
        P(None, "chan"),
        P("chan"),
        P(None, "chan"),
        P("chan"),
        P("tile", "chan"),
    )
    return jax.shard_map(
        body_by_column if by_column else body_by_owner,
        mesh=mesh,
        in_specs=placed,
        out_specs=P("chan", "tile", None),
        check_vma=False,
    )
```

```python
import functools

import jax
import jax.numpy as jnp
from jax import lax
from jax.experimental import pallas as pl
from jax.experimental.pallas import tpu as pltpu
from jax.sharding import PartitionSpec as P

VMEM_BYTES = 24 * 1024 * 1024
WHOLE_VMEM_BYTES = 63 * 1024 * 1024
SLACK_FLOPS = 2 * 10**9
NT_DIMS = (((1,), (1,)), ((), ()))


def padded_2(value, sides, width, wrap):
    for axis, dim in sides:
        devices, length = (lax.axis_size(axis), value.shape[dim])
        up = [(i, (i + 1) % devices) for i in range(devices if wrap else devices - 1)]
        down = [(j, i) for i, j in up]
        last = lax.slice_in_dim(value, length - width, length, axis=dim)
        first = lax.slice_in_dim(value, 0, width, axis=dim)
        before = lax.ppermute(last, axis, up)
        after = lax.ppermute(first, axis, down)
        value = jnp.concatenate([before, value, after], axis=dim)
    return value


def add_rims(values):
    rowwise = padded_2(values, (("chan", 0),), 1, False)
    return padded_2(rowwise, (("tile", 1),), 1, True)


def body_by_owner(
    fields,
    diffusivity,
    owners,
    observed,
    usable,
    w_hidden,
    b_hidden,
    w_radiance,
    b_radiance,
    inv_cov,
):
    tile_count = lax.axis_size("tile")
    chan_count = lax.axis_size("chan")
    tile_index = lax.axis_index("tile")
    chan_index = lax.axis_index("chan")
    slot_count = observed.shape[0]
    capacity = slot_count // tile_count
    cells_across, cells_along, features = fields.shape
    own_cols = cells_across // 4 * (cells_along // 4)
    tile_cols = chan_count * own_cols
    hidden_dev = w_hidden.shape[1]
    owner_table = owners[:, 0].reshape(tile_count, tile_cols)
    owner_hits = (
        owner_table[:, :, None] == jnp.arange(tile_count, dtype=jnp.int32)[None, None, :]
    ).astype(jnp.int32)
    before = jnp.sum((jnp.cumsum(owner_hits, axis=1) - owner_hits) * owner_hits, axis=2)
    tallies = jnp.sum(owner_hits, axis=1)
    slot_of = lax.dynamic_index_in_dim(
        owner_table * capacity + before, tile_index, 0, keepdims=False
    )
    arriving = lax.dynamic_index_in_dim(tallies, tile_index, 1, keepdims=False)
    occupied = (jnp.arange(capacity, dtype=jnp.int32)[None, :] < arriving[:, None]).reshape(
        slot_count
    )
    grouped = fields.reshape(cells_across // 4, 4, cells_along // 4, 4, features)
    columns = (
        (jnp.sum(grouped, axis=(1, 3)) * 0.0625).reshape(own_cols, features).astype(jnp.bfloat16)
    )
    placer = (slot_of[None, :] == jnp.arange(slot_count, dtype=jnp.int32)[:, None]).astype(
        jnp.bfloat16
    )
    outgoing = jnp.dot(
        placer,
        lax.all_gather(columns, "chan", axis=0, tiled=True),
        preferred_element_type=jnp.float32,
    )
    incoming = lax.all_to_all(
        outgoing.astype(jnp.bfloat16), "tile", split_axis=0, concat_axis=0, tiled=True
    )
    preact = lax.dot_general(
        w_hidden, incoming, (((0,), (1,)), ((), ())), preferred_element_type=jnp.float32
    )
    preact = preact + b_hidden[:, None]
    squash = jax.nn.sigmoid(preact)
    active = (preact * squash).astype(jnp.bfloat16)
    radiance = lax.dot_general(
        lax.all_gather(active, "chan", axis=0, tiled=True),
        w_radiance,
        (((0,), (0,)), ((), ())),
        preferred_element_type=jnp.float32,
    )
    radiance = radiance + b_radiance[None, :]
    in_use = usable.astype(jnp.float32) * occupied.astype(jnp.float32)
    departure = ((radiance - observed.astype(jnp.float32)) * in_use[:, None]).astype(jnp.bfloat16)
    cotangent = jnp.dot(
        lax.all_gather(departure, "chan", axis=1, tiled=True),
        lax.all_gather(inv_cov, "tile", axis=0, tiled=True),
        preferred_element_type=jnp.float32,
    )
    cotangent = cotangent.astype(jnp.bfloat16)
    full_sum = lax.psum(
        lax.dot_general(w_radiance, cotangent, NT_DIMS, preferred_element_type=jnp.float32),
        "chan",
    )
    grad_hidden = lax.dynamic_slice_in_dim(full_sum, chan_index * hidden_dev, hidden_dev, 0)
    slope_term = squash * (1.0 + preact * (1.0 - squash))
    grad_pre = (grad_hidden * slope_term).astype(jnp.bfloat16)
    part_grad = lax.dot_general(
        grad_pre, w_hidden, (((0,), (1,)), ((), ())), preferred_element_type=jnp.float32
    )
    returned = lax.all_to_all(part_grad, "tile", split_axis=0, concat_axis=0, tiled=True)
    column_grad = lax.psum_scatter(
        jnp.take(returned, slot_of, axis=0), "chan", scatter_dimension=0, tiled=True
    )
    spread = jnp.repeat(
        column_grad.reshape(cells_across // 4, cells_along // 4, features), 4, axis=0
    )
    adjoint = jnp.repeat(spread, 4, axis=1) * 0.0625
    kappa_root = jnp.sqrt(diffusivity)
    root_rim = add_rims(kappa_root)
    coef_north = (kappa_root * root_rim[2:, 1:-1])[:, :, None]
    coef_south = (kappa_root * root_rim[:-2, 1:-1])[:, :, None]
    coef_east = (kappa_root * root_rim[1:-1, 2:])[:, :, None]
    coef_west = (kappa_root * root_rim[1:-1, :-2])[:, :, None]
    for sweep_index in range(2):
        padded = add_rims(adjoint)
        adjoint = (
            adjoint
            + coef_north * (padded[2:, 1:-1] - adjoint)
            + coef_south * (padded[:-2, 1:-1] - adjoint)
            + coef_east * (padded[1:-1, 2:] - adjoint)
            + coef_west * (padded[1:-1, :-2] - adjoint)
        )
    return adjoint


def up_to(value, multiple):
    return -(-value // multiple) * multiple


def dot(left, right):
    return jnp.dot(left, right, preferred_element_type=jnp.float32)


def dot_nt(left, right):
    return lax.dot_general(left, right, NT_DIMS, preferred_element_type=jnp.float32)


def split_three(value):
    high = value.astype(jnp.bfloat16).astype(jnp.float32)
    middle = (value - high).astype(jnp.bfloat16).astype(jnp.float32)
    return high, middle, value - high - middle


def call(
    kernel, out_shape, args, in_hbm=(), out_hbm=False, scratch=(), flops=0, vmem=VMEM_BYTES
):
    far, near = pl.BlockSpec(memory_space=pl.ANY), pl.BlockSpec(memory_space=pltpu.VMEM)
    bytes_accessed = sum(a.size * a.dtype.itemsize for a in args)
    return pl.pallas_call(
        kernel,
        out_shape=out_shape,
        in_specs=[far if k in in_hbm else near for k in range(len(args))],
        out_specs=jax.tree.map(lambda _: far if out_hbm else near, out_shape),
        scratch_shapes=list(scratch),
        compiler_params=pltpu.CompilerParams(vmem_limit_bytes=vmem),
        cost_estimate=pl.CostEstimate(
            flops=flops, bytes_accessed=bytes_accessed, transcendentals=0
        ),
    )(*args)


class Plan:
    def __init__(self, tiles, chans, fields, owners, observed, w_hidden):
        self.tiles, self.chans = tiles, chans
        self.across, self.along, self.features = fields
        self.own_cols = self.across // 4 * (self.along // 4)
        self.rows = owners[0]
        self.tile_cols = self.rows // tiles
        self.slots = observed[0]
        self.shard = observed[1]
        self.capacity = self.slots // tiles
        self.hidden = w_hidden[1]
        self.group = chans // tiles
        self.chips = chans // self.group
        self.steps = self.chips.bit_length() - 1
        self.lane = up_to(self.along, 128)
        self.flag_at = up_to(self.hidden, 128)
        self.width = max(
            up_to(self.features, 128),
            2 * self.flag_at,
            self.flag_at + up_to(self.slots, 128),
            3 * self.lane,
        )
        self.block = up_to(self.own_cols + 2 + self.across, 16)
        self.per_row = self.own_cols + 2
        self.rows_each = chans // self.group
        self.around = (self.group + 2) * self.per_row
        self.deep = up_to(self.features, 16)
        self.strips = self.chips * tiles * self.block

    def order(self, mask):
        return mask % self.group * self.chips + mask // self.group

    def layer(self, refs, k):
        at = k % self.chips * self.deep
        return refs[k // self.chips][at : at + self.features, :]

    def mask(self, k):
        return k % self.chips * self.group + k // self.chips


def prepare_kernel(p, *refs):
    ins, out_ref = refs[:4], refs[4]
    fields_ref, diffusivity_ref, usable_ref, bias_ref, flat, packed, sems = refs[5:]
    copies = [
        pltpu.make_async_copy(source, target, sems.at[k])
        for k, (source, target) in enumerate(zip(ins, refs[5:9]))
    ]
    for copy in copies:
        copy.start()
    flat[...] = jnp.zeros(flat.shape, jnp.float32)
    for copy in copies:
        copy.wait()
    shape = (p.own_cols, p.along)
    row = lax.broadcasted_iota(jnp.int32, shape, 0)
    member = row == lax.broadcasted_iota(jnp.int32, shape, 1) // 4
    total = jnp.dot(
        member.astype(jnp.float32),
        fields_ref[0] + fields_ref[1] + fields_ref[2] + fields_ref[3],
        precision=lax.Precision.HIGHEST,
        preferred_element_type=jnp.float32,
    )
    flat[: p.own_cols, : p.features] = total * 0.0625
    at = p.own_cols
    high, middle, low = split_three(bias_ref[...].reshape(1, p.hidden))
    flat[at : at + 1, : p.hidden] = high
    flat[at : at + 1, p.flag_at : p.flag_at + p.hidden] = middle
    flat[at + 1 : at + 2, : p.hidden] = low
    flags = usable_ref[...].reshape(1, p.slots).astype(jnp.float32)
    flat[at + 1 : at + 2, p.flag_at : p.flag_at + p.slots] = flags
    for k, part in enumerate(split_three(diffusivity_ref[...])):
        flat[at + 2 : at + 2 + p.across, k * p.lane : k * p.lane + p.along] = part
    packed[...] = flat[...].astype(jnp.bfloat16)
    copy = pltpu.make_async_copy(packed, out_ref, sems.at[4])
    copy.start()
    copy.wait()


def place_kernel(p, owners_ref, place_ref, source_ref, cell_ref, *target_refs):
    t, c = lax.axis_index("tile"), lax.axis_index("chan")
    across = owners_ref[...]
    shape = (p.rows, p.rows)
    row = lax.broadcasted_iota(jnp.int32, shape, 0)
    other = lax.broadcasted_iota(jnp.int32, shape, 1)
    owner = jnp.sum(jnp.where(row == other, across, 0), axis=1, keepdims=True)
    first = lax.broadcasted_iota(jnp.int32, owner.shape, 0)
    begin = first // p.tile_cols * p.tile_cols
    same = (owner == across) & (other >= begin) & (other < row)
    rank = jnp.sum(jnp.where(same, 1, 0), axis=1, keepdims=True)
    tile = first // p.tile_cols
    place_ref[...] = (owner ^ t) * p.slots + tile * p.capacity + rank

    def strip(tile, chan):
        other = chan ^ c
        return p.order(other) * p.tiles + (tile ^ t)

    source_ref[...] = (
        strip(tile, first % p.tile_cols // p.own_cols) * p.block + first % p.own_cols
    )

    row = lax.broadcasted_iota(jnp.int32, cell_ref.shape, 0)
    reach = p.across + 4
    tile = (t + row // reach - 1 + p.tiles) % p.tiles
    cell = c * p.across - 2 + row % reach
    inside = (cell >= 0) & (cell < p.chans * p.across)
    cell = jnp.where(inside, cell, 0)
    wanted = strip(tile, cell // p.across) * p.block + p.own_cols + 2 + cell % p.across
    cell_ref[...] = jnp.where(inside, wanted, -1)

    each = p.rows_each * p.own_cols
    target = lax.broadcasted_iota(jnp.int32, target_refs[0].shape, 0)
    for k, target_ref in enumerate(target_refs):
        first = (c % p.group ^ k) * each
        target_ref[...] = target // each * p.tile_cols + first + target % each


def join_kernel(count, *refs):
    ins, out_ref, sems = refs[:count], refs[-2], refs[-1]
    size = out_ref.shape[0] // count
    copies = [
        pltpu.make_async_copy(
            ref, out_ref.at[k] if ref.ndim < out_ref.ndim else out_ref.at[pl.ds(k * size, size)],
            sems.at[k],
        )
        for k, ref in enumerate(ins)
    ]
    for copy in copies:
        copy.start()
    for copy in copies:
        copy.wait()


def stack_kernel(p, *refs):
    for k, ref in enumerate(refs[: p.chips]):
        refs[-1][k * p.deep : k * p.deep + p.features, :] = ref[...]
        refs[-1][k * p.deep + p.features : (k + 1) * p.deep, :] = jnp.zeros(
            (p.deep - p.features, p.hidden), jnp.bfloat16
        )


def one_hot(wanted, first, count):
    source = lax.broadcasted_iota(jnp.int32, (wanted.shape[0], count), 1)
    return (source + first == wanted).astype(jnp.bfloat16)


def forward_kernel(p, *refs):
    refs = list(refs)
    take = lambda n: [refs.pop(0) for _ in range(n)]
    place_ref, source_ref, cell_ref, bias_ref, w_radiance_ref = take(5)
    strip_refs, weight_refs, seen_refs = take(p.group), take(p.group), take(p.tiles)
    part_refs = take(p.steps)
    preact_ref, kappa_ref, active = refs
    c = lax.axis_index("chan")
    gathered = [ref[...] for ref in strip_refs]
    columns = sum(
        dot(one_hot(source_ref[...], k * p.strips, p.strips), strips)
        for k, strips in enumerate(gathered)
    )
    columns = columns.astype(jnp.bfloat16)[:, : p.features]
    for k in range(p.chans):
        member, chip = k // p.chips, k % p.chips
        at = chip * p.tiles * p.block + p.own_cols
        low = strip_refs[member][at : at + 2, :].astype(jnp.float32)
        bias = (
            low[:1, : p.hidden]
            + low[:1, p.flag_at : p.flag_at + p.hidden]
            + low[1:, : p.hidden]
        )
        preact = dot(columns, p.layer(weight_refs, k)) + bias
        preact_ref[k] = preact
        at = pl.multiple_of((c ^ p.mask(k)) * p.hidden, p.hidden)
        active[:, pl.ds(at, p.hidden)] = (preact * jax.nn.sigmoid(preact)).astype(jnp.bfloat16)
    part = p.rows // p.steps
    count = seen_refs[0].shape[0]
    for j, part_ref in enumerate(part_refs):
        at = slice(j * part, (j + 1) * part)
        in_use = jnp.zeros((part, 1), jnp.float32)
        for k in range(p.tiles):
            slot = lax.broadcasted_iota(jnp.int32, (part, p.slots), 1) + k * p.slots
            low = k * p.block + p.own_cols + 1
            flags = strip_refs[0][low : low + 1, p.flag_at : p.flag_at + p.slots]
            flags = jnp.where(place_ref[at, :] == slot, flags.astype(jnp.float32), 0.0)
            in_use = in_use + jnp.sum(flags, axis=1, keepdims=True)
        observed = sum(
            dot(one_hot(place_ref[at, :], k * count, count), ref[...])
            for k, ref in enumerate(seen_refs)
        )
        radiance = dot(active[at, :], w_radiance_ref[...]) + bias_ref[...].reshape(1, p.shard)
        part_ref[...] = ((radiance - observed) * in_use).astype(jnp.bfloat16)
    parts = sum(
        dot(one_hot(cell_ref[...], k * p.strips, p.strips), strips)
        for k, strips in enumerate(gathered)
    )
    kappa_ref[...] = sum(parts[:, k * p.lane : (k + 1) * p.lane] for k in range(3))


def slope_kernel(preact_ref, slope_ref):
    for k in range(preact_ref.shape[0]):
        preact = preact_ref[k]
        squash = jax.nn.sigmoid(preact)
        slope_ref[k] = (squash * (1.0 + preact * (1.0 - squash))).T


def choose_kernel(p, choices, *refs):
    refs, out_ref, sems = refs[:-3], refs[-2], refs[-1]
    size = refs[0].shape[0]
    role = (lax.axis_index("chan") // p.group) ^ lax.axis_index("tile")
    for place in range(p.chips):

        @pl.when(role == place)
        def _():
            copies = [
                pltpu.make_async_copy(
                    refs[choices[place, j]], out_ref.at[pl.ds(j * size, size)], sems.at[j]
                )
                for j in range(p.steps)
            ]
            for copy in copies:
                copy.start()
            for copy in copies:
                copy.wait()


def backward_kernel(p, *refs):
    refs = list(refs)
    take = lambda n: [refs.pop(0) for _ in range(n)]
    w_radiance_ref, inv_cov_ref, slope_ref = take(3)
    depart_refs, weight_refs, target_refs = take(p.group), take(p.group), take(p.group)
    out_refs = refs
    c = lax.axis_index("chan")
    cotangent = None
    for k, ref in enumerate(depart_refs):
        at = pl.multiple_of((c % p.group ^ k) * p.shard, p.shard)
        term = dot(ref[...], inv_cov_ref[pl.ds(at, p.shard), :])
        cotangent = term if cotangent is None else cotangent + term
    cotangent = cotangent.T.astype(jnp.bfloat16)
    total = jnp.zeros((p.features, p.rows), jnp.float32)
    for k in range(p.chans):
        at = pl.multiple_of((c ^ p.mask(k)) * p.hidden, p.hidden)
        grad_hidden = dot(w_radiance_ref[pl.ds(at, p.hidden), :], cotangent)
        grad_pre = (grad_hidden * slope_ref[k]).astype(jnp.bfloat16)
        total = total + dot(p.layer(weight_refs, k), grad_pre)
    total = total.astype(jnp.bfloat16)
    for target_ref, out_ref in zip(target_refs, out_refs):
        out_ref[...] = dot_nt(one_hot(target_ref[...], 0, p.rows), total).astype(jnp.bfloat16)


def add(refs):
    total = refs[0][...].astype(jnp.float32)
    for ref in refs[1:]:
        total = total + ref[...].astype(jnp.float32)
    return total


def rows_and_cells(p, count):
    target = lax.broadcasted_iota(jnp.int32, (count, 1), 0)
    return target // p.per_row, target % p.per_row - 1


def add_group_kernel(p, *refs):
    ins, outs = refs[: p.group], refs[p.group :]
    total = add(ins).astype(jnp.bfloat16)
    row, along = rows_and_cells(p, outs[0].shape[0])
    for k, out_ref in enumerate(outs):
        tile = lax.axis_index("tile") ^ k
        cell = (tile * p.own_cols + along + p.tiles * p.own_cols) % (p.tiles * p.own_cols)
        wanted = (cell // p.own_cols * p.rows_each + row) * p.own_cols + cell % p.own_cols
        out_ref[...] = dot(one_hot(wanted, 0, total.shape[0]), total).astype(jnp.bfloat16)


def add_tiles_kernel(p, *refs):
    ins, outs = refs[: p.tiles], refs[p.tiles :]
    total = add(ins).astype(jnp.bfloat16)
    row, along = rows_and_cells(p, p.around)
    c = lax.axis_index("chan")
    for k, out_ref in enumerate(outs):
        held = ((c // p.group) ^ k) * p.group - 1 + row - c % p.group * p.rows_each
        wanted = jnp.where(
            (held >= 0) & (held < p.rows_each), held * p.per_row + along + 1, -1
        )
        out_ref[...] = dot(one_hot(wanted, 0, total.shape[0]), total).astype(jnp.bfloat16)


def add_chips_kernel(*refs):
    refs[-1][...] = add(refs[:-1])


def diffuse_kernel(p, edge, *refs):
    ins, root_ref, out_ref = refs[: p.group], refs[-2], refs[-1]
    total = add(ins) * 0.0625
    length = p.along + 2 * edge
    shape = (length, p.around)
    cell = lax.broadcasted_iota(jnp.int32, shape, 0)
    source = lax.broadcasted_iota(jnp.int32, shape, 1)
    column = (cell - edge + 4) // 4
    spread = []
    for k in range(3):
        row = lax.axis_index("chan") % p.group + k
        pick = (source == column + row * p.per_row) & (column >= 0) & (column < p.per_row)
        spread.append(
            jnp.dot(
                pick.astype(jnp.float32),
                total,
                precision=lax.Precision.HIGHEST,
                preferred_element_type=jnp.float32,
            )
        )
    root = root_ref[...]
    state = [spread[(row + 2) // 4] for row in range(p.across + 4)]
    east_of = functools.partial(pltpu.roll, shift=length - 1, axis=0)
    west_of = functools.partial(pltpu.roll, shift=1, axis=0)
    north = root[:, :-1] * root[:, 1:]
    east, west = root * east_of(root), root * west_of(root)
    for sweep in range(2):
        fresh = list(state)
        for row in range(1 + sweep, p.across + 3 - sweep):
            here = state[row]
            fresh[row] = (
                here
                + north[:, row : row + 1] * (state[row + 1] - here)
                + north[:, row - 1 : row] * (state[row - 1] - here)
                + east[:, row : row + 1] * (east_of(here) - here)
                + west[:, row : row + 1] * (west_of(here) - here)
            )
        state = fresh
    for row in range(p.across):
        out_ref[row] = state[row + 2][edge : edge + p.along, : p.features]


def body_by_column(
    fields,
    diffusivity,
    owners,
    observed,
    usable,
    w_hidden,
    b_hidden,
    w_radiance,
    b_radiance,
    inv_cov,
):
    p = Plan(
        lax.axis_size("tile"),
        lax.axis_size("chan"),
        fields.shape,
        owners.shape,
        observed.shape,
        w_hidden.shape,
    )
    half, single = jnp.bfloat16, jnp.float32
    shape = jax.ShapeDtypeStruct
    both = ("tile", "chan")
    everyone = [(a, b) for a in range(p.tiles) for b in range(p.chans)]

    def flip(value, mask):
        return lax.ppermute(value, "chan", [(b, b ^ mask) for b in range(p.chans)])

    def trade(value, mask):
        return lax.ppermute(value, "tile", [(a, a ^ mask) for a in range(p.tiles)])

    def send(value, wanted):
        pairs = dict(wanted)
        pairs.update({target: source for source, target in wanted.items()})
        for a, b in everyone:
            if (a, b) not in pairs:
                pairs[a, b] = (a, b ^ 1)
        number = lambda place: place[0] * p.chans + place[1]
        return lax.ppermute(
            value, both, sorted((number(a), number(b)) for a, b in pairs.items())
        )

    def join(values, kernel_shape, after=()):
        return call(
            functools.partial(join_kernel, len(values)),
            shape(kernel_shape, half),
            [*values, *after],
            in_hbm=range(len(values) + len(after)),
            out_hbm=True,
            scratch=[pltpu.SemaphoreType.DMA((len(values),))],
            flops=0,
        )

    strips = call(
        functools.partial(prepare_kernel, p),
        shape((p.block, p.width), half),
        [fields, diffusivity, usable, b_hidden],
        in_hbm=range(4),
        out_hbm=True,
        scratch=[
            pltpu.VMEM(fields.shape, single),
            pltpu.VMEM(diffusivity.shape, single),
            pltpu.VMEM(usable.shape, jnp.int32),
            pltpu.VMEM(b_hidden.shape, single),
            pltpu.VMEM((p.block, p.width), single),
            pltpu.VMEM((p.block, p.width), half),
            pltpu.SemaphoreType.DMA((5,)),
        ],
        vmem=WHOLE_VMEM_BYTES,
    )
    near = [w_hidden] + [flip(w_hidden, chip * p.group) for chip in range(1, p.chips)]
    held, bit = [observed], 1
    while 2 * bit < p.tiles:
        held += [trade(value, bit) for value in held]
        bit *= 2

    bit = 1
    while bit < p.tiles:
        before = held[1:] if bit == 1 else weights[1:]
        strips = join([strips, trade(strips, bit)], (2 * strips.shape[0], p.width), before)
        if bit == 1:
            near = call(
                functools.partial(stack_kernel, p),
                shape((p.chips * p.deep, p.hidden), half),
                near + [strips],
                in_hbm=[len(near)],
            )
            weights = [near] + [flip(near, k) for k in range(1, p.group)]
        bit *= 2

    _, *leaving = lax.optimization_barrier((strips, *held))
    wanted = {(b // p.group ^ p.tiles // 2, b): (b // p.group, b) for b in range(p.chans)}
    far = [send(value, wanted) for value in leaving]
    seen = held + far
    strips = join(
        [strips] + [flip(strips, k * p.group) for k in range(1, p.chips)],
        (p.strips, p.width),
        far,
    )
    strips = [strips] + [flip(strips, k) for k in range(1, p.group)]

    reach = p.across + 4
    place, source, cell, *targets = call(
        functools.partial(place_kernel, p),
        [shape((p.rows, 1), jnp.int32)] * 2
        + [shape((3 * reach, 1), jnp.int32)]
        + [shape((p.rows // p.group, 1), jnp.int32)] * p.group,
        [owners.reshape(1, p.rows)],
        flops=SLACK_FLOPS,
    )
    *parts, preact, kappa = call(
        functools.partial(forward_kernel, p),
        [shape((p.rows // p.steps, p.shard), half)] * p.steps
        + [shape((p.chans, p.rows, p.hidden), single), shape((3 * reach, p.lane), single)],
        [place, source, cell, b_radiance, w_radiance] + strips + weights + seen,
        scratch=[pltpu.VMEM((p.rows, p.hidden * p.chans), half)],
        flops=2 * p.rows * p.hidden * p.chans * (p.features + p.shard),
    )

    slope = call(
        slope_kernel,
        shape((p.chans, p.hidden, p.rows), single),
        [preact],
        flops=40 * preact.size,
    )

    pool, held, choices = list(parts), {}, {}
    for j in range(p.steps):
        held[0, j] = choices[0, j] = j
    for step in range(p.steps):
        for since in range(-1, step):
            for j in range(p.steps):
                order = [1 << (j + k) % p.steps for k in range(p.steps)]
                roles = [0] if since < 0 else [
                    order[since] + rest
                    for rest in range(p.chips)
                    if rest & ~sum(order[:since]) == 0
                ]
                wanted = {
                    (a, b): (a, b ^ order[step] * p.group)
                    for a, b in everyone
                    if (b // p.group ^ a) in roles
                }
                source = pool[choices[roles[0], j]]
                for role in roles:
                    choices[role + order[step], j] = len(pool)
                pool.append(send(source, wanted))
    chosen = call(
        functools.partial(choose_kernel, p, choices),
        shape((p.rows, p.shard), half),
        pool + [slope],
        in_hbm=range(len(pool) + 1),
        out_hbm=True,
        scratch=[pltpu.SemaphoreType.DMA((p.steps,))],
    )
    depart = [chosen] + [flip(chosen, k) for k in range(1, p.group)]

    partial = call(
        functools.partial(backward_kernel, p),
        [shape((p.rows // p.group, p.features), half)] * p.group,
        [w_radiance, inv_cov, slope] + depart + weights + targets,
        flops=2 * p.rows * (p.hidden * p.chans * (p.features + p.shard) + inv_cov.size),
    )
    partial = [partial[0]] + [flip(partial[k], k) for k in range(1, p.group)]
    partial = call(
        functools.partial(add_group_kernel, p),
        [shape((p.rows_each * p.per_row, p.features), half)] * p.tiles,
        partial,
    )
    partial = [partial[0]] + [trade(partial[k], k) for k in range(1, p.tiles)]
    partial = call(
        functools.partial(add_tiles_kernel, p),
        [shape((p.around, p.features), half)] * p.chips,
        partial,
    )
    partial = [partial[0]] + [flip(partial[k], k * p.group) for k in range(1, p.chips)]
    partial = call(add_chips_kernel, shape((p.around, p.features), single), partial)
    partial = [partial] + [flip(partial, k) for k in range(1, p.group)]

    edge = 8
    kappa = kappa.reshape(3, reach, p.lane)
    root = jnp.sqrt(
        jnp.concatenate(
            [kappa[0, :, p.along - edge : p.along], kappa[1, :, : p.along], kappa[2, :, :edge]],
            axis=1,
        ).T
    )
    return call(
        functools.partial(diffuse_kernel, p, edge),
        shape(fields.shape, single),
        partial + [root],
        flops=100 * fields.size,
    )


def solution(mesh):
    tiles, chans = mesh.shape["tile"], mesh.shape["chan"]
    by_column = tiles > 1 and chans % tiles == 0 and chans & (chans - 1) == 0 and chans > tiles
    placed = (
        P("chan", "tile", None),
        P("chan", "tile"),
        P(),
        P("tile", "chan"),
        P("tile"),
        P(None, "chan"),
        P("chan"),
        P(None, "chan"),
        P("chan"),
        P("tile", "chan"),
    )
    return jax.shard_map(
        body_by_column if by_column else body_by_owner,
        mesh=mesh,
        in_specs=placed,
        out_specs=P("chan", "tile", None),
        check_vma=False,
    )
```

```python
import functools

import jax
import jax.numpy as jnp
from jax import lax
from jax.experimental import pallas as pl
from jax.experimental.pallas import tpu as pltpu
from jax.sharding import PartitionSpec as P

VMEM_BYTES = 24 * 1024 * 1024
WHOLE_VMEM_BYTES = 63 * 1024 * 1024
SLACK_FLOPS = 2 * 10**9
FORWARD_FLOPS = 10**8
NT_DIMS = (((1,), (1,)), ((), ()))


def padded_2(value, sides, width, wrap):
    for axis, dim in sides:
        devices, length = (lax.axis_size(axis), value.shape[dim])
        up = [(i, (i + 1) % devices) for i in range(devices if wrap else devices - 1)]
        down = [(j, i) for i, j in up]
        last = lax.slice_in_dim(value, length - width, length, axis=dim)
        first = lax.slice_in_dim(value, 0, width, axis=dim)
        before = lax.ppermute(last, axis, up)
        after = lax.ppermute(first, axis, down)
        value = jnp.concatenate([before, value, after], axis=dim)
    return value


def add_rims(values):
    rowwise = padded_2(values, (("chan", 0),), 1, False)
    return padded_2(rowwise, (("tile", 1),), 1, True)


def body_by_owner(
    fields,
    diffusivity,
    owners,
    observed,
    usable,
    w_hidden,
    b_hidden,
    w_radiance,
    b_radiance,
    inv_cov,
):
    tile_count = lax.axis_size("tile")
    chan_count = lax.axis_size("chan")
    tile_index = lax.axis_index("tile")
    chan_index = lax.axis_index("chan")
    slot_count = observed.shape[0]
    capacity = slot_count // tile_count
    cells_across, cells_along, features = fields.shape
    own_cols = cells_across // 4 * (cells_along // 4)
    tile_cols = chan_count * own_cols
    hidden_dev = w_hidden.shape[1]
    owner_table = owners[:, 0].reshape(tile_count, tile_cols)
    owner_hits = (
        owner_table[:, :, None] == jnp.arange(tile_count, dtype=jnp.int32)[None, None, :]
    ).astype(jnp.int32)
    before = jnp.sum((jnp.cumsum(owner_hits, axis=1) - owner_hits) * owner_hits, axis=2)
    tallies = jnp.sum(owner_hits, axis=1)
    slot_of = lax.dynamic_index_in_dim(
        owner_table * capacity + before, tile_index, 0, keepdims=False
    )
    arriving = lax.dynamic_index_in_dim(tallies, tile_index, 1, keepdims=False)
    occupied = (jnp.arange(capacity, dtype=jnp.int32)[None, :] < arriving[:, None]).reshape(
        slot_count
    )
    grouped = fields.reshape(cells_across // 4, 4, cells_along // 4, 4, features)
    columns = (
        (jnp.sum(grouped, axis=(1, 3)) * 0.0625).reshape(own_cols, features).astype(jnp.bfloat16)
    )
    placer = (slot_of[None, :] == jnp.arange(slot_count, dtype=jnp.int32)[:, None]).astype(
        jnp.bfloat16
    )
    outgoing = jnp.dot(
        placer,
        lax.all_gather(columns, "chan", axis=0, tiled=True),
        preferred_element_type=jnp.float32,
    )
    incoming = lax.all_to_all(
        outgoing.astype(jnp.bfloat16), "tile", split_axis=0, concat_axis=0, tiled=True
    )
    preact = lax.dot_general(
        w_hidden, incoming, (((0,), (1,)), ((), ())), preferred_element_type=jnp.float32
    )
    preact = preact + b_hidden[:, None]
    squash = jax.nn.sigmoid(preact)
    active = (preact * squash).astype(jnp.bfloat16)
    radiance = lax.dot_general(
        lax.all_gather(active, "chan", axis=0, tiled=True),
        w_radiance,
        (((0,), (0,)), ((), ())),
        preferred_element_type=jnp.float32,
    )
    radiance = radiance + b_radiance[None, :]
    in_use = usable.astype(jnp.float32) * occupied.astype(jnp.float32)
    departure = ((radiance - observed.astype(jnp.float32)) * in_use[:, None]).astype(jnp.bfloat16)
    cotangent = jnp.dot(
        lax.all_gather(departure, "chan", axis=1, tiled=True),
        lax.all_gather(inv_cov, "tile", axis=0, tiled=True),
        preferred_element_type=jnp.float32,
    )
    cotangent = cotangent.astype(jnp.bfloat16)
    full_sum = lax.psum(
        lax.dot_general(w_radiance, cotangent, NT_DIMS, preferred_element_type=jnp.float32),
        "chan",
    )
    grad_hidden = lax.dynamic_slice_in_dim(full_sum, chan_index * hidden_dev, hidden_dev, 0)
    slope_term = squash * (1.0 + preact * (1.0 - squash))
    grad_pre = (grad_hidden * slope_term).astype(jnp.bfloat16)
    part_grad = lax.dot_general(
        grad_pre, w_hidden, (((0,), (1,)), ((), ())), preferred_element_type=jnp.float32
    )
    returned = lax.all_to_all(part_grad, "tile", split_axis=0, concat_axis=0, tiled=True)
    column_grad = lax.psum_scatter(
        jnp.take(returned, slot_of, axis=0), "chan", scatter_dimension=0, tiled=True
    )
    spread = jnp.repeat(
        column_grad.reshape(cells_across // 4, cells_along // 4, features), 4, axis=0
    )
    adjoint = jnp.repeat(spread, 4, axis=1) * 0.0625
    kappa_root = jnp.sqrt(diffusivity)
    root_rim = add_rims(kappa_root)
    coef_north = (kappa_root * root_rim[2:, 1:-1])[:, :, None]
    coef_south = (kappa_root * root_rim[:-2, 1:-1])[:, :, None]
    coef_east = (kappa_root * root_rim[1:-1, 2:])[:, :, None]
    coef_west = (kappa_root * root_rim[1:-1, :-2])[:, :, None]
    for sweep_index in range(2):
        padded = add_rims(adjoint)
        adjoint = (
            adjoint
            + coef_north * (padded[2:, 1:-1] - adjoint)
            + coef_south * (padded[:-2, 1:-1] - adjoint)
            + coef_east * (padded[1:-1, 2:] - adjoint)
            + coef_west * (padded[1:-1, :-2] - adjoint)
        )
    return adjoint


def up_to(value, multiple):
    return -(-value // multiple) * multiple


def dot(left, right):
    return jnp.dot(left, right, preferred_element_type=jnp.float32)


def dot_nt(left, right):
    return lax.dot_general(left, right, NT_DIMS, preferred_element_type=jnp.float32)


def split_three(value):
    high = value.astype(jnp.bfloat16).astype(jnp.float32)
    middle = (value - high).astype(jnp.bfloat16).astype(jnp.float32)
    return high, middle, value - high - middle


def call(
    kernel, out_shape, args, in_hbm=(), out_hbm=False, scratch=(), flops=0, vmem=VMEM_BYTES
):
    far, near = pl.BlockSpec(memory_space=pl.ANY), pl.BlockSpec(memory_space=pltpu.VMEM)
    bytes_accessed = sum(a.size * a.dtype.itemsize for a in args)
    return pl.pallas_call(
        kernel,
        out_shape=out_shape,
        in_specs=[far if k in in_hbm else near for k in range(len(args))],
        out_specs=jax.tree.map(lambda _: far if out_hbm else near, out_shape),
        scratch_shapes=list(scratch),
        compiler_params=pltpu.CompilerParams(vmem_limit_bytes=vmem),
        cost_estimate=pl.CostEstimate(
            flops=flops, bytes_accessed=bytes_accessed, transcendentals=0
        ),
    )(*args)


class Plan:
    def __init__(self, tiles, chans, fields, owners, observed, w_hidden):
        self.tiles, self.chans = tiles, chans
        self.across, self.along, self.features = fields
        self.own_cols = self.across // 4 * (self.along // 4)
        self.rows = owners[0]
        self.tile_cols = self.rows // tiles
        self.slots = observed[0]
        self.shard = observed[1]
        self.capacity = self.slots // tiles
        self.hidden = w_hidden[1]
        self.group = chans // tiles
        self.chips = chans // self.group
        self.steps = self.chips.bit_length() - 1
        self.lane = up_to(self.along, 128)
        self.flag_at = up_to(self.hidden, 128)
        self.width = max(
            up_to(self.features, 128),
            2 * self.flag_at,
            self.flag_at + up_to(self.slots, 128),
            3 * self.lane,
        )
        self.block = up_to(self.own_cols + 2 + self.across, 16)
        self.per_row = self.own_cols + 2
        self.rows_each = chans // self.group
        self.around = (self.group + 2) * self.per_row
        self.deep = up_to(self.features, 16)
        self.strips = self.chips * tiles * self.block

    def order(self, mask):
        return mask % self.group * self.chips + mask // self.group

    def layer(self, refs, k):
        at = k % self.chips * self.deep
        return refs[k // self.chips][at : at + self.features, :]

    def mask(self, k):
        return k % self.chips * self.group + k // self.chips


def prepare_kernel(p, *refs):
    ins, out_ref = refs[:4], refs[4]
    fields_ref, diffusivity_ref, usable_ref, bias_ref, flat, packed, sems = refs[5:]
    copies = [
        pltpu.make_async_copy(source, target, sems.at[k])
        for k, (source, target) in enumerate(zip(ins, refs[5:9]))
    ]
    for copy in copies:
        copy.start()
    flat[...] = jnp.zeros(flat.shape, jnp.float32)
    for copy in copies:
        copy.wait()
    shape = (p.own_cols, p.along)
    row = lax.broadcasted_iota(jnp.int32, shape, 0)
    member = row == lax.broadcasted_iota(jnp.int32, shape, 1) // 4
    total = jnp.dot(
        member.astype(jnp.float32),
        fields_ref[0] + fields_ref[1] + fields_ref[2] + fields_ref[3],
        precision=lax.Precision.HIGHEST,
        preferred_element_type=jnp.float32,
    )
    flat[: p.own_cols, : p.features] = total * 0.0625
    at = p.own_cols
    high, middle, low = split_three(bias_ref[...].reshape(1, p.hidden))
    flat[at : at + 1, : p.hidden] = high
    flat[at : at + 1, p.flag_at : p.flag_at + p.hidden] = middle
    flat[at + 1 : at + 2, : p.hidden] = low
    flags = usable_ref[...].reshape(1, p.slots).astype(jnp.float32)
    flat[at + 1 : at + 2, p.flag_at : p.flag_at + p.slots] = flags
    for k, part in enumerate(split_three(diffusivity_ref[...])):
        flat[at + 2 : at + 2 + p.across, k * p.lane : k * p.lane + p.along] = part
    packed[...] = flat[...].astype(jnp.bfloat16)
    copy = pltpu.make_async_copy(packed, out_ref, sems.at[4])
    copy.start()
    copy.wait()


def place_kernel(p, owners_ref, place_ref, source_ref, cell_ref, *target_refs):
    t, c = lax.axis_index("tile"), lax.axis_index("chan")
    across = owners_ref[...]
    shape = (p.rows, p.rows)
    row = lax.broadcasted_iota(jnp.int32, shape, 0)
    other = lax.broadcasted_iota(jnp.int32, shape, 1)
    owner = jnp.sum(jnp.where(row == other, across, 0), axis=1, keepdims=True)
    first = lax.broadcasted_iota(jnp.int32, owner.shape, 0)
    begin = first // p.tile_cols * p.tile_cols
    same = (owner == across) & (other >= begin) & (other < row)
    rank = jnp.sum(jnp.where(same, 1, 0), axis=1, keepdims=True)
    tile = first // p.tile_cols
    place_ref[...] = (owner ^ t) * p.slots + tile * p.capacity + rank

    def strip(tile, chan):
        other = chan ^ c
        return p.order(other) * p.tiles + (tile ^ t)

    source_ref[...] = (
        strip(tile, first % p.tile_cols // p.own_cols) * p.block + first % p.own_cols
    )

    row = lax.broadcasted_iota(jnp.int32, cell_ref.shape, 0)
    reach = p.across + 4
    tile = (t + row // reach - 1 + p.tiles) % p.tiles
    cell = c * p.across - 2 + row % reach
    inside = (cell >= 0) & (cell < p.chans * p.across)
    cell = jnp.where(inside, cell, 0)
    wanted = strip(tile, cell // p.across) * p.block + p.own_cols + 2 + cell % p.across
    cell_ref[...] = jnp.where(inside, wanted, -1)

    each = p.rows_each * p.own_cols
    target = lax.broadcasted_iota(jnp.int32, target_refs[0].shape, 0)
    for k, target_ref in enumerate(target_refs):
        first = (c % p.group ^ k) * each
        target_ref[...] = target // each * p.tile_cols + first + target % each


def join_kernel(count, *refs):
    ins, out_ref, sems = refs[:count], refs[-2], refs[-1]
    size = out_ref.shape[0] // count
    copies = [
        pltpu.make_async_copy(
            ref, out_ref.at[k] if ref.ndim < out_ref.ndim else out_ref.at[pl.ds(k * size, size)],
            sems.at[k],
        )
        for k, ref in enumerate(ins)
    ]
    for copy in copies:
        copy.start()
    for copy in copies:
        copy.wait()


def stack_kernel(p, *refs):
    for k, ref in enumerate(refs[: p.chips]):
        refs[-1][k * p.deep : k * p.deep + p.features, :] = ref[...]
        refs[-1][k * p.deep + p.features : (k + 1) * p.deep, :] = jnp.zeros(
            (p.deep - p.features, p.hidden), jnp.bfloat16
        )


def one_hot(wanted, first, count):
    source = lax.broadcasted_iota(jnp.int32, (wanted.shape[0], count), 1)
    return (source + first == wanted).astype(jnp.bfloat16)


def forward_kernel(p, *refs):
    refs = list(refs)
    take = lambda n: [refs.pop(0) for _ in range(n)]
    place_ref, source_ref, cell_ref, bias_ref, w_radiance_ref = take(5)
    strip_refs, weight_refs = take(p.group), take(p.group)
    radiance_ref, in_use_ref, preact_ref, kappa_ref, active = refs
    c = lax.axis_index("chan")
    gathered = [ref[...] for ref in strip_refs]
    columns = sum(
        dot(one_hot(source_ref[...], k * p.strips, p.strips), strips)
        for k, strips in enumerate(gathered)
    )
    columns = columns.astype(jnp.bfloat16)[:, : p.features]
    for k in range(p.chans):
        member, chip = k // p.chips, k % p.chips
        at = chip * p.tiles * p.block + p.own_cols
        low = strip_refs[member][at : at + 2, :].astype(jnp.float32)
        bias = (
            low[:1, : p.hidden]
            + low[:1, p.flag_at : p.flag_at + p.hidden]
            + low[1:, : p.hidden]
        )
        preact = dot(columns, p.layer(weight_refs, k)) + bias
        preact_ref[k] = preact
        at = pl.multiple_of((c ^ p.mask(k)) * p.hidden, p.hidden)
        active[:, pl.ds(at, p.hidden)] = (preact * jax.nn.sigmoid(preact)).astype(jnp.bfloat16)
    in_use = jnp.zeros((p.rows, 1), jnp.float32)
    for k in range(p.tiles):
        slot = lax.broadcasted_iota(jnp.int32, (p.rows, p.slots), 1) + k * p.slots
        low = k * p.block + p.own_cols + 1
        flags = strip_refs[0][low : low + 1, p.flag_at : p.flag_at + p.slots]
        flags = jnp.where(place_ref[...] == slot, flags.astype(jnp.float32), 0.0)
        in_use = in_use + jnp.sum(flags, axis=1, keepdims=True)
    in_use_ref[...] = in_use
    radiance_ref[...] = dot(active[...], w_radiance_ref[...]) + bias_ref[...].reshape(1, p.shard)
    parts = sum(
        dot(one_hot(cell_ref[...], k * p.strips, p.strips), strips)
        for k, strips in enumerate(gathered)
    )
    kappa_ref[...] = sum(parts[:, k * p.lane : (k + 1) * p.lane] for k in range(3))


def depart_kernel(p, radiance_ref, in_use_ref, place_ref, *refs):
    seen_refs, part_refs = refs[: -p.steps], refs[-p.steps :]
    part, count = p.rows // p.steps, seen_refs[0].shape[0]
    for j, part_ref in enumerate(part_refs):
        at = slice(j * part, (j + 1) * part)
        observed = sum(
            dot(one_hot(place_ref[at, :], k * count, count), ref[...])
            for k, ref in enumerate(seen_refs)
        )
        departure = (radiance_ref[at, :] - observed) * in_use_ref[at, :]
        part_ref[...] = departure.astype(jnp.bfloat16)


def slope_kernel(preact_ref, slope_ref):
    for k in range(preact_ref.shape[0]):
        preact = preact_ref[k]
        squash = jax.nn.sigmoid(preact)
        slope_ref[k] = (squash * (1.0 + preact * (1.0 - squash))).T


def choose_kernel(p, choices, *refs):
    refs, out_ref, sems = refs[:-3], refs[-2], refs[-1]
    size = refs[0].shape[0]
    role = (lax.axis_index("chan") // p.group) ^ lax.axis_index("tile")
    for place in range(p.chips):

        @pl.when(role == place)
        def _():
            copies = [
                pltpu.make_async_copy(
                    refs[choices[place, j]], out_ref.at[pl.ds(j * size, size)], sems.at[j]
                )
                for j in range(p.steps)
            ]
            for copy in copies:
                copy.start()
            for copy in copies:
                copy.wait()


def near_kernel(p, depart_ref, inv_cov_ref, out_ref):
    at = pl.multiple_of(lax.axis_index("chan") % p.group * p.shard, p.shard)
    out_ref[...] = dot(depart_ref[...], inv_cov_ref[pl.ds(at, p.shard), :])


def backward_kernel(p, *refs):
    refs = list(refs)
    take = lambda n: [refs.pop(0) for _ in range(n)]
    w_radiance_ref, inv_cov_ref, slope_ref, near_ref = take(4)
    depart_refs, weight_refs, target_refs = take(p.group - 1), take(p.group), take(p.group)
    out_refs = refs
    c = lax.axis_index("chan")
    cotangent = near_ref[...]
    for k, ref in enumerate(depart_refs):
        at = pl.multiple_of((c % p.group ^ (k + 1)) * p.shard, p.shard)
        cotangent = cotangent + dot(ref[...], inv_cov_ref[pl.ds(at, p.shard), :])
    cotangent = cotangent.T.astype(jnp.bfloat16)
    total = jnp.zeros((p.features, p.rows), jnp.float32)
    for k in range(p.chans):
        at = pl.multiple_of((c ^ p.mask(k)) * p.hidden, p.hidden)
        grad_hidden = dot(w_radiance_ref[pl.ds(at, p.hidden), :], cotangent)
        grad_pre = (grad_hidden * slope_ref[k]).astype(jnp.bfloat16)
        total = total + dot(p.layer(weight_refs, k), grad_pre)
    total = total.astype(jnp.bfloat16)
    for target_ref, out_ref in zip(target_refs, out_refs):
        out_ref[...] = dot_nt(one_hot(target_ref[...], 0, p.rows), total).astype(jnp.bfloat16)


def add(refs):
    total = refs[0][...].astype(jnp.float32)
    for ref in refs[1:]:
        total = total + ref[...].astype(jnp.float32)
    return total


def rows_and_cells(p, count):
    target = lax.broadcasted_iota(jnp.int32, (count, 1), 0)
    return target // p.per_row, target % p.per_row - 1


def add_group_kernel(p, *refs):
    ins, outs = refs[: p.group], refs[p.group :]
    total = add(ins).astype(jnp.bfloat16)
    row, along = rows_and_cells(p, outs[0].shape[0])
    for k, out_ref in enumerate(outs):
        tile = lax.axis_index("tile") ^ k
        cell = (tile * p.own_cols + along + p.tiles * p.own_cols) % (p.tiles * p.own_cols)
        wanted = (cell // p.own_cols * p.rows_each + row) * p.own_cols + cell % p.own_cols
        out_ref[...] = dot(one_hot(wanted, 0, total.shape[0]), total).astype(jnp.bfloat16)


def add_tiles_kernel(p, *refs):
    ins, outs = refs[: p.tiles], refs[p.tiles :]
    total = add(ins).astype(jnp.bfloat16)
    row, along = rows_and_cells(p, p.around)
    c = lax.axis_index("chan")
    for k, out_ref in enumerate(outs):
        held = ((c // p.group) ^ k) * p.group - 1 + row - c % p.group * p.rows_each
        wanted = jnp.where(
            (held >= 0) & (held < p.rows_each), held * p.per_row + along + 1, -1
        )
        out_ref[...] = dot(one_hot(wanted, 0, total.shape[0]), total).astype(jnp.bfloat16)


def add_chips_kernel(*refs):
    refs[-1][...] = add(refs[:-1])


def diffuse_kernel(p, edge, *refs):
    ins, root_ref, out_ref = refs[: p.group], refs[-2], refs[-1]
    total = add(ins) * 0.0625
    length = p.along + 2 * edge
    shape = (length, p.around)
    cell = lax.broadcasted_iota(jnp.int32, shape, 0)
    source = lax.broadcasted_iota(jnp.int32, shape, 1)
    column = (cell - edge + 4) // 4
    spread = []
    for k in range(3):
        row = lax.axis_index("chan") % p.group + k
        pick = (source == column + row * p.per_row) & (column >= 0) & (column < p.per_row)
        spread.append(
            jnp.dot(
                pick.astype(jnp.float32),
                total,
                precision=lax.Precision.HIGHEST,
                preferred_element_type=jnp.float32,
            )
        )
    root = root_ref[...]
    state = [spread[(row + 2) // 4] for row in range(p.across + 4)]
    east_of = functools.partial(pltpu.roll, shift=length - 1, axis=0)
    west_of = functools.partial(pltpu.roll, shift=1, axis=0)
    north = root[:, :-1] * root[:, 1:]
    east, west = root * east_of(root), root * west_of(root)
    for sweep in range(2):
        fresh = list(state)
        for row in range(1 + sweep, p.across + 3 - sweep):
            here = state[row]
            fresh[row] = (
                here
                + north[:, row : row + 1] * (state[row + 1] - here)
                + north[:, row - 1 : row] * (state[row - 1] - here)
                + east[:, row : row + 1] * (east_of(here) - here)
                + west[:, row : row + 1] * (west_of(here) - here)
            )
        state = fresh
    for row in range(p.across):
        out_ref[row] = state[row + 2][edge : edge + p.along, : p.features]


def body_by_column(
    fields,
    diffusivity,
    owners,
    observed,
    usable,
    w_hidden,
    b_hidden,
    w_radiance,
    b_radiance,
    inv_cov,
):
    p = Plan(
        lax.axis_size("tile"),
        lax.axis_size("chan"),
        fields.shape,
        owners.shape,
        observed.shape,
        w_hidden.shape,
    )
    half, single = jnp.bfloat16, jnp.float32
    shape = jax.ShapeDtypeStruct
    both = ("tile", "chan")
    everyone = [(a, b) for a in range(p.tiles) for b in range(p.chans)]

    def flip(value, mask):
        return lax.ppermute(value, "chan", [(b, b ^ mask) for b in range(p.chans)])

    def trade(value, mask):
        return lax.ppermute(value, "tile", [(a, a ^ mask) for a in range(p.tiles)])

    def send(value, wanted):
        pairs = dict(wanted)
        pairs.update({target: source for source, target in wanted.items()})
        for a, b in everyone:
            if (a, b) not in pairs:
                pairs[a, b] = (a, b ^ 1)
        number = lambda place: place[0] * p.chans + place[1]
        return lax.ppermute(
            value, both, sorted((number(a), number(b)) for a, b in pairs.items())
        )

    def join(values, kernel_shape, after=()):
        return call(
            functools.partial(join_kernel, len(values)),
            shape(kernel_shape, half),
            [*values, *after],
            in_hbm=range(len(values) + len(after)),
            out_hbm=True,
            scratch=[pltpu.SemaphoreType.DMA((len(values),))],
            flops=0,
        )

    def grow(value, over, after=()):
        return join([value, over(value)], (2 * value.shape[0],) + value.shape[1:], after)

    strips = call(
        functools.partial(prepare_kernel, p),
        shape((p.block, p.width), half),
        [fields, diffusivity, usable, b_hidden],
        in_hbm=range(4),
        out_hbm=True,
        scratch=[
            pltpu.VMEM(fields.shape, single),
            pltpu.VMEM(diffusivity.shape, single),
            pltpu.VMEM(usable.shape, jnp.int32),
            pltpu.VMEM(b_hidden.shape, single),
            pltpu.VMEM((p.block, p.width), single),
            pltpu.VMEM((p.block, p.width), half),
            pltpu.SemaphoreType.DMA((5,)),
        ],
        vmem=WHOLE_VMEM_BYTES,
    )
    seen, stages = observed, []
    bit = 1
    while bit < p.tiles:
        if 2 * bit < p.tiles:
            seen = grow(seen, lambda value: trade(value, bit))
        strips = grow(strips, lambda value: trade(value, bit), [seen] if bit == 1 else ())
        stages.append(strips)
        bit *= 2
    strips = join(
        [strips] + [flip(strips, k * p.group) for k in range(1, p.chips)], (p.strips, p.width)
    )
    strips = [strips] + [flip(strips, k) for k in range(1, p.group)]

    near = [w_hidden] + [flip(w_hidden, chip * p.group) for chip in range(1, p.chips)]
    near = call(
        functools.partial(stack_kernel, p),
        shape((p.chips * p.deep, p.hidden), half),
        near + [stages[-1]],
        in_hbm=[len(near)],
    )
    weights = [near] + [flip(near, k) for k in range(1, p.group)]

    far_half = p.tiles // 2
    seen = [
        seen,
        send(seen, {(b // p.group ^ far_half, b): (b // p.group, b) for b in range(p.chans)}),
    ]

    reach = p.across + 4
    place, source, cell, *targets = call(
        functools.partial(place_kernel, p),
        [shape((p.rows, 1), jnp.int32)] * 2
        + [shape((3 * reach, 1), jnp.int32)]
        + [shape((p.rows // p.group, 1), jnp.int32)] * p.group,
        [owners.reshape(1, p.rows)],
        flops=SLACK_FLOPS,
    )
    radiance, in_use, preact, kappa = call(
        functools.partial(forward_kernel, p),
        [
            shape((p.rows, p.shard), single),
            shape((p.rows, 1), single),
            shape((p.chans, p.rows, p.hidden), single),
            shape((3 * reach, p.lane), single),
        ],
        [place, source, cell, b_radiance, w_radiance] + strips + weights,
        scratch=[pltpu.VMEM((p.rows, p.hidden * p.chans), half)],
        flops=FORWARD_FLOPS,
    )
    parts = call(
        functools.partial(depart_kernel, p),
        [shape((p.rows // p.steps, p.shard), half)] * p.steps,
        [radiance, in_use, place] + seen,
    )

    slope = call(
        slope_kernel,
        shape((p.chans, p.hidden, p.rows), single),
        [preact],
        flops=40 * preact.size,
    )

    pool, held, choices = list(parts), {}, {}
    for j in range(p.steps):
        held[0, j] = choices[0, j] = j
    for step in range(p.steps):
        for since in range(-1, step):
            for j in range(p.steps):
                order = [1 << (j + k) % p.steps for k in range(p.steps)]
                roles = [0] if since < 0 else [
                    order[since] + rest
                    for rest in range(p.chips)
                    if rest & ~sum(order[:since]) == 0
                ]
                wanted = {
                    (a, b): (a, b ^ order[step] * p.group)
                    for a, b in everyone
                    if (b // p.group ^ a) in roles
                }
                source = pool[choices[roles[0], j]]
                for role in roles:
                    choices[role + order[step], j] = len(pool)
                pool.append(send(source, wanted))
    chosen = call(
        functools.partial(choose_kernel, p, choices),
        shape((p.rows, p.shard), half),
        pool + [slope],
        in_hbm=range(len(pool) + 1),
        out_hbm=True,
        scratch=[pltpu.SemaphoreType.DMA((p.steps,))],
    )
    depart = [flip(chosen, k) for k in range(1, p.group)]

    partial = call(
        functools.partial(near_kernel, p),
        shape((p.rows, p.shard), single),
        [chosen, inv_cov],
        flops=2 * p.rows * p.shard * p.shard,
    )
    partial = call(
        functools.partial(backward_kernel, p),
        [shape((p.rows // p.group, p.features), half)] * p.group,
        [w_radiance, inv_cov, slope, partial] + depart + weights + targets,
        flops=2 * p.rows * (p.hidden * p.chans * (p.features + p.shard) + inv_cov.size),
    )
    partial = [partial[0]] + [flip(partial[k], k) for k in range(1, p.group)]
    partial = call(
        functools.partial(add_group_kernel, p),
        [shape((p.rows_each * p.per_row, p.features), half)] * p.tiles,
        partial,
    )
    partial = [partial[0]] + [trade(partial[k], k) for k in range(1, p.tiles)]
    partial = call(
        functools.partial(add_tiles_kernel, p),
        [shape((p.around, p.features), half)] * p.chips,
        partial,
    )
    partial = [partial[0]] + [flip(partial[k], k * p.group) for k in range(1, p.chips)]
    partial = call(add_chips_kernel, shape((p.around, p.features), single), partial)
    partial = [partial] + [flip(partial, k) for k in range(1, p.group)]

    edge = 8
    kappa = kappa.reshape(3, reach, p.lane)
    root = jnp.sqrt(
        jnp.concatenate(
            [kappa[0, :, p.along - edge : p.along], kappa[1, :, : p.along], kappa[2, :, :edge]],
            axis=1,
        ).T
    )
    return call(
        functools.partial(diffuse_kernel, p, edge),
        shape(fields.shape, single),
        partial + [root],
        flops=100 * fields.size,
    )


def solution(mesh):
    tiles, chans = mesh.shape["tile"], mesh.shape["chan"]
    by_column = tiles > 1 and chans % tiles == 0 and chans & (chans - 1) == 0 and chans > tiles
    placed = (
        P("chan", "tile", None),
        P("chan", "tile"),
        P(),
        P("tile", "chan"),
        P("tile"),
        P(None, "chan"),
        P("chan"),
        P(None, "chan"),
        P("chan"),
        P("tile", "chan"),
    )
    return jax.shard_map(
        body_by_column if by_column else body_by_owner,
        mesh=mesh,
        in_specs=placed,
        out_specs=P("chan", "tile", None),
        check_vma=False,
    )
```

```python
import functools

import jax
import jax.numpy as jnp
from jax import lax
from jax.experimental import pallas as pl
from jax.experimental.pallas import tpu as pltpu
from jax.sharding import PartitionSpec as P

VMEM_BYTES = 24 * 1024 * 1024
SLACK_FLOPS = 2 * 10**9
FORWARD_FLOPS = 10**8
NT_DIMS = (((1,), (1,)), ((), ()))


def padded_2(value, sides, width, wrap):
    for axis, dim in sides:
        devices, length = (lax.axis_size(axis), value.shape[dim])
        up = [(i, (i + 1) % devices) for i in range(devices if wrap else devices - 1)]
        down = [(j, i) for i, j in up]
        last = lax.slice_in_dim(value, length - width, length, axis=dim)
        first = lax.slice_in_dim(value, 0, width, axis=dim)
        before = lax.ppermute(last, axis, up)
        after = lax.ppermute(first, axis, down)
        value = jnp.concatenate([before, value, after], axis=dim)
    return value


def add_rims(values):
    rowwise = padded_2(values, (("chan", 0),), 1, False)
    return padded_2(rowwise, (("tile", 1),), 1, True)


def body_by_owner(
    fields,
    diffusivity,
    owners,
    observed,
    usable,
    w_hidden,
    b_hidden,
    w_radiance,
    b_radiance,
    inv_cov,
):
    tile_count = lax.axis_size("tile")
    chan_count = lax.axis_size("chan")
    tile_index = lax.axis_index("tile")
    chan_index = lax.axis_index("chan")
    slot_count = observed.shape[0]
    capacity = slot_count // tile_count
    cells_across, cells_along, features = fields.shape
    own_cols = cells_across // 4 * (cells_along // 4)
    tile_cols = chan_count * own_cols
    hidden_dev = w_hidden.shape[1]
    owner_table = owners[:, 0].reshape(tile_count, tile_cols)
    owner_hits = (
        owner_table[:, :, None] == jnp.arange(tile_count, dtype=jnp.int32)[None, None, :]
    ).astype(jnp.int32)
    before = jnp.sum((jnp.cumsum(owner_hits, axis=1) - owner_hits) * owner_hits, axis=2)
    tallies = jnp.sum(owner_hits, axis=1)
    slot_of = lax.dynamic_index_in_dim(
        owner_table * capacity + before, tile_index, 0, keepdims=False
    )
    arriving = lax.dynamic_index_in_dim(tallies, tile_index, 1, keepdims=False)
    occupied = (jnp.arange(capacity, dtype=jnp.int32)[None, :] < arriving[:, None]).reshape(
        slot_count
    )
    grouped = fields.reshape(cells_across // 4, 4, cells_along // 4, 4, features)
    columns = (
        (jnp.sum(grouped, axis=(1, 3)) * 0.0625).reshape(own_cols, features).astype(jnp.bfloat16)
    )
    placer = (slot_of[None, :] == jnp.arange(slot_count, dtype=jnp.int32)[:, None]).astype(
        jnp.bfloat16
    )
    outgoing = jnp.dot(
        placer,
        lax.all_gather(columns, "chan", axis=0, tiled=True),
        preferred_element_type=jnp.float32,
    )
    incoming = lax.all_to_all(
        outgoing.astype(jnp.bfloat16), "tile", split_axis=0, concat_axis=0, tiled=True
    )
    preact = lax.dot_general(
        w_hidden, incoming, (((0,), (1,)), ((), ())), preferred_element_type=jnp.float32
    )
    preact = preact + b_hidden[:, None]
    squash = jax.nn.sigmoid(preact)
    active = (preact * squash).astype(jnp.bfloat16)
    radiance = lax.dot_general(
        lax.all_gather(active, "chan", axis=0, tiled=True),
        w_radiance,
        (((0,), (0,)), ((), ())),
        preferred_element_type=jnp.float32,
    )
    radiance = radiance + b_radiance[None, :]
    in_use = usable.astype(jnp.float32) * occupied.astype(jnp.float32)
    departure = ((radiance - observed.astype(jnp.float32)) * in_use[:, None]).astype(jnp.bfloat16)
    cotangent = jnp.dot(
        lax.all_gather(departure, "chan", axis=1, tiled=True),
        lax.all_gather(inv_cov, "tile", axis=0, tiled=True),
        preferred_element_type=jnp.float32,
    )
    cotangent = cotangent.astype(jnp.bfloat16)
    full_sum = lax.psum(
        lax.dot_general(w_radiance, cotangent, NT_DIMS, preferred_element_type=jnp.float32),
        "chan",
    )
    grad_hidden = lax.dynamic_slice_in_dim(full_sum, chan_index * hidden_dev, hidden_dev, 0)
    slope_term = squash * (1.0 + preact * (1.0 - squash))
    grad_pre = (grad_hidden * slope_term).astype(jnp.bfloat16)
    part_grad = lax.dot_general(
        grad_pre, w_hidden, (((0,), (1,)), ((), ())), preferred_element_type=jnp.float32
    )
    returned = lax.all_to_all(part_grad, "tile", split_axis=0, concat_axis=0, tiled=True)
    column_grad = lax.psum_scatter(
        jnp.take(returned, slot_of, axis=0), "chan", scatter_dimension=0, tiled=True
    )
    spread = jnp.repeat(
        column_grad.reshape(cells_across // 4, cells_along // 4, features), 4, axis=0
    )
    adjoint = jnp.repeat(spread, 4, axis=1) * 0.0625
    kappa_root = jnp.sqrt(diffusivity)
    root_rim = add_rims(kappa_root)
    coef_north = (kappa_root * root_rim[2:, 1:-1])[:, :, None]
    coef_south = (kappa_root * root_rim[:-2, 1:-1])[:, :, None]
    coef_east = (kappa_root * root_rim[1:-1, 2:])[:, :, None]
    coef_west = (kappa_root * root_rim[1:-1, :-2])[:, :, None]
    for sweep_index in range(2):
        padded = add_rims(adjoint)
        adjoint = (
            adjoint
            + coef_north * (padded[2:, 1:-1] - adjoint)
            + coef_south * (padded[:-2, 1:-1] - adjoint)
            + coef_east * (padded[1:-1, 2:] - adjoint)
            + coef_west * (padded[1:-1, :-2] - adjoint)
        )
    return adjoint


def up_to(value, multiple):
    return -(-value // multiple) * multiple


def dot(left, right):
    return jnp.dot(left, right, preferred_element_type=jnp.float32)


def dot_nt(left, right):
    return lax.dot_general(left, right, NT_DIMS, preferred_element_type=jnp.float32)


def split_three(value):
    high = value.astype(jnp.bfloat16).astype(jnp.float32)
    middle = (value - high).astype(jnp.bfloat16).astype(jnp.float32)
    return high, middle, value - high - middle


def call(
    kernel, out_shape, args, in_hbm=(), out_hbm=False, scratch=(), flops=0, vmem=VMEM_BYTES
):
    far, near = pl.BlockSpec(memory_space=pl.ANY), pl.BlockSpec(memory_space=pltpu.VMEM)
    bytes_accessed = sum(a.size * a.dtype.itemsize for a in args)
    return pl.pallas_call(
        kernel,
        out_shape=out_shape,
        in_specs=[far if k in in_hbm else near for k in range(len(args))],
        out_specs=jax.tree.map(lambda _: far if out_hbm else near, out_shape),
        scratch_shapes=list(scratch),
        compiler_params=pltpu.CompilerParams(vmem_limit_bytes=vmem),
        cost_estimate=pl.CostEstimate(
            flops=flops, bytes_accessed=bytes_accessed, transcendentals=0
        ),
    )(*args)


class Plan:
    def __init__(self, tiles, chans, fields, owners, observed, w_hidden):
        self.tiles, self.chans = tiles, chans
        self.across, self.along, self.features = fields
        self.own_cols = self.across // 4 * (self.along // 4)
        self.rows = owners[0]
        self.tile_cols = self.rows // tiles
        self.slots = observed[0]
        self.shard = observed[1]
        self.capacity = self.slots // tiles
        self.hidden = w_hidden[1]
        self.group = chans // tiles
        self.chips = chans // self.group
        self.steps = self.chips.bit_length() - 1
        self.lane = up_to(self.along, 128)
        self.flag_at = up_to(self.hidden, 128)
        self.width = max(
            up_to(self.features, 128),
            2 * self.flag_at,
            self.flag_at + up_to(self.slots, 128),
            3 * self.lane,
        )
        self.block = up_to(self.own_cols + 2 + self.across, 16)
        self.per_row = self.own_cols + 2
        self.rows_each = chans // self.group
        self.room = up_to(self.per_row, 16)
        self.deep = up_to(self.features, 16)
        self.strips = self.chips * tiles * self.block

    def order(self, mask):
        return mask % self.group * self.chips + mask // self.group

    def layer(self, refs, k):
        at = k % self.chips * self.deep
        return refs[k // self.chips][at : at + self.features, :]

    def mask(self, k):
        return k % self.chips * self.group + k // self.chips


def prepare_kernel(p, fields_ref, diffusivity_ref, usable_ref, bias_ref, after_ref, out_ref, flat):
    flat[...] = jnp.zeros(flat.shape, jnp.float32)
    shape = (p.own_cols, p.along)
    row = lax.broadcasted_iota(jnp.int32, shape, 0)
    member = row == lax.broadcasted_iota(jnp.int32, shape, 1) // 4
    total = jnp.dot(
        member.astype(jnp.float32),
        fields_ref[0] + fields_ref[1] + fields_ref[2] + fields_ref[3],
        precision=lax.Precision.HIGHEST,
        preferred_element_type=jnp.float32,
    )
    flat[: p.own_cols, : p.features] = total * 0.0625
    at = p.own_cols
    high, middle, low = split_three(bias_ref[...].reshape(1, p.hidden))
    flat[at : at + 1, : p.hidden] = high
    flat[at : at + 1, p.flag_at : p.flag_at + p.hidden] = middle
    flat[at + 1 : at + 2, : p.hidden] = low
    flags = usable_ref[...].reshape(1, p.slots).astype(jnp.float32)
    flat[at + 1 : at + 2, p.flag_at : p.flag_at + p.slots] = flags
    for k, part in enumerate(split_three(diffusivity_ref[...])):
        flat[at + 2 : at + 2 + p.across, k * p.lane : k * p.lane + p.along] = part
    out_ref[...] = flat[...].astype(jnp.bfloat16)


def strip_of(p, tile, chan):
    other = chan ^ lax.axis_index("chan")
    return p.order(other) * p.tiles + (tile ^ lax.axis_index("tile"))


def index_kernel(p, cell_ref, *target_refs):
    t, c = lax.axis_index("tile"), lax.axis_index("chan")
    row = lax.broadcasted_iota(jnp.int32, cell_ref.shape, 0)
    reach = p.across + 4
    tile = (t + row // reach - 1 + p.tiles) % p.tiles
    cell = c * p.across - 2 + row % reach
    inside = (cell >= 0) & (cell < p.chans * p.across)
    cell = jnp.where(inside, cell, 0)
    wanted = strip_of(p, tile, cell // p.across) * p.block + p.own_cols + 2 + cell % p.across
    cell_ref[...] = jnp.where(inside, wanted, -1)

    each = p.tiles * p.own_cols
    target = lax.broadcasted_iota(jnp.int32, target_refs[0].shape, 0)
    chip, inner = target // each, target % each
    for k, target_ref in enumerate(target_refs):
        row = (chip ^ (c // p.group)) * p.group + (c % p.group ^ k)
        target_ref[...] = (
            inner // p.own_cols * p.tile_cols + row * p.own_cols + inner % p.own_cols
        )


def place_kernel(p, owners_ref, place_ref, source_ref):
    t = lax.axis_index("tile")
    across = owners_ref[...]
    shape = (p.rows, p.rows)
    row = lax.broadcasted_iota(jnp.int32, shape, 0)
    other = lax.broadcasted_iota(jnp.int32, shape, 1)
    owner = jnp.sum(jnp.where(row == other, across, 0), axis=1, keepdims=True)
    first = lax.broadcasted_iota(jnp.int32, owner.shape, 0)
    begin = first // p.tile_cols * p.tile_cols
    same = (owner == across) & (other >= begin) & (other < row)
    rank = jnp.sum(jnp.where(same, 1, 0), axis=1, keepdims=True)
    tile = first // p.tile_cols
    place_ref[...] = (owner ^ t) * p.slots + tile * p.capacity + rank
    source_ref[...] = (
        strip_of(p, tile, first % p.tile_cols // p.own_cols) * p.block + first % p.own_cols
    )


def join_kernel(count, *refs):
    ins, out_ref, sems = refs[:count], refs[-2], refs[-1]
    size = out_ref.shape[0] // count
    copies = [
        pltpu.make_async_copy(
            ref, out_ref.at[k] if ref.ndim < out_ref.ndim else out_ref.at[pl.ds(k * size, size)],
            sems.at[k],
        )
        for k, ref in enumerate(ins)
    ]
    for copy in copies:
        copy.start()
    for copy in copies:
        copy.wait()


def stack_kernel(p, *refs):
    for k, ref in enumerate(refs[: p.chips]):
        refs[-1][k * p.deep : k * p.deep + p.features, :] = ref[...]
        refs[-1][k * p.deep + p.features : (k + 1) * p.deep, :] = jnp.zeros(
            (p.deep - p.features, p.hidden), jnp.bfloat16
        )


def one_hot(wanted, first, count):
    source = lax.broadcasted_iota(jnp.int32, (wanted.shape[0], count), 1)
    return (source + first == wanted).astype(jnp.bfloat16)


def forward_kernel(p, *refs):
    refs = list(refs)
    take = lambda n: [refs.pop(0) for _ in range(n)]
    place_ref, source_ref, cell_ref, bias_ref, w_radiance_ref = take(5)
    strip_refs, weight_refs = take(p.group), take(p.group)
    radiance_ref, in_use_ref, preact_ref, kappa_ref, active = refs
    c = lax.axis_index("chan")
    gathered = [ref[...] for ref in strip_refs]
    columns = sum(
        dot(one_hot(source_ref[...], k * p.strips, p.strips), strips)
        for k, strips in enumerate(gathered)
    )
    columns = columns.astype(jnp.bfloat16)[:, : p.features]
    for k in range(p.chans):
        member, chip = k // p.chips, k % p.chips
        at = chip * p.tiles * p.block + p.own_cols
        low = strip_refs[member][at : at + 2, :].astype(jnp.float32)
        bias = (
            low[:1, : p.hidden]
            + low[:1, p.flag_at : p.flag_at + p.hidden]
            + low[1:, : p.hidden]
        )
        preact = dot(columns, p.layer(weight_refs, k)) + bias
        preact_ref[k] = preact
        at = pl.multiple_of((c ^ p.mask(k)) * p.hidden, p.hidden)
        active[:, pl.ds(at, p.hidden)] = (preact * jax.nn.sigmoid(preact)).astype(jnp.bfloat16)
    in_use = jnp.zeros((p.rows, 1), jnp.float32)
    for k in range(p.tiles):
        slot = lax.broadcasted_iota(jnp.int32, (p.rows, p.slots), 1) + k * p.slots
        low = k * p.block + p.own_cols + 1
        flags = strip_refs[0][low : low + 1, p.flag_at : p.flag_at + p.slots]
        flags = jnp.where(place_ref[...] == slot, flags.astype(jnp.float32), 0.0)
        in_use = in_use + jnp.sum(flags, axis=1, keepdims=True)
    in_use_ref[...] = in_use
    radiance_ref[...] = dot(active[...], w_radiance_ref[...]) + bias_ref[...].reshape(1, p.shard)
    parts = sum(
        dot(one_hot(cell_ref[...], k * p.strips, p.strips), strips)
        for k, strips in enumerate(gathered)
    )
    kappa_ref[...] = sum(parts[:, k * p.lane : (k + 1) * p.lane] for k in range(3))


def depart_kernel(p, radiance_ref, in_use_ref, place_ref, *refs):
    seen_refs, part_refs = refs[: -p.steps], refs[-p.steps :]
    part, count = p.rows // p.steps, seen_refs[0].shape[0]
    for j, part_ref in enumerate(part_refs):
        at = slice(j * part, (j + 1) * part)
        observed = sum(
            dot(one_hot(place_ref[at, :], k * count, count), ref[...])
            for k, ref in enumerate(seen_refs)
        )
        departure = (radiance_ref[at, :] - observed) * in_use_ref[at, :]
        part_ref[...] = departure.astype(jnp.bfloat16)


def slope_kernel(preact_ref, slope_ref):
    for k in range(preact_ref.shape[0]):
        preact = preact_ref[k]
        squash = jax.nn.sigmoid(preact)
        slope_ref[k] = (squash * (1.0 + preact * (1.0 - squash))).T


def choose_kernel(p, choices, *refs):
    refs, out_ref, sems = refs[:-3], refs[-2], refs[-1]
    size = refs[0].shape[0]
    role = (lax.axis_index("chan") // p.group) ^ lax.axis_index("tile")
    for place in range(p.chips):

        @pl.when(role == place)
        def _():
            copies = [
                pltpu.make_async_copy(
                    refs[choices[place, j]], out_ref.at[pl.ds(j * size, size)], sems.at[j]
                )
                for j in range(p.steps)
            ]
            for copy in copies:
                copy.start()
            for copy in copies:
                copy.wait()


def near_kernel(p, depart_ref, inv_cov_ref, out_ref):
    at = pl.multiple_of(lax.axis_index("chan") % p.group * p.shard, p.shard)
    out_ref[...] = dot(depart_ref[...], inv_cov_ref[pl.ds(at, p.shard), :])


def backward_kernel(p, *refs):
    refs = list(refs)
    take = lambda n: [refs.pop(0) for _ in range(n)]
    w_radiance_ref, inv_cov_ref, slope_ref, near_ref = take(4)
    depart_refs, weight_refs, target_refs = take(p.group - 1), take(p.group), take(p.group)
    out_refs = refs
    c = lax.axis_index("chan")
    cotangent = near_ref[...]
    for k, ref in enumerate(depart_refs):
        at = pl.multiple_of((c % p.group ^ (k + 1)) * p.shard, p.shard)
        cotangent = cotangent + dot(ref[...], inv_cov_ref[pl.ds(at, p.shard), :])
    cotangent = cotangent.T.astype(jnp.bfloat16)
    total = jnp.zeros((p.features, p.rows), jnp.float32)
    for k in range(p.chans):
        at = pl.multiple_of((c ^ p.mask(k)) * p.hidden, p.hidden)
        grad_hidden = dot(w_radiance_ref[pl.ds(at, p.hidden), :], cotangent)
        grad_pre = (grad_hidden * slope_ref[k]).astype(jnp.bfloat16)
        total = total + dot(p.layer(weight_refs, k), grad_pre)
    total = total.astype(jnp.bfloat16)
    for target_ref, out_ref in zip(target_refs, out_refs):
        out_ref[...] = dot_nt(one_hot(target_ref[...], 0, p.rows), total).astype(jnp.bfloat16)


def add(refs):
    total = refs[0][...].astype(jnp.float32)
    for ref in refs[1:]:
        total = total + ref[...].astype(jnp.float32)
    return total


def add_group_kernel(p, *refs):
    ins, outs = refs[: p.group], refs[p.group :]
    total = add(ins).astype(jnp.bfloat16)
    each = p.tiles * p.own_cols
    for k, out_ref in enumerate(outs):
        out_ref[...] = total[k * each : (k + 1) * each]


def add_chips_kernel(p, *refs):
    ins, outs = refs[: p.chips], refs[p.chips :]
    total = add(ins).astype(jnp.bfloat16)
    along = lax.broadcasted_iota(jnp.int32, (p.room, 1), 0) - 1
    count = p.tiles * p.own_cols
    for k, out_ref in enumerate(outs):
        tile = lax.axis_index("tile") ^ k
        wanted = (tile * p.own_cols + along + count) % count
        out_ref[...] = dot(one_hot(wanted, 0, count), total).astype(jnp.bfloat16)


def add_tiles_kernel(*refs):
    refs[-1][...] = add(refs[:-1])


def diffuse_kernel(p, edge, *refs):
    ins, root_ref, out_ref = refs[:3], refs[-2], refs[-1]
    length = p.along + 2 * edge
    shape = (length, p.room)
    cell = lax.broadcasted_iota(jnp.int32, shape, 0)
    source = lax.broadcasted_iota(jnp.int32, shape, 1)
    column = (cell - edge + 4) // 4
    spread = []
    for k in range(3):
        pick = (source == column) & (column >= 0) & (column < p.per_row)
        spread.append(
            jnp.dot(
                pick.astype(jnp.float32),
                ins[k][...] * 0.0625,
                precision=lax.Precision.HIGHEST,
                preferred_element_type=jnp.float32,
            )
        )
    root = root_ref[...]
    state = [spread[(row + 2) // 4] for row in range(p.across + 4)]
    east_of = functools.partial(pltpu.roll, shift=length - 1, axis=0)
    west_of = functools.partial(pltpu.roll, shift=1, axis=0)
    north = root[:, :-1] * root[:, 1:]
    east, west = root * east_of(root), root * west_of(root)
    for sweep in range(2):
        fresh = list(state)
        for row in range(1 + sweep, p.across + 3 - sweep):
            here = state[row]
            fresh[row] = (
                here
                + north[:, row : row + 1] * (state[row + 1] - here)
                + north[:, row - 1 : row] * (state[row - 1] - here)
                + east[:, row : row + 1] * (east_of(here) - here)
                + west[:, row : row + 1] * (west_of(here) - here)
            )
        state = fresh
    for row in range(p.across):
        out_ref[row] = state[row + 2][edge : edge + p.along, : p.features]


def body_by_column(
    fields,
    diffusivity,
    owners,
    observed,
    usable,
    w_hidden,
    b_hidden,
    w_radiance,
    b_radiance,
    inv_cov,
):
    p = Plan(
        lax.axis_size("tile"),
        lax.axis_size("chan"),
        fields.shape,
        owners.shape,
        observed.shape,
        w_hidden.shape,
    )
    half, single = jnp.bfloat16, jnp.float32
    shape = jax.ShapeDtypeStruct
    both = ("tile", "chan")
    everyone = [(a, b) for a in range(p.tiles) for b in range(p.chans)]

    def flip(value, mask):
        return lax.ppermute(value, "chan", [(b, b ^ mask) for b in range(p.chans)])

    def trade(value, mask):
        return lax.ppermute(value, "tile", [(a, a ^ mask) for a in range(p.tiles)])

    def send(value, wanted):
        pairs = dict(wanted)
        pairs.update({target: source for source, target in wanted.items()})
        for a, b in everyone:
            if (a, b) not in pairs:
                pairs[a, b] = (a, b ^ 1)
        number = lambda place: place[0] * p.chans + place[1]
        return lax.ppermute(
            value, both, sorted((number(a), number(b)) for a, b in pairs.items())
        )

    def join(values, kernel_shape, after=()):
        return call(
            functools.partial(join_kernel, len(values)),
            shape(kernel_shape, half),
            [*values, *after],
            in_hbm=range(len(values) + len(after)),
            out_hbm=True,
            scratch=[pltpu.SemaphoreType.DMA((len(values),))],
            flops=0,
        )

    def grow(value, over, after=()):
        return join([value, over(value)], (2 * value.shape[0],) + value.shape[1:], after)

    reach = p.across + 4
    cell, *targets = call(
        functools.partial(index_kernel, p),
        [shape((3 * reach, 1), jnp.int32)] + [shape((p.rows // p.group, 1), jnp.int32)] * p.group,
        [],
        flops=SLACK_FLOPS,
    )

    strips = call(
        functools.partial(prepare_kernel, p),
        shape((p.block, p.width), half),
        [fields, diffusivity, usable, b_hidden, cell],
        in_hbm=[4],
        scratch=[pltpu.VMEM((p.block, p.width), single)],
    )
    seen, stages = observed, []
    bit = 1
    while bit < p.tiles:
        if 2 * bit < p.tiles:
            seen = grow(seen, lambda value: trade(value, bit))
        strips = grow(strips, lambda value: trade(value, bit), [seen] if bit == 1 else ())
        stages.append(strips)
        bit *= 2
    strips = join(
        [strips] + [flip(strips, k * p.group) for k in range(1, p.chips)], (p.strips, p.width)
    )
    strips = [strips] + [flip(strips, k) for k in range(1, p.group)]

    near = [w_hidden] + [flip(w_hidden, chip * p.group) for chip in range(1, p.chips)]
    near = call(
        functools.partial(stack_kernel, p),
        shape((p.chips * p.deep, p.hidden), half),
        near + [stages[-1]],
        in_hbm=[len(near)],
    )
    weights = [near] + [flip(near, k) for k in range(1, p.group)]

    far_half = p.tiles // 2
    seen = [
        seen,
        send(seen, {(b // p.group ^ far_half, b): (b // p.group, b) for b in range(p.chans)}),
    ]

    place, source = call(
        functools.partial(place_kernel, p),
        [shape((p.rows, 1), jnp.int32)] * 2,
        [owners.reshape(1, p.rows)],
        flops=SLACK_FLOPS,
    )
    radiance, in_use, preact, kappa = call(
        functools.partial(forward_kernel, p),
        [
            shape((p.rows, p.shard), single),
            shape((p.rows, 1), single),
            shape((p.chans, p.rows, p.hidden), single),
            shape((3 * reach, p.lane), single),
        ],
        [place, source, cell, b_radiance, w_radiance] + strips + weights,
        scratch=[pltpu.VMEM((p.rows, p.hidden * p.chans), half)],
        flops=FORWARD_FLOPS,
    )
    parts = call(
        functools.partial(depart_kernel, p),
        [shape((p.rows // p.steps, p.shard), half)] * p.steps,
        [radiance, in_use, place] + seen,
    )

    slope = call(
        slope_kernel,
        shape((p.chans, p.hidden, p.rows), single),
        [preact],
        flops=40 * preact.size,
    )

    pool, held, choices = list(parts), {}, {}
    for j in range(p.steps):
        held[0, j] = choices[0, j] = j
    for step in range(p.steps):
        for since in range(-1, step):
            for j in range(p.steps):
                order = [1 << (j + k) % p.steps for k in range(p.steps)]
                roles = [0] if since < 0 else [
                    order[since] + rest
                    for rest in range(p.chips)
                    if rest & ~sum(order[:since]) == 0
                ]
                wanted = {
                    (a, b): (a, b ^ order[step] * p.group)
                    for a, b in everyone
                    if (b // p.group ^ a) in roles
                }
                source = pool[choices[roles[0], j]]
                for role in roles:
                    choices[role + order[step], j] = len(pool)
                pool.append(send(source, wanted))
    chosen = call(
        functools.partial(choose_kernel, p, choices),
        shape((p.rows, p.shard), half),
        pool + [slope],
        in_hbm=range(len(pool) + 1),
        out_hbm=True,
        scratch=[pltpu.SemaphoreType.DMA((p.steps,))],
    )
    depart = [flip(chosen, k) for k in range(1, p.group)]

    partial = call(
        functools.partial(near_kernel, p),
        shape((p.rows, p.shard), single),
        [chosen, inv_cov],
        flops=2 * p.rows * p.shard * p.shard,
    )
    partial = call(
        functools.partial(backward_kernel, p),
        [shape((p.rows // p.group, p.features), half)] * p.group,
        [w_radiance, inv_cov, slope, partial] + depart + weights + targets,
        flops=2 * p.rows * (p.hidden * p.chans * (p.features + p.shard) + inv_cov.size),
    )
    partial = [partial[0]] + [flip(partial[k], k) for k in range(1, p.group)]
    partial = call(
        functools.partial(add_group_kernel, p),
        [shape((p.tiles * p.own_cols, p.features), half)] * p.chips,
        partial,
    )
    partial = [partial[0]] + [flip(partial[k], k * p.group) for k in range(1, p.chips)]
    partial = call(
        functools.partial(add_chips_kernel, p),
        [shape((p.room, p.features), half)] * p.tiles,
        partial,
    )
    partial = [partial[0]] + [trade(partial[k], k) for k in range(1, p.tiles)]
    partial = call(add_tiles_kernel, shape((p.room, p.features), single), partial)
    before = lax.ppermute(partial, "chan", [(b, (b + 1) % p.chans) for b in range(p.chans)])
    after = lax.ppermute(partial, "chan", [((b + 1) % p.chans, b) for b in range(p.chans)])
    partial = [before, partial, after]

    edge = 8
    kappa = kappa.reshape(3, reach, p.lane)
    root = jnp.sqrt(
        jnp.concatenate(
            [kappa[0, :, p.along - edge : p.along], kappa[1, :, : p.along], kappa[2, :, :edge]],
            axis=1,
        ).T
    )
    return call(
        functools.partial(diffuse_kernel, p, edge),
        shape(fields.shape, single),
        partial + [root],
        flops=100 * fields.size,
    )


def solution(mesh):
    tiles, chans = mesh.shape["tile"], mesh.shape["chan"]
    by_column = tiles > 1 and chans % tiles == 0 and chans & (chans - 1) == 0 and chans > tiles
    placed = (
        P("chan", "tile", None),
        P("chan", "tile"),
        P(),
        P("tile", "chan"),
        P("tile"),
        P(None, "chan"),
        P("chan"),
        P(None, "chan"),
        P("chan"),
        P("tile", "chan"),
    )
    return jax.shard_map(
        body_by_column if by_column else body_by_owner,
        mesh=mesh,
        in_specs=placed,
        out_specs=P("chan", "tile", None),
        check_vma=False,
    )
```

```python
import functools

import jax
import jax.numpy as jnp
from jax import lax
from jax.experimental import pallas as pl
from jax.experimental.pallas import tpu as pltpu
from jax.sharding import PartitionSpec as P

VMEM_BYTES = 24 * 1024 * 1024
SLACK_FLOPS = 2 * 10**9
FORWARD_FLOPS = 10**8
NT_DIMS = (((1,), (1,)), ((), ()))


def padded_2(value, sides, width, wrap):
    for axis, dim in sides:
        devices, length = (lax.axis_size(axis), value.shape[dim])
        up = [(i, (i + 1) % devices) for i in range(devices if wrap else devices - 1)]
        down = [(j, i) for i, j in up]
        last = lax.slice_in_dim(value, length - width, length, axis=dim)
        first = lax.slice_in_dim(value, 0, width, axis=dim)
        before = lax.ppermute(last, axis, up)
        after = lax.ppermute(first, axis, down)
        value = jnp.concatenate([before, value, after], axis=dim)
    return value


def add_rims(values):
    rowwise = padded_2(values, (("chan", 0),), 1, False)
    return padded_2(rowwise, (("tile", 1),), 1, True)


def body_by_owner(
    fields,
    diffusivity,
    owners,
    observed,
    usable,
    w_hidden,
    b_hidden,
    w_radiance,
    b_radiance,
    inv_cov,
):
    tile_count = lax.axis_size("tile")
    chan_count = lax.axis_size("chan")
    tile_index = lax.axis_index("tile")
    chan_index = lax.axis_index("chan")
    slot_count = observed.shape[0]
    capacity = slot_count // tile_count
    cells_across, cells_along, features = fields.shape
    own_cols = cells_across // 4 * (cells_along // 4)
    tile_cols = chan_count * own_cols
    hidden_dev = w_hidden.shape[1]
    owner_table = owners[:, 0].reshape(tile_count, tile_cols)
    owner_hits = (
        owner_table[:, :, None] == jnp.arange(tile_count, dtype=jnp.int32)[None, None, :]
    ).astype(jnp.int32)
    before = jnp.sum((jnp.cumsum(owner_hits, axis=1) - owner_hits) * owner_hits, axis=2)
    tallies = jnp.sum(owner_hits, axis=1)
    slot_of = lax.dynamic_index_in_dim(
        owner_table * capacity + before, tile_index, 0, keepdims=False
    )
    arriving = lax.dynamic_index_in_dim(tallies, tile_index, 1, keepdims=False)
    occupied = (jnp.arange(capacity, dtype=jnp.int32)[None, :] < arriving[:, None]).reshape(
        slot_count
    )
    grouped = fields.reshape(cells_across // 4, 4, cells_along // 4, 4, features)
    columns = (
        (jnp.sum(grouped, axis=(1, 3)) * 0.0625).reshape(own_cols, features).astype(jnp.bfloat16)
    )
    placer = (slot_of[None, :] == jnp.arange(slot_count, dtype=jnp.int32)[:, None]).astype(
        jnp.bfloat16
    )
    outgoing = jnp.dot(
        placer,
        lax.all_gather(columns, "chan", axis=0, tiled=True),
        preferred_element_type=jnp.float32,
    )
    incoming = lax.all_to_all(
        outgoing.astype(jnp.bfloat16), "tile", split_axis=0, concat_axis=0, tiled=True
    )
    preact = lax.dot_general(
        w_hidden, incoming, (((0,), (1,)), ((), ())), preferred_element_type=jnp.float32
    )
    preact = preact + b_hidden[:, None]
    squash = jax.nn.sigmoid(preact)
    active = (preact * squash).astype(jnp.bfloat16)
    radiance = lax.dot_general(
        lax.all_gather(active, "chan", axis=0, tiled=True),
        w_radiance,
        (((0,), (0,)), ((), ())),
        preferred_element_type=jnp.float32,
    )
    radiance = radiance + b_radiance[None, :]
    in_use = usable.astype(jnp.float32) * occupied.astype(jnp.float32)
    departure = ((radiance - observed.astype(jnp.float32)) * in_use[:, None]).astype(jnp.bfloat16)
    cotangent = jnp.dot(
        lax.all_gather(departure, "chan", axis=1, tiled=True),
        lax.all_gather(inv_cov, "tile", axis=0, tiled=True),
        preferred_element_type=jnp.float32,
    )
    cotangent = cotangent.astype(jnp.bfloat16)
    full_sum = lax.psum(
        lax.dot_general(w_radiance, cotangent, NT_DIMS, preferred_element_type=jnp.float32),
        "chan",
    )
    grad_hidden = lax.dynamic_slice_in_dim(full_sum, chan_index * hidden_dev, hidden_dev, 0)
    slope_term = squash * (1.0 + preact * (1.0 - squash))
    grad_pre = (grad_hidden * slope_term).astype(jnp.bfloat16)
    part_grad = lax.dot_general(
        grad_pre, w_hidden, (((0,), (1,)), ((), ())), preferred_element_type=jnp.float32
    )
    returned = lax.all_to_all(part_grad, "tile", split_axis=0, concat_axis=0, tiled=True)
    column_grad = lax.psum_scatter(
        jnp.take(returned, slot_of, axis=0), "chan", scatter_dimension=0, tiled=True
    )
    spread = jnp.repeat(
        column_grad.reshape(cells_across // 4, cells_along // 4, features), 4, axis=0
    )
    adjoint = jnp.repeat(spread, 4, axis=1) * 0.0625
    kappa_root = jnp.sqrt(diffusivity)
    root_rim = add_rims(kappa_root)
    coef_north = (kappa_root * root_rim[2:, 1:-1])[:, :, None]
    coef_south = (kappa_root * root_rim[:-2, 1:-1])[:, :, None]
    coef_east = (kappa_root * root_rim[1:-1, 2:])[:, :, None]
    coef_west = (kappa_root * root_rim[1:-1, :-2])[:, :, None]
    for sweep_index in range(2):
        padded = add_rims(adjoint)
        adjoint = (
            adjoint
            + coef_north * (padded[2:, 1:-1] - adjoint)
            + coef_south * (padded[:-2, 1:-1] - adjoint)
            + coef_east * (padded[1:-1, 2:] - adjoint)
            + coef_west * (padded[1:-1, :-2] - adjoint)
        )
    return adjoint


def up_to(value, multiple):
    return -(-value // multiple) * multiple


def dot(left, right):
    return jnp.dot(left, right, preferred_element_type=jnp.float32)


def dot_nt(left, right):
    return lax.dot_general(left, right, NT_DIMS, preferred_element_type=jnp.float32)


def split_three(value):
    high = value.astype(jnp.bfloat16).astype(jnp.float32)
    middle = (value - high).astype(jnp.bfloat16).astype(jnp.float32)
    return high, middle, value - high - middle


def call(
    kernel, out_shape, args, in_hbm=(), out_hbm=False, scratch=(), flops=0, vmem=VMEM_BYTES
):
    far, near = pl.BlockSpec(memory_space=pl.ANY), pl.BlockSpec(memory_space=pltpu.VMEM)
    bytes_accessed = sum(a.size * a.dtype.itemsize for a in args)
    return pl.pallas_call(
        kernel,
        out_shape=out_shape,
        in_specs=[far if k in in_hbm else near for k in range(len(args))],
        out_specs=jax.tree.map(lambda _: far if out_hbm else near, out_shape),
        scratch_shapes=list(scratch),
        compiler_params=pltpu.CompilerParams(vmem_limit_bytes=vmem),
        cost_estimate=pl.CostEstimate(
            flops=flops, bytes_accessed=bytes_accessed, transcendentals=0
        ),
    )(*args)


class Plan:
    def __init__(self, tiles, chans, fields, owners, observed, w_hidden):
        self.tiles, self.chans = tiles, chans
        self.across, self.along, self.features = fields
        self.own_cols = self.across // 4 * (self.along // 4)
        self.rows = owners[0]
        self.tile_cols = self.rows // tiles
        self.slots = observed[0]
        self.shard = observed[1]
        self.capacity = self.slots // tiles
        self.hidden = w_hidden[1]
        self.group = chans // tiles
        self.chips = chans // self.group
        self.steps = self.chips.bit_length() - 1
        self.lane = up_to(self.along, 128)
        self.flag_at = up_to(self.hidden, 128)
        self.width = max(
            up_to(self.features, 128),
            2 * self.flag_at,
            self.flag_at + up_to(self.slots, 128),
            3 * self.lane,
        )
        self.block = up_to(self.own_cols + 2 + self.across, 16)
        self.per_row = self.own_cols + 2
        self.patch = 3 * tiles * self.own_cols
        self.room = up_to(3 * self.per_row, 16)
        self.deep = up_to(self.features, 16)
        self.strips = self.chips * tiles * self.block

    def order(self, mask):
        return mask % self.group * self.chips + mask // self.group

    def layer(self, refs, k):
        at = k % self.chips * self.deep
        return refs[k // self.chips][at : at + self.features, :]

    def mask(self, k):
        return k % self.chips * self.group + k // self.chips


def prepare_kernel(p, fields_ref, diffusivity_ref, usable_ref, bias_ref, after_ref, out_ref, flat):
    flat[...] = jnp.zeros(flat.shape, jnp.float32)
    shape = (p.own_cols, p.along)
    row = lax.broadcasted_iota(jnp.int32, shape, 0)
    member = row == lax.broadcasted_iota(jnp.int32, shape, 1) // 4
    total = jnp.dot(
        member.astype(jnp.float32),
        fields_ref[0] + fields_ref[1] + fields_ref[2] + fields_ref[3],
        precision=lax.Precision.HIGHEST,
        preferred_element_type=jnp.float32,
    )
    flat[: p.own_cols, : p.features] = total * 0.0625
    at = p.own_cols
    high, middle, low = split_three(bias_ref[...].reshape(1, p.hidden))
    flat[at : at + 1, : p.hidden] = high
    flat[at : at + 1, p.flag_at : p.flag_at + p.hidden] = middle
    flat[at + 1 : at + 2, : p.hidden] = low
    flags = usable_ref[...].reshape(1, p.slots).astype(jnp.float32)
    flat[at + 1 : at + 2, p.flag_at : p.flag_at + p.slots] = flags
    for k, part in enumerate(split_three(diffusivity_ref[...])):
        flat[at + 2 : at + 2 + p.across, k * p.lane : k * p.lane + p.along] = part
    out_ref[...] = flat[...].astype(jnp.bfloat16)


def strip_of(p, tile, chan):
    other = chan ^ lax.axis_index("chan")
    return p.order(other) * p.tiles + (tile ^ lax.axis_index("tile"))


def index_kernel(p, cell_ref, *target_refs):
    t, c = lax.axis_index("tile"), lax.axis_index("chan")
    row = lax.broadcasted_iota(jnp.int32, cell_ref.shape, 0)
    reach = p.across + 4
    tile = (t + row // reach - 1 + p.tiles) % p.tiles
    cell = c * p.across - 2 + row % reach
    inside = (cell >= 0) & (cell < p.chans * p.across)
    cell = jnp.where(inside, cell, 0)
    wanted = strip_of(p, tile, cell // p.across) * p.block + p.own_cols + 2 + cell % p.across
    cell_ref[...] = jnp.where(inside, wanted, -1)

    target = lax.broadcasted_iota(jnp.int32, target_refs[0].shape, 0)
    chip, inner = target // p.patch, target % p.patch
    beside, inner = inner // (p.patch // 3) - 1, inner % (p.patch // 3)
    tile, along = inner // p.own_cols, inner % p.own_cols
    for k, target_ref in enumerate(target_refs):
        row = (chip ^ (c // p.group)) * p.group + (c % p.group ^ k) + beside
        wanted = tile * p.tile_cols + row * p.own_cols + along
        target_ref[...] = jnp.where((row >= 0) & (row < p.chans), wanted, -1)


def place_kernel(p, owners_ref, place_ref, source_ref):
    t = lax.axis_index("tile")
    across = owners_ref[...]
    shape = (p.rows, p.rows)
    row = lax.broadcasted_iota(jnp.int32, shape, 0)
    other = lax.broadcasted_iota(jnp.int32, shape, 1)
    owner = jnp.sum(jnp.where(row == other, across, 0), axis=1, keepdims=True)
    first = lax.broadcasted_iota(jnp.int32, owner.shape, 0)
    begin = first // p.tile_cols * p.tile_cols
    same = (owner == across) & (other >= begin) & (other < row)
    rank = jnp.sum(jnp.where(same, 1, 0), axis=1, keepdims=True)
    tile = first // p.tile_cols
    place_ref[...] = (owner ^ t) * p.slots + tile * p.capacity + rank
    source_ref[...] = (
        strip_of(p, tile, first % p.tile_cols // p.own_cols) * p.block + first % p.own_cols
    )


def join_kernel(count, *refs):
    ins, out_ref, sems = refs[:count], refs[-2], refs[-1]
    size = out_ref.shape[0] // count
    copies = [
        pltpu.make_async_copy(
            ref, out_ref.at[k] if ref.ndim < out_ref.ndim else out_ref.at[pl.ds(k * size, size)],
            sems.at[k],
        )
        for k, ref in enumerate(ins)
    ]
    for copy in copies:
        copy.start()
    for copy in copies:
        copy.wait()


def stack_kernel(p, *refs):
    for k, ref in enumerate(refs[: p.chips]):
        refs[-1][k * p.deep : k * p.deep + p.features, :] = ref[...]
        refs[-1][k * p.deep + p.features : (k + 1) * p.deep, :] = jnp.zeros(
            (p.deep - p.features, p.hidden), jnp.bfloat16
        )


def one_hot(wanted, first, count):
    source = lax.broadcasted_iota(jnp.int32, (wanted.shape[0], count), 1)
    return (source + first == wanted).astype(jnp.bfloat16)


def forward_kernel(p, *refs):
    refs = list(refs)
    take = lambda n: [refs.pop(0) for _ in range(n)]
    place_ref, source_ref, cell_ref, bias_ref, w_radiance_ref = take(5)
    strip_refs, weight_refs = take(p.group), take(p.group)
    radiance_ref, in_use_ref, preact_ref, kappa_ref, active = refs
    c = lax.axis_index("chan")
    gathered = [ref[...] for ref in strip_refs]
    columns = sum(
        dot(one_hot(source_ref[...], k * p.strips, p.strips), strips)
        for k, strips in enumerate(gathered)
    )
    columns = columns.astype(jnp.bfloat16)[:, : p.features]
    for k in range(p.chans):
        member, chip = k // p.chips, k % p.chips
        at = chip * p.tiles * p.block + p.own_cols
        low = strip_refs[member][at : at + 2, :].astype(jnp.float32)
        bias = (
            low[:1, : p.hidden]
            + low[:1, p.flag_at : p.flag_at + p.hidden]
            + low[1:, : p.hidden]
        )
        preact = dot(columns, p.layer(weight_refs, k)) + bias
        preact_ref[k] = preact
        at = pl.multiple_of((c ^ p.mask(k)) * p.hidden, p.hidden)
        active[:, pl.ds(at, p.hidden)] = (preact * jax.nn.sigmoid(preact)).astype(jnp.bfloat16)
    in_use = jnp.zeros((p.rows, 1), jnp.float32)
    for k in range(p.tiles):
        slot = lax.broadcasted_iota(jnp.int32, (p.rows, p.slots), 1) + k * p.slots
        low = k * p.block + p.own_cols + 1
        flags = strip_refs[0][low : low + 1, p.flag_at : p.flag_at + p.slots]
        flags = jnp.where(place_ref[...] == slot, flags.astype(jnp.float32), 0.0)
        in_use = in_use + jnp.sum(flags, axis=1, keepdims=True)
    in_use_ref[...] = in_use
    radiance_ref[...] = dot(active[...], w_radiance_ref[...]) + bias_ref[...].reshape(1, p.shard)
    parts = sum(
        dot(one_hot(cell_ref[...], k * p.strips, p.strips), strips)
        for k, strips in enumerate(gathered)
    )
    kappa_ref[...] = sum(parts[:, k * p.lane : (k + 1) * p.lane] for k in range(3))


def depart_kernel(p, radiance_ref, in_use_ref, place_ref, *refs):
    seen_refs, part_refs = refs[: -p.steps], refs[-p.steps :]
    part, count = p.rows // p.steps, seen_refs[0].shape[0]
    for j, part_ref in enumerate(part_refs):
        at = slice(j * part, (j + 1) * part)
        observed = sum(
            dot(one_hot(place_ref[at, :], k * count, count), ref[...])
            for k, ref in enumerate(seen_refs)
        )
        departure = (radiance_ref[at, :] - observed) * in_use_ref[at, :]
        part_ref[...] = departure.astype(jnp.bfloat16)


def slope_kernel(preact_ref, slope_ref):
    for k in range(preact_ref.shape[0]):
        preact = preact_ref[k]
        squash = jax.nn.sigmoid(preact)
        slope_ref[k] = (squash * (1.0 + preact * (1.0 - squash))).T


def choose_kernel(p, choices, *refs):
    refs, out_ref, sems = refs[:-3], refs[-2], refs[-1]
    size = refs[0].shape[0]
    role = (lax.axis_index("chan") // p.group) ^ lax.axis_index("tile")
    for place in range(p.chips):

        @pl.when(role == place)
        def _():
            copies = [
                pltpu.make_async_copy(
                    refs[choices[place, j]], out_ref.at[pl.ds(j * size, size)], sems.at[j]
                )
                for j in range(p.steps)
            ]
            for copy in copies:
                copy.start()
            for copy in copies:
                copy.wait()


def near_kernel(p, depart_ref, inv_cov_ref, out_ref):
    at = pl.multiple_of(lax.axis_index("chan") % p.group * p.shard, p.shard)
    out_ref[...] = dot(depart_ref[...], inv_cov_ref[pl.ds(at, p.shard), :])


def backward_kernel(p, *refs):
    refs = list(refs)
    take = lambda n: [refs.pop(0) for _ in range(n)]
    w_radiance_ref, inv_cov_ref, slope_ref, near_ref = take(4)
    depart_refs, weight_refs, target_refs = take(p.group - 1), take(p.group), take(p.group)
    out_refs = refs
    c = lax.axis_index("chan")
    cotangent = near_ref[...]
    for k, ref in enumerate(depart_refs):
        at = pl.multiple_of((c % p.group ^ (k + 1)) * p.shard, p.shard)
        cotangent = cotangent + dot(ref[...], inv_cov_ref[pl.ds(at, p.shard), :])
    cotangent = cotangent.T.astype(jnp.bfloat16)
    total = jnp.zeros((p.features, p.rows), jnp.float32)
    for k in range(p.chans):
        at = pl.multiple_of((c ^ p.mask(k)) * p.hidden, p.hidden)
        grad_hidden = dot(w_radiance_ref[pl.ds(at, p.hidden), :], cotangent)
        grad_pre = (grad_hidden * slope_ref[k]).astype(jnp.bfloat16)
        total = total + dot(p.layer(weight_refs, k), grad_pre)
    total = total.astype(jnp.bfloat16)
    for target_ref, out_ref in zip(target_refs, out_refs):
        out_ref[...] = dot_nt(one_hot(target_ref[...], 0, p.rows), total).astype(jnp.bfloat16)


def add(refs, at=slice(None)):
    total = refs[0][at, :].astype(jnp.float32)
    for ref in refs[1:]:
        total = total + ref[at, :].astype(jnp.float32)
    return total


def add_group_kernel(p, *refs):
    ins, outs = refs[: p.group], refs[p.group :]
    for k, out_ref in enumerate(outs):
        out_ref[...] = add(ins, slice(k * p.patch, (k + 1) * p.patch)).astype(jnp.bfloat16)


def add_chips_kernel(p, *refs):
    ins, outs = refs[: p.chips], refs[p.chips :]
    total = add(ins).astype(jnp.bfloat16)
    target = lax.broadcasted_iota(jnp.int32, (p.room, 1), 0)
    row, along = target // p.per_row, target % p.per_row - 1
    count = p.tiles * p.own_cols
    for k, out_ref in enumerate(outs):
        cell = ((lax.axis_index("tile") ^ k) * p.own_cols + along + count) % count
        wanted = jnp.where(row < 3, row * count + cell, -1)
        out_ref[...] = dot(one_hot(wanted, 0, p.patch), total).astype(jnp.bfloat16)


def diffuse_kernel(p, edge, *refs):
    ins, root_ref, out_ref = refs[: p.tiles], refs[-2], refs[-1]
    total = add(ins) * 0.0625
    length = p.along + 2 * edge
    shape = (length, p.room)
    cell = lax.broadcasted_iota(jnp.int32, shape, 0)
    source = lax.broadcasted_iota(jnp.int32, shape, 1)
    column = (cell - edge + 4) // 4
    spread = []
    for k in range(3):
        pick = (source == column + k * p.per_row) & (column >= 0) & (column < p.per_row)
        spread.append(
            jnp.dot(
                pick.astype(jnp.float32),
                total,
                precision=lax.Precision.HIGHEST,
                preferred_element_type=jnp.float32,
            )
        )
    root = root_ref[...]
    state = [spread[(row + 2) // 4] for row in range(p.across + 4)]
    east_of = functools.partial(pltpu.roll, shift=length - 1, axis=0)
    west_of = functools.partial(pltpu.roll, shift=1, axis=0)
    north = root[:, :-1] * root[:, 1:]
    east, west = root * east_of(root), root * west_of(root)
    for sweep in range(2):
        fresh = list(state)
        for row in range(1 + sweep, p.across + 3 - sweep):
            here = state[row]
            fresh[row] = (
                here
                + north[:, row : row + 1] * (state[row + 1] - here)
                + north[:, row - 1 : row] * (state[row - 1] - here)
                + east[:, row : row + 1] * (east_of(here) - here)
                + west[:, row : row + 1] * (west_of(here) - here)
            )
        state = fresh
    for row in range(p.across):
        out_ref[row] = state[row + 2][edge : edge + p.along, : p.features]


def body_by_column(
    fields,
    diffusivity,
    owners,
    observed,
    usable,
    w_hidden,
    b_hidden,
    w_radiance,
    b_radiance,
    inv_cov,
):
    p = Plan(
        lax.axis_size("tile"),
        lax.axis_size("chan"),
        fields.shape,
        owners.shape,
        observed.shape,
        w_hidden.shape,
    )
    half, single = jnp.bfloat16, jnp.float32
    shape = jax.ShapeDtypeStruct
    both = ("tile", "chan")
    everyone = [(a, b) for a in range(p.tiles) for b in range(p.chans)]

    def flip(value, mask):
        return lax.ppermute(value, "chan", [(b, b ^ mask) for b in range(p.chans)])

    def trade(value, mask):
        return lax.ppermute(value, "tile", [(a, a ^ mask) for a in range(p.tiles)])

    def send(value, wanted):
        pairs = dict(wanted)
        pairs.update({target: source for source, target in wanted.items()})
        for a, b in everyone:
            if (a, b) not in pairs:
                pairs[a, b] = (a, b ^ 1)
        number = lambda place: place[0] * p.chans + place[1]
        return lax.ppermute(
            value, both, sorted((number(a), number(b)) for a, b in pairs.items())
        )

    def join(values, kernel_shape, after=()):
        return call(
            functools.partial(join_kernel, len(values)),
            shape(kernel_shape, half),
            [*values, *after],
            in_hbm=range(len(values) + len(after)),
            out_hbm=True,
            scratch=[pltpu.SemaphoreType.DMA((len(values),))],
            flops=0,
        )

    def grow(value, over, after=()):
        return join([value, over(value)], (2 * value.shape[0],) + value.shape[1:], after)

    reach = p.across + 4
    cell, *targets = call(
        functools.partial(index_kernel, p),
        [shape((3 * reach, 1), jnp.int32)] + [shape((p.chips * p.patch, 1), jnp.int32)] * p.group,
        [],
        flops=SLACK_FLOPS,
    )

    strips = call(
        functools.partial(prepare_kernel, p),
        shape((p.block, p.width), half),
        [fields, diffusivity, usable, b_hidden, cell],
        in_hbm=[4],
        scratch=[pltpu.VMEM((p.block, p.width), single)],
    )
    seen, stages, before = observed, [], ()
    bit = 1
    while bit < p.tiles:
        strips = grow(strips, lambda value: trade(value, bit), before)
        if 2 * bit < p.tiles:
            seen = grow(seen, lambda value: trade(value, bit), [strips])
            before = [seen]
        stages.append(strips)
        bit *= 2
    strips = join(
        [strips] + [flip(strips, k * p.group) for k in range(1, p.chips)], (p.strips, p.width)
    )
    strips = [strips] + [flip(strips, k) for k in range(1, p.group)]

    near = [w_hidden] + [flip(w_hidden, chip * p.group) for chip in range(1, p.chips)]
    near = call(
        functools.partial(stack_kernel, p),
        shape((p.chips * p.deep, p.hidden), half),
        near + [stages[-1]],
        in_hbm=[len(near)],
    )
    weights = [near] + [flip(near, k) for k in range(1, p.group)]

    far_half = p.tiles // 2
    seen = [
        seen,
        send(seen, {(b // p.group ^ far_half, b): (b // p.group, b) for b in range(p.chans)}),
    ]

    place, source = call(
        functools.partial(place_kernel, p),
        [shape((p.rows, 1), jnp.int32)] * 2,
        [owners.reshape(1, p.rows)],
        flops=SLACK_FLOPS,
    )
    radiance, in_use, preact, kappa = call(
        functools.partial(forward_kernel, p),
        [
            shape((p.rows, p.shard), single),
            shape((p.rows, 1), single),
            shape((p.chans, p.rows, p.hidden), single),
            shape((3 * reach, p.lane), single),
        ],
        [place, source, cell, b_radiance, w_radiance] + strips + weights,
        scratch=[pltpu.VMEM((p.rows, p.hidden * p.chans), half)],
        flops=FORWARD_FLOPS,
    )
    parts = call(
        functools.partial(depart_kernel, p),
        [shape((p.rows // p.steps, p.shard), half)] * p.steps,
        [radiance, in_use, place] + seen,
    )

    slope = call(
        slope_kernel,
        shape((p.chans, p.hidden, p.rows), single),
        [preact],
        flops=40 * preact.size,
    )

    pool, held, choices = list(parts), {}, {}
    for j in range(p.steps):
        held[0, j] = choices[0, j] = j
    for step in range(p.steps):
        for since in range(-1, step):
            for j in range(p.steps):
                order = [1 << (j + k) % p.steps for k in range(p.steps)]
                roles = [0] if since < 0 else [
                    order[since] + rest
                    for rest in range(p.chips)
                    if rest & ~sum(order[:since]) == 0
                ]
                wanted = {
                    (a, b): (a, b ^ order[step] * p.group)
                    for a, b in everyone
                    if (b // p.group ^ a) in roles
                }
                source = pool[choices[roles[0], j]]
                for role in roles:
                    choices[role + order[step], j] = len(pool)
                pool.append(send(source, wanted))
    chosen = call(
        functools.partial(choose_kernel, p, choices),
        shape((p.rows, p.shard), half),
        pool + [slope],
        in_hbm=range(len(pool) + 1),
        out_hbm=True,
        scratch=[pltpu.SemaphoreType.DMA((p.steps,))],
    )
    depart = [flip(chosen, k) for k in range(1, p.group)]

    partial = call(
        functools.partial(near_kernel, p),
        shape((p.rows, p.shard), single),
        [chosen, inv_cov],
        flops=2 * p.rows * p.shard * p.shard,
    )
    partial = call(
        functools.partial(backward_kernel, p),
        [shape((p.chips * p.patch, p.features), half)] * p.group,
        [w_radiance, inv_cov, slope, partial] + depart + weights + targets,
        flops=2 * p.rows * (p.hidden * p.chans * (p.features + p.shard) + inv_cov.size),
    )
    partial = [partial[0]] + [flip(partial[k], k) for k in range(1, p.group)]
    partial = call(
        functools.partial(add_group_kernel, p),
        [shape((p.patch, p.features), half)] * p.chips,
        partial,
    )
    partial = [partial[0]] + [flip(partial[k], k * p.group) for k in range(1, p.chips)]
    partial = call(
        functools.partial(add_chips_kernel, p),
        [shape((p.room, p.features), half)] * p.tiles,
        partial,
    )
    partial = [partial[0]] + [trade(partial[k], k) for k in range(1, p.tiles)]
    edge = 8
    kappa = kappa.reshape(3, reach, p.lane)
    root = jnp.sqrt(
        jnp.concatenate(
            [kappa[0, :, p.along - edge : p.along], kappa[1, :, : p.along], kappa[2, :, :edge]],
            axis=1,
        ).T
    )
    return call(
        functools.partial(diffuse_kernel, p, edge),
        shape(fields.shape, single),
        partial + [root],
        flops=100 * fields.size,
    )


def solution(mesh):
    tiles, chans = mesh.shape["tile"], mesh.shape["chan"]
    by_column = tiles > 1 and chans % tiles == 0 and chans & (chans - 1) == 0 and chans > tiles
    placed = (
        P("chan", "tile", None),
        P("chan", "tile"),
        P(),
        P("tile", "chan"),
        P("tile"),
        P(None, "chan"),
        P("chan"),
        P(None, "chan"),
        P("chan"),
        P("tile", "chan"),
    )
    return jax.shard_map(
        body_by_column if by_column else body_by_owner,
        mesh=mesh,
        in_specs=placed,
        out_specs=P("chan", "tile", None),
        check_vma=False,
    )
```

```python
import functools

import jax
import jax.numpy as jnp
from jax import lax
from jax.experimental import pallas as pl
from jax.experimental.pallas import tpu as pltpu
from jax.sharding import PartitionSpec as P

VMEM_BYTES = 24 * 1024 * 1024
SLACK_FLOPS = 2 * 10**9
FORWARD_FLOPS = 10**8
NT_DIMS = (((1,), (1,)), ((), ()))


def padded_2(value, sides, width, wrap):
    for axis, dim in sides:
        devices, length = (lax.axis_size(axis), value.shape[dim])
        up = [(i, (i + 1) % devices) for i in range(devices if wrap else devices - 1)]
        down = [(j, i) for i, j in up]
        last = lax.slice_in_dim(value, length - width, length, axis=dim)
        first = lax.slice_in_dim(value, 0, width, axis=dim)
        before = lax.ppermute(last, axis, up)
        after = lax.ppermute(first, axis, down)
        value = jnp.concatenate([before, value, after], axis=dim)
    return value


def add_rims(values):
    rowwise = padded_2(values, (("chan", 0),), 1, False)
    return padded_2(rowwise, (("tile", 1),), 1, True)


def body_by_owner(
    fields,
    diffusivity,
    owners,
    observed,
    usable,
    w_hidden,
    b_hidden,
    w_radiance,
    b_radiance,
    inv_cov,
):
    tile_count = lax.axis_size("tile")
    chan_count = lax.axis_size("chan")
    tile_index = lax.axis_index("tile")
    chan_index = lax.axis_index("chan")
    slot_count = observed.shape[0]
    capacity = slot_count // tile_count
    cells_across, cells_along, features = fields.shape
    own_cols = cells_across // 4 * (cells_along // 4)
    tile_cols = chan_count * own_cols
    hidden_dev = w_hidden.shape[1]
    owner_table = owners[:, 0].reshape(tile_count, tile_cols)
    owner_hits = (
        owner_table[:, :, None] == jnp.arange(tile_count, dtype=jnp.int32)[None, None, :]
    ).astype(jnp.int32)
    before = jnp.sum((jnp.cumsum(owner_hits, axis=1) - owner_hits) * owner_hits, axis=2)
    tallies = jnp.sum(owner_hits, axis=1)
    slot_of = lax.dynamic_index_in_dim(
        owner_table * capacity + before, tile_index, 0, keepdims=False
    )
    arriving = lax.dynamic_index_in_dim(tallies, tile_index, 1, keepdims=False)
    occupied = (jnp.arange(capacity, dtype=jnp.int32)[None, :] < arriving[:, None]).reshape(
        slot_count
    )
    grouped = fields.reshape(cells_across // 4, 4, cells_along // 4, 4, features)
    columns = (
        (jnp.sum(grouped, axis=(1, 3)) * 0.0625).reshape(own_cols, features).astype(jnp.bfloat16)
    )
    placer = (slot_of[None, :] == jnp.arange(slot_count, dtype=jnp.int32)[:, None]).astype(
        jnp.bfloat16
    )
    outgoing = jnp.dot(
        placer,
        lax.all_gather(columns, "chan", axis=0, tiled=True),
        preferred_element_type=jnp.float32,
    )
    incoming = lax.all_to_all(
        outgoing.astype(jnp.bfloat16), "tile", split_axis=0, concat_axis=0, tiled=True
    )
    preact = lax.dot_general(
        w_hidden, incoming, (((0,), (1,)), ((), ())), preferred_element_type=jnp.float32
    )
    preact = preact + b_hidden[:, None]
    squash = jax.nn.sigmoid(preact)
    active = (preact * squash).astype(jnp.bfloat16)
    radiance = lax.dot_general(
        lax.all_gather(active, "chan", axis=0, tiled=True),
        w_radiance,
        (((0,), (0,)), ((), ())),
        preferred_element_type=jnp.float32,
    )
    radiance = radiance + b_radiance[None, :]
    in_use = usable.astype(jnp.float32) * occupied.astype(jnp.float32)
    departure = ((radiance - observed.astype(jnp.float32)) * in_use[:, None]).astype(jnp.bfloat16)
    cotangent = jnp.dot(
        lax.all_gather(departure, "chan", axis=1, tiled=True),
        lax.all_gather(inv_cov, "tile", axis=0, tiled=True),
        preferred_element_type=jnp.float32,
    )
    cotangent = cotangent.astype(jnp.bfloat16)
    full_sum = lax.psum(
        lax.dot_general(w_radiance, cotangent, NT_DIMS, preferred_element_type=jnp.float32),
        "chan",
    )
    grad_hidden = lax.dynamic_slice_in_dim(full_sum, chan_index * hidden_dev, hidden_dev, 0)
    slope_term = squash * (1.0 + preact * (1.0 - squash))
    grad_pre = (grad_hidden * slope_term).astype(jnp.bfloat16)
    part_grad = lax.dot_general(
        grad_pre, w_hidden, (((0,), (1,)), ((), ())), preferred_element_type=jnp.float32
    )
    returned = lax.all_to_all(part_grad, "tile", split_axis=0, concat_axis=0, tiled=True)
    column_grad = lax.psum_scatter(
        jnp.take(returned, slot_of, axis=0), "chan", scatter_dimension=0, tiled=True
    )
    spread = jnp.repeat(
        column_grad.reshape(cells_across // 4, cells_along // 4, features), 4, axis=0
    )
    adjoint = jnp.repeat(spread, 4, axis=1) * 0.0625
    kappa_root = jnp.sqrt(diffusivity)
    root_rim = add_rims(kappa_root)
    coef_north = (kappa_root * root_rim[2:, 1:-1])[:, :, None]
    coef_south = (kappa_root * root_rim[:-2, 1:-1])[:, :, None]
    coef_east = (kappa_root * root_rim[1:-1, 2:])[:, :, None]
    coef_west = (kappa_root * root_rim[1:-1, :-2])[:, :, None]
    for sweep_index in range(2):
        padded = add_rims(adjoint)
        adjoint = (
            adjoint
            + coef_north * (padded[2:, 1:-1] - adjoint)
            + coef_south * (padded[:-2, 1:-1] - adjoint)
            + coef_east * (padded[1:-1, 2:] - adjoint)
            + coef_west * (padded[1:-1, :-2] - adjoint)
        )
    return adjoint


def up_to(value, multiple):
    return -(-value // multiple) * multiple


def dot(left, right):
    return jnp.dot(left, right, preferred_element_type=jnp.float32)


def dot_nt(left, right):
    return lax.dot_general(left, right, NT_DIMS, preferred_element_type=jnp.float32)


def split_three(value):
    high = value.astype(jnp.bfloat16).astype(jnp.float32)
    middle = (value - high).astype(jnp.bfloat16).astype(jnp.float32)
    return high, middle, value - high - middle


def call(
    kernel, out_shape, args, in_hbm=(), out_hbm=False, scratch=(), flops=0, vmem=VMEM_BYTES
):
    far, near = pl.BlockSpec(memory_space=pl.ANY), pl.BlockSpec(memory_space=pltpu.VMEM)
    bytes_accessed = sum(a.size * a.dtype.itemsize for a in args)
    return pl.pallas_call(
        kernel,
        out_shape=out_shape,
        in_specs=[far if k in in_hbm else near for k in range(len(args))],
        out_specs=jax.tree.map(lambda _: far if out_hbm else near, out_shape),
        scratch_shapes=list(scratch),
        compiler_params=pltpu.CompilerParams(vmem_limit_bytes=vmem),
        cost_estimate=pl.CostEstimate(
            flops=flops, bytes_accessed=bytes_accessed, transcendentals=0
        ),
    )(*args)


class Plan:
    def __init__(self, tiles, chans, fields, owners, observed, w_hidden):
        self.tiles, self.chans = tiles, chans
        self.across, self.along, self.features = fields
        self.own_cols = self.across // 4 * (self.along // 4)
        self.rows = owners[0]
        self.tile_cols = self.rows // tiles
        self.slots = observed[0]
        self.shard = observed[1]
        self.capacity = self.slots // tiles
        self.hidden = w_hidden[1]
        self.group = chans // tiles
        self.chips = chans // self.group
        self.steps = self.chips.bit_length() - 1
        self.lane = up_to(self.along, 128)
        self.flag_at = up_to(self.hidden, 128)
        self.width = max(
            up_to(self.features, 128),
            2 * self.flag_at,
            self.flag_at + up_to(self.slots, 128),
            3 * self.lane,
        )
        self.block = up_to(self.own_cols + 2 + self.across, 16)
        self.per_row = self.own_cols + 2
        self.patch = 3 * tiles * self.own_cols
        self.room = up_to(3 * self.per_row, 16)
        self.deep = up_to(self.features, 16)
        self.strips = self.chips * tiles * self.block

    def order(self, mask):
        return mask % self.group * self.chips + mask // self.group

    def layer(self, refs, k):
        at = k % self.chips * self.deep
        return refs[k // self.chips][at : at + self.features, :]

    def mask(self, k):
        return k % self.chips * self.group + k // self.chips


def prepare_kernel(p, fields_ref, diffusivity_ref, usable_ref, bias_ref, after_ref, out_ref, flat):
    flat[...] = jnp.zeros(flat.shape, jnp.float32)
    shape = (p.own_cols, p.along)
    row = lax.broadcasted_iota(jnp.int32, shape, 0)
    member = row == lax.broadcasted_iota(jnp.int32, shape, 1) // 4
    total = jnp.dot(
        member.astype(jnp.float32),
        fields_ref[0] + fields_ref[1] + fields_ref[2] + fields_ref[3],
        precision=lax.Precision.HIGHEST,
        preferred_element_type=jnp.float32,
    )
    flat[: p.own_cols, : p.features] = total * 0.0625
    at = p.own_cols
    high, middle, low = split_three(bias_ref[...].reshape(1, p.hidden))
    flat[at : at + 1, : p.hidden] = high
    flat[at : at + 1, p.flag_at : p.flag_at + p.hidden] = middle
    flat[at + 1 : at + 2, : p.hidden] = low
    flags = usable_ref[...].reshape(1, p.slots).astype(jnp.float32)
    flat[at + 1 : at + 2, p.flag_at : p.flag_at + p.slots] = flags
    for k, part in enumerate(split_three(diffusivity_ref[...])):
        flat[at + 2 : at + 2 + p.across, k * p.lane : k * p.lane + p.along] = part
    out_ref[...] = flat[...].astype(jnp.bfloat16)


def strip_of(p, tile, chan):
    other = chan ^ lax.axis_index("chan")
    return p.order(other) * p.tiles + (tile ^ lax.axis_index("tile"))


def index_kernel(p, cell_ref, *target_refs):
    t, c = lax.axis_index("tile"), lax.axis_index("chan")
    row = lax.broadcasted_iota(jnp.int32, cell_ref.shape, 0)
    reach = p.across + 4
    tile = (t + row // reach - 1 + p.tiles) % p.tiles
    cell = c * p.across - 2 + row % reach
    inside = (cell >= 0) & (cell < p.chans * p.across)
    cell = jnp.where(inside, cell, 0)
    wanted = strip_of(p, tile, cell // p.across) * p.block + p.own_cols + 2 + cell % p.across
    cell_ref[...] = jnp.where(inside, wanted, -1)

    target = lax.broadcasted_iota(jnp.int32, target_refs[0].shape, 0)
    chip, inner = target // p.patch, target % p.patch
    beside, inner = inner // (p.patch // 3) - 1, inner % (p.patch // 3)
    tile, along = inner // p.own_cols, inner % p.own_cols
    for k, target_ref in enumerate(target_refs):
        row = (chip ^ (c // p.group)) * p.group + (c % p.group ^ k) + beside
        wanted = tile * p.tile_cols + row * p.own_cols + along
        target_ref[...] = jnp.where((row >= 0) & (row < p.chans), wanted, -1)


def place_kernel(p, owners_ref, place_ref, source_ref):
    t = lax.axis_index("tile")
    across = owners_ref[...]
    shape = (p.rows, p.rows)
    row = lax.broadcasted_iota(jnp.int32, shape, 0)
    other = lax.broadcasted_iota(jnp.int32, shape, 1)
    owner = jnp.sum(jnp.where(row == other, across, 0), axis=1, keepdims=True)
    first = lax.broadcasted_iota(jnp.int32, owner.shape, 0)
    begin = first // p.tile_cols * p.tile_cols
    same = (owner == across) & (other >= begin) & (other < row)
    rank = jnp.sum(jnp.where(same, 1, 0), axis=1, keepdims=True)
    tile = first // p.tile_cols
    place_ref[...] = (owner ^ t) * p.slots + tile * p.capacity + rank
    source_ref[...] = (
        strip_of(p, tile, first % p.tile_cols // p.own_cols) * p.block + first % p.own_cols
    )


def join_kernel(count, *refs):
    ins, out_ref, sems = refs[:count], refs[-2], refs[-1]
    size = out_ref.shape[0] // count
    copies = [
        pltpu.make_async_copy(
            ref, out_ref.at[k] if ref.ndim < out_ref.ndim else out_ref.at[pl.ds(k * size, size)],
            sems.at[k],
        )
        for k, ref in enumerate(ins)
    ]
    for copy in copies:
        copy.start()
    for copy in copies:
        copy.wait()


def stack_kernel(p, *refs):
    for k, ref in enumerate(refs[: p.chips]):
        refs[-1][k * p.deep : k * p.deep + p.features, :] = ref[...]
        refs[-1][k * p.deep + p.features : (k + 1) * p.deep, :] = jnp.zeros(
            (p.deep - p.features, p.hidden), jnp.bfloat16
        )


def one_hot(wanted, first, count):
    source = lax.broadcasted_iota(jnp.int32, (wanted.shape[0], count), 1)
    return (source + first == wanted).astype(jnp.bfloat16)


def forward_kernel(p, *refs):
    refs = list(refs)
    take = lambda n: [refs.pop(0) for _ in range(n)]
    place_ref, source_ref, cell_ref, bias_ref, w_radiance_ref = take(5)
    strip_refs, weight_refs = take(p.group), take(p.group)
    radiance_ref, in_use_ref, preact_ref, kappa_ref, active = refs
    c = lax.axis_index("chan")
    gathered = [ref[...] for ref in strip_refs]
    columns = sum(
        dot(one_hot(source_ref[...], k * p.strips, p.strips), strips)
        for k, strips in enumerate(gathered)
    )
    columns = columns.astype(jnp.bfloat16)[:, : p.features]
    for k in range(p.chans):
        member, chip = k // p.chips, k % p.chips
        at = chip * p.tiles * p.block + p.own_cols
        low = strip_refs[member][at : at + 2, :].astype(jnp.float32)
        bias = (
            low[:1, : p.hidden]
            + low[:1, p.flag_at : p.flag_at + p.hidden]
            + low[1:, : p.hidden]
        )
        preact = dot(columns, p.layer(weight_refs, k)) + bias
        preact_ref[k] = preact
        at = pl.multiple_of((c ^ p.mask(k)) * p.hidden, p.hidden)
        active[:, pl.ds(at, p.hidden)] = (preact * jax.nn.sigmoid(preact)).astype(jnp.bfloat16)
    in_use = jnp.zeros((p.rows, 1), jnp.float32)
    for k in range(p.tiles):
        slot = lax.broadcasted_iota(jnp.int32, (p.rows, p.slots), 1) + k * p.slots
        low = k * p.block + p.own_cols + 1
        flags = strip_refs[0][low : low + 1, p.flag_at : p.flag_at + p.slots]
        flags = jnp.where(place_ref[...] == slot, flags.astype(jnp.float32), 0.0)
        in_use = in_use + jnp.sum(flags, axis=1, keepdims=True)
    in_use_ref[...] = in_use
    radiance_ref[...] = dot(active[...], w_radiance_ref[...]) + bias_ref[...].reshape(1, p.shard)
    parts = sum(
        dot(one_hot(cell_ref[...], k * p.strips, p.strips), strips)
        for k, strips in enumerate(gathered)
    )
    kappa_ref[...] = sum(parts[:, k * p.lane : (k + 1) * p.lane] for k in range(3))


def depart_kernel(p, radiance_ref, in_use_ref, place_ref, *refs):
    seen_refs, part_refs = refs[: -p.steps], refs[-p.steps :]
    part, count = p.rows // p.steps, seen_refs[0].shape[0]
    for j, part_ref in enumerate(part_refs):
        at = slice(j * part, (j + 1) * part)
        observed = sum(
            dot(one_hot(place_ref[at, :], k * count, count), ref[...])
            for k, ref in enumerate(seen_refs)
        )
        departure = (radiance_ref[at, :] - observed) * in_use_ref[at, :]
        part_ref[...] = departure.astype(jnp.bfloat16)


def slope_kernel(preact_ref, slope_ref):
    for k in range(preact_ref.shape[0]):
        preact = preact_ref[k]
        squash = jax.nn.sigmoid(preact)
        slope_ref[k] = (squash * (1.0 + preact * (1.0 - squash))).T


def choose_kernel(p, choices, *refs):
    refs, out_ref, sems = refs[:-3], refs[-2], refs[-1]
    size = refs[0].shape[0]
    role = (lax.axis_index("chan") // p.group) ^ lax.axis_index("tile")
    for place in range(p.chips):

        @pl.when(role == place)
        def _():
            copies = [
                pltpu.make_async_copy(
                    refs[choices[place, j]], out_ref.at[pl.ds(j * size, size)], sems.at[j]
                )
                for j in range(p.steps)
            ]
            for copy in copies:
                copy.start()
            for copy in copies:
                copy.wait()


def near_kernel(p, depart_ref, inv_cov_ref, out_ref):
    at = pl.multiple_of(lax.axis_index("chan") % p.group * p.shard, p.shard)
    out_ref[...] = dot(depart_ref[...], inv_cov_ref[pl.ds(at, p.shard), :])


def backward_kernel(p, *refs):
    refs = list(refs)
    take = lambda n: [refs.pop(0) for _ in range(n)]
    w_radiance_ref, inv_cov_ref, slope_ref, near_ref = take(4)
    depart_refs, weight_refs, target_refs = take(p.group - 1), take(p.group), take(p.group)
    out_refs = refs
    c = lax.axis_index("chan")
    cotangent = near_ref[...]
    for k, ref in enumerate(depart_refs):
        at = pl.multiple_of((c % p.group ^ (k + 1)) * p.shard, p.shard)
        cotangent = cotangent + dot(ref[...], inv_cov_ref[pl.ds(at, p.shard), :])
    cotangent = cotangent.T.astype(jnp.bfloat16)
    total = jnp.zeros((p.features, p.rows), jnp.float32)
    for k in range(p.chans):
        at = pl.multiple_of((c ^ p.mask(k)) * p.hidden, p.hidden)
        grad_hidden = dot(w_radiance_ref[pl.ds(at, p.hidden), :], cotangent)
        grad_pre = (grad_hidden * slope_ref[k]).astype(jnp.bfloat16)
        total = total + dot(p.layer(weight_refs, k), grad_pre)
    total = total.astype(jnp.bfloat16)
    for target_ref, out_ref in zip(target_refs, out_refs):
        out_ref[...] = dot_nt(one_hot(target_ref[...], 0, p.rows), total).astype(jnp.bfloat16)


def add(refs, at=slice(None)):
    total = refs[0][at, :].astype(jnp.float32)
    for ref in refs[1:]:
        total = total + ref[at, :].astype(jnp.float32)
    return total


def add_group_kernel(p, *refs):
    ins, outs = refs[: p.group], refs[p.group :]
    for k, out_ref in enumerate(outs):
        out_ref[...] = add(ins, slice(k * p.patch, (k + 1) * p.patch)).astype(jnp.bfloat16)


def add_chips_kernel(p, *refs):
    ins, outs = refs[: p.chips], refs[p.chips :]
    total = add(ins).astype(jnp.bfloat16)
    target = lax.broadcasted_iota(jnp.int32, (p.room, 1), 0)
    row, along = target // p.per_row, target % p.per_row - 1
    count = p.tiles * p.own_cols
    for k, out_ref in enumerate(outs):
        cell = ((lax.axis_index("tile") ^ k) * p.own_cols + along + count) % count
        wanted = jnp.where(row < 3, row * count + cell, -1)
        out_ref[...] = dot(one_hot(wanted, 0, p.patch), total).astype(jnp.bfloat16)


def diffuse_kernel(p, edge, *refs):
    ins, root_ref, out_ref = refs[: p.tiles], refs[-2], refs[-1]
    total = add(ins) * 0.0625
    length = p.along + 2 * edge
    shape = (length, p.room)
    cell = lax.broadcasted_iota(jnp.int32, shape, 0)
    source = lax.broadcasted_iota(jnp.int32, shape, 1)
    column = (cell - edge + 4) // 4
    spread = []
    for k in range(3):
        pick = (source == column + k * p.per_row) & (column >= 0) & (column < p.per_row)
        spread.append(
            jnp.dot(
                pick.astype(jnp.float32),
                total,
                precision=lax.Precision.HIGHEST,
                preferred_element_type=jnp.float32,
            )
        )
    root = root_ref[...]
    state = [spread[(row + 2) // 4] for row in range(p.across + 4)]
    east_of = functools.partial(pltpu.roll, shift=length - 1, axis=0)
    west_of = functools.partial(pltpu.roll, shift=1, axis=0)
    north = root[:, :-1] * root[:, 1:]
    east, west = root * east_of(root), root * west_of(root)
    for sweep in range(2):
        fresh = list(state)
        for row in range(1 + sweep, p.across + 3 - sweep):
            here = state[row]
            fresh[row] = (
                here
                + north[:, row : row + 1] * (state[row + 1] - here)
                + north[:, row - 1 : row] * (state[row - 1] - here)
                + east[:, row : row + 1] * (east_of(here) - here)
                + west[:, row : row + 1] * (west_of(here) - here)
            )
        state = fresh
    for row in range(p.across):
        out_ref[row] = state[row + 2][edge : edge + p.along, : p.features]


def body_by_column(
    fields,
    diffusivity,
    owners,
    observed,
    usable,
    w_hidden,
    b_hidden,
    w_radiance,
    b_radiance,
    inv_cov,
):
    p = Plan(
        lax.axis_size("tile"),
        lax.axis_size("chan"),
        fields.shape,
        owners.shape,
        observed.shape,
        w_hidden.shape,
    )
    half, single = jnp.bfloat16, jnp.float32
    shape = jax.ShapeDtypeStruct
    both = ("tile", "chan")
    everyone = [(a, b) for a in range(p.tiles) for b in range(p.chans)]

    def flip(value, mask):
        return lax.ppermute(value, "chan", [(b, b ^ mask) for b in range(p.chans)])

    def trade(value, mask):
        return lax.ppermute(value, "tile", [(a, a ^ mask) for a in range(p.tiles)])

    def send(value, wanted):
        pairs = dict(wanted)
        pairs.update({target: source for source, target in wanted.items()})
        for a, b in everyone:
            if (a, b) not in pairs:
                pairs[a, b] = (a, b ^ 1)
        number = lambda place: place[0] * p.chans + place[1]
        return lax.ppermute(
            value, both, sorted((number(a), number(b)) for a, b in pairs.items())
        )

    def join(values, kernel_shape, after=()):
        return call(
            functools.partial(join_kernel, len(values)),
            shape(kernel_shape, half),
            [*values, *after],
            in_hbm=range(len(values) + len(after)),
            out_hbm=True,
            scratch=[pltpu.SemaphoreType.DMA((len(values),))],
            flops=0,
        )

    def grow(value, over, after=()):
        return join([value, over(value)], (2 * value.shape[0],) + value.shape[1:], after)

    reach = p.across + 4
    cell, *targets = call(
        functools.partial(index_kernel, p),
        [shape((3 * reach, 1), jnp.int32)] + [shape((p.chips * p.patch, 1), jnp.int32)] * p.group,
        [],
        flops=10**9,
    )

    strips = call(
        functools.partial(prepare_kernel, p),
        shape((p.block, p.width), half),
        [fields, diffusivity, usable, b_hidden, cell],
        in_hbm=[4],
        scratch=[pltpu.VMEM((p.block, p.width), single)],
    )
    seen, stages, before = observed, [], ()
    bit = 1
    while bit < p.tiles:
        if 2 * bit < p.tiles:
            seen = grow(seen, lambda value: trade(value, bit))
            before = [seen]
        strips = grow(strips, lambda value: trade(value, bit), before)
        before = ()
        stages.append(strips)
        bit *= 2
    strips = join(
        [strips] + [flip(strips, k * p.group) for k in range(1, p.chips)], (p.strips, p.width)
    )
    strips = [strips] + [flip(strips, k) for k in range(1, p.group)]

    near = [w_hidden] + [flip(w_hidden, chip * p.group) for chip in range(1, p.chips)]
    near = call(
        functools.partial(stack_kernel, p),
        shape((p.chips * p.deep, p.hidden), half),
        near + [stages[-1]],
        in_hbm=[len(near)],
    )
    weights = [near] + [flip(near, k) for k in range(1, p.group)]

    far_half = p.tiles // 2
    seen = [
        seen,
        send(seen, {(b // p.group ^ far_half, b): (b // p.group, b) for b in range(p.chans)}),
    ]

    place, source = call(
        functools.partial(place_kernel, p),
        [shape((p.rows, 1), jnp.int32)] * 2,
        [owners.reshape(1, p.rows)],
        flops=SLACK_FLOPS,
    )
    radiance, in_use, preact, kappa = call(
        functools.partial(forward_kernel, p),
        [
            shape((p.rows, p.shard), single),
            shape((p.rows, 1), single),
            shape((p.chans, p.rows, p.hidden), single),
            shape((3 * reach, p.lane), single),
        ],
        [place, source, cell, b_radiance, w_radiance] + strips + weights,
        scratch=[pltpu.VMEM((p.rows, p.hidden * p.chans), half)],
        flops=FORWARD_FLOPS,
    )
    parts = call(
        functools.partial(depart_kernel, p),
        [shape((p.rows // p.steps, p.shard), half)] * p.steps,
        [radiance, in_use, place] + seen,
    )

    slope = call(
        slope_kernel,
        shape((p.chans, p.hidden, p.rows), single),
        [preact],
        flops=40 * preact.size,
    )

    pool, held, choices = list(parts), {}, {}
    for j in range(p.steps):
        held[0, j] = choices[0, j] = j
    for step in range(p.steps):
        for since in range(-1, step):
            for j in range(p.steps):
                order = [1 << (j + k) % p.steps for k in range(p.steps)]
                roles = [0] if since < 0 else [
                    order[since] + rest
                    for rest in range(p.chips)
                    if rest & ~sum(order[:since]) == 0
                ]
                wanted = {
                    (a, b): (a, b ^ order[step] * p.group)
                    for a, b in everyone
                    if (b // p.group ^ a) in roles
                }
                source = pool[choices[roles[0], j]]
                for role in roles:
                    choices[role + order[step], j] = len(pool)
                pool.append(send(source, wanted))
    chosen = call(
        functools.partial(choose_kernel, p, choices),
        shape((p.rows, p.shard), half),
        pool + [slope],
        in_hbm=range(len(pool) + 1),
        out_hbm=True,
        scratch=[pltpu.SemaphoreType.DMA((p.steps,))],
    )
    depart = [flip(chosen, k) for k in range(1, p.group)]

    partial = call(
        functools.partial(near_kernel, p),
        shape((p.rows, p.shard), single),
        [chosen, inv_cov],
        flops=2 * p.rows * p.shard * p.shard,
    )
    partial = call(
        functools.partial(backward_kernel, p),
        [shape((p.chips * p.patch, p.features), half)] * p.group,
        [w_radiance, inv_cov, slope, partial] + depart + weights + targets,
        flops=2 * p.rows * (p.hidden * p.chans * (p.features + p.shard) + inv_cov.size),
    )
    partial = [partial[0]] + [flip(partial[k], k) for k in range(1, p.group)]
    partial = call(
        functools.partial(add_group_kernel, p),
        [shape((p.patch, p.features), half)] * p.chips,
        partial,
    )
    partial = [partial[0]] + [flip(partial[k], k * p.group) for k in range(1, p.chips)]
    partial = call(
        functools.partial(add_chips_kernel, p),
        [shape((p.room, p.features), half)] * p.tiles,
        partial,
    )
    partial = [partial[0]] + [trade(partial[k], k) for k in range(1, p.tiles)]
    edge = 8
    kappa = kappa.reshape(3, reach, p.lane)
    root = jnp.sqrt(
        jnp.concatenate(
            [kappa[0, :, p.along - edge : p.along], kappa[1, :, : p.along], kappa[2, :, :edge]],
            axis=1,
        ).T
    )
    return call(
        functools.partial(diffuse_kernel, p, edge),
        shape(fields.shape, single),
        partial + [root],
        flops=100 * fields.size,
    )


def solution(mesh):
    tiles, chans = mesh.shape["tile"], mesh.shape["chan"]
    by_column = tiles > 1 and chans % tiles == 0 and chans & (chans - 1) == 0 and chans > tiles
    placed = (
        P("chan", "tile", None),
        P("chan", "tile"),
        P(),
        P("tile", "chan"),
        P("tile"),
        P(None, "chan"),
        P("chan"),
        P(None, "chan"),
        P("chan"),
        P("tile", "chan"),
    )
    return jax.shard_map(
        body_by_column if by_column else body_by_owner,
        mesh=mesh,
        in_specs=placed,
        out_specs=P("chan", "tile", None),
        check_vma=False,
    )
```

```python
import functools

import jax
import jax.numpy as jnp
from jax import lax
from jax.experimental import pallas as pl
from jax.experimental.pallas import tpu as pltpu
from jax.sharding import PartitionSpec as P

VMEM_BYTES = 24 * 1024 * 1024
SLACK_FLOPS = 2 * 10**9
FORWARD_FLOPS = 10**8
NT_DIMS = (((1,), (1,)), ((), ()))


def padded_2(value, sides, width, wrap):
    for axis, dim in sides:
        devices, length = (lax.axis_size(axis), value.shape[dim])
        up = [(i, (i + 1) % devices) for i in range(devices if wrap else devices - 1)]
        down = [(j, i) for i, j in up]
        last = lax.slice_in_dim(value, length - width, length, axis=dim)
        first = lax.slice_in_dim(value, 0, width, axis=dim)
        before = lax.ppermute(last, axis, up)
        after = lax.ppermute(first, axis, down)
        value = jnp.concatenate([before, value, after], axis=dim)
    return value


def add_rims(values):
    rowwise = padded_2(values, (("chan", 0),), 1, False)
    return padded_2(rowwise, (("tile", 1),), 1, True)


def body_by_owner(
    fields,
    diffusivity,
    owners,
    observed,
    usable,
    w_hidden,
    b_hidden,
    w_radiance,
    b_radiance,
    inv_cov,
):
    tile_count = lax.axis_size("tile")
    chan_count = lax.axis_size("chan")
    tile_index = lax.axis_index("tile")
    chan_index = lax.axis_index("chan")
    slot_count = observed.shape[0]
    capacity = slot_count // tile_count
    cells_across, cells_along, features = fields.shape
    own_cols = cells_across // 4 * (cells_along // 4)
    tile_cols = chan_count * own_cols
    hidden_dev = w_hidden.shape[1]
    owner_table = owners[:, 0].reshape(tile_count, tile_cols)
    owner_hits = (
        owner_table[:, :, None] == jnp.arange(tile_count, dtype=jnp.int32)[None, None, :]
    ).astype(jnp.int32)
    before = jnp.sum((jnp.cumsum(owner_hits, axis=1) - owner_hits) * owner_hits, axis=2)
    tallies = jnp.sum(owner_hits, axis=1)
    slot_of = lax.dynamic_index_in_dim(
        owner_table * capacity + before, tile_index, 0, keepdims=False
    )
    arriving = lax.dynamic_index_in_dim(tallies, tile_index, 1, keepdims=False)
    occupied = (jnp.arange(capacity, dtype=jnp.int32)[None, :] < arriving[:, None]).reshape(
        slot_count
    )
    grouped = fields.reshape(cells_across // 4, 4, cells_along // 4, 4, features)
    columns = (
        (jnp.sum(grouped, axis=(1, 3)) * 0.0625).reshape(own_cols, features).astype(jnp.bfloat16)
    )
    placer = (slot_of[None, :] == jnp.arange(slot_count, dtype=jnp.int32)[:, None]).astype(
        jnp.bfloat16
    )
    outgoing = jnp.dot(
        placer,
        lax.all_gather(columns, "chan", axis=0, tiled=True),
        preferred_element_type=jnp.float32,
    )
    incoming = lax.all_to_all(
        outgoing.astype(jnp.bfloat16), "tile", split_axis=0, concat_axis=0, tiled=True
    )
    preact = lax.dot_general(
        w_hidden, incoming, (((0,), (1,)), ((), ())), preferred_element_type=jnp.float32
    )
    preact = preact + b_hidden[:, None]
    squash = jax.nn.sigmoid(preact)
    active = (preact * squash).astype(jnp.bfloat16)
    radiance = lax.dot_general(
        lax.all_gather(active, "chan", axis=0, tiled=True),
        w_radiance,
        (((0,), (0,)), ((), ())),
        preferred_element_type=jnp.float32,
    )
    radiance = radiance + b_radiance[None, :]
    in_use = usable.astype(jnp.float32) * occupied.astype(jnp.float32)
    departure = ((radiance - observed.astype(jnp.float32)) * in_use[:, None]).astype(jnp.bfloat16)
    cotangent = jnp.dot(
        lax.all_gather(departure, "chan", axis=1, tiled=True),
        lax.all_gather(inv_cov, "tile", axis=0, tiled=True),
        preferred_element_type=jnp.float32,
    )
    cotangent = cotangent.astype(jnp.bfloat16)
    full_sum = lax.psum(
        lax.dot_general(w_radiance, cotangent, NT_DIMS, preferred_element_type=jnp.float32),
        "chan",
    )
    grad_hidden = lax.dynamic_slice_in_dim(full_sum, chan_index * hidden_dev, hidden_dev, 0)
    slope_term = squash * (1.0 + preact * (1.0 - squash))
    grad_pre = (grad_hidden * slope_term).astype(jnp.bfloat16)
    part_grad = lax.dot_general(
        grad_pre, w_hidden, (((0,), (1,)), ((), ())), preferred_element_type=jnp.float32
    )
    returned = lax.all_to_all(part_grad, "tile", split_axis=0, concat_axis=0, tiled=True)
    column_grad = lax.psum_scatter(
        jnp.take(returned, slot_of, axis=0), "chan", scatter_dimension=0, tiled=True
    )
    spread = jnp.repeat(
        column_grad.reshape(cells_across // 4, cells_along // 4, features), 4, axis=0
    )
    adjoint = jnp.repeat(spread, 4, axis=1) * 0.0625
    kappa_root = jnp.sqrt(diffusivity)
    root_rim = add_rims(kappa_root)
    coef_north = (kappa_root * root_rim[2:, 1:-1])[:, :, None]
    coef_south = (kappa_root * root_rim[:-2, 1:-1])[:, :, None]
    coef_east = (kappa_root * root_rim[1:-1, 2:])[:, :, None]
    coef_west = (kappa_root * root_rim[1:-1, :-2])[:, :, None]
    for sweep_index in range(2):
        padded = add_rims(adjoint)
        adjoint = (
            adjoint
            + coef_north * (padded[2:, 1:-1] - adjoint)
            + coef_south * (padded[:-2, 1:-1] - adjoint)
            + coef_east * (padded[1:-1, 2:] - adjoint)
            + coef_west * (padded[1:-1, :-2] - adjoint)
        )
    return adjoint


def up_to(value, multiple):
    return -(-value // multiple) * multiple


def dot(left, right):
    return jnp.dot(left, right, preferred_element_type=jnp.float32)


def dot_nt(left, right):
    return lax.dot_general(left, right, NT_DIMS, preferred_element_type=jnp.float32)


def split_three(value):
    high = value.astype(jnp.bfloat16).astype(jnp.float32)
    middle = (value - high).astype(jnp.bfloat16).astype(jnp.float32)
    return high, middle, value - high - middle


def call(
    kernel, out_shape, args, in_hbm=(), out_hbm=False, scratch=(), flops=0, vmem=VMEM_BYTES
):
    far, near = pl.BlockSpec(memory_space=pl.ANY), pl.BlockSpec(memory_space=pltpu.VMEM)
    bytes_accessed = sum(a.size * a.dtype.itemsize for a in args)
    return pl.pallas_call(
        kernel,
        out_shape=out_shape,
        in_specs=[far if k in in_hbm else near for k in range(len(args))],
        out_specs=jax.tree.map(lambda _: far if out_hbm else near, out_shape),
        scratch_shapes=list(scratch),
        compiler_params=pltpu.CompilerParams(vmem_limit_bytes=vmem),
        cost_estimate=pl.CostEstimate(
            flops=flops, bytes_accessed=bytes_accessed, transcendentals=0
        ),
    )(*args)


class Plan:
    def __init__(self, tiles, chans, fields, owners, observed, w_hidden):
        self.tiles, self.chans = tiles, chans
        self.across, self.along, self.features = fields
        self.own_cols = self.across // 4 * (self.along // 4)
        self.rows = owners[0]
        self.tile_cols = self.rows // tiles
        self.slots = observed[0]
        self.shard = observed[1]
        self.capacity = self.slots // tiles
        self.hidden = w_hidden[1]
        self.group = chans // tiles
        self.chips = chans // self.group
        self.steps = self.chips.bit_length() - 1
        self.lane = up_to(self.along, 128)
        self.flag_at = up_to(self.hidden, 128)
        self.width = max(
            up_to(self.features, 128),
            2 * self.flag_at,
            self.flag_at + up_to(self.slots, 128),
            3 * self.lane,
        )
        self.block = up_to(self.own_cols + 2 + self.across, 16)
        self.per_row = self.own_cols + 2
        self.patch = 3 * tiles * self.own_cols
        self.room = up_to(3 * self.per_row, 16)
        self.deep = up_to(self.features, 16)
        self.strips = self.chips * tiles * self.block

    def order(self, mask):
        return mask % self.group * self.chips + mask // self.group

    def layer(self, refs, k):
        at = k % self.chips * self.deep
        return refs[k // self.chips][at : at + self.features, :]

    def mask(self, k):
        return k % self.chips * self.group + k // self.chips


def prepare_kernel(p, fields_ref, diffusivity_ref, usable_ref, bias_ref, after_ref, out_ref, flat):
    flat[...] = jnp.zeros(flat.shape, jnp.float32)
    shape = (p.own_cols, p.along)
    row = lax.broadcasted_iota(jnp.int32, shape, 0)
    member = row == lax.broadcasted_iota(jnp.int32, shape, 1) // 4
    total = jnp.dot(
        member.astype(jnp.float32),
        fields_ref[0] + fields_ref[1] + fields_ref[2] + fields_ref[3],
        precision=lax.Precision.HIGHEST,
        preferred_element_type=jnp.float32,
    )
    flat[: p.own_cols, : p.features] = total * 0.0625
    at = p.own_cols
    high, middle, low = split_three(bias_ref[...].reshape(1, p.hidden))
    flat[at : at + 1, : p.hidden] = high
    flat[at : at + 1, p.flag_at : p.flag_at + p.hidden] = middle
    flat[at + 1 : at + 2, : p.hidden] = low
    flags = usable_ref[...].reshape(1, p.slots).astype(jnp.float32)
    flat[at + 1 : at + 2, p.flag_at : p.flag_at + p.slots] = flags
    for k, part in enumerate(split_three(diffusivity_ref[...])):
        flat[at + 2 : at + 2 + p.across, k * p.lane : k * p.lane + p.along] = part
    out_ref[...] = flat[...].astype(jnp.bfloat16)


def strip_of(p, tile, chan):
    other = chan ^ lax.axis_index("chan")
    return p.order(other) * p.tiles + (tile ^ lax.axis_index("tile"))


def index_kernel(p, cell_ref, *target_refs):
    t, c = lax.axis_index("tile"), lax.axis_index("chan")
    row = lax.broadcasted_iota(jnp.int32, cell_ref.shape, 0)
    reach = p.across + 4
    tile = (t + row // reach - 1 + p.tiles) % p.tiles
    cell = c * p.across - 2 + row % reach
    inside = (cell >= 0) & (cell < p.chans * p.across)
    cell = jnp.where(inside, cell, 0)
    wanted = strip_of(p, tile, cell // p.across) * p.block + p.own_cols + 2 + cell % p.across
    cell_ref[...] = jnp.where(inside, wanted, -1)

    target = lax.broadcasted_iota(jnp.int32, target_refs[0].shape, 0)
    chip, inner = target // p.patch, target % p.patch
    beside, inner = inner // (p.patch // 3) - 1, inner % (p.patch // 3)
    tile, along = inner // p.own_cols, inner % p.own_cols
    for k, target_ref in enumerate(target_refs):
        row = (chip ^ (c // p.group)) * p.group + (c % p.group ^ k) + beside
        wanted = tile * p.tile_cols + row * p.own_cols + along
        target_ref[...] = jnp.where((row >= 0) & (row < p.chans), wanted, -1)


def place_kernel(p, owners_ref, place_ref, source_ref):
    t = lax.axis_index("tile")
    across = owners_ref[...]
    shape = (p.rows, p.rows)
    row = lax.broadcasted_iota(jnp.int32, shape, 0)
    other = lax.broadcasted_iota(jnp.int32, shape, 1)
    owner = jnp.sum(jnp.where(row == other, across, 0), axis=1, keepdims=True)
    first = lax.broadcasted_iota(jnp.int32, owner.shape, 0)
    begin = first // p.tile_cols * p.tile_cols
    same = (owner == across) & (other >= begin) & (other < row)
    rank = jnp.sum(jnp.where(same, 1, 0), axis=1, keepdims=True)
    tile = first // p.tile_cols
    place_ref[...] = (owner ^ t) * p.slots + tile * p.capacity + rank
    source_ref[...] = (
        strip_of(p, tile, first % p.tile_cols // p.own_cols) * p.block + first % p.own_cols
    )


def join_kernel(count, *refs):
    ins, out_ref, sems = refs[:count], refs[-2], refs[-1]
    size = out_ref.shape[0] // count
    copies = [
        pltpu.make_async_copy(
            ref, out_ref.at[k] if ref.ndim < out_ref.ndim else out_ref.at[pl.ds(k * size, size)],
            sems.at[k],
        )
        for k, ref in enumerate(ins)
    ]
    for copy in copies:
        copy.start()
    for copy in copies:
        copy.wait()


def stack_kernel(p, *refs):
    for k, ref in enumerate(refs[: p.chips]):
        refs[-1][k * p.deep : k * p.deep + p.features, :] = ref[...]
        refs[-1][k * p.deep + p.features : (k + 1) * p.deep, :] = jnp.zeros(
            (p.deep - p.features, p.hidden), jnp.bfloat16
        )


def one_hot(wanted, first, count):
    source = lax.broadcasted_iota(jnp.int32, (wanted.shape[0], count), 1)
    return (source + first == wanted).astype(jnp.bfloat16)


def forward_kernel(p, *refs):
    refs = list(refs)
    take = lambda n: [refs.pop(0) for _ in range(n)]
    place_ref, source_ref, cell_ref, bias_ref, w_radiance_ref = take(5)
    strip_refs, weight_refs = take(p.group), take(p.group)
    radiance_ref, in_use_ref, preact_ref, kappa_ref, active = refs
    c = lax.axis_index("chan")
    gathered = [ref[...] for ref in strip_refs]
    columns = sum(
        dot(one_hot(source_ref[...], k * p.strips, p.strips), strips)
        for k, strips in enumerate(gathered)
    )
    columns = columns.astype(jnp.bfloat16)[:, : p.features]
    for k in range(p.chans):
        member, chip = k // p.chips, k % p.chips
        at = chip * p.tiles * p.block + p.own_cols
        low = strip_refs[member][at : at + 2, :].astype(jnp.float32)
        bias = (
            low[:1, : p.hidden]
            + low[:1, p.flag_at : p.flag_at + p.hidden]
            + low[1:, : p.hidden]
        )
        preact = dot(columns, p.layer(weight_refs, k)) + bias
        preact_ref[k] = preact
        at = pl.multiple_of((c ^ p.mask(k)) * p.hidden, p.hidden)
        active[:, pl.ds(at, p.hidden)] = (preact * jax.nn.sigmoid(preact)).astype(jnp.bfloat16)
    in_use = jnp.zeros((p.rows, 1), jnp.float32)
    for k in range(p.tiles):
        slot = lax.broadcasted_iota(jnp.int32, (p.rows, p.slots), 1) + k * p.slots
        low = k * p.block + p.own_cols + 1
        flags = strip_refs[0][low : low + 1, p.flag_at : p.flag_at + p.slots]
        flags = jnp.where(place_ref[...] == slot, flags.astype(jnp.float32), 0.0)
        in_use = in_use + jnp.sum(flags, axis=1, keepdims=True)
    in_use_ref[...] = in_use
    radiance_ref[...] = dot(active[...], w_radiance_ref[...]) + bias_ref[...].reshape(1, p.shard)
    parts = sum(
        dot(one_hot(cell_ref[...], k * p.strips, p.strips), strips)
        for k, strips in enumerate(gathered)
    )
    kappa_ref[...] = sum(parts[:, k * p.lane : (k + 1) * p.lane] for k in range(3))


def depart_kernel(p, radiance_ref, in_use_ref, place_ref, *refs):
    seen_refs, part_refs = refs[: -p.steps], refs[-p.steps :]
    part, count = p.rows // p.steps, seen_refs[0].shape[0]
    for j, part_ref in enumerate(part_refs):
        at = slice(j * part, (j + 1) * part)
        observed = sum(
            dot(one_hot(place_ref[at, :], k * count, count), ref[...])
            for k, ref in enumerate(seen_refs)
        )
        departure = (radiance_ref[at, :] - observed) * in_use_ref[at, :]
        part_ref[...] = departure.astype(jnp.bfloat16)


def slope_kernel(preact_ref, slope_ref):
    for k in range(preact_ref.shape[0]):
        preact = preact_ref[k]
        squash = jax.nn.sigmoid(preact)
        slope_ref[k] = (squash * (1.0 + preact * (1.0 - squash))).T


def choose_kernel(p, choices, *refs):
    refs, out_ref, sems = refs[:-3], refs[-2], refs[-1]
    size = refs[0].shape[0]
    role = (lax.axis_index("chan") // p.group) ^ lax.axis_index("tile")
    for place in range(p.chips):

        @pl.when(role == place)
        def _():
            copies = [
                pltpu.make_async_copy(
                    refs[choices[place, j]], out_ref.at[pl.ds(j * size, size)], sems.at[j]
                )
                for j in range(p.steps)
            ]
            for copy in copies:
                copy.start()
            for copy in copies:
                copy.wait()


def near_kernel(p, depart_ref, inv_cov_ref, out_ref):
    at = pl.multiple_of(lax.axis_index("chan") % p.group * p.shard, p.shard)
    out_ref[...] = dot(depart_ref[...], inv_cov_ref[pl.ds(at, p.shard), :])


def backward_kernel(p, *refs):
    refs = list(refs)
    take = lambda n: [refs.pop(0) for _ in range(n)]
    w_radiance_ref, inv_cov_ref, slope_ref, near_ref = take(4)
    depart_refs, weight_refs, target_refs = take(p.group - 1), take(p.group), take(p.group)
    out_refs = refs
    c = lax.axis_index("chan")
    cotangent = near_ref[...]
    for k, ref in enumerate(depart_refs):
        at = pl.multiple_of((c % p.group ^ (k + 1)) * p.shard, p.shard)
        cotangent = cotangent + dot(ref[...], inv_cov_ref[pl.ds(at, p.shard), :])
    cotangent = cotangent.T.astype(jnp.bfloat16)
    total = jnp.zeros((p.features, p.rows), jnp.float32)
    for k in range(p.chans):
        at = pl.multiple_of((c ^ p.mask(k)) * p.hidden, p.hidden)
        grad_hidden = dot(w_radiance_ref[pl.ds(at, p.hidden), :], cotangent)
        grad_pre = (grad_hidden * slope_ref[k]).astype(jnp.bfloat16)
        total = total + dot(p.layer(weight_refs, k), grad_pre)
    total = total.astype(jnp.bfloat16)
    for target_ref, out_ref in zip(target_refs, out_refs):
        out_ref[...] = dot_nt(one_hot(target_ref[...], 0, p.rows), total).astype(jnp.bfloat16)


def add(refs, at=slice(None)):
    total = refs[0][at, :].astype(jnp.float32)
    for ref in refs[1:]:
        total = total + ref[at, :].astype(jnp.float32)
    return total


def add_group_kernel(p, *refs):
    ins, outs = refs[: p.group], refs[p.group :]
    for k, out_ref in enumerate(outs):
        out_ref[...] = add(ins, slice(k * p.patch, (k + 1) * p.patch)).astype(jnp.bfloat16)


def add_chips_kernel(p, *refs):
    ins, outs = refs[: p.chips], refs[p.chips :]
    total = add(ins).astype(jnp.bfloat16)
    target = lax.broadcasted_iota(jnp.int32, (p.room, 1), 0)
    row, along = target // p.per_row, target % p.per_row - 1
    count = p.tiles * p.own_cols
    for k, out_ref in enumerate(outs):
        cell = ((lax.axis_index("tile") ^ k) * p.own_cols + along + count) % count
        wanted = jnp.where(row < 3, row * count + cell, -1)
        out_ref[...] = dot(one_hot(wanted, 0, p.patch), total).astype(jnp.bfloat16)


def diffuse_kernel(p, edge, *refs):
    ins, root_ref, out_ref = refs[: p.tiles], refs[-2], refs[-1]
    total = add(ins) * 0.0625
    length = p.along + 2 * edge
    shape = (length, p.room)
    cell = lax.broadcasted_iota(jnp.int32, shape, 0)
    source = lax.broadcasted_iota(jnp.int32, shape, 1)
    column = (cell - edge + 4) // 4
    spread = []
    for k in range(3):
        pick = (source == column + k * p.per_row) & (column >= 0) & (column < p.per_row)
        spread.append(
            jnp.dot(
                pick.astype(jnp.float32),
                total,
                precision=lax.Precision.HIGHEST,
                preferred_element_type=jnp.float32,
            )
        )
    root = root_ref[...]
    state = [spread[(row + 2) // 4] for row in range(p.across + 4)]
    east_of = functools.partial(pltpu.roll, shift=length - 1, axis=0)
    west_of = functools.partial(pltpu.roll, shift=1, axis=0)
    north = root[:, :-1] * root[:, 1:]
    east, west = root * east_of(root), root * west_of(root)
    for sweep in range(2):
        fresh = list(state)
        for row in range(1 + sweep, p.across + 3 - sweep):
            here = state[row]
            fresh[row] = (
                here
                + north[:, row : row + 1] * (state[row + 1] - here)
                + north[:, row - 1 : row] * (state[row - 1] - here)
                + east[:, row : row + 1] * (east_of(here) - here)
                + west[:, row : row + 1] * (west_of(here) - here)
            )
        state = fresh
    for row in range(p.across):
        out_ref[row] = state[row + 2][edge : edge + p.along, : p.features]


def body_by_column(
    fields,
    diffusivity,
    owners,
    observed,
    usable,
    w_hidden,
    b_hidden,
    w_radiance,
    b_radiance,
    inv_cov,
):
    p = Plan(
        lax.axis_size("tile"),
        lax.axis_size("chan"),
        fields.shape,
        owners.shape,
        observed.shape,
        w_hidden.shape,
    )
    half, single = jnp.bfloat16, jnp.float32
    shape = jax.ShapeDtypeStruct
    both = ("tile", "chan")
    everyone = [(a, b) for a in range(p.tiles) for b in range(p.chans)]

    def flip(value, mask):
        return lax.ppermute(value, "chan", [(b, b ^ mask) for b in range(p.chans)])

    def trade(value, mask):
        return lax.ppermute(value, "tile", [(a, a ^ mask) for a in range(p.tiles)])

    def send(value, wanted):
        pairs = dict(wanted)
        pairs.update({target: source for source, target in wanted.items()})
        for a, b in everyone:
            if (a, b) not in pairs:
                pairs[a, b] = (a, b ^ 1)
        number = lambda place: place[0] * p.chans + place[1]
        return lax.ppermute(
            value, both, sorted((number(a), number(b)) for a, b in pairs.items())
        )

    def join(values, kernel_shape, after=()):
        return call(
            functools.partial(join_kernel, len(values)),
            shape(kernel_shape, half),
            [*values, *after],
            in_hbm=range(len(values) + len(after)),
            out_hbm=True,
            scratch=[pltpu.SemaphoreType.DMA((len(values),))],
            flops=0,
        )

    def grow(value, over, after=()):
        return join([value, over(value)], (2 * value.shape[0],) + value.shape[1:], after)

    reach = p.across + 4
    cell, *targets = call(
        functools.partial(index_kernel, p),
        [shape((3 * reach, 1), jnp.int32)] + [shape((p.chips * p.patch, 1), jnp.int32)] * p.group,
        [],
        flops=10**9,
    )

    strips = call(
        functools.partial(prepare_kernel, p),
        shape((p.block, p.width), half),
        [fields, diffusivity, usable, b_hidden, cell],
        in_hbm=[4],
        scratch=[pltpu.VMEM((p.block, p.width), single)],
    )
    seen, stages, before = observed, [], ()
    bit = 1
    while bit < p.tiles:
        if 2 * bit < p.tiles:
            seen = grow(seen, lambda value: trade(value, bit))
            before = [seen]
        strips = grow(strips, lambda value: trade(value, bit), before)
        before = ()
        stages.append(strips)
        bit *= 2
    strips = join(
        [strips] + [flip(strips, k * p.group) for k in range(1, p.chips)], (p.strips, p.width)
    )
    strips = [strips] + [flip(strips, k) for k in range(1, p.group)]

    near = [w_hidden] + [flip(w_hidden, chip * p.group) for chip in range(1, p.chips)]
    near = call(
        functools.partial(stack_kernel, p),
        shape((p.chips * p.deep, p.hidden), half),
        near + [stages[-1]],
        in_hbm=[len(near)],
    )
    weights = [near] + [flip(near, k) for k in range(1, p.group)]

    far_half = p.tiles // 2
    seen = [
        seen,
        send(seen, {(b // p.group ^ far_half, b): (b // p.group, b) for b in range(p.chans)}),
    ]

    place, source = call(
        functools.partial(place_kernel, p),
        [shape((p.rows, 1), jnp.int32)] * 2,
        [owners.reshape(1, p.rows)],
        flops=SLACK_FLOPS,
    )
    radiance, in_use, preact, kappa = call(
        functools.partial(forward_kernel, p),
        [
            shape((p.rows, p.shard), single),
            shape((p.rows, 1), single),
            shape((p.chans, p.rows, p.hidden), single),
            shape((3 * reach, p.lane), single),
        ],
        [place, source, cell, b_radiance, w_radiance] + strips + weights,
        scratch=[pltpu.VMEM((p.rows, p.hidden * p.chans), half)],
        flops=FORWARD_FLOPS,
    )
    parts = call(
        functools.partial(depart_kernel, p),
        [shape((p.rows // p.steps, p.shard), half)] * p.steps,
        [radiance, in_use, place] + seen,
    )

    slope = call(
        slope_kernel,
        shape((p.chans, p.hidden, p.rows), single),
        [preact],
        flops=40 * preact.size,
    )

    pool, held, choices = list(parts), {}, {}
    for j in range(p.steps):
        held[0, j] = choices[0, j] = j
    for step in range(p.steps):
        for since in range(-1, step):
            for j in range(p.steps):
                order = [1 << (j + k) % p.steps for k in range(p.steps)]
                roles = [0] if since < 0 else [
                    order[since] + rest
                    for rest in range(p.chips)
                    if rest & ~sum(order[:since]) == 0
                ]
                wanted = {
                    (a, b): (a, b ^ order[step] * p.group)
                    for a, b in everyone
                    if (b // p.group ^ a) in roles
                }
                source = pool[choices[roles[0], j]]
                for role in roles:
                    choices[role + order[step], j] = len(pool)
                pool.append(send(source, wanted))
    chosen = call(
        functools.partial(choose_kernel, p, choices),
        shape((p.rows, p.shard), half),
        pool + [slope],
        in_hbm=range(len(pool) + 1),
        out_hbm=True,
        scratch=[pltpu.SemaphoreType.DMA((p.steps,))],
    )
    depart = [flip(chosen, k) for k in range(1, p.group)]

    partial = call(
        functools.partial(near_kernel, p),
        shape((p.rows, p.shard), single),
        [chosen, inv_cov],
        flops=2 * p.rows * p.shard * p.shard,
    )
    partial = call(
        functools.partial(backward_kernel, p),
        [shape((p.chips * p.patch, p.features), half)] * p.group,
        [w_radiance, inv_cov, slope, partial] + depart + weights + targets,
        flops=2 * p.rows * (p.hidden * p.chans * (p.features + p.shard) + inv_cov.size),
    )
    partial = [partial[0]] + [flip(partial[k], k) for k in range(1, p.group)]
    partial = call(
        functools.partial(add_group_kernel, p),
        [shape((p.patch, p.features), half)] * p.chips,
        partial,
    )
    partial = [flip(partial[k], k * p.group) for k in range(p.chips - 1, 0, -1)] + [partial[0]]
    partial = call(
        functools.partial(add_chips_kernel, p),
        [shape((p.room, p.features), half)] * p.tiles,
        partial,
    )
    partial = [trade(partial[k], k) for k in range(p.tiles - 1, 0, -1)] + [partial[0]]
    edge = 8
    kappa = kappa.reshape(3, reach, p.lane)
    root = jnp.sqrt(
        jnp.concatenate(
            [kappa[0, :, p.along - edge : p.along], kappa[1, :, : p.along], kappa[2, :, :edge]],
            axis=1,
        ).T
    )
    return call(
        functools.partial(diffuse_kernel, p, edge),
        shape(fields.shape, single),
        partial + [root],
        flops=100 * fields.size,
    )


def solution(mesh):
    tiles, chans = mesh.shape["tile"], mesh.shape["chan"]
    by_column = tiles > 1 and chans % tiles == 0 and chans & (chans - 1) == 0 and chans > tiles
    placed = (
        P("chan", "tile", None),
        P("chan", "tile"),
        P(),
        P("tile", "chan"),
        P("tile"),
        P(None, "chan"),
        P("chan"),
        P(None, "chan"),
        P("chan"),
        P("tile", "chan"),
    )
    return jax.shard_map(
        body_by_column if by_column else body_by_owner,
        mesh=mesh,
        in_specs=placed,
        out_specs=P("chan", "tile", None),
        check_vma=False,
    )
```

```python
import functools

import jax
import jax.numpy as jnp
from jax import lax
from jax.experimental import pallas as pl
from jax.experimental.pallas import tpu as pltpu
from jax.sharding import PartitionSpec as P

VMEM_BYTES = 24 * 1024 * 1024
SLACK_FLOPS = 2 * 10**9
FORWARD_FLOPS = 10**8
NT_DIMS = (((1,), (1,)), ((), ()))


def padded_2(value, sides, width, wrap):
    for axis, dim in sides:
        devices, length = (lax.axis_size(axis), value.shape[dim])
        up = [(i, (i + 1) % devices) for i in range(devices if wrap else devices - 1)]
        down = [(j, i) for i, j in up]
        last = lax.slice_in_dim(value, length - width, length, axis=dim)
        first = lax.slice_in_dim(value, 0, width, axis=dim)
        before = lax.ppermute(last, axis, up)
        after = lax.ppermute(first, axis, down)
        value = jnp.concatenate([before, value, after], axis=dim)
    return value


def add_rims(values):
    rowwise = padded_2(values, (("chan", 0),), 1, False)
    return padded_2(rowwise, (("tile", 1),), 1, True)


def body_by_owner(
    fields,
    diffusivity,
    owners,
    observed,
    usable,
    w_hidden,
    b_hidden,
    w_radiance,
    b_radiance,
    inv_cov,
):
    tile_count = lax.axis_size("tile")
    chan_count = lax.axis_size("chan")
    tile_index = lax.axis_index("tile")
    chan_index = lax.axis_index("chan")
    slot_count = observed.shape[0]
    capacity = slot_count // tile_count
    cells_across, cells_along, features = fields.shape
    own_cols = cells_across // 4 * (cells_along // 4)
    tile_cols = chan_count * own_cols
    hidden_dev = w_hidden.shape[1]
    owner_table = owners[:, 0].reshape(tile_count, tile_cols)
    owner_hits = (
        owner_table[:, :, None] == jnp.arange(tile_count, dtype=jnp.int32)[None, None, :]
    ).astype(jnp.int32)
    before = jnp.sum((jnp.cumsum(owner_hits, axis=1) - owner_hits) * owner_hits, axis=2)
    tallies = jnp.sum(owner_hits, axis=1)
    slot_of = lax.dynamic_index_in_dim(
        owner_table * capacity + before, tile_index, 0, keepdims=False
    )
    arriving = lax.dynamic_index_in_dim(tallies, tile_index, 1, keepdims=False)
    occupied = (jnp.arange(capacity, dtype=jnp.int32)[None, :] < arriving[:, None]).reshape(
        slot_count
    )
    grouped = fields.reshape(cells_across // 4, 4, cells_along // 4, 4, features)
    columns = (
        (jnp.sum(grouped, axis=(1, 3)) * 0.0625).reshape(own_cols, features).astype(jnp.bfloat16)
    )
    placer = (slot_of[None, :] == jnp.arange(slot_count, dtype=jnp.int32)[:, None]).astype(
        jnp.bfloat16
    )
    outgoing = jnp.dot(
        placer,
        lax.all_gather(columns, "chan", axis=0, tiled=True),
        preferred_element_type=jnp.float32,
    )
    incoming = lax.all_to_all(
        outgoing.astype(jnp.bfloat16), "tile", split_axis=0, concat_axis=0, tiled=True
    )
    preact = lax.dot_general(
        w_hidden, incoming, (((0,), (1,)), ((), ())), preferred_element_type=jnp.float32
    )
    preact = preact + b_hidden[:, None]
    squash = jax.nn.sigmoid(preact)
    active = (preact * squash).astype(jnp.bfloat16)
    radiance = lax.dot_general(
        lax.all_gather(active, "chan", axis=0, tiled=True),
        w_radiance,
        (((0,), (0,)), ((), ())),
        preferred_element_type=jnp.float32,
    )
    radiance = radiance + b_radiance[None, :]
    in_use = usable.astype(jnp.float32) * occupied.astype(jnp.float32)
    departure = ((radiance - observed.astype(jnp.float32)) * in_use[:, None]).astype(jnp.bfloat16)
    cotangent = jnp.dot(
        lax.all_gather(departure, "chan", axis=1, tiled=True),
        lax.all_gather(inv_cov, "tile", axis=0, tiled=True),
        preferred_element_type=jnp.float32,
    )
    cotangent = cotangent.astype(jnp.bfloat16)
    full_sum = lax.psum(
        lax.dot_general(w_radiance, cotangent, NT_DIMS, preferred_element_type=jnp.float32),
        "chan",
    )
    grad_hidden = lax.dynamic_slice_in_dim(full_sum, chan_index * hidden_dev, hidden_dev, 0)
    slope_term = squash * (1.0 + preact * (1.0 - squash))
    grad_pre = (grad_hidden * slope_term).astype(jnp.bfloat16)
    part_grad = lax.dot_general(
        grad_pre, w_hidden, (((0,), (1,)), ((), ())), preferred_element_type=jnp.float32
    )
    returned = lax.all_to_all(part_grad, "tile", split_axis=0, concat_axis=0, tiled=True)
    column_grad = lax.psum_scatter(
        jnp.take(returned, slot_of, axis=0), "chan", scatter_dimension=0, tiled=True
    )
    spread = jnp.repeat(
        column_grad.reshape(cells_across // 4, cells_along // 4, features), 4, axis=0
    )
    adjoint = jnp.repeat(spread, 4, axis=1) * 0.0625
    kappa_root = jnp.sqrt(diffusivity)
    root_rim = add_rims(kappa_root)
    coef_north = (kappa_root * root_rim[2:, 1:-1])[:, :, None]
    coef_south = (kappa_root * root_rim[:-2, 1:-1])[:, :, None]
    coef_east = (kappa_root * root_rim[1:-1, 2:])[:, :, None]
    coef_west = (kappa_root * root_rim[1:-1, :-2])[:, :, None]
    for sweep_index in range(2):
        padded = add_rims(adjoint)
        adjoint = (
            adjoint
            + coef_north * (padded[2:, 1:-1] - adjoint)
            + coef_south * (padded[:-2, 1:-1] - adjoint)
            + coef_east * (padded[1:-1, 2:] - adjoint)
            + coef_west * (padded[1:-1, :-2] - adjoint)
        )
    return adjoint


def up_to(value, multiple):
    return -(-value // multiple) * multiple


def dot(left, right):
    return jnp.dot(left, right, preferred_element_type=jnp.float32)


def dot_nt(left, right):
    return lax.dot_general(left, right, NT_DIMS, preferred_element_type=jnp.float32)


def split_three(value):
    high = value.astype(jnp.bfloat16).astype(jnp.float32)
    middle = (value - high).astype(jnp.bfloat16).astype(jnp.float32)
    return high, middle, value - high - middle


def call(
    kernel, out_shape, args, in_hbm=(), out_hbm=False, scratch=(), flops=0, vmem=VMEM_BYTES
):
    far, near = pl.BlockSpec(memory_space=pl.ANY), pl.BlockSpec(memory_space=pltpu.VMEM)
    bytes_accessed = sum(a.size * a.dtype.itemsize for a in args)
    return pl.pallas_call(
        kernel,
        out_shape=out_shape,
        in_specs=[far if k in in_hbm else near for k in range(len(args))],
        out_specs=jax.tree.map(lambda _: far if out_hbm else near, out_shape),
        scratch_shapes=list(scratch),
        compiler_params=pltpu.CompilerParams(vmem_limit_bytes=vmem),
        cost_estimate=pl.CostEstimate(
            flops=flops, bytes_accessed=bytes_accessed, transcendentals=0
        ),
    )(*args)


class Plan:
    def __init__(self, tiles, chans, fields, owners, observed, w_hidden):
        self.tiles, self.chans = tiles, chans
        self.across, self.along, self.features = fields
        self.own_cols = self.across // 4 * (self.along // 4)
        self.rows = owners[0]
        self.tile_cols = self.rows // tiles
        self.slots = observed[0]
        self.shard = observed[1]
        self.capacity = self.slots // tiles
        self.hidden = w_hidden[1]
        self.group = chans // tiles
        self.chips = chans // self.group
        self.steps = self.chips.bit_length() - 1
        self.lane = up_to(self.along, 128)
        self.flag_at = up_to(self.hidden, 128)
        self.width = max(
            up_to(self.features, 128),
            2 * self.flag_at,
            self.flag_at + up_to(self.slots, 128),
            3 * self.lane,
        )
        self.block = up_to(self.own_cols + 2 + self.across, 16)
        self.per_row = self.own_cols + 2
        self.patch = 3 * tiles * self.own_cols
        self.room = up_to(3 * self.per_row, 16)
        self.deep = up_to(self.features, 16)
        self.strips = self.chips * tiles * self.block

    def order(self, mask):
        return mask % self.group * self.chips + mask // self.group

    def layer(self, refs, k):
        at = k % self.chips * self.deep
        return refs[k // self.chips][at : at + self.features, :]

    def mask(self, k):
        return k % self.chips * self.group + k // self.chips


def prepare_kernel(p, fields_ref, diffusivity_ref, usable_ref, bias_ref, after_ref, out_ref, flat):
    flat[...] = jnp.zeros(flat.shape, jnp.float32)
    shape = (p.own_cols, p.along)
    row = lax.broadcasted_iota(jnp.int32, shape, 0)
    member = row == lax.broadcasted_iota(jnp.int32, shape, 1) // 4
    total = jnp.dot(
        member.astype(jnp.float32),
        fields_ref[0] + fields_ref[1] + fields_ref[2] + fields_ref[3],
        precision=lax.Precision.HIGHEST,
        preferred_element_type=jnp.float32,
    )
    flat[: p.own_cols, : p.features] = total * 0.0625
    at = p.own_cols
    high, middle, low = split_three(bias_ref[...].reshape(1, p.hidden))
    flat[at : at + 1, : p.hidden] = high
    flat[at : at + 1, p.flag_at : p.flag_at + p.hidden] = middle
    flat[at + 1 : at + 2, : p.hidden] = low
    flags = usable_ref[...].reshape(1, p.slots).astype(jnp.float32)
    flat[at + 1 : at + 2, p.flag_at : p.flag_at + p.slots] = flags
    for k, part in enumerate(split_three(diffusivity_ref[...])):
        flat[at + 2 : at + 2 + p.across, k * p.lane : k * p.lane + p.along] = part
    out_ref[...] = flat[...].astype(jnp.bfloat16)


def strip_of(p, tile, chan):
    other = chan ^ lax.axis_index("chan")
    return p.order(other) * p.tiles + (tile ^ lax.axis_index("tile"))


def index_kernel(p, cell_ref, *target_refs):
    t, c = lax.axis_index("tile"), lax.axis_index("chan")
    row = lax.broadcasted_iota(jnp.int32, cell_ref.shape, 0)
    reach = p.across + 4
    tile = (t + row // reach - 1 + p.tiles) % p.tiles
    cell = c * p.across - 2 + row % reach
    inside = (cell >= 0) & (cell < p.chans * p.across)
    cell = jnp.where(inside, cell, 0)
    wanted = strip_of(p, tile, cell // p.across) * p.block + p.own_cols + 2 + cell % p.across
    cell_ref[...] = jnp.where(inside, wanted, -1)

    target = lax.broadcasted_iota(jnp.int32, target_refs[0].shape, 0)
    chip, inner = target // p.patch, target % p.patch
    beside, inner = inner // (p.patch // 3) - 1, inner % (p.patch // 3)
    tile, along = inner // p.own_cols, inner % p.own_cols
    for k, target_ref in enumerate(target_refs):
        row = (chip ^ (c // p.group)) * p.group + (c % p.group ^ k) + beside
        wanted = tile * p.tile_cols + row * p.own_cols + along
        target_ref[...] = jnp.where((row >= 0) & (row < p.chans), wanted, -1)


def place_kernel(p, owners_ref, place_ref, source_ref):
    t = lax.axis_index("tile")
    across = owners_ref[...]
    shape = (p.rows, p.rows)
    row = lax.broadcasted_iota(jnp.int32, shape, 0)
    other = lax.broadcasted_iota(jnp.int32, shape, 1)
    owner = jnp.sum(jnp.where(row == other, across, 0), axis=1, keepdims=True)
    first = lax.broadcasted_iota(jnp.int32, owner.shape, 0)
    begin = first // p.tile_cols * p.tile_cols
    same = (owner == across) & (other >= begin) & (other < row)
    rank = jnp.sum(jnp.where(same, 1, 0), axis=1, keepdims=True)
    tile = first // p.tile_cols
    place_ref[...] = (owner ^ t) * p.slots + tile * p.capacity + rank
    source_ref[...] = (
        strip_of(p, tile, first % p.tile_cols // p.own_cols) * p.block + first % p.own_cols
    )


def join_kernel(count, *refs):
    ins, out_ref = refs[:count], refs[-1]
    size = out_ref.shape[0] // count
    for k, ref in enumerate(ins):
        out_ref[k * size : (k + 1) * size, :] = ref[...]


def stack_kernel(p, *refs):
    for k, ref in enumerate(refs[: p.chips]):
        refs[-1][k * p.deep : k * p.deep + p.features, :] = ref[...]
        refs[-1][k * p.deep + p.features : (k + 1) * p.deep, :] = jnp.zeros(
            (p.deep - p.features, p.hidden), jnp.bfloat16
        )


def one_hot(wanted, first, count):
    source = lax.broadcasted_iota(jnp.int32, (wanted.shape[0], count), 1)
    return (source + first == wanted).astype(jnp.bfloat16)


def forward_kernel(p, *refs):
    refs = list(refs)
    take = lambda n: [refs.pop(0) for _ in range(n)]
    place_ref, source_ref, cell_ref, bias_ref, w_radiance_ref = take(5)
    strip_refs, weight_refs = take(p.group), take(p.group)
    radiance_ref, in_use_ref, preact_ref, kappa_ref, active = refs
    c = lax.axis_index("chan")
    gathered = [ref[...] for ref in strip_refs]
    columns = sum(
        dot(one_hot(source_ref[...], k * p.strips, p.strips), strips)
        for k, strips in enumerate(gathered)
    )
    columns = columns.astype(jnp.bfloat16)[:, : p.features]
    for k in range(p.chans):
        member, chip = k // p.chips, k % p.chips
        at = chip * p.tiles * p.block + p.own_cols
        low = strip_refs[member][at : at + 2, :].astype(jnp.float32)
        bias = (
            low[:1, : p.hidden]
            + low[:1, p.flag_at : p.flag_at + p.hidden]
            + low[1:, : p.hidden]
        )
        preact = dot(columns, p.layer(weight_refs, k)) + bias
        preact_ref[k] = preact
        at = pl.multiple_of((c ^ p.mask(k)) * p.hidden, p.hidden)
        active[:, pl.ds(at, p.hidden)] = (preact * jax.nn.sigmoid(preact)).astype(jnp.bfloat16)
    in_use = jnp.zeros((p.rows, 1), jnp.float32)
    for k in range(p.tiles):
        slot = lax.broadcasted_iota(jnp.int32, (p.rows, p.slots), 1) + k * p.slots
        low = k * p.block + p.own_cols + 1
        flags = strip_refs[0][low : low + 1, p.flag_at : p.flag_at + p.slots]
        flags = jnp.where(place_ref[...] == slot, flags.astype(jnp.float32), 0.0)
        in_use = in_use + jnp.sum(flags, axis=1, keepdims=True)
    in_use_ref[...] = in_use
    radiance_ref[...] = dot(active[...], w_radiance_ref[...]) + bias_ref[...].reshape(1, p.shard)
    parts = sum(
        dot(one_hot(cell_ref[...], k * p.strips, p.strips), strips)
        for k, strips in enumerate(gathered)
    )
    kappa_ref[...] = sum(parts[:, k * p.lane : (k + 1) * p.lane] for k in range(3))


def depart_kernel(p, radiance_ref, in_use_ref, place_ref, *refs):
    seen_refs, part_refs = refs[: -p.steps], refs[-p.steps :]
    part, count = p.rows // p.steps, seen_refs[0].shape[0]
    for j, part_ref in enumerate(part_refs):
        at = slice(j * part, (j + 1) * part)
        observed = sum(
            dot(one_hot(place_ref[at, :], k * count, count), ref[...])
            for k, ref in enumerate(seen_refs)
        )
        departure = (radiance_ref[at, :] - observed) * in_use_ref[at, :]
        part_ref[...] = departure.astype(jnp.bfloat16)


def slope_kernel(preact_ref, slope_ref):
    for k in range(preact_ref.shape[0]):
        preact = preact_ref[k]
        squash = jax.nn.sigmoid(preact)
        slope_ref[k] = (squash * (1.0 + preact * (1.0 - squash))).T


def choose_kernel(p, choices, *refs):
    refs, out_ref = refs[:-2], refs[-1]
    size = refs[0].shape[0]
    role = (lax.axis_index("chan") // p.group) ^ lax.axis_index("tile")
    for place in range(p.chips):

        @pl.when(role == place)
        def _():
            for j in range(p.steps):
                out_ref[j * size : (j + 1) * size, :] = refs[choices[place, j]][...]


def near_kernel(p, depart_ref, inv_cov_ref, out_ref):
    at = pl.multiple_of(lax.axis_index("chan") % p.group * p.shard, p.shard)
    out_ref[...] = dot(depart_ref[...], inv_cov_ref[pl.ds(at, p.shard), :])


def backward_kernel(p, *refs):
    refs = list(refs)
    take = lambda n: [refs.pop(0) for _ in range(n)]
    w_radiance_ref, inv_cov_ref, slope_ref, near_ref = take(4)
    depart_refs, weight_refs, target_refs = take(p.group - 1), take(p.group), take(p.group - 1)
    out_refs = refs
    c = lax.axis_index("chan")
    cotangent = near_ref[...]
    for k, ref in enumerate(depart_refs):
        at = pl.multiple_of((c % p.group ^ (k + 1)) * p.shard, p.shard)
        cotangent = cotangent + dot(ref[...], inv_cov_ref[pl.ds(at, p.shard), :])
    cotangent = cotangent.T.astype(jnp.bfloat16)
    total = jnp.zeros((p.features, p.rows), jnp.float32)
    for k in range(p.chans):
        at = pl.multiple_of((c ^ p.mask(k)) * p.hidden, p.hidden)
        grad_hidden = dot(w_radiance_ref[pl.ds(at, p.hidden), :], cotangent)
        grad_pre = (grad_hidden * slope_ref[k]).astype(jnp.bfloat16)
        total = total + dot(p.layer(weight_refs, k), grad_pre)
    total = total.astype(jnp.bfloat16)
    out_refs[0][...] = total
    for target_ref, out_ref in zip(target_refs, out_refs[1:]):
        out_ref[...] = dot_nt(one_hot(target_ref[...], 0, p.rows), total).astype(jnp.bfloat16)


def keep_kernel(total_ref, target_ref, out_ref):
    pick = one_hot(target_ref[...], 0, total_ref.shape[1])
    out_ref[...] = dot_nt(pick, total_ref[...]).astype(jnp.bfloat16)


def add(refs, at=slice(None)):
    total = refs[0][at, :].astype(jnp.float32)
    for ref in refs[1:]:
        total = total + ref[at, :].astype(jnp.float32)
    return total


def add_group_kernel(p, *refs):
    ins, outs = refs[: p.group], refs[p.group :]
    for k, out_ref in enumerate(outs):
        out_ref[...] = add(ins, slice(k * p.patch, (k + 1) * p.patch)).astype(jnp.bfloat16)


def add_chips_kernel(p, *refs):
    ins, outs = refs[: p.chips], refs[p.chips :]
    total = add(ins).astype(jnp.bfloat16)
    target = lax.broadcasted_iota(jnp.int32, (p.room, 1), 0)
    row, along = target // p.per_row, target % p.per_row - 1
    count = p.tiles * p.own_cols
    for k, out_ref in enumerate(outs):
        cell = ((lax.axis_index("tile") ^ k) * p.own_cols + along + count) % count
        wanted = jnp.where(row < 3, row * count + cell, -1)
        out_ref[...] = dot(one_hot(wanted, 0, p.patch), total).astype(jnp.bfloat16)


def diffuse_kernel(p, edge, *refs):
    ins, root_ref, out_ref = refs[: p.tiles], refs[-2], refs[-1]
    total = add(ins) * 0.0625
    length = p.along + 2 * edge
    shape = (length, p.room)
    cell = lax.broadcasted_iota(jnp.int32, shape, 0)
    source = lax.broadcasted_iota(jnp.int32, shape, 1)
    column = (cell - edge + 4) // 4
    spread = []
    for k in range(3):
        pick = (source == column + k * p.per_row) & (column >= 0) & (column < p.per_row)
        spread.append(
            jnp.dot(
                pick.astype(jnp.float32),
                total,
                precision=lax.Precision.HIGHEST,
                preferred_element_type=jnp.float32,
            )
        )
    root = root_ref[...]
    state = [spread[(row + 2) // 4] for row in range(p.across + 4)]
    east_of = functools.partial(pltpu.roll, shift=length - 1, axis=0)
    west_of = functools.partial(pltpu.roll, shift=1, axis=0)
    north = root[:, :-1] * root[:, 1:]
    east, west = root * east_of(root), root * west_of(root)
    for sweep in range(2):
        fresh = list(state)
        for row in range(1 + sweep, p.across + 3 - sweep):
            here = state[row]
            fresh[row] = (
                here
                + north[:, row : row + 1] * (state[row + 1] - here)
                + north[:, row - 1 : row] * (state[row - 1] - here)
                + east[:, row : row + 1] * (east_of(here) - here)
                + west[:, row : row + 1] * (west_of(here) - here)
            )
        state = fresh
    for row in range(p.across):
        out_ref[row] = state[row + 2][edge : edge + p.along, : p.features]


def body_by_column(
    fields,
    diffusivity,
    owners,
    observed,
    usable,
    w_hidden,
    b_hidden,
    w_radiance,
    b_radiance,
    inv_cov,
):
    p = Plan(
        lax.axis_size("tile"),
        lax.axis_size("chan"),
        fields.shape,
        owners.shape,
        observed.shape,
        w_hidden.shape,
    )
    half, single = jnp.bfloat16, jnp.float32
    shape = jax.ShapeDtypeStruct
    both = ("tile", "chan")
    everyone = [(a, b) for a in range(p.tiles) for b in range(p.chans)]

    def flip(value, mask):
        return lax.ppermute(value, "chan", [(b, b ^ mask) for b in range(p.chans)])

    def trade(value, mask):
        return lax.ppermute(value, "tile", [(a, a ^ mask) for a in range(p.tiles)])

    def send(value, wanted):
        pairs = dict(wanted)
        pairs.update({target: source for source, target in wanted.items()})
        for a, b in everyone:
            if (a, b) not in pairs:
                pairs[a, b] = (a, b ^ 1)
        number = lambda place: place[0] * p.chans + place[1]
        return lax.ppermute(
            value, both, sorted((number(a), number(b)) for a, b in pairs.items())
        )

    def join(values, kernel_shape, after=()):
        return call(
            functools.partial(join_kernel, len(values)),
            shape(kernel_shape, half),
            [*values, *after],
            in_hbm=range(len(values), len(values) + len(after)),
        )

    def grow(value, over, after=()):
        return join([value, over(value)], (2 * value.shape[0],) + value.shape[1:], after)

    reach = p.across + 4
    cell, *targets = call(
        functools.partial(index_kernel, p),
        [shape((3 * reach, 1), jnp.int32)] + [shape((p.chips * p.patch, 1), jnp.int32)] * p.group,
        [],
        flops=10**9,
    )

    strips = call(
        functools.partial(prepare_kernel, p),
        shape((p.block, p.width), half),
        [fields, diffusivity, usable, b_hidden, cell],
        in_hbm=[4],
        scratch=[pltpu.VMEM((p.block, p.width), single)],
    )
    seen, stages, before = observed, [], ()
    bit = 1
    while bit < p.tiles:
        if 2 * bit < p.tiles:
            seen = grow(seen, lambda value: trade(value, bit))
            before = [seen]
        strips = grow(strips, lambda value: trade(value, bit), before)
        before = ()
        stages.append(strips)
        bit *= 2
    strips = join(
        [strips] + [flip(strips, k * p.group) for k in range(1, p.chips)], (p.strips, p.width)
    )
    strips = [strips] + [flip(strips, k) for k in range(1, p.group)]

    near = [w_hidden] + [flip(w_hidden, chip * p.group) for chip in range(1, p.chips)]
    near = call(
        functools.partial(stack_kernel, p),
        shape((p.chips * p.deep, p.hidden), half),
        near + [stages[-1]],
        in_hbm=[len(near)],
    )
    weights = [near] + [flip(near, k) for k in range(1, p.group)]

    far_half = p.tiles // 2
    seen = [
        seen,
        send(seen, {(b // p.group ^ far_half, b): (b // p.group, b) for b in range(p.chans)}),
    ]

    place, source = call(
        functools.partial(place_kernel, p),
        [shape((p.rows, 1), jnp.int32)] * 2,
        [owners.reshape(1, p.rows)],
        flops=SLACK_FLOPS,
    )
    radiance, in_use, preact, kappa = call(
        functools.partial(forward_kernel, p),
        [
            shape((p.rows, p.shard), single),
            shape((p.rows, 1), single),
            shape((p.chans, p.rows, p.hidden), single),
            shape((3 * reach, p.lane), single),
        ],
        [place, source, cell, b_radiance, w_radiance] + strips + weights,
        scratch=[pltpu.VMEM((p.rows, p.hidden * p.chans), half)],
        flops=FORWARD_FLOPS,
    )
    parts = call(
        functools.partial(depart_kernel, p),
        [shape((p.rows // p.steps, p.shard), half)] * p.steps,
        [radiance, in_use, place] + seen,
    )

    slope = call(
        slope_kernel,
        shape((p.chans, p.hidden, p.rows), single),
        [preact],
        flops=40 * preact.size,
    )

    pool, held, choices = list(parts), {}, {}
    for j in range(p.steps):
        held[0, j] = choices[0, j] = j
    for step in range(p.steps):
        for since in range(-1, step):
            for j in range(p.steps):
                order = [1 << (j + k) % p.steps for k in range(p.steps)]
                roles = [0] if since < 0 else [
                    order[since] + rest
                    for rest in range(p.chips)
                    if rest & ~sum(order[:since]) == 0
                ]
                wanted = {
                    (a, b): (a, b ^ order[step] * p.group)
                    for a, b in everyone
                    if (b // p.group ^ a) in roles
                }
                source = pool[choices[roles[0], j]]
                for role in roles:
                    choices[role + order[step], j] = len(pool)
                pool.append(send(source, wanted))
    chosen = call(
        functools.partial(choose_kernel, p, choices),
        shape((p.rows, p.shard), half),
        pool + [slope],
        in_hbm=[len(pool)],
    )
    depart = [flip(chosen, k) for k in range(1, p.group)]

    partial = call(
        functools.partial(near_kernel, p),
        shape((p.rows, p.shard), single),
        [chosen, inv_cov],
        flops=2 * p.rows * p.shard * p.shard,
    )
    partial = call(
        functools.partial(backward_kernel, p),
        [shape((p.features, p.rows), half)]
        + [shape((p.chips * p.patch, p.features), half)] * (p.group - 1),
        [w_radiance, inv_cov, slope, partial] + depart + weights + targets[1:],
        flops=2 * p.rows * (p.hidden * p.chans * (p.features + p.shard) + inv_cov.size),
    )
    kept = call(
        keep_kernel, shape((p.chips * p.patch, p.features), half), [partial[0], targets[0]]
    )
    partial = [kept] + [flip(partial[k], k) for k in range(1, p.group)]
    partial = call(
        functools.partial(add_group_kernel, p),
        [shape((p.patch, p.features), half)] * p.chips,
        partial,
    )
    partial = [flip(partial[k], k * p.group) for k in range(p.chips - 1, 0, -1)] + [partial[0]]
    partial = call(
        functools.partial(add_chips_kernel, p),
        [shape((p.room, p.features), half)] * p.tiles,
        partial,
    )
    partial = [trade(partial[k], k) for k in range(p.tiles - 1, 0, -1)] + [partial[0]]
    edge = 8
    kappa = kappa.reshape(3, reach, p.lane)
    root = jnp.sqrt(
        jnp.concatenate(
            [kappa[0, :, p.along - edge : p.along], kappa[1, :, : p.along], kappa[2, :, :edge]],
            axis=1,
        ).T
    )
    return call(
        functools.partial(diffuse_kernel, p, edge),
        shape(fields.shape, single),
        partial + [root],
        flops=100 * fields.size,
    )


def solution(mesh):
    tiles, chans = mesh.shape["tile"], mesh.shape["chan"]
    by_column = tiles > 1 and chans % tiles == 0 and chans & (chans - 1) == 0 and chans > tiles
    placed = (
        P("chan", "tile", None),
        P("chan", "tile"),
        P(),
        P("tile", "chan"),
        P("tile"),
        P(None, "chan"),
        P("chan"),
        P(None, "chan"),
        P("chan"),
        P("tile", "chan"),
    )
    return jax.shard_map(
        body_by_column if by_column else body_by_owner,
        mesh=mesh,
        in_specs=placed,
        out_specs=P("chan", "tile", None),
        check_vma=False,
    )
```

```python
import functools

import jax
import jax.numpy as jnp
from jax import lax
from jax.experimental import pallas as pl
from jax.experimental.pallas import tpu as pltpu
from jax.sharding import PartitionSpec as P

VMEM_BYTES = 24 * 1024 * 1024
SLACK_FLOPS = 2 * 10**9
FORWARD_FLOPS = 10**8
NT_DIMS = (((1,), (1,)), ((), ()))


def padded_2(value, sides, width, wrap):
    for axis, dim in sides:
        devices, length = (lax.axis_size(axis), value.shape[dim])
        up = [(i, (i + 1) % devices) for i in range(devices if wrap else devices - 1)]
        down = [(j, i) for i, j in up]
        last = lax.slice_in_dim(value, length - width, length, axis=dim)
        first = lax.slice_in_dim(value, 0, width, axis=dim)
        before = lax.ppermute(last, axis, up)
        after = lax.ppermute(first, axis, down)
        value = jnp.concatenate([before, value, after], axis=dim)
    return value


def add_rims(values):
    rowwise = padded_2(values, (("chan", 0),), 1, False)
    return padded_2(rowwise, (("tile", 1),), 1, True)


def body_by_owner(
    fields,
    diffusivity,
    owners,
    observed,
    usable,
    w_hidden,
    b_hidden,
    w_radiance,
    b_radiance,
    inv_cov,
):
    tile_count = lax.axis_size("tile")
    chan_count = lax.axis_size("chan")
    tile_index = lax.axis_index("tile")
    chan_index = lax.axis_index("chan")
    slot_count = observed.shape[0]
    capacity = slot_count // tile_count
    cells_across, cells_along, features = fields.shape
    own_cols = cells_across // 4 * (cells_along // 4)
    tile_cols = chan_count * own_cols
    hidden_dev = w_hidden.shape[1]
    owner_table = owners[:, 0].reshape(tile_count, tile_cols)
    owner_hits = (
        owner_table[:, :, None] == jnp.arange(tile_count, dtype=jnp.int32)[None, None, :]
    ).astype(jnp.int32)
    before = jnp.sum((jnp.cumsum(owner_hits, axis=1) - owner_hits) * owner_hits, axis=2)
    tallies = jnp.sum(owner_hits, axis=1)
    slot_of = lax.dynamic_index_in_dim(
        owner_table * capacity + before, tile_index, 0, keepdims=False
    )
    arriving = lax.dynamic_index_in_dim(tallies, tile_index, 1, keepdims=False)
    occupied = (jnp.arange(capacity, dtype=jnp.int32)[None, :] < arriving[:, None]).reshape(
        slot_count
    )
    grouped = fields.reshape(cells_across // 4, 4, cells_along // 4, 4, features)
    columns = (
        (jnp.sum(grouped, axis=(1, 3)) * 0.0625).reshape(own_cols, features).astype(jnp.bfloat16)
    )
    placer = (slot_of[None, :] == jnp.arange(slot_count, dtype=jnp.int32)[:, None]).astype(
        jnp.bfloat16
    )
    outgoing = jnp.dot(
        placer,
        lax.all_gather(columns, "chan", axis=0, tiled=True),
        preferred_element_type=jnp.float32,
    )
    incoming = lax.all_to_all(
        outgoing.astype(jnp.bfloat16), "tile", split_axis=0, concat_axis=0, tiled=True
    )
    preact = lax.dot_general(
        w_hidden, incoming, (((0,), (1,)), ((), ())), preferred_element_type=jnp.float32
    )
    preact = preact + b_hidden[:, None]
    squash = jax.nn.sigmoid(preact)
    active = (preact * squash).astype(jnp.bfloat16)
    radiance = lax.dot_general(
        lax.all_gather(active, "chan", axis=0, tiled=True),
        w_radiance,
        (((0,), (0,)), ((), ())),
        preferred_element_type=jnp.float32,
    )
    radiance = radiance + b_radiance[None, :]
    in_use = usable.astype(jnp.float32) * occupied.astype(jnp.float32)
    departure = ((radiance - observed.astype(jnp.float32)) * in_use[:, None]).astype(jnp.bfloat16)
    cotangent = jnp.dot(
        lax.all_gather(departure, "chan", axis=1, tiled=True),
        lax.all_gather(inv_cov, "tile", axis=0, tiled=True),
        preferred_element_type=jnp.float32,
    )
    cotangent = cotangent.astype(jnp.bfloat16)
    full_sum = lax.psum(
        lax.dot_general(w_radiance, cotangent, NT_DIMS, preferred_element_type=jnp.float32),
        "chan",
    )
    grad_hidden = lax.dynamic_slice_in_dim(full_sum, chan_index * hidden_dev, hidden_dev, 0)
    slope_term = squash * (1.0 + preact * (1.0 - squash))
    grad_pre = (grad_hidden * slope_term).astype(jnp.bfloat16)
    part_grad = lax.dot_general(
        grad_pre, w_hidden, (((0,), (1,)), ((), ())), preferred_element_type=jnp.float32
    )
    returned = lax.all_to_all(part_grad, "tile", split_axis=0, concat_axis=0, tiled=True)
    column_grad = lax.psum_scatter(
        jnp.take(returned, slot_of, axis=0), "chan", scatter_dimension=0, tiled=True
    )
    spread = jnp.repeat(
        column_grad.reshape(cells_across // 4, cells_along // 4, features), 4, axis=0
    )
    adjoint = jnp.repeat(spread, 4, axis=1) * 0.0625
    kappa_root = jnp.sqrt(diffusivity)
    root_rim = add_rims(kappa_root)
    coef_north = (kappa_root * root_rim[2:, 1:-1])[:, :, None]
    coef_south = (kappa_root * root_rim[:-2, 1:-1])[:, :, None]
    coef_east = (kappa_root * root_rim[1:-1, 2:])[:, :, None]
    coef_west = (kappa_root * root_rim[1:-1, :-2])[:, :, None]
    for sweep_index in range(2):
        padded = add_rims(adjoint)
        adjoint = (
            adjoint
            + coef_north * (padded[2:, 1:-1] - adjoint)
            + coef_south * (padded[:-2, 1:-1] - adjoint)
            + coef_east * (padded[1:-1, 2:] - adjoint)
            + coef_west * (padded[1:-1, :-2] - adjoint)
        )
    return adjoint


def up_to(value, multiple):
    return -(-value // multiple) * multiple


def dot(left, right):
    return jnp.dot(left, right, preferred_element_type=jnp.float32)


def dot_nt(left, right):
    return lax.dot_general(left, right, NT_DIMS, preferred_element_type=jnp.float32)


def split_three(value):
    high = value.astype(jnp.bfloat16).astype(jnp.float32)
    middle = (value - high).astype(jnp.bfloat16).astype(jnp.float32)
    return high, middle, value - high - middle


def call(
    kernel, out_shape, args, in_hbm=(), out_hbm=False, scratch=(), flops=0, vmem=VMEM_BYTES
):
    far, near = pl.BlockSpec(memory_space=pl.ANY), pl.BlockSpec(memory_space=pltpu.VMEM)
    bytes_accessed = sum(a.size * a.dtype.itemsize for a in args)
    return pl.pallas_call(
        kernel,
        out_shape=out_shape,
        in_specs=[far if k in in_hbm else near for k in range(len(args))],
        out_specs=jax.tree.map(lambda _: far if out_hbm else near, out_shape),
        scratch_shapes=list(scratch),
        compiler_params=pltpu.CompilerParams(vmem_limit_bytes=vmem),
        cost_estimate=pl.CostEstimate(
            flops=flops, bytes_accessed=bytes_accessed, transcendentals=0
        ),
    )(*args)


class Plan:
    def __init__(self, tiles, chans, fields, owners, observed, w_hidden):
        self.tiles, self.chans = tiles, chans
        self.across, self.along, self.features = fields
        self.own_cols = self.across // 4 * (self.along // 4)
        self.rows = owners[0]
        self.tile_cols = self.rows // tiles
        self.slots = observed[0]
        self.shard = observed[1]
        self.capacity = self.slots // tiles
        self.hidden = w_hidden[1]
        self.group = chans // tiles
        self.chips = chans // self.group
        self.steps = self.chips.bit_length() - 1
        self.lane = up_to(self.along, 128)
        self.flag_at = up_to(self.hidden, 128)
        self.width = max(
            up_to(self.features, 128),
            2 * self.flag_at,
            self.flag_at + up_to(self.slots, 128),
            3 * self.lane,
        )
        self.block = up_to(self.own_cols + 2 + self.across, 16)
        self.per_row = self.own_cols + 2
        self.patch = 3 * tiles * self.own_cols
        self.room = up_to(3 * self.per_row, 16)
        self.deep = up_to(self.features, 16)
        self.strips = self.chips * tiles * self.block

    def order(self, mask):
        return mask % self.group * self.chips + mask // self.group

    def layer(self, refs, k):
        at = k % self.chips * self.deep
        return refs[k // self.chips][at : at + self.features, :]

    def mask(self, k):
        return k % self.chips * self.group + k // self.chips


def prepare_kernel(p, fields_ref, diffusivity_ref, usable_ref, bias_ref, after_ref, out_ref, flat):
    flat[...] = jnp.zeros(flat.shape, jnp.float32)
    shape = (p.own_cols, p.along)
    row = lax.broadcasted_iota(jnp.int32, shape, 0)
    member = row == lax.broadcasted_iota(jnp.int32, shape, 1) // 4
    total = jnp.dot(
        member.astype(jnp.float32),
        fields_ref[0] + fields_ref[1] + fields_ref[2] + fields_ref[3],
        precision=lax.Precision.HIGHEST,
        preferred_element_type=jnp.float32,
    )
    flat[: p.own_cols, : p.features] = total * 0.0625
    at = p.own_cols
    high, middle, low = split_three(bias_ref[...].reshape(1, p.hidden))
    flat[at : at + 1, : p.hidden] = high
    flat[at : at + 1, p.flag_at : p.flag_at + p.hidden] = middle
    flat[at + 1 : at + 2, : p.hidden] = low
    flags = usable_ref[...].reshape(1, p.slots).astype(jnp.float32)
    flat[at + 1 : at + 2, p.flag_at : p.flag_at + p.slots] = flags
    for k, part in enumerate(split_three(diffusivity_ref[...])):
        flat[at + 2 : at + 2 + p.across, k * p.lane : k * p.lane + p.along] = part
    out_ref[...] = flat[...].astype(jnp.bfloat16)


def strip_of(p, tile, chan):
    other = chan ^ lax.axis_index("chan")
    return p.order(other) * p.tiles + (tile ^ lax.axis_index("tile"))


def index_kernel(p, cell_ref):
    t, c = lax.axis_index("tile"), lax.axis_index("chan")
    row = lax.broadcasted_iota(jnp.int32, cell_ref.shape, 0)
    reach = p.across + 4
    tile = (t + row // reach - 1 + p.tiles) % p.tiles
    cell = c * p.across - 2 + row % reach
    inside = (cell >= 0) & (cell < p.chans * p.across)
    cell = jnp.where(inside, cell, 0)
    wanted = strip_of(p, tile, cell // p.across) * p.block + p.own_cols + 2 + cell % p.across
    cell_ref[...] = jnp.where(inside, wanted, -1)


def place_kernel(p, owners_ref, place_ref, source_ref, *target_refs):
    t = lax.axis_index("tile")
    across = owners_ref[...]
    shape = (p.rows, p.rows)
    row = lax.broadcasted_iota(jnp.int32, shape, 0)
    other = lax.broadcasted_iota(jnp.int32, shape, 1)
    owner = jnp.sum(jnp.where(row == other, across, 0), axis=1, keepdims=True)
    first = lax.broadcasted_iota(jnp.int32, owner.shape, 0)
    begin = first // p.tile_cols * p.tile_cols
    same = (owner == across) & (other >= begin) & (other < row)
    rank = jnp.sum(jnp.where(same, 1, 0), axis=1, keepdims=True)
    tile = first // p.tile_cols
    place_ref[...] = (owner ^ t) * p.slots + tile * p.capacity + rank
    source_ref[...] = (
        strip_of(p, tile, first % p.tile_cols // p.own_cols) * p.block + first % p.own_cols
    )

    c = lax.axis_index("chan")
    target = lax.broadcasted_iota(jnp.int32, target_refs[0].shape, 0)
    chip, inner = target // p.patch, target % p.patch
    beside, inner = inner // (p.patch // 3) - 1, inner % (p.patch // 3)
    tile, along = inner // p.own_cols, inner % p.own_cols
    for k, target_ref in enumerate(target_refs):
        row = (chip ^ (c // p.group)) * p.group + (c % p.group ^ k) + beside
        wanted = tile * p.tile_cols + row * p.own_cols + along
        target_ref[...] = jnp.where((row >= 0) & (row < p.chans), wanted, -1)


def join_kernel(count, *refs):
    ins, out_ref = refs[:count], refs[-1]
    size = out_ref.shape[0] // count
    for k, ref in enumerate(ins):
        out_ref[k * size : (k + 1) * size, :] = ref[...]


def stack_kernel(p, *refs):
    for k, ref in enumerate(refs[: p.chips]):
        refs[-1][k * p.deep : k * p.deep + p.features, :] = ref[...]
        refs[-1][k * p.deep + p.features : (k + 1) * p.deep, :] = jnp.zeros(
            (p.deep - p.features, p.hidden), jnp.bfloat16
        )


def one_hot(wanted, first, count):
    source = lax.broadcasted_iota(jnp.int32, (wanted.shape[0], count), 1)
    return (source + first == wanted).astype(jnp.bfloat16)


def forward_kernel(p, *refs):
    refs = list(refs)
    take = lambda n: [refs.pop(0) for _ in range(n)]
    place_ref, source_ref, cell_ref, bias_ref, w_radiance_ref = take(5)
    strip_refs, weight_refs = take(p.group), take(p.group)
    radiance_ref, in_use_ref, preact_ref, kappa_ref, active = refs
    c = lax.axis_index("chan")
    gathered = [ref[...] for ref in strip_refs]
    columns = sum(
        dot(one_hot(source_ref[...], k * p.strips, p.strips), strips)
        for k, strips in enumerate(gathered)
    )
    columns = columns.astype(jnp.bfloat16)[:, : p.features]
    for k in range(p.chans):
        member, chip = k // p.chips, k % p.chips
        at = chip * p.tiles * p.block + p.own_cols
        low = strip_refs[member][at : at + 2, :].astype(jnp.float32)
        bias = (
            low[:1, : p.hidden]
            + low[:1, p.flag_at : p.flag_at + p.hidden]
            + low[1:, : p.hidden]
        )
        preact = dot(columns, p.layer(weight_refs, k)) + bias
        preact_ref[k] = preact
        at = pl.multiple_of((c ^ p.mask(k)) * p.hidden, p.hidden)
        active[:, pl.ds(at, p.hidden)] = (preact * jax.nn.sigmoid(preact)).astype(jnp.bfloat16)
    in_use = jnp.zeros((p.rows, 1), jnp.float32)
    for k in range(p.tiles):
        slot = lax.broadcasted_iota(jnp.int32, (p.rows, p.slots), 1) + k * p.slots
        low = k * p.block + p.own_cols + 1
        flags = strip_refs[0][low : low + 1, p.flag_at : p.flag_at + p.slots]
        flags = jnp.where(place_ref[...] == slot, flags.astype(jnp.float32), 0.0)
        in_use = in_use + jnp.sum(flags, axis=1, keepdims=True)
    in_use_ref[...] = in_use
    radiance_ref[...] = dot(active[...], w_radiance_ref[...]) + bias_ref[...].reshape(1, p.shard)
    parts = sum(
        dot(one_hot(cell_ref[...], k * p.strips, p.strips), strips)
        for k, strips in enumerate(gathered)
    )
    kappa_ref[...] = sum(parts[:, k * p.lane : (k + 1) * p.lane] for k in range(3))


def depart_kernel(p, radiance_ref, in_use_ref, place_ref, *refs):
    seen_refs, part_refs = refs[: -p.steps], refs[-p.steps :]
    part, count = p.rows // p.steps, seen_refs[0].shape[0]
    for j, part_ref in enumerate(part_refs):
        at = slice(j * part, (j + 1) * part)
        observed = sum(
            dot(one_hot(place_ref[at, :], k * count, count), ref[...])
            for k, ref in enumerate(seen_refs)
        )
        departure = (radiance_ref[at, :] - observed) * in_use_ref[at, :]
        part_ref[...] = departure.astype(jnp.bfloat16)


def slope_kernel(preact_ref, slope_ref):
    for k in range(preact_ref.shape[0]):
        preact = preact_ref[k]
        squash = jax.nn.sigmoid(preact)
        slope_ref[k] = (squash * (1.0 + preact * (1.0 - squash))).T


def choose_kernel(p, choices, *refs):
    refs, out_ref = refs[:-2], refs[-1]
    size = refs[0].shape[0]
    role = (lax.axis_index("chan") // p.group) ^ lax.axis_index("tile")
    for place in range(p.chips):

        @pl.when(role == place)
        def _():
            for j in range(p.steps):
                out_ref[j * size : (j + 1) * size, :] = refs[choices[place, j]][...]


def near_kernel(p, depart_ref, inv_cov_ref, out_ref):
    at = pl.multiple_of(lax.axis_index("chan") % p.group * p.shard, p.shard)
    out_ref[...] = dot(depart_ref[...], inv_cov_ref[pl.ds(at, p.shard), :])


def backward_kernel(p, *refs):
    refs = list(refs)
    take = lambda n: [refs.pop(0) for _ in range(n)]
    w_radiance_ref, inv_cov_ref, slope_ref, near_ref = take(4)
    depart_refs, weight_refs, target_refs = take(p.group - 1), take(p.group), take(p.group - 1)
    out_refs = refs
    c = lax.axis_index("chan")
    cotangent = near_ref[...]
    for k, ref in enumerate(depart_refs):
        at = pl.multiple_of((c % p.group ^ (k + 1)) * p.shard, p.shard)
        cotangent = cotangent + dot(ref[...], inv_cov_ref[pl.ds(at, p.shard), :])
    cotangent = cotangent.T.astype(jnp.bfloat16)
    total = jnp.zeros((p.features, p.rows), jnp.float32)
    for k in range(p.chans):
        at = pl.multiple_of((c ^ p.mask(k)) * p.hidden, p.hidden)
        grad_hidden = dot(w_radiance_ref[pl.ds(at, p.hidden), :], cotangent)
        grad_pre = (grad_hidden * slope_ref[k]).astype(jnp.bfloat16)
        total = total + dot(p.layer(weight_refs, k), grad_pre)
    total = total.astype(jnp.bfloat16)
    out_refs[0][...] = total
    for target_ref, out_ref in zip(target_refs, out_refs[1:]):
        out_ref[...] = dot_nt(one_hot(target_ref[...], 0, p.rows), total).astype(jnp.bfloat16)


def keep_kernel(total_ref, target_ref, out_ref):
    pick = one_hot(target_ref[...], 0, total_ref.shape[1])
    out_ref[...] = dot_nt(pick, total_ref[...]).astype(jnp.bfloat16)


def add(refs, at=slice(None)):
    total = refs[0][at, :].astype(jnp.float32)
    for ref in refs[1:]:
        total = total + ref[at, :].astype(jnp.float32)
    return total


def add_group_kernel(p, *refs):
    ins, outs = refs[: p.group], refs[p.group :]
    for k, out_ref in enumerate(outs):
        out_ref[...] = add(ins, slice(k * p.patch, (k + 1) * p.patch)).astype(jnp.bfloat16)


def add_chips_kernel(p, *refs):
    ins, outs = refs[: p.chips], refs[p.chips :]
    total = add(ins).astype(jnp.bfloat16)
    target = lax.broadcasted_iota(jnp.int32, (p.room, 1), 0)
    row, along = target // p.per_row, target % p.per_row - 1
    count = p.tiles * p.own_cols
    for k, out_ref in enumerate(outs):
        cell = ((lax.axis_index("tile") ^ k) * p.own_cols + along + count) % count
        wanted = jnp.where(row < 3, row * count + cell, -1)
        out_ref[...] = dot(one_hot(wanted, 0, p.patch), total).astype(jnp.bfloat16)


def diffuse_kernel(p, edge, *refs):
    ins, root_ref, out_ref = refs[: p.tiles], refs[-2], refs[-1]
    total = add(ins) * 0.0625
    length = p.along + 2 * edge
    shape = (length, p.room)
    cell = lax.broadcasted_iota(jnp.int32, shape, 0)
    source = lax.broadcasted_iota(jnp.int32, shape, 1)
    column = (cell - edge + 4) // 4
    spread = []
    for k in range(3):
        pick = (source == column + k * p.per_row) & (column >= 0) & (column < p.per_row)
        spread.append(
            jnp.dot(
                pick.astype(jnp.float32),
                total,
                precision=lax.Precision.HIGHEST,
                preferred_element_type=jnp.float32,
            )
        )
    root = root_ref[...]
    state = [spread[(row + 2) // 4] for row in range(p.across + 4)]
    east_of = functools.partial(pltpu.roll, shift=length - 1, axis=0)
    west_of = functools.partial(pltpu.roll, shift=1, axis=0)
    north = root[:, :-1] * root[:, 1:]
    east, west = root * east_of(root), root * west_of(root)
    for sweep in range(2):
        fresh = list(state)
        for row in range(1 + sweep, p.across + 3 - sweep):
            here = state[row]
            fresh[row] = (
                here
                + north[:, row : row + 1] * (state[row + 1] - here)
                + north[:, row - 1 : row] * (state[row - 1] - here)
                + east[:, row : row + 1] * (east_of(here) - here)
                + west[:, row : row + 1] * (west_of(here) - here)
            )
        state = fresh
    for row in range(p.across):
        out_ref[row] = state[row + 2][edge : edge + p.along, : p.features]


def body_by_column(
    fields,
    diffusivity,
    owners,
    observed,
    usable,
    w_hidden,
    b_hidden,
    w_radiance,
    b_radiance,
    inv_cov,
):
    p = Plan(
        lax.axis_size("tile"),
        lax.axis_size("chan"),
        fields.shape,
        owners.shape,
        observed.shape,
        w_hidden.shape,
    )
    half, single = jnp.bfloat16, jnp.float32
    shape = jax.ShapeDtypeStruct
    both = ("tile", "chan")
    everyone = [(a, b) for a in range(p.tiles) for b in range(p.chans)]

    def flip(value, mask):
        return lax.ppermute(value, "chan", [(b, b ^ mask) for b in range(p.chans)])

    def trade(value, mask):
        return lax.ppermute(value, "tile", [(a, a ^ mask) for a in range(p.tiles)])

    def send(value, wanted):
        pairs = dict(wanted)
        pairs.update({target: source for source, target in wanted.items()})
        for a, b in everyone:
            if (a, b) not in pairs:
                pairs[a, b] = (a, b ^ 1)
        number = lambda place: place[0] * p.chans + place[1]
        return lax.ppermute(
            value, both, sorted((number(a), number(b)) for a, b in pairs.items())
        )

    def join(values, kernel_shape, after=()):
        return call(
            functools.partial(join_kernel, len(values)),
            shape(kernel_shape, half),
            [*values, *after],
            in_hbm=range(len(values), len(values) + len(after)),
        )

    def grow(value, over, after=()):
        return join([value, over(value)], (2 * value.shape[0],) + value.shape[1:], after)

    reach = p.across + 4
    cell = call(
        functools.partial(index_kernel, p),
        shape((3 * reach, 1), jnp.int32),
        [],
        flops=10**9,
    )

    strips = call(
        functools.partial(prepare_kernel, p),
        shape((p.block, p.width), half),
        [fields, diffusivity, usable, b_hidden, cell],
        in_hbm=[4],
        scratch=[pltpu.VMEM((p.block, p.width), single)],
    )
    seen, stages, before = observed, [], ()
    bit = 1
    while bit < p.tiles:
        if 2 * bit < p.tiles:
            seen = grow(seen, lambda value: trade(value, bit))
            before = [seen]
        strips = grow(strips, lambda value: trade(value, bit), before)
        before = ()
        stages.append(strips)
        bit *= 2
    strips = join(
        [strips] + [flip(strips, k * p.group) for k in range(1, p.chips)], (p.strips, p.width)
    )
    strips = [strips] + [flip(strips, k) for k in range(1, p.group)]

    near = [w_hidden] + [flip(w_hidden, chip * p.group) for chip in range(1, p.chips)]
    near = call(
        functools.partial(stack_kernel, p),
        shape((p.chips * p.deep, p.hidden), half),
        near + [stages[-1]],
        in_hbm=[len(near)],
    )
    weights = [near] + [flip(near, k) for k in range(1, p.group)]

    far_half = p.tiles // 2
    seen = [
        seen,
        send(seen, {(b // p.group ^ far_half, b): (b // p.group, b) for b in range(p.chans)}),
    ]

    place, source, *targets = call(
        functools.partial(place_kernel, p),
        [shape((p.rows, 1), jnp.int32)] * 2
        + [shape((p.chips * p.patch, 1), jnp.int32)] * p.group,
        [owners.reshape(1, p.rows)],
        flops=SLACK_FLOPS,
    )
    radiance, in_use, preact, kappa = call(
        functools.partial(forward_kernel, p),
        [
            shape((p.rows, p.shard), single),
            shape((p.rows, 1), single),
            shape((p.chans, p.rows, p.hidden), single),
            shape((3 * reach, p.lane), single),
        ],
        [place, source, cell, b_radiance, w_radiance] + strips + weights,
        scratch=[pltpu.VMEM((p.rows, p.hidden * p.chans), half)],
        flops=FORWARD_FLOPS,
    )
    parts = call(
        functools.partial(depart_kernel, p),
        [shape((p.rows // p.steps, p.shard), half)] * p.steps,
        [radiance, in_use, place] + seen,
    )

    slope = call(
        slope_kernel,
        shape((p.chans, p.hidden, p.rows), single),
        [preact],
        flops=40 * preact.size,
    )

    pool, held, choices = list(parts), {}, {}
    for j in range(p.steps):
        held[0, j] = choices[0, j] = j
    for step in range(p.steps):
        for since in range(-1, step):
            for j in range(p.steps):
                order = [1 << (j + k) % p.steps for k in range(p.steps)]
                roles = [0] if since < 0 else [
                    order[since] + rest
                    for rest in range(p.chips)
                    if rest & ~sum(order[:since]) == 0
                ]
                wanted = {
                    (a, b): (a, b ^ order[step] * p.group)
                    for a, b in everyone
                    if (b // p.group ^ a) in roles
                }
                source = pool[choices[roles[0], j]]
                for role in roles:
                    choices[role + order[step], j] = len(pool)
                pool.append(send(source, wanted))
    chosen = call(
        functools.partial(choose_kernel, p, choices),
        shape((p.rows, p.shard), half),
        pool + [slope],
        in_hbm=[len(pool)],
    )
    depart = [flip(chosen, k) for k in range(1, p.group)]

    partial = call(
        functools.partial(near_kernel, p),
        shape((p.rows, p.shard), single),
        [chosen, inv_cov],
        flops=2 * p.rows * p.shard * p.shard,
    )
    partial = call(
        functools.partial(backward_kernel, p),
        [shape((p.features, p.rows), half)]
        + [shape((p.chips * p.patch, p.features), half)] * (p.group - 1),
        [w_radiance, inv_cov, slope, partial] + depart + weights + targets[1:],
        flops=2 * p.rows * (p.hidden * p.chans * (p.features + p.shard) + inv_cov.size),
    )
    kept = call(
        keep_kernel, shape((p.chips * p.patch, p.features), half), [partial[0], targets[0]]
    )
    partial = [kept] + [flip(partial[k], k) for k in range(1, p.group)]
    partial = call(
        functools.partial(add_group_kernel, p),
        [shape((p.patch, p.features), half)] * p.chips,
        partial,
    )
    partial = [flip(partial[k], k * p.group) for k in range(p.chips - 1, 0, -1)] + [partial[0]]
    partial = call(
        functools.partial(add_chips_kernel, p),
        [shape((p.room, p.features), half)] * p.tiles,
        partial,
    )
    partial = [trade(partial[k], k) for k in range(p.tiles - 1, 0, -1)] + [partial[0]]
    edge = 8
    kappa = kappa.reshape(3, reach, p.lane)
    root = jnp.sqrt(
        jnp.concatenate(
            [kappa[0, :, p.along - edge : p.along], kappa[1, :, : p.along], kappa[2, :, :edge]],
            axis=1,
        ).T
    )
    return call(
        functools.partial(diffuse_kernel, p, edge),
        shape(fields.shape, single),
        partial + [root],
        flops=100 * fields.size,
    )


def solution(mesh):
    tiles, chans = mesh.shape["tile"], mesh.shape["chan"]
    by_column = tiles > 1 and chans % tiles == 0 and chans & (chans - 1) == 0 and chans > tiles
    placed = (
        P("chan", "tile", None),
        P("chan", "tile"),
        P(),
        P("tile", "chan"),
        P("tile"),
        P(None, "chan"),
        P("chan"),
        P(None, "chan"),
        P("chan"),
        P("tile", "chan"),
    )
    return jax.shard_map(
        body_by_column if by_column else body_by_owner,
        mesh=mesh,
        in_specs=placed,
        out_specs=P("chan", "tile", None),
        check_vma=False,
    )
```

```python
import functools

import jax
import jax.numpy as jnp
from jax import lax
from jax.experimental import pallas as pl
from jax.experimental.pallas import tpu as pltpu
from jax.sharding import PartitionSpec as P

VMEM_BYTES = 24 * 1024 * 1024
SLACK_FLOPS = 2 * 10**9
FORWARD_FLOPS = 10**8
NT_DIMS = (((1,), (1,)), ((), ()))


def padded_2(value, sides, width, wrap):
    for axis, dim in sides:
        devices, length = (lax.axis_size(axis), value.shape[dim])
        up = [(i, (i + 1) % devices) for i in range(devices if wrap else devices - 1)]
        down = [(j, i) for i, j in up]
        last = lax.slice_in_dim(value, length - width, length, axis=dim)
        first = lax.slice_in_dim(value, 0, width, axis=dim)
        before = lax.ppermute(last, axis, up)
        after = lax.ppermute(first, axis, down)
        value = jnp.concatenate([before, value, after], axis=dim)
    return value


def add_rims(values):
    rowwise = padded_2(values, (("chan", 0),), 1, False)
    return padded_2(rowwise, (("tile", 1),), 1, True)


def body_by_owner(
    fields,
    diffusivity,
    owners,
    observed,
    usable,
    w_hidden,
    b_hidden,
    w_radiance,
    b_radiance,
    inv_cov,
):
    tile_count = lax.axis_size("tile")
    chan_count = lax.axis_size("chan")
    tile_index = lax.axis_index("tile")
    chan_index = lax.axis_index("chan")
    slot_count = observed.shape[0]
    capacity = slot_count // tile_count
    cells_across, cells_along, features = fields.shape
    own_cols = cells_across // 4 * (cells_along // 4)
    tile_cols = chan_count * own_cols
    hidden_dev = w_hidden.shape[1]
    owner_table = owners[:, 0].reshape(tile_count, tile_cols)
    owner_hits = (
        owner_table[:, :, None] == jnp.arange(tile_count, dtype=jnp.int32)[None, None, :]
    ).astype(jnp.int32)
    before = jnp.sum((jnp.cumsum(owner_hits, axis=1) - owner_hits) * owner_hits, axis=2)
    tallies = jnp.sum(owner_hits, axis=1)
    slot_of = lax.dynamic_index_in_dim(
        owner_table * capacity + before, tile_index, 0, keepdims=False
    )
    arriving = lax.dynamic_index_in_dim(tallies, tile_index, 1, keepdims=False)
    occupied = (jnp.arange(capacity, dtype=jnp.int32)[None, :] < arriving[:, None]).reshape(
        slot_count
    )
    grouped = fields.reshape(cells_across // 4, 4, cells_along // 4, 4, features)
    columns = (
        (jnp.sum(grouped, axis=(1, 3)) * 0.0625).reshape(own_cols, features).astype(jnp.bfloat16)
    )
    placer = (slot_of[None, :] == jnp.arange(slot_count, dtype=jnp.int32)[:, None]).astype(
        jnp.bfloat16
    )
    outgoing = jnp.dot(
        placer,
        lax.all_gather(columns, "chan", axis=0, tiled=True),
        preferred_element_type=jnp.float32,
    )
    incoming = lax.all_to_all(
        outgoing.astype(jnp.bfloat16), "tile", split_axis=0, concat_axis=0, tiled=True
    )
    preact = lax.dot_general(
        w_hidden, incoming, (((0,), (1,)), ((), ())), preferred_element_type=jnp.float32
    )
    preact = preact + b_hidden[:, None]
    squash = jax.nn.sigmoid(preact)
    active = (preact * squash).astype(jnp.bfloat16)
    radiance = lax.dot_general(
        lax.all_gather(active, "chan", axis=0, tiled=True),
        w_radiance,
        (((0,), (0,)), ((), ())),
        preferred_element_type=jnp.float32,
    )
    radiance = radiance + b_radiance[None, :]
    in_use = usable.astype(jnp.float32) * occupied.astype(jnp.float32)
    departure = ((radiance - observed.astype(jnp.float32)) * in_use[:, None]).astype(jnp.bfloat16)
    cotangent = jnp.dot(
        lax.all_gather(departure, "chan", axis=1, tiled=True),
        lax.all_gather(inv_cov, "tile", axis=0, tiled=True),
        preferred_element_type=jnp.float32,
    )
    cotangent = cotangent.astype(jnp.bfloat16)
    full_sum = lax.psum(
        lax.dot_general(w_radiance, cotangent, NT_DIMS, preferred_element_type=jnp.float32),
        "chan",
    )
    grad_hidden = lax.dynamic_slice_in_dim(full_sum, chan_index * hidden_dev, hidden_dev, 0)
    slope_term = squash * (1.0 + preact * (1.0 - squash))
    grad_pre = (grad_hidden * slope_term).astype(jnp.bfloat16)
    part_grad = lax.dot_general(
        grad_pre, w_hidden, (((0,), (1,)), ((), ())), preferred_element_type=jnp.float32
    )
    returned = lax.all_to_all(part_grad, "tile", split_axis=0, concat_axis=0, tiled=True)
    column_grad = lax.psum_scatter(
        jnp.take(returned, slot_of, axis=0), "chan", scatter_dimension=0, tiled=True
    )
    spread = jnp.repeat(
        column_grad.reshape(cells_across // 4, cells_along // 4, features), 4, axis=0
    )
    adjoint = jnp.repeat(spread, 4, axis=1) * 0.0625
    kappa_root = jnp.sqrt(diffusivity)
    root_rim = add_rims(kappa_root)
    coef_north = (kappa_root * root_rim[2:, 1:-1])[:, :, None]
    coef_south = (kappa_root * root_rim[:-2, 1:-1])[:, :, None]
    coef_east = (kappa_root * root_rim[1:-1, 2:])[:, :, None]
    coef_west = (kappa_root * root_rim[1:-1, :-2])[:, :, None]
    for sweep_index in range(2):
        padded = add_rims(adjoint)
        adjoint = (
            adjoint
            + coef_north * (padded[2:, 1:-1] - adjoint)
            + coef_south * (padded[:-2, 1:-1] - adjoint)
            + coef_east * (padded[1:-1, 2:] - adjoint)
            + coef_west * (padded[1:-1, :-2] - adjoint)
        )
    return adjoint


def up_to(value, multiple):
    return -(-value // multiple) * multiple


def dot(left, right):
    return jnp.dot(left, right, preferred_element_type=jnp.float32)


def dot_nt(left, right):
    return lax.dot_general(left, right, NT_DIMS, preferred_element_type=jnp.float32)


def split_three(value):
    high = value.astype(jnp.bfloat16).astype(jnp.float32)
    middle = (value - high).astype(jnp.bfloat16).astype(jnp.float32)
    return high, middle, value - high - middle


def call(
    kernel, out_shape, args, in_hbm=(), out_hbm=False, scratch=(), flops=0, vmem=VMEM_BYTES
):
    far, near = pl.BlockSpec(memory_space=pl.ANY), pl.BlockSpec(memory_space=pltpu.VMEM)
    bytes_accessed = sum(a.size * a.dtype.itemsize for a in args)
    return pl.pallas_call(
        kernel,
        out_shape=out_shape,
        in_specs=[far if k in in_hbm else near for k in range(len(args))],
        out_specs=jax.tree.map(lambda _: far if out_hbm else near, out_shape),
        scratch_shapes=list(scratch),
        compiler_params=pltpu.CompilerParams(vmem_limit_bytes=vmem),
        cost_estimate=pl.CostEstimate(
            flops=flops, bytes_accessed=bytes_accessed, transcendentals=0
        ),
    )(*args)


class Plan:
    def __init__(self, tiles, chans, fields, owners, observed, w_hidden):
        self.tiles, self.chans = tiles, chans
        self.across, self.along, self.features = fields
        self.own_cols = self.across // 4 * (self.along // 4)
        self.rows = owners[0]
        self.tile_cols = self.rows // tiles
        self.slots = observed[0]
        self.shard = observed[1]
        self.capacity = self.slots // tiles
        self.hidden = w_hidden[1]
        self.group = chans // tiles
        self.chips = chans // self.group
        self.steps = self.chips.bit_length() - 1
        self.lane = up_to(self.along, 128)
        self.flag_at = up_to(self.hidden, 128)
        self.width = max(
            up_to(self.features, 128),
            2 * self.flag_at,
            self.flag_at + up_to(self.slots, 128),
            3 * self.lane,
        )
        self.block = up_to(self.own_cols + 2 + self.across, 16)
        self.per_row = self.own_cols + 2
        self.patch = 3 * tiles * self.own_cols
        self.room = up_to(3 * self.per_row, 16)
        self.deep = up_to(self.features, 16)
        self.strips = self.chips * tiles * self.block

    def order(self, mask):
        return mask % self.group * self.chips + mask // self.group

    def layer(self, refs, k):
        at = k % self.chips * self.deep
        return refs[k // self.chips][at : at + self.features, :]

    def mask(self, k):
        return k % self.chips * self.group + k // self.chips


def prepare_kernel(p, fields_ref, diffusivity_ref, usable_ref, bias_ref, after_ref, out_ref, flat):
    flat[...] = jnp.zeros(flat.shape, jnp.float32)
    shape = (p.own_cols, p.along)
    row = lax.broadcasted_iota(jnp.int32, shape, 0)
    member = row == lax.broadcasted_iota(jnp.int32, shape, 1) // 4
    total = jnp.dot(
        member.astype(jnp.float32),
        fields_ref[0] + fields_ref[1] + fields_ref[2] + fields_ref[3],
        precision=lax.Precision.HIGHEST,
        preferred_element_type=jnp.float32,
    )
    flat[: p.own_cols, : p.features] = total * 0.0625
    at = p.own_cols
    high, middle, low = split_three(bias_ref[...].reshape(1, p.hidden))
    flat[at : at + 1, : p.hidden] = high
    flat[at : at + 1, p.flag_at : p.flag_at + p.hidden] = middle
    flat[at + 1 : at + 2, : p.hidden] = low
    flags = usable_ref[...].reshape(1, p.slots).astype(jnp.float32)
    flat[at + 1 : at + 2, p.flag_at : p.flag_at + p.slots] = flags
    for k, part in enumerate(split_three(diffusivity_ref[...])):
        flat[at + 2 : at + 2 + p.across, k * p.lane : k * p.lane + p.along] = part
    out_ref[...] = flat[...].astype(jnp.bfloat16)


def strip_of(p, tile, chan):
    other = chan ^ lax.axis_index("chan")
    return p.order(other) * p.tiles + (tile ^ lax.axis_index("tile"))


def index_kernel(p, cell_ref):
    t, c = lax.axis_index("tile"), lax.axis_index("chan")
    row = lax.broadcasted_iota(jnp.int32, cell_ref.shape, 0)
    reach = p.across + 4
    tile = (t + row // reach - 1 + p.tiles) % p.tiles
    cell = c * p.across - 2 + row % reach
    inside = (cell >= 0) & (cell < p.chans * p.across)
    cell = jnp.where(inside, cell, 0)
    wanted = strip_of(p, tile, cell // p.across) * p.block + p.own_cols + 2 + cell % p.across
    cell_ref[...] = jnp.where(inside, wanted, -1)


def place_kernel(p, owners_ref, place_ref, source_ref, *target_refs):
    t = lax.axis_index("tile")
    across = owners_ref[...]
    shape = (p.rows, p.rows)
    row = lax.broadcasted_iota(jnp.int32, shape, 0)
    other = lax.broadcasted_iota(jnp.int32, shape, 1)
    owner = jnp.sum(jnp.where(row == other, across, 0), axis=1, keepdims=True)
    first = lax.broadcasted_iota(jnp.int32, owner.shape, 0)
    begin = first // p.tile_cols * p.tile_cols
    same = (owner == across) & (other >= begin) & (other < row)
    rank = jnp.sum(jnp.where(same, 1, 0), axis=1, keepdims=True)
    tile = first // p.tile_cols
    place_ref[...] = (owner ^ t) * p.slots + tile * p.capacity + rank
    source_ref[...] = (
        strip_of(p, tile, first % p.tile_cols // p.own_cols) * p.block + first % p.own_cols
    )

    c = lax.axis_index("chan")
    target = lax.broadcasted_iota(jnp.int32, target_refs[0].shape, 0)
    chip, inner = target // p.patch, target % p.patch
    beside, inner = inner // (p.patch // 3) - 1, inner % (p.patch // 3)
    tile, along = inner // p.own_cols, inner % p.own_cols
    for k, target_ref in enumerate(target_refs):
        row = (chip ^ (c // p.group)) * p.group + (c % p.group ^ k) + beside
        wanted = tile * p.tile_cols + row * p.own_cols + along
        target_ref[...] = jnp.where((row >= 0) & (row < p.chans), wanted, -1)


def join_kernel(count, *refs):
    ins, out_ref = refs[:count], refs[-1]
    size = out_ref.shape[0] // count
    for k, ref in enumerate(ins):
        out_ref[k * size : (k + 1) * size, :] = ref[...]


def stack_kernel(p, *refs):
    for k, ref in enumerate(refs[: p.chips]):
        refs[-1][k * p.deep : k * p.deep + p.features, :] = ref[...]
        refs[-1][k * p.deep + p.features : (k + 1) * p.deep, :] = jnp.zeros(
            (p.deep - p.features, p.hidden), jnp.bfloat16
        )


def one_hot(wanted, first, count):
    source = lax.broadcasted_iota(jnp.int32, (wanted.shape[0], count), 1)
    return (source + first == wanted).astype(jnp.bfloat16)


def forward_kernel(p, *refs):
    refs = list(refs)
    take = lambda n: [refs.pop(0) for _ in range(n)]
    place_ref, source_ref, cell_ref, bias_ref, w_radiance_ref = take(5)
    strip_refs, weight_refs = take(p.group), take(p.group)
    radiance_ref, in_use_ref, preact_ref, kappa_ref, active = refs
    c = lax.axis_index("chan")
    gathered = [ref[...] for ref in strip_refs]
    columns = sum(
        dot(one_hot(source_ref[...], k * p.strips, p.strips), strips)
        for k, strips in enumerate(gathered)
    )
    columns = columns.astype(jnp.bfloat16)[:, : p.features]
    for k in range(p.chans):
        member, chip = k // p.chips, k % p.chips
        at = chip * p.tiles * p.block + p.own_cols
        low = strip_refs[member][at : at + 2, :].astype(jnp.float32)
        bias = (
            low[:1, : p.hidden]
            + low[:1, p.flag_at : p.flag_at + p.hidden]
            + low[1:, : p.hidden]
        )
        preact = dot(columns, p.layer(weight_refs, k)) + bias
        preact_ref[k] = preact
        at = pl.multiple_of((c ^ p.mask(k)) * p.hidden, p.hidden)
        active[:, pl.ds(at, p.hidden)] = (preact * jax.nn.sigmoid(preact)).astype(jnp.bfloat16)
    in_use = jnp.zeros((p.rows, 1), jnp.float32)
    for k in range(p.tiles):
        slot = lax.broadcasted_iota(jnp.int32, (p.rows, p.slots), 1) + k * p.slots
        low = k * p.block + p.own_cols + 1
        flags = strip_refs[0][low : low + 1, p.flag_at : p.flag_at + p.slots]
        flags = jnp.where(place_ref[...] == slot, flags.astype(jnp.float32), 0.0)
        in_use = in_use + jnp.sum(flags, axis=1, keepdims=True)
    in_use_ref[...] = in_use
    radiance_ref[...] = dot(active[...], w_radiance_ref[...]) + bias_ref[...].reshape(1, p.shard)
    parts = sum(
        dot(one_hot(cell_ref[...], k * p.strips, p.strips), strips)
        for k, strips in enumerate(gathered)
    )
    kappa_ref[...] = sum(parts[:, k * p.lane : (k + 1) * p.lane] for k in range(3))


def depart_kernel(p, radiance_ref, in_use_ref, place_ref, *refs):
    seen_refs, part_refs = refs[: -p.steps], refs[-p.steps :]
    part, count = p.rows // p.steps, seen_refs[0].shape[0]
    for j, part_ref in enumerate(part_refs):
        at = slice(j * part, (j + 1) * part)
        observed = sum(
            dot(one_hot(place_ref[at, :], k * count, count), ref[...])
            for k, ref in enumerate(seen_refs)
        )
        departure = (radiance_ref[at, :] - observed) * in_use_ref[at, :]
        part_ref[...] = departure.astype(jnp.bfloat16)


def slope_kernel(preact_ref, slope_ref):
    for k in range(preact_ref.shape[0]):
        preact = preact_ref[k]
        squash = jax.nn.sigmoid(preact)
        slope_ref[k] = (squash * (1.0 + preact * (1.0 - squash))).T


def choose_kernel(p, choices, *refs):
    refs, out_ref = refs[:-2], refs[-1]
    size = refs[0].shape[0]
    role = (lax.axis_index("chan") // p.group) ^ lax.axis_index("tile")
    for place in range(p.chips):

        @pl.when(role == place)
        def _():
            for j in range(p.steps):
                out_ref[j * size : (j + 1) * size, :] = refs[choices[place, j]][...]


def near_kernel(p, depart_ref, inv_cov_ref, out_ref):
    at = pl.multiple_of(lax.axis_index("chan") % p.group * p.shard, p.shard)
    out_ref[...] = dot(depart_ref[...], inv_cov_ref[pl.ds(at, p.shard), :])


def backward_kernel(p, *refs):
    refs = list(refs)
    take = lambda n: [refs.pop(0) for _ in range(n)]
    w_radiance_ref, inv_cov_ref, slope_ref, near_ref = take(4)
    depart_refs, weight_refs, target_refs = take(p.group - 1), take(p.group), take(p.group - 1)
    out_refs = refs
    c = lax.axis_index("chan")
    cotangent = near_ref[...]
    for k, ref in enumerate(depart_refs):
        at = pl.multiple_of((c % p.group ^ (k + 1)) * p.shard, p.shard)
        cotangent = cotangent + dot(ref[...], inv_cov_ref[pl.ds(at, p.shard), :])
    cotangent = cotangent.T.astype(jnp.bfloat16)
    total = jnp.zeros((p.features, p.rows), jnp.float32)
    for k in range(p.chans):
        at = pl.multiple_of((c ^ p.mask(k)) * p.hidden, p.hidden)
        grad_hidden = dot(w_radiance_ref[pl.ds(at, p.hidden), :], cotangent)
        grad_pre = (grad_hidden * slope_ref[k]).astype(jnp.bfloat16)
        total = total + dot(p.layer(weight_refs, k), grad_pre)
    total = total.astype(jnp.bfloat16)
    out_refs[0][...] = total
    for target_ref, out_ref in zip(target_refs, out_refs[1:]):
        out_ref[...] = dot_nt(one_hot(target_ref[...], 0, p.rows), total).astype(jnp.bfloat16)


def keep_kernel(total_ref, target_ref, out_ref):
    pick = one_hot(target_ref[...], 0, total_ref.shape[1])
    out_ref[...] = dot_nt(pick, total_ref[...]).astype(jnp.bfloat16)


def add(refs, at=slice(None)):
    total = refs[0][at, :].astype(jnp.float32)
    for ref in refs[1:]:
        total = total + ref[at, :].astype(jnp.float32)
    return total


def add_group_kernel(p, *refs):
    ins, outs = refs[: p.group], refs[p.group :]
    for k, out_ref in enumerate(outs):
        out_ref[...] = add(ins, slice(k * p.patch, (k + 1) * p.patch)).astype(jnp.bfloat16)


def add_chips_kernel(p, *refs):
    ins, outs = refs[: p.chips], refs[p.chips :]
    total = add(ins).astype(jnp.bfloat16)
    target = lax.broadcasted_iota(jnp.int32, (p.room, 1), 0)
    row, along = target // p.per_row, target % p.per_row - 1
    count = p.tiles * p.own_cols
    for k, out_ref in enumerate(outs):
        cell = ((lax.axis_index("tile") ^ k) * p.own_cols + along + count) % count
        wanted = jnp.where(row < 3, row * count + cell, -1)
        out_ref[...] = dot(one_hot(wanted, 0, p.patch), total).astype(jnp.bfloat16)


def diffuse_kernel(p, edge, *refs):
    ins, root_ref, out_ref = refs[: p.tiles], refs[-2], refs[-1]
    total = add(ins) * 0.0625
    length = p.along + 2 * edge
    shape = (length, p.room)
    cell = lax.broadcasted_iota(jnp.int32, shape, 0)
    source = lax.broadcasted_iota(jnp.int32, shape, 1)
    column = (cell - edge + 4) // 4
    spread = []
    terms = [term.astype(jnp.bfloat16) for term in split_three(total)]
    for k in range(3):
        pick = (source == column + k * p.per_row) & (column >= 0) & (column < p.per_row)
        spread.append(sum(dot(pick.astype(jnp.bfloat16), term) for term in terms))
    root = root_ref[...]
    state = [spread[(row + 2) // 4] for row in range(p.across + 4)]
    east_of = functools.partial(pltpu.roll, shift=length - 1, axis=0)
    west_of = functools.partial(pltpu.roll, shift=1, axis=0)
    north = root[:, :-1] * root[:, 1:]
    east, west = root * east_of(root), root * west_of(root)
    for sweep in range(2):
        fresh = list(state)
        for row in range(1 + sweep, p.across + 3 - sweep):
            here = state[row]
            fresh[row] = (
                here
                + north[:, row : row + 1] * (state[row + 1] - here)
                + north[:, row - 1 : row] * (state[row - 1] - here)
                + east[:, row : row + 1] * (east_of(here) - here)
                + west[:, row : row + 1] * (west_of(here) - here)
            )
        state = fresh
    for row in range(p.across):
        out_ref[row] = state[row + 2][edge : edge + p.along, : p.features]


def body_by_column(
    fields,
    diffusivity,
    owners,
    observed,
    usable,
    w_hidden,
    b_hidden,
    w_radiance,
    b_radiance,
    inv_cov,
):
    p = Plan(
        lax.axis_size("tile"),
        lax.axis_size("chan"),
        fields.shape,
        owners.shape,
        observed.shape,
        w_hidden.shape,
    )
    half, single = jnp.bfloat16, jnp.float32
    shape = jax.ShapeDtypeStruct
    both = ("tile", "chan")
    everyone = [(a, b) for a in range(p.tiles) for b in range(p.chans)]

    def flip(value, mask):
        return lax.ppermute(value, "chan", [(b, b ^ mask) for b in range(p.chans)])

    def trade(value, mask):
        return lax.ppermute(value, "tile", [(a, a ^ mask) for a in range(p.tiles)])

    def send(value, wanted):
        pairs = dict(wanted)
        pairs.update({target: source for source, target in wanted.items()})
        for a, b in everyone:
            if (a, b) not in pairs:
                pairs[a, b] = (a, b ^ 1)
        number = lambda place: place[0] * p.chans + place[1]
        return lax.ppermute(
            value, both, sorted((number(a), number(b)) for a, b in pairs.items())
        )

    def join(values, kernel_shape, after=()):
        return call(
            functools.partial(join_kernel, len(values)),
            shape(kernel_shape, half),
            [*values, *after],
            in_hbm=range(len(values), len(values) + len(after)),
        )

    def grow(value, over, after=()):
        return join([value, over(value)], (2 * value.shape[0],) + value.shape[1:], after)

    reach = p.across + 4
    cell = call(
        functools.partial(index_kernel, p),
        shape((3 * reach, 1), jnp.int32),
        [],
        flops=10**9,
    )

    strips = call(
        functools.partial(prepare_kernel, p),
        shape((p.block, p.width), half),
        [fields, diffusivity, usable, b_hidden, cell],
        in_hbm=[4],
        scratch=[pltpu.VMEM((p.block, p.width), single)],
    )
    seen, stages, before = observed, [], ()
    bit = 1
    while bit < p.tiles:
        if 2 * bit < p.tiles:
            seen = grow(seen, lambda value: trade(value, bit))
            before = [seen]
        strips = grow(strips, lambda value: trade(value, bit), before)
        before = ()
        stages.append(strips)
        bit *= 2
    strips = join(
        [strips] + [flip(strips, k * p.group) for k in range(1, p.chips)], (p.strips, p.width)
    )
    strips = [strips] + [flip(strips, k) for k in range(1, p.group)]

    near = [flip(w_hidden, chip * p.group) for chip in range(p.chips - 1, 0, -1)]
    near = [w_hidden] + near[::-1]
    near = call(
        functools.partial(stack_kernel, p),
        shape((p.chips * p.deep, p.hidden), half),
        near + [stages[-1]],
        in_hbm=[len(near)],
    )
    weights = [near] + [flip(near, k) for k in range(1, p.group)]

    far_half = p.tiles // 2
    seen = [
        seen,
        send(seen, {(b // p.group ^ far_half, b): (b // p.group, b) for b in range(p.chans)}),
    ]

    place, source, *targets = call(
        functools.partial(place_kernel, p),
        [shape((p.rows, 1), jnp.int32)] * 2
        + [shape((p.chips * p.patch, 1), jnp.int32)] * p.group,
        [owners.reshape(1, p.rows)],
        flops=SLACK_FLOPS,
    )
    radiance, in_use, preact, kappa = call(
        functools.partial(forward_kernel, p),
        [
            shape((p.rows, p.shard), single),
            shape((p.rows, 1), single),
            shape((p.chans, p.rows, p.hidden), single),
            shape((3 * reach, p.lane), single),
        ],
        [place, source, cell, b_radiance, w_radiance] + strips + weights,
        scratch=[pltpu.VMEM((p.rows, p.hidden * p.chans), half)],
        flops=FORWARD_FLOPS,
    )
    parts = call(
        functools.partial(depart_kernel, p),
        [shape((p.rows // p.steps, p.shard), half)] * p.steps,
        [radiance, in_use, place] + seen,
    )

    slope = call(
        slope_kernel,
        shape((p.chans, p.hidden, p.rows), single),
        [preact],
        flops=40 * preact.size,
    )

    pool, held, choices = list(parts), {}, {}
    for j in range(p.steps):
        held[0, j] = choices[0, j] = j
    for step in range(p.steps):
        for since in range(-1, step):
            for j in range(p.steps):
                order = [1 << (j + k) % p.steps for k in range(p.steps)]
                roles = [0] if since < 0 else [
                    order[since] + rest
                    for rest in range(p.chips)
                    if rest & ~sum(order[:since]) == 0
                ]
                wanted = {
                    (a, b): (a, b ^ order[step] * p.group)
                    for a, b in everyone
                    if (b // p.group ^ a) in roles
                }
                source = pool[choices[roles[0], j]]
                for role in roles:
                    choices[role + order[step], j] = len(pool)
                pool.append(send(source, wanted))
    chosen = call(
        functools.partial(choose_kernel, p, choices),
        shape((p.rows, p.shard), half),
        pool + [slope],
        in_hbm=[len(pool)],
    )
    depart = [flip(chosen, k) for k in range(1, p.group)]

    partial = call(
        functools.partial(near_kernel, p),
        shape((p.rows, p.shard), single),
        [chosen, inv_cov],
        flops=2 * p.rows * p.shard * p.shard,
    )
    partial = call(
        functools.partial(backward_kernel, p),
        [shape((p.features, p.rows), half)]
        + [shape((p.chips * p.patch, p.features), half)] * (p.group - 1),
        [w_radiance, inv_cov, slope, partial] + depart + weights + targets[1:],
        flops=2 * p.rows * (p.hidden * p.chans * (p.features + p.shard) + inv_cov.size),
    )
    kept = call(
        keep_kernel, shape((p.chips * p.patch, p.features), half), [partial[0], targets[0]]
    )
    partial = [kept] + [flip(partial[k], k) for k in range(1, p.group)]
    partial = call(
        functools.partial(add_group_kernel, p),
        [shape((p.patch, p.features), half)] * p.chips,
        partial,
    )
    partial = [flip(partial[k], k * p.group) for k in range(p.chips - 1, 0, -1)] + [partial[0]]
    partial = call(
        functools.partial(add_chips_kernel, p),
        [shape((p.room, p.features), half)] * p.tiles,
        partial,
    )
    partial = [trade(partial[k], k) for k in range(p.tiles - 1, 0, -1)] + [partial[0]]
    edge = 8
    kappa = kappa.reshape(3, reach, p.lane)
    root = jnp.sqrt(
        jnp.concatenate(
            [kappa[0, :, p.along - edge : p.along], kappa[1, :, : p.along], kappa[2, :, :edge]],
            axis=1,
        ).T
    )
    return call(
        functools.partial(diffuse_kernel, p, edge),
        shape(fields.shape, single),
        partial + [root],
        flops=100 * fields.size,
    )


def solution(mesh):
    tiles, chans = mesh.shape["tile"], mesh.shape["chan"]
    by_column = tiles > 1 and chans % tiles == 0 and chans & (chans - 1) == 0 and chans > tiles
    placed = (
        P("chan", "tile", None),
        P("chan", "tile"),
        P(),
        P("tile", "chan"),
        P("tile"),
        P(None, "chan"),
        P("chan"),
        P(None, "chan"),
        P("chan"),
        P("tile", "chan"),
    )
    return jax.shard_map(
        body_by_column if by_column else body_by_owner,
        mesh=mesh,
        in_specs=placed,
        out_specs=P("chan", "tile", None),
        check_vma=False,
    )
```

```python
import functools

import jax
import jax.numpy as jnp
from jax import lax
from jax.experimental import pallas as pl
from jax.experimental.pallas import tpu as pltpu
from jax.sharding import PartitionSpec as P

VMEM_BYTES = 24 * 1024 * 1024
SLACK_FLOPS = 2 * 10**9
FORWARD_FLOPS = 10**8
NT_DIMS = (((1,), (1,)), ((), ()))


def padded_2(value, sides, width, wrap):
    for axis, dim in sides:
        devices, length = (lax.axis_size(axis), value.shape[dim])
        up = [(i, (i + 1) % devices) for i in range(devices if wrap else devices - 1)]
        down = [(j, i) for i, j in up]
        last = lax.slice_in_dim(value, length - width, length, axis=dim)
        first = lax.slice_in_dim(value, 0, width, axis=dim)
        before = lax.ppermute(last, axis, up)
        after = lax.ppermute(first, axis, down)
        value = jnp.concatenate([before, value, after], axis=dim)
    return value


def add_rims(values):
    rowwise = padded_2(values, (("chan", 0),), 1, False)
    return padded_2(rowwise, (("tile", 1),), 1, True)


def body_by_owner(
    fields,
    diffusivity,
    owners,
    observed,
    usable,
    w_hidden,
    b_hidden,
    w_radiance,
    b_radiance,
    inv_cov,
):
    tile_count = lax.axis_size("tile")
    chan_count = lax.axis_size("chan")
    tile_index = lax.axis_index("tile")
    chan_index = lax.axis_index("chan")
    slot_count = observed.shape[0]
    capacity = slot_count // tile_count
    cells_across, cells_along, features = fields.shape
    own_cols = cells_across // 4 * (cells_along // 4)
    tile_cols = chan_count * own_cols
    hidden_dev = w_hidden.shape[1]
    owner_table = owners[:, 0].reshape(tile_count, tile_cols)
    owner_hits = (
        owner_table[:, :, None] == jnp.arange(tile_count, dtype=jnp.int32)[None, None, :]
    ).astype(jnp.int32)
    before = jnp.sum((jnp.cumsum(owner_hits, axis=1) - owner_hits) * owner_hits, axis=2)
    tallies = jnp.sum(owner_hits, axis=1)
    slot_of = lax.dynamic_index_in_dim(
        owner_table * capacity + before, tile_index, 0, keepdims=False
    )
    arriving = lax.dynamic_index_in_dim(tallies, tile_index, 1, keepdims=False)
    occupied = (jnp.arange(capacity, dtype=jnp.int32)[None, :] < arriving[:, None]).reshape(
        slot_count
    )
    grouped = fields.reshape(cells_across // 4, 4, cells_along // 4, 4, features)
    columns = (
        (jnp.sum(grouped, axis=(1, 3)) * 0.0625).reshape(own_cols, features).astype(jnp.bfloat16)
    )
    placer = (slot_of[None, :] == jnp.arange(slot_count, dtype=jnp.int32)[:, None]).astype(
        jnp.bfloat16
    )
    outgoing = jnp.dot(
        placer,
        lax.all_gather(columns, "chan", axis=0, tiled=True),
        preferred_element_type=jnp.float32,
    )
    incoming = lax.all_to_all(
        outgoing.astype(jnp.bfloat16), "tile", split_axis=0, concat_axis=0, tiled=True
    )
    preact = lax.dot_general(
        w_hidden, incoming, (((0,), (1,)), ((), ())), preferred_element_type=jnp.float32
    )
    preact = preact + b_hidden[:, None]
    squash = jax.nn.sigmoid(preact)
    active = (preact * squash).astype(jnp.bfloat16)
    radiance = lax.dot_general(
        lax.all_gather(active, "chan", axis=0, tiled=True),
        w_radiance,
        (((0,), (0,)), ((), ())),
        preferred_element_type=jnp.float32,
    )
    radiance = radiance + b_radiance[None, :]
    in_use = usable.astype(jnp.float32) * occupied.astype(jnp.float32)
    departure = ((radiance - observed.astype(jnp.float32)) * in_use[:, None]).astype(jnp.bfloat16)
    cotangent = jnp.dot(
        lax.all_gather(departure, "chan", axis=1, tiled=True),
        lax.all_gather(inv_cov, "tile", axis=0, tiled=True),
        preferred_element_type=jnp.float32,
    )
    cotangent = cotangent.astype(jnp.bfloat16)
    full_sum = lax.psum(
        lax.dot_general(w_radiance, cotangent, NT_DIMS, preferred_element_type=jnp.float32),
        "chan",
    )
    grad_hidden = lax.dynamic_slice_in_dim(full_sum, chan_index * hidden_dev, hidden_dev, 0)
    slope_term = squash * (1.0 + preact * (1.0 - squash))
    grad_pre = (grad_hidden * slope_term).astype(jnp.bfloat16)
    part_grad = lax.dot_general(
        grad_pre, w_hidden, (((0,), (1,)), ((), ())), preferred_element_type=jnp.float32
    )
    returned = lax.all_to_all(part_grad, "tile", split_axis=0, concat_axis=0, tiled=True)
    column_grad = lax.psum_scatter(
        jnp.take(returned, slot_of, axis=0), "chan", scatter_dimension=0, tiled=True
    )
    spread = jnp.repeat(
        column_grad.reshape(cells_across // 4, cells_along // 4, features), 4, axis=0
    )
    adjoint = jnp.repeat(spread, 4, axis=1) * 0.0625
    kappa_root = jnp.sqrt(diffusivity)
    root_rim = add_rims(kappa_root)
    coef_north = (kappa_root * root_rim[2:, 1:-1])[:, :, None]
    coef_south = (kappa_root * root_rim[:-2, 1:-1])[:, :, None]
    coef_east = (kappa_root * root_rim[1:-1, 2:])[:, :, None]
    coef_west = (kappa_root * root_rim[1:-1, :-2])[:, :, None]
    for sweep_index in range(2):
        padded = add_rims(adjoint)
        adjoint = (
            adjoint
            + coef_north * (padded[2:, 1:-1] - adjoint)
            + coef_south * (padded[:-2, 1:-1] - adjoint)
            + coef_east * (padded[1:-1, 2:] - adjoint)
            + coef_west * (padded[1:-1, :-2] - adjoint)
        )
    return adjoint


def up_to(value, multiple):
    return -(-value // multiple) * multiple


def dot(left, right):
    return jnp.dot(left, right, preferred_element_type=jnp.float32)


def dot_nt(left, right):
    return lax.dot_general(left, right, NT_DIMS, preferred_element_type=jnp.float32)


def split_three(value):
    high = value.astype(jnp.bfloat16).astype(jnp.float32)
    middle = (value - high).astype(jnp.bfloat16).astype(jnp.float32)
    return high, middle, value - high - middle


def call(
    kernel, out_shape, args, in_hbm=(), out_hbm=False, scratch=(), flops=0, vmem=VMEM_BYTES
):
    far, near = pl.BlockSpec(memory_space=pl.ANY), pl.BlockSpec(memory_space=pltpu.VMEM)
    bytes_accessed = sum(a.size * a.dtype.itemsize for a in args)
    return pl.pallas_call(
        kernel,
        out_shape=out_shape,
        in_specs=[far if k in in_hbm else near for k in range(len(args))],
        out_specs=jax.tree.map(lambda _: far if out_hbm else near, out_shape),
        scratch_shapes=list(scratch),
        compiler_params=pltpu.CompilerParams(vmem_limit_bytes=vmem),
        cost_estimate=pl.CostEstimate(
            flops=flops, bytes_accessed=bytes_accessed, transcendentals=0
        ),
    )(*args)


class Plan:
    def __init__(self, tiles, chans, fields, owners, observed, w_hidden):
        self.tiles, self.chans = tiles, chans
        self.across, self.along, self.features = fields
        self.own_cols = self.across // 4 * (self.along // 4)
        self.rows = owners[0]
        self.tile_cols = self.rows // tiles
        self.slots = observed[0]
        self.shard = observed[1]
        self.capacity = self.slots // tiles
        self.hidden = w_hidden[1]
        self.group = chans // tiles
        self.chips = chans // self.group
        self.steps = self.chips.bit_length() - 1
        self.lane = up_to(self.along, 128)
        self.flag_at = up_to(self.hidden, 128)
        self.width = max(
            up_to(self.features, 128),
            2 * self.flag_at,
            self.flag_at + up_to(self.slots, 128),
            3 * self.lane,
        )
        self.block = up_to(self.own_cols + 2 + self.across, 16)
        self.per_row = self.own_cols + 2
        self.patch = 3 * tiles * self.own_cols
        self.room = up_to(3 * self.per_row, 16)
        self.deep = up_to(self.features, 16)
        self.strips = self.chips * tiles * self.block

    def order(self, mask):
        return mask % self.group * self.chips + mask // self.group

    def layer(self, refs, k):
        at = k % self.chips * self.deep
        return refs[k // self.chips][at : at + self.features, :]

    def mask(self, k):
        return k % self.chips * self.group + k // self.chips


def prepare_kernel(p, fields_ref, diffusivity_ref, usable_ref, bias_ref, after_ref, out_ref, flat):
    flat[...] = jnp.zeros(flat.shape, jnp.float32)
    shape = (p.own_cols, p.along)
    row = lax.broadcasted_iota(jnp.int32, shape, 0)
    member = row == lax.broadcasted_iota(jnp.int32, shape, 1) // 4
    total = jnp.dot(
        member.astype(jnp.float32),
        fields_ref[0] + fields_ref[1] + fields_ref[2] + fields_ref[3],
        precision=lax.Precision.HIGHEST,
        preferred_element_type=jnp.float32,
    )
    flat[: p.own_cols, : p.features] = total * 0.0625
    at = p.own_cols
    high, middle, low = split_three(bias_ref[...].reshape(1, p.hidden))
    flat[at : at + 1, : p.hidden] = high
    flat[at : at + 1, p.flag_at : p.flag_at + p.hidden] = middle
    flat[at + 1 : at + 2, : p.hidden] = low
    flags = usable_ref[...].reshape(1, p.slots).astype(jnp.float32)
    flat[at + 1 : at + 2, p.flag_at : p.flag_at + p.slots] = flags
    for k, part in enumerate(split_three(diffusivity_ref[...])):
        flat[at + 2 : at + 2 + p.across, k * p.lane : k * p.lane + p.along] = part
    out_ref[...] = flat[...].astype(jnp.bfloat16)


def strip_of(p, tile, chan):
    other = chan ^ lax.axis_index("chan")
    return p.order(other) * p.tiles + (tile ^ lax.axis_index("tile"))


def index_kernel(p, cell_ref):
    t, c = lax.axis_index("tile"), lax.axis_index("chan")
    row = lax.broadcasted_iota(jnp.int32, cell_ref.shape, 0)
    reach = p.across + 4
    tile = (t + row // reach - 1 + p.tiles) % p.tiles
    cell = c * p.across - 2 + row % reach
    inside = (cell >= 0) & (cell < p.chans * p.across)
    cell = jnp.where(inside, cell, 0)
    wanted = strip_of(p, tile, cell // p.across) * p.block + p.own_cols + 2 + cell % p.across
    cell_ref[...] = jnp.where(inside, wanted, -1)


def place_kernel(p, owners_ref, place_ref, source_ref, *target_refs):
    t = lax.axis_index("tile")
    across = owners_ref[...]
    shape = (p.rows, p.rows)
    row = lax.broadcasted_iota(jnp.int32, shape, 0)
    other = lax.broadcasted_iota(jnp.int32, shape, 1)
    owner = jnp.sum(jnp.where(row == other, across, 0), axis=1, keepdims=True)
    first = lax.broadcasted_iota(jnp.int32, owner.shape, 0)
    begin = first // p.tile_cols * p.tile_cols
    same = (owner == across) & (other >= begin) & (other < row)
    rank = jnp.sum(jnp.where(same, 1, 0), axis=1, keepdims=True)
    tile = first // p.tile_cols
    place_ref[...] = (owner ^ t) * p.slots + tile * p.capacity + rank
    source_ref[...] = (
        strip_of(p, tile, first % p.tile_cols // p.own_cols) * p.block + first % p.own_cols
    )

    c = lax.axis_index("chan")
    target = lax.broadcasted_iota(jnp.int32, target_refs[0].shape, 0)
    chip, inner = target // p.patch, target % p.patch
    beside, inner = inner // (p.patch // 3) - 1, inner % (p.patch // 3)
    tile, along = inner // p.own_cols, inner % p.own_cols
    for k, target_ref in enumerate(target_refs):
        row = (chip ^ (c // p.group)) * p.group + (c % p.group ^ k) + beside
        wanted = tile * p.tile_cols + row * p.own_cols + along
        target_ref[...] = jnp.where((row >= 0) & (row < p.chans), wanted, -1)


def join_kernel(count, *refs):
    ins, out_ref = refs[:count], refs[-1]
    size = out_ref.shape[0] // count
    for k, ref in enumerate(ins):
        out_ref[k * size : (k + 1) * size, :] = ref[...]


def stack_kernel(p, *refs):
    for k, ref in enumerate(refs[: p.chips]):
        refs[-1][k * p.deep : k * p.deep + p.features, :] = ref[...]
        refs[-1][k * p.deep + p.features : (k + 1) * p.deep, :] = jnp.zeros(
            (p.deep - p.features, p.hidden), jnp.bfloat16
        )


def one_hot(wanted, first, count):
    source = lax.broadcasted_iota(jnp.int32, (wanted.shape[0], count), 1)
    return (source + first == wanted).astype(jnp.bfloat16)


def forward_kernel(p, *refs):
    refs = list(refs)
    take = lambda n: [refs.pop(0) for _ in range(n)]
    place_ref, source_ref, cell_ref, bias_ref, w_radiance_ref = take(5)
    strip_refs, weight_refs = take(p.group), take(p.group)
    radiance_ref, in_use_ref, preact_ref, kappa_ref, active = refs
    c = lax.axis_index("chan")
    gathered = [ref[...] for ref in strip_refs]
    columns = sum(
        dot(one_hot(source_ref[...], k * p.strips, p.strips), strips)
        for k, strips in enumerate(gathered)
    )
    columns = columns.astype(jnp.bfloat16)[:, : p.features]
    for k in range(p.chans):
        member, chip = k // p.chips, k % p.chips
        at = chip * p.tiles * p.block + p.own_cols
        low = strip_refs[member][at : at + 2, :].astype(jnp.float32)
        bias = (
            low[:1, : p.hidden]
            + low[:1, p.flag_at : p.flag_at + p.hidden]
            + low[1:, : p.hidden]
        )
        preact = dot(columns, p.layer(weight_refs, k)) + bias
        preact_ref[k] = preact
        at = pl.multiple_of((c ^ p.mask(k)) * p.hidden, p.hidden)
        active[:, pl.ds(at, p.hidden)] = (preact * jax.nn.sigmoid(preact)).astype(jnp.bfloat16)
    in_use = jnp.zeros((p.rows, 1), jnp.float32)
    for k in range(p.tiles):
        slot = lax.broadcasted_iota(jnp.int32, (p.rows, p.slots), 1) + k * p.slots
        low = k * p.block + p.own_cols + 1
        flags = strip_refs[0][low : low + 1, p.flag_at : p.flag_at + p.slots]
        flags = jnp.where(place_ref[...] == slot, flags.astype(jnp.float32), 0.0)
        in_use = in_use + jnp.sum(flags, axis=1, keepdims=True)
    in_use_ref[...] = in_use
    radiance_ref[...] = dot(active[...], w_radiance_ref[...]) + bias_ref[...].reshape(1, p.shard)
    parts = sum(
        dot(one_hot(cell_ref[...], k * p.strips, p.strips), strips)
        for k, strips in enumerate(gathered)
    )
    kappa_ref[...] = sum(parts[:, k * p.lane : (k + 1) * p.lane] for k in range(3))


def depart_kernel(p, radiance_ref, in_use_ref, place_ref, *refs):
    seen_refs, part_refs = refs[: -p.steps], refs[-p.steps :]
    part, count = p.rows // p.steps, seen_refs[0].shape[0]
    for j, part_ref in enumerate(part_refs):
        at = slice(j * part, (j + 1) * part)
        observed = sum(
            dot(one_hot(place_ref[at, :], k * count, count), ref[...])
            for k, ref in enumerate(seen_refs)
        )
        departure = (radiance_ref[at, :] - observed) * in_use_ref[at, :]
        part_ref[...] = departure.astype(jnp.bfloat16)


def slope_kernel(preact_ref, slope_ref):
    for k in range(preact_ref.shape[0]):
        preact = preact_ref[k]
        squash = jax.nn.sigmoid(preact)
        slope_ref[k] = (squash * (1.0 + preact * (1.0 - squash))).T


def choose_kernel(p, choices, *refs):
    refs, out_ref = refs[:-2], refs[-1]
    size = refs[0].shape[0]
    role = (lax.axis_index("chan") // p.group) ^ lax.axis_index("tile")
    for place in range(p.chips):

        @pl.when(role == place)
        def _():
            for j in range(p.steps):
                out_ref[j * size : (j + 1) * size, :] = refs[choices[place, j]][...]


def near_kernel(p, depart_ref, inv_cov_ref, out_ref):
    at = pl.multiple_of(lax.axis_index("chan") % p.group * p.shard, p.shard)
    out_ref[...] = dot(depart_ref[...], inv_cov_ref[pl.ds(at, p.shard), :])


def backward_kernel(p, *refs):
    refs = list(refs)
    take = lambda n: [refs.pop(0) for _ in range(n)]
    w_radiance_ref, inv_cov_ref, slope_ref, near_ref = take(4)
    depart_refs, weight_refs, target_refs = take(p.group - 1), take(p.group), take(p.group - 1)
    out_refs = refs
    c = lax.axis_index("chan")
    cotangent = near_ref[...]
    for k, ref in enumerate(depart_refs):
        at = pl.multiple_of((c % p.group ^ (k + 1)) * p.shard, p.shard)
        cotangent = cotangent + dot(ref[...], inv_cov_ref[pl.ds(at, p.shard), :])
    cotangent = cotangent.T.astype(jnp.bfloat16)
    total = jnp.zeros((p.features, p.rows), jnp.float32)
    for k in range(p.chans):
        at = pl.multiple_of((c ^ p.mask(k)) * p.hidden, p.hidden)
        grad_hidden = dot(w_radiance_ref[pl.ds(at, p.hidden), :], cotangent)
        grad_pre = (grad_hidden * slope_ref[k]).astype(jnp.bfloat16)
        total = total + dot(p.layer(weight_refs, k), grad_pre)
    total = total.astype(jnp.bfloat16)
    out_refs[0][...] = total
    for target_ref, out_ref in zip(target_refs, out_refs[1:]):
        out_ref[...] = dot_nt(one_hot(target_ref[...], 0, p.rows), total).astype(jnp.bfloat16)


def keep_kernel(total_ref, target_ref, out_ref):
    pick = one_hot(target_ref[...], 0, total_ref.shape[1])
    out_ref[...] = dot_nt(pick, total_ref[...]).astype(jnp.bfloat16)


def add(refs, at=slice(None)):
    total = refs[0][at, :].astype(jnp.float32)
    for ref in refs[1:]:
        total = total + ref[at, :].astype(jnp.float32)
    return total


def add_group_kernel(p, *refs):
    ins, outs = refs[: p.group], refs[p.group :]
    for k, out_ref in enumerate(outs):
        out_ref[...] = add(ins, slice(k * p.patch, (k + 1) * p.patch)).astype(jnp.bfloat16)


def add_chips_kernel(p, *refs):
    ins, outs = refs[: p.chips], refs[p.chips :]
    total = add(ins).astype(jnp.bfloat16)
    target = lax.broadcasted_iota(jnp.int32, (p.room, 1), 0)
    row, along = target // p.per_row, target % p.per_row - 1
    count = p.tiles * p.own_cols
    for k, out_ref in enumerate(outs):
        cell = ((lax.axis_index("tile") ^ k) * p.own_cols + along + count) % count
        wanted = jnp.where(row < 3, row * count + cell, -1)
        out_ref[...] = dot(one_hot(wanted, 0, p.patch), total).astype(jnp.bfloat16)


def diffuse_kernel(p, edge, *refs):
    ins, root_ref, out_ref = refs[: p.tiles], refs[-2], refs[-1]
    total = add(ins) * 0.0625
    length = p.along + 2 * edge
    shape = (length, p.room)
    cell = lax.broadcasted_iota(jnp.int32, shape, 0)
    source = lax.broadcasted_iota(jnp.int32, shape, 1)
    column = (cell - edge + 4) // 4
    spread = []
    terms = [term.astype(jnp.bfloat16) for term in split_three(total)]
    for k in range(3):
        pick = (source == column + k * p.per_row) & (column >= 0) & (column < p.per_row)
        spread.append(sum(dot(pick.astype(jnp.bfloat16), term) for term in terms))
    root = root_ref[...]
    state = [spread[(row + 2) // 4] for row in range(p.across + 4)]
    east_of = functools.partial(pltpu.roll, shift=length - 1, axis=0)
    west_of = functools.partial(pltpu.roll, shift=1, axis=0)
    north = root[:, :-1] * root[:, 1:]
    east, west = root * east_of(root), root * west_of(root)
    for sweep in range(2):
        fresh = list(state)
        for row in range(1 + sweep, p.across + 3 - sweep):
            here = state[row]
            fresh[row] = (
                here
                + north[:, row : row + 1] * (state[row + 1] - here)
                + north[:, row - 1 : row] * (state[row - 1] - here)
                + east[:, row : row + 1] * (east_of(here) - here)
                + west[:, row : row + 1] * (west_of(here) - here)
            )
        state = fresh
    for row in range(p.across):
        out_ref[row] = state[row + 2][edge : edge + p.along, : p.features]


def body_by_column(
    fields,
    diffusivity,
    owners,
    observed,
    usable,
    w_hidden,
    b_hidden,
    w_radiance,
    b_radiance,
    inv_cov,
):
    p = Plan(
        lax.axis_size("tile"),
        lax.axis_size("chan"),
        fields.shape,
        owners.shape,
        observed.shape,
        w_hidden.shape,
    )
    half, single = jnp.bfloat16, jnp.float32
    shape = jax.ShapeDtypeStruct
    both = ("tile", "chan")
    everyone = [(a, b) for a in range(p.tiles) for b in range(p.chans)]

    def flip(value, mask):
        return lax.ppermute(value, "chan", [(b, b ^ mask) for b in range(p.chans)])

    def trade(value, mask):
        return lax.ppermute(value, "tile", [(a, a ^ mask) for a in range(p.tiles)])

    def send(value, wanted):
        pairs = dict(wanted)
        pairs.update({target: source for source, target in wanted.items()})
        for a, b in everyone:
            if (a, b) not in pairs:
                pairs[a, b] = (a, b)
        number = lambda place: place[0] * p.chans + place[1]
        return lax.ppermute(
            value, both, sorted((number(a), number(b)) for a, b in pairs.items())
        )

    def join(values, kernel_shape, after=()):
        return call(
            functools.partial(join_kernel, len(values)),
            shape(kernel_shape, half),
            [*values, *after],
            in_hbm=range(len(values), len(values) + len(after)),
        )

    def grow(value, over, after=()):
        return join([value, over(value)], (2 * value.shape[0],) + value.shape[1:], after)

    reach = p.across + 4
    cell = call(
        functools.partial(index_kernel, p),
        shape((3 * reach, 1), jnp.int32),
        [],
        flops=10**9,
    )

    strips = call(
        functools.partial(prepare_kernel, p),
        shape((p.block, p.width), half),
        [fields, diffusivity, usable, b_hidden, cell],
        in_hbm=[4],
        scratch=[pltpu.VMEM((p.block, p.width), single)],
    )
    seen, stages, before = observed, [], ()
    bit = 1
    while bit < p.tiles:
        if 2 * bit < p.tiles:
            seen = grow(seen, lambda value: trade(value, bit))
            before = [seen]
        strips = grow(strips, lambda value: trade(value, bit), before)
        before = ()
        stages.append(strips)
        bit *= 2
    strips = join(
        [strips] + [flip(strips, k * p.group) for k in range(1, p.chips)], (p.strips, p.width)
    )
    strips = [strips] + [flip(strips, k) for k in range(1, p.group)]

    near = [flip(w_hidden, chip * p.group) for chip in range(p.chips - 1, 0, -1)]
    near = [w_hidden] + near[::-1]
    near = call(
        functools.partial(stack_kernel, p),
        shape((p.chips * p.deep, p.hidden), half),
        near + [stages[-1]],
        in_hbm=[len(near)],
    )
    weights = [near] + [flip(near, k) for k in range(1, p.group)]

    far_half = p.tiles // 2
    seen = [
        seen,
        send(seen, {(b // p.group ^ far_half, b): (b // p.group, b) for b in range(p.chans)}),
    ]

    place, source, *targets = call(
        functools.partial(place_kernel, p),
        [shape((p.rows, 1), jnp.int32)] * 2
        + [shape((p.chips * p.patch, 1), jnp.int32)] * p.group,
        [owners.reshape(1, p.rows)],
        flops=SLACK_FLOPS,
    )
    radiance, in_use, preact, kappa = call(
        functools.partial(forward_kernel, p),
        [
            shape((p.rows, p.shard), single),
            shape((p.rows, 1), single),
            shape((p.chans, p.rows, p.hidden), single),
            shape((3 * reach, p.lane), single),
        ],
        [place, source, cell, b_radiance, w_radiance] + strips + weights,
        scratch=[pltpu.VMEM((p.rows, p.hidden * p.chans), half)],
        flops=FORWARD_FLOPS,
    )
    parts = call(
        functools.partial(depart_kernel, p),
        [shape((p.rows // p.steps, p.shard), half)] * p.steps,
        [radiance, in_use, place] + seen,
    )

    slope = call(
        slope_kernel,
        shape((p.chans, p.hidden, p.rows), single),
        [preact],
        flops=40 * preact.size,
    )

    pool, held, choices = list(parts), {}, {}
    for j in range(p.steps):
        held[0, j] = choices[0, j] = j
    for step in range(p.steps):
        for since in range(-1, step):
            for j in range(p.steps):
                order = [1 << (j + k) % p.steps for k in range(p.steps)]
                roles = [0] if since < 0 else [
                    order[since] + rest
                    for rest in range(p.chips)
                    if rest & ~sum(order[:since]) == 0
                ]
                wanted = {
                    (a, b): (a, b ^ order[step] * p.group)
                    for a, b in everyone
                    if (b // p.group ^ a) in roles
                }
                source = pool[choices[roles[0], j]]
                for role in roles:
                    choices[role + order[step], j] = len(pool)
                pool.append(send(source, wanted))
    chosen = call(
        functools.partial(choose_kernel, p, choices),
        shape((p.rows, p.shard), half),
        pool + [slope],
        in_hbm=[len(pool)],
    )
    depart = [flip(chosen, k) for k in range(1, p.group)]

    partial = call(
        functools.partial(near_kernel, p),
        shape((p.rows, p.shard), single),
        [chosen, inv_cov],
        flops=2 * p.rows * p.shard * p.shard,
    )
    partial = call(
        functools.partial(backward_kernel, p),
        [shape((p.features, p.rows), half)]
        + [shape((p.chips * p.patch, p.features), half)] * (p.group - 1),
        [w_radiance, inv_cov, slope, partial] + depart + weights + targets[1:],
        flops=2 * p.rows * (p.hidden * p.chans * (p.features + p.shard) + inv_cov.size),
    )
    kept = call(
        keep_kernel, shape((p.chips * p.patch, p.features), half), [partial[0], targets[0]]
    )
    partial = [kept] + [flip(partial[k], k) for k in range(1, p.group)]
    partial = call(
        functools.partial(add_group_kernel, p),
        [shape((p.patch, p.features), half)] * p.chips,
        partial,
    )
    partial = [flip(partial[k], k * p.group) for k in range(p.chips - 1, 0, -1)] + [partial[0]]
    partial = call(
        functools.partial(add_chips_kernel, p),
        [shape((p.room, p.features), half)] * p.tiles,
        partial,
    )
    partial = [trade(partial[k], k) for k in range(p.tiles - 1, 0, -1)] + [partial[0]]
    edge = 8
    kappa = kappa.reshape(3, reach, p.lane)
    root = jnp.sqrt(
        jnp.concatenate(
            [kappa[0, :, p.along - edge : p.along], kappa[1, :, : p.along], kappa[2, :, :edge]],
            axis=1,
        ).T
    )
    return call(
        functools.partial(diffuse_kernel, p, edge),
        shape(fields.shape, single),
        partial + [root],
        flops=100 * fields.size,
    )


def solution(mesh):
    tiles, chans = mesh.shape["tile"], mesh.shape["chan"]
    by_column = tiles > 1 and chans % tiles == 0 and chans & (chans - 1) == 0 and chans > tiles
    placed = (
        P("chan", "tile", None),
        P("chan", "tile"),
        P(),
        P("tile", "chan"),
        P("tile"),
        P(None, "chan"),
        P("chan"),
        P(None, "chan"),
        P("chan"),
        P("tile", "chan"),
    )
    return jax.shard_map(
        body_by_column if by_column else body_by_owner,
        mesh=mesh,
        in_specs=placed,
        out_specs=P("chan", "tile", None),
        check_vma=False,
    )
```

```python
import functools

import jax
import jax.numpy as jnp
from jax import lax
from jax.experimental import pallas as pl
from jax.experimental.pallas import tpu as pltpu
from jax.sharding import PartitionSpec as P

VMEM_BYTES = 24 * 1024 * 1024
SLACK_FLOPS = 2 * 10**9
FORWARD_FLOPS = 10**8
NT_DIMS = (((1,), (1,)), ((), ()))


def padded_2(value, sides, width, wrap):
    for axis, dim in sides:
        devices, length = (lax.axis_size(axis), value.shape[dim])
        up = [(i, (i + 1) % devices) for i in range(devices if wrap else devices - 1)]
        down = [(j, i) for i, j in up]
        last = lax.slice_in_dim(value, length - width, length, axis=dim)
        first = lax.slice_in_dim(value, 0, width, axis=dim)
        before = lax.ppermute(last, axis, up)
        after = lax.ppermute(first, axis, down)
        value = jnp.concatenate([before, value, after], axis=dim)
    return value


def add_rims(values):
    rowwise = padded_2(values, (("chan", 0),), 1, False)
    return padded_2(rowwise, (("tile", 1),), 1, True)


def body_by_owner(
    fields,
    diffusivity,
    owners,
    observed,
    usable,
    w_hidden,
    b_hidden,
    w_radiance,
    b_radiance,
    inv_cov,
):
    tile_count = lax.axis_size("tile")
    chan_count = lax.axis_size("chan")
    tile_index = lax.axis_index("tile")
    chan_index = lax.axis_index("chan")
    slot_count = observed.shape[0]
    capacity = slot_count // tile_count
    cells_across, cells_along, features = fields.shape
    own_cols = cells_across // 4 * (cells_along // 4)
    tile_cols = chan_count * own_cols
    hidden_dev = w_hidden.shape[1]
    owner_table = owners[:, 0].reshape(tile_count, tile_cols)
    owner_hits = (
        owner_table[:, :, None] == jnp.arange(tile_count, dtype=jnp.int32)[None, None, :]
    ).astype(jnp.int32)
    before = jnp.sum((jnp.cumsum(owner_hits, axis=1) - owner_hits) * owner_hits, axis=2)
    tallies = jnp.sum(owner_hits, axis=1)
    slot_of = lax.dynamic_index_in_dim(
        owner_table * capacity + before, tile_index, 0, keepdims=False
    )
    arriving = lax.dynamic_index_in_dim(tallies, tile_index, 1, keepdims=False)
    occupied = (jnp.arange(capacity, dtype=jnp.int32)[None, :] < arriving[:, None]).reshape(
        slot_count
    )
    grouped = fields.reshape(cells_across // 4, 4, cells_along // 4, 4, features)
    columns = (
        (jnp.sum(grouped, axis=(1, 3)) * 0.0625).reshape(own_cols, features).astype(jnp.bfloat16)
    )
    placer = (slot_of[None, :] == jnp.arange(slot_count, dtype=jnp.int32)[:, None]).astype(
        jnp.bfloat16
    )
    outgoing = jnp.dot(
        placer,
        lax.all_gather(columns, "chan", axis=0, tiled=True),
        preferred_element_type=jnp.float32,
    )
    incoming = lax.all_to_all(
        outgoing.astype(jnp.bfloat16), "tile", split_axis=0, concat_axis=0, tiled=True
    )
    preact = lax.dot_general(
        w_hidden, incoming, (((0,), (1,)), ((), ())), preferred_element_type=jnp.float32
    )
    preact = preact + b_hidden[:, None]
    squash = jax.nn.sigmoid(preact)
    active = (preact * squash).astype(jnp.bfloat16)
    radiance = lax.dot_general(
        lax.all_gather(active, "chan", axis=0, tiled=True),
        w_radiance,
        (((0,), (0,)), ((), ())),
        preferred_element_type=jnp.float32,
    )
    radiance = radiance + b_radiance[None, :]
    in_use = usable.astype(jnp.float32) * occupied.astype(jnp.float32)
    departure = ((radiance - observed.astype(jnp.float32)) * in_use[:, None]).astype(jnp.bfloat16)
    cotangent = jnp.dot(
        lax.all_gather(departure, "chan", axis=1, tiled=True),
        lax.all_gather(inv_cov, "tile", axis=0, tiled=True),
        preferred_element_type=jnp.float32,
    )
    cotangent = cotangent.astype(jnp.bfloat16)
    full_sum = lax.psum(
        lax.dot_general(w_radiance, cotangent, NT_DIMS, preferred_element_type=jnp.float32),
        "chan",
    )
    grad_hidden = lax.dynamic_slice_in_dim(full_sum, chan_index * hidden_dev, hidden_dev, 0)
    slope_term = squash * (1.0 + preact * (1.0 - squash))
    grad_pre = (grad_hidden * slope_term).astype(jnp.bfloat16)
    part_grad = lax.dot_general(
        grad_pre, w_hidden, (((0,), (1,)), ((), ())), preferred_element_type=jnp.float32
    )
    returned = lax.all_to_all(part_grad, "tile", split_axis=0, concat_axis=0, tiled=True)
    column_grad = lax.psum_scatter(
        jnp.take(returned, slot_of, axis=0), "chan", scatter_dimension=0, tiled=True
    )
    spread = jnp.repeat(
        column_grad.reshape(cells_across // 4, cells_along // 4, features), 4, axis=0
    )
    adjoint = jnp.repeat(spread, 4, axis=1) * 0.0625
    kappa_root = jnp.sqrt(diffusivity)
    root_rim = add_rims(kappa_root)
    coef_north = (kappa_root * root_rim[2:, 1:-1])[:, :, None]
    coef_south = (kappa_root * root_rim[:-2, 1:-1])[:, :, None]
    coef_east = (kappa_root * root_rim[1:-1, 2:])[:, :, None]
    coef_west = (kappa_root * root_rim[1:-1, :-2])[:, :, None]
    for sweep_index in range(2):
        padded = add_rims(adjoint)
        adjoint = (
            adjoint
            + coef_north * (padded[2:, 1:-1] - adjoint)
            + coef_south * (padded[:-2, 1:-1] - adjoint)
            + coef_east * (padded[1:-1, 2:] - adjoint)
            + coef_west * (padded[1:-1, :-2] - adjoint)
        )
    return adjoint


def up_to(value, multiple):
    return -(-value // multiple) * multiple


def dot(left, right):
    return jnp.dot(left, right, preferred_element_type=jnp.float32)


def dot_nt(left, right):
    return lax.dot_general(left, right, NT_DIMS, preferred_element_type=jnp.float32)


def split_three(value):
    high = value.astype(jnp.bfloat16).astype(jnp.float32)
    middle = (value - high).astype(jnp.bfloat16).astype(jnp.float32)
    return high, middle, value - high - middle


def call(
    kernel, out_shape, args, in_hbm=(), out_hbm=False, scratch=(), flops=0, vmem=VMEM_BYTES
):
    far, near = pl.BlockSpec(memory_space=pl.ANY), pl.BlockSpec(memory_space=pltpu.VMEM)
    bytes_accessed = sum(a.size * a.dtype.itemsize for a in args)
    return pl.pallas_call(
        kernel,
        out_shape=out_shape,
        in_specs=[far if k in in_hbm else near for k in range(len(args))],
        out_specs=jax.tree.map(lambda _: far if out_hbm else near, out_shape),
        scratch_shapes=list(scratch),
        compiler_params=pltpu.CompilerParams(vmem_limit_bytes=vmem),
        cost_estimate=pl.CostEstimate(
            flops=flops, bytes_accessed=bytes_accessed, transcendentals=0
        ),
    )(*args)


class Plan:
    def __init__(self, tiles, chans, fields, owners, observed, w_hidden):
        self.tiles, self.chans = tiles, chans
        self.across, self.along, self.features = fields
        self.own_cols = self.across // 4 * (self.along // 4)
        self.rows = owners[0]
        self.tile_cols = self.rows // tiles
        self.slots = observed[0]
        self.shard = observed[1]
        self.capacity = self.slots // tiles
        self.hidden = w_hidden[1]
        self.group = chans // tiles
        self.chips = chans // self.group
        self.steps = self.chips.bit_length() - 1
        self.lane = up_to(self.along, 128)
        self.flag_at = up_to(self.hidden, 128)
        self.width = max(
            up_to(self.features, 128),
            2 * self.flag_at,
            self.flag_at + up_to(self.slots, 128),
            3 * self.lane,
        )
        self.block = up_to(self.own_cols + 2 + self.across, 16)
        self.per_row = self.own_cols + 2
        self.patch = 3 * tiles * self.own_cols
        self.room = up_to(3 * self.per_row, 16)
        self.deep = up_to(self.features, 16)
        self.strips = self.chips * tiles * self.block

    def order(self, mask):
        return mask % self.group * self.chips + mask // self.group

    def layer(self, refs, k):
        at = k % self.chips * self.deep
        return refs[k // self.chips][at : at + self.features, :]

    def mask(self, k):
        return k % self.chips * self.group + k // self.chips


def prepare_kernel(p, fields_ref, diffusivity_ref, usable_ref, bias_ref, after_ref, out_ref, flat):
    flat[...] = jnp.zeros(flat.shape, jnp.float32)
    shape = (p.own_cols, p.along)
    row = lax.broadcasted_iota(jnp.int32, shape, 0)
    member = row == lax.broadcasted_iota(jnp.int32, shape, 1) // 4
    total = jnp.dot(
        member.astype(jnp.float32),
        fields_ref[0] + fields_ref[1] + fields_ref[2] + fields_ref[3],
        precision=lax.Precision.HIGHEST,
        preferred_element_type=jnp.float32,
    )
    flat[: p.own_cols, : p.features] = total * 0.0625
    at = p.own_cols
    high, middle, low = split_three(bias_ref[...].reshape(1, p.hidden))
    flat[at : at + 1, : p.hidden] = high
    flat[at : at + 1, p.flag_at : p.flag_at + p.hidden] = middle
    flat[at + 1 : at + 2, : p.hidden] = low
    flags = usable_ref[...].reshape(1, p.slots).astype(jnp.float32)
    flat[at + 1 : at + 2, p.flag_at : p.flag_at + p.slots] = flags
    for k, part in enumerate(split_three(diffusivity_ref[...])):
        flat[at + 2 : at + 2 + p.across, k * p.lane : k * p.lane + p.along] = part
    out_ref[...] = flat[...].astype(jnp.bfloat16)


def strip_of(p, tile, chan):
    other = chan ^ lax.axis_index("chan")
    return p.order(other) * p.tiles + (tile ^ lax.axis_index("tile"))


def index_kernel(p, cell_ref):
    t, c = lax.axis_index("tile"), lax.axis_index("chan")
    row = lax.broadcasted_iota(jnp.int32, cell_ref.shape, 0)
    reach = p.across + 4
    tile = (t + row // reach - 1 + p.tiles) % p.tiles
    cell = c * p.across - 2 + row % reach
    inside = (cell >= 0) & (cell < p.chans * p.across)
    cell = jnp.where(inside, cell, 0)
    wanted = strip_of(p, tile, cell // p.across) * p.block + p.own_cols + 2 + cell % p.across
    cell_ref[...] = jnp.where(inside, wanted, -1)


def place_kernel(p, owners_ref, place_ref, source_ref, *target_refs):
    t = lax.axis_index("tile")
    across = owners_ref[...]
    shape = (p.rows, p.rows)
    row = lax.broadcasted_iota(jnp.int32, shape, 0)
    other = lax.broadcasted_iota(jnp.int32, shape, 1)
    owner = jnp.sum(jnp.where(row == other, across, 0), axis=1, keepdims=True)
    first = lax.broadcasted_iota(jnp.int32, owner.shape, 0)
    begin = first // p.tile_cols * p.tile_cols
    same = (owner == across) & (other >= begin) & (other < row)
    rank = jnp.sum(jnp.where(same, 1, 0), axis=1, keepdims=True)
    tile = first // p.tile_cols
    place_ref[...] = (owner ^ t) * p.slots + tile * p.capacity + rank
    source_ref[...] = (
        strip_of(p, tile, first % p.tile_cols // p.own_cols) * p.block + first % p.own_cols
    )

    c = lax.axis_index("chan")
    target = lax.broadcasted_iota(jnp.int32, target_refs[0].shape, 0)
    chip, inner = target // p.patch, target % p.patch
    beside, inner = inner // (p.patch // 3) - 1, inner % (p.patch // 3)
    tile, along = inner // p.own_cols, inner % p.own_cols
    for k, target_ref in enumerate(target_refs):
        row = (chip ^ (c // p.group)) * p.group + (c % p.group ^ k) + beside
        wanted = tile * p.tile_cols + row * p.own_cols + along
        target_ref[...] = jnp.where((row >= 0) & (row < p.chans), wanted, -1)


def join_kernel(count, *refs):
    ins, out_ref = refs[:count], refs[-1]
    size = out_ref.shape[0] // count
    for k, ref in enumerate(ins):
        out_ref[k * size : (k + 1) * size, :] = ref[...]


def stack_kernel(p, *refs):
    for k, ref in enumerate(refs[: p.chips]):
        refs[-1][k * p.deep : k * p.deep + p.features, :] = ref[...]
        refs[-1][k * p.deep + p.features : (k + 1) * p.deep, :] = jnp.zeros(
            (p.deep - p.features, p.hidden), jnp.bfloat16
        )


def one_hot(wanted, first, count):
    source = lax.broadcasted_iota(jnp.int32, (wanted.shape[0], count), 1)
    return (source + first == wanted).astype(jnp.bfloat16)


def forward_kernel(p, *refs):
    refs = list(refs)
    take = lambda n: [refs.pop(0) for _ in range(n)]
    place_ref, source_ref, cell_ref, bias_ref, w_radiance_ref = take(5)
    strip_refs, weight_refs, (seen_ref,) = take(p.group), take(p.group), take(1)
    radiance_ref, in_use_ref, preact_ref, kappa_ref, active = refs
    c = lax.axis_index("chan")
    gathered = [ref[...] for ref in strip_refs]
    columns = sum(
        dot(one_hot(source_ref[...], k * p.strips, p.strips), strips)
        for k, strips in enumerate(gathered)
    )
    columns = columns.astype(jnp.bfloat16)[:, : p.features]
    for k in range(p.chans):
        member, chip = k // p.chips, k % p.chips
        at = chip * p.tiles * p.block + p.own_cols
        low = strip_refs[member][at : at + 2, :].astype(jnp.float32)
        bias = (
            low[:1, : p.hidden]
            + low[:1, p.flag_at : p.flag_at + p.hidden]
            + low[1:, : p.hidden]
        )
        preact = dot(columns, p.layer(weight_refs, k)) + bias
        preact_ref[k] = preact
        at = pl.multiple_of((c ^ p.mask(k)) * p.hidden, p.hidden)
        active[:, pl.ds(at, p.hidden)] = (preact * jax.nn.sigmoid(preact)).astype(jnp.bfloat16)
    in_use = jnp.zeros((p.rows, 1), jnp.float32)
    for k in range(p.tiles):
        slot = lax.broadcasted_iota(jnp.int32, (p.rows, p.slots), 1) + k * p.slots
        low = k * p.block + p.own_cols + 1
        flags = strip_refs[0][low : low + 1, p.flag_at : p.flag_at + p.slots]
        flags = jnp.where(place_ref[...] == slot, flags.astype(jnp.float32), 0.0)
        in_use = in_use + jnp.sum(flags, axis=1, keepdims=True)
    in_use_ref[...] = in_use
    observed = dot(one_hot(place_ref[...], 0, seen_ref.shape[0]), seen_ref[...])
    radiance = dot(active[...], w_radiance_ref[...]) + bias_ref[...].reshape(1, p.shard)
    radiance_ref[...] = radiance - observed
    parts = sum(
        dot(one_hot(cell_ref[...], k * p.strips, p.strips), strips)
        for k, strips in enumerate(gathered)
    )
    kappa_ref[...] = sum(parts[:, k * p.lane : (k + 1) * p.lane] for k in range(3))


def depart_kernel(p, radiance_ref, in_use_ref, place_ref, *refs):
    seen_refs, part_refs = refs[: -p.steps], refs[-p.steps :]
    part, count = p.rows // p.steps, seen_refs[0].shape[0]
    for j, part_ref in enumerate(part_refs):
        at = slice(j * part, (j + 1) * part)
        observed = sum(
            dot(one_hot(place_ref[at, :], (k + 1) * count, count), ref[...])
            for k, ref in enumerate(seen_refs)
        )
        departure = (radiance_ref[at, :] - observed) * in_use_ref[at, :]
        part_ref[...] = departure.astype(jnp.bfloat16)


def slope_kernel(preact_ref, slope_ref):
    for k in range(preact_ref.shape[0]):
        preact = preact_ref[k]
        squash = jax.nn.sigmoid(preact)
        slope_ref[k] = (squash * (1.0 + preact * (1.0 - squash))).T


def choose_kernel(p, choices, *refs):
    refs, out_ref = refs[:-2], refs[-1]
    size = refs[0].shape[0]
    role = (lax.axis_index("chan") // p.group) ^ lax.axis_index("tile")
    for place in range(p.chips):

        @pl.when(role == place)
        def _():
            for j in range(p.steps):
                out_ref[j * size : (j + 1) * size, :] = refs[choices[place, j]][...]


def near_kernel(p, depart_ref, inv_cov_ref, out_ref):
    at = pl.multiple_of(lax.axis_index("chan") % p.group * p.shard, p.shard)
    out_ref[...] = dot(depart_ref[...], inv_cov_ref[pl.ds(at, p.shard), :])


def backward_kernel(p, *refs):
    refs = list(refs)
    take = lambda n: [refs.pop(0) for _ in range(n)]
    w_radiance_ref, inv_cov_ref, slope_ref, near_ref = take(4)
    depart_refs, weight_refs, target_refs = take(p.group - 1), take(p.group), take(p.group - 1)
    out_refs = refs
    c = lax.axis_index("chan")
    cotangent = near_ref[...]
    for k, ref in enumerate(depart_refs):
        at = pl.multiple_of((c % p.group ^ (k + 1)) * p.shard, p.shard)
        cotangent = cotangent + dot(ref[...], inv_cov_ref[pl.ds(at, p.shard), :])
    cotangent = cotangent.T.astype(jnp.bfloat16)
    total = jnp.zeros((p.features, p.rows), jnp.float32)
    for k in range(p.chans):
        at = pl.multiple_of((c ^ p.mask(k)) * p.hidden, p.hidden)
        grad_hidden = dot(w_radiance_ref[pl.ds(at, p.hidden), :], cotangent)
        grad_pre = (grad_hidden * slope_ref[k]).astype(jnp.bfloat16)
        total = total + dot(p.layer(weight_refs, k), grad_pre)
    total = total.astype(jnp.bfloat16)
    out_refs[0][...] = total
    for target_ref, out_ref in zip(target_refs, out_refs[1:]):
        out_ref[...] = dot_nt(one_hot(target_ref[...], 0, p.rows), total).astype(jnp.bfloat16)


def keep_kernel(total_ref, target_ref, out_ref):
    pick = one_hot(target_ref[...], 0, total_ref.shape[1])
    out_ref[...] = dot_nt(pick, total_ref[...]).astype(jnp.bfloat16)


def add(refs, at=slice(None)):
    total = refs[0][at, :].astype(jnp.float32)
    for ref in refs[1:]:
        total = total + ref[at, :].astype(jnp.float32)
    return total


def add_group_kernel(p, *refs):
    ins, outs = refs[: p.group], refs[p.group :]
    for k, out_ref in enumerate(outs):
        out_ref[...] = add(ins, slice(k * p.patch, (k + 1) * p.patch)).astype(jnp.bfloat16)


def add_chips_kernel(p, *refs):
    ins, outs = refs[: p.chips], refs[p.chips :]
    total = add(ins).astype(jnp.bfloat16)
    target = lax.broadcasted_iota(jnp.int32, (p.room, 1), 0)
    row, along = target // p.per_row, target % p.per_row - 1
    count = p.tiles * p.own_cols
    for k, out_ref in enumerate(outs):
        cell = ((lax.axis_index("tile") ^ k) * p.own_cols + along + count) % count
        wanted = jnp.where(row < 3, row * count + cell, -1)
        out_ref[...] = dot(one_hot(wanted, 0, p.patch), total).astype(jnp.bfloat16)


def diffuse_kernel(p, edge, *refs):
    ins, root_ref, out_ref = refs[: p.tiles], refs[-2], refs[-1]
    total = add(ins) * 0.0625
    length = p.along + 2 * edge
    shape = (length, p.room)
    cell = lax.broadcasted_iota(jnp.int32, shape, 0)
    source = lax.broadcasted_iota(jnp.int32, shape, 1)
    column = (cell - edge + 4) // 4
    spread = []
    terms = [term.astype(jnp.bfloat16) for term in split_three(total)]
    for k in range(3):
        pick = (source == column + k * p.per_row) & (column >= 0) & (column < p.per_row)
        spread.append(sum(dot(pick.astype(jnp.bfloat16), term) for term in terms))
    root = root_ref[...]
    state = [spread[(row + 2) // 4] for row in range(p.across + 4)]
    east_of = functools.partial(pltpu.roll, shift=length - 1, axis=0)
    west_of = functools.partial(pltpu.roll, shift=1, axis=0)
    north = root[:, :-1] * root[:, 1:]
    east, west = root * east_of(root), root * west_of(root)
    for sweep in range(2):
        fresh = list(state)
        for row in range(1 + sweep, p.across + 3 - sweep):
            here = state[row]
            fresh[row] = (
                here
                + north[:, row : row + 1] * (state[row + 1] - here)
                + north[:, row - 1 : row] * (state[row - 1] - here)
                + east[:, row : row + 1] * (east_of(here) - here)
                + west[:, row : row + 1] * (west_of(here) - here)
            )
        state = fresh
    for row in range(p.across):
        out_ref[row] = state[row + 2][edge : edge + p.along, : p.features]


def body_by_column(
    fields,
    diffusivity,
    owners,
    observed,
    usable,
    w_hidden,
    b_hidden,
    w_radiance,
    b_radiance,
    inv_cov,
):
    p = Plan(
        lax.axis_size("tile"),
        lax.axis_size("chan"),
        fields.shape,
        owners.shape,
        observed.shape,
        w_hidden.shape,
    )
    half, single = jnp.bfloat16, jnp.float32
    shape = jax.ShapeDtypeStruct
    both = ("tile", "chan")
    everyone = [(a, b) for a in range(p.tiles) for b in range(p.chans)]

    def flip(value, mask):
        return lax.ppermute(value, "chan", [(b, b ^ mask) for b in range(p.chans)])

    def trade(value, mask):
        return lax.ppermute(value, "tile", [(a, a ^ mask) for a in range(p.tiles)])

    def send(value, wanted):
        pairs = dict(wanted)
        pairs.update({target: source for source, target in wanted.items()})
        for a, b in everyone:
            if (a, b) not in pairs:
                pairs[a, b] = (a, b ^ 1)
        number = lambda place: place[0] * p.chans + place[1]
        return lax.ppermute(
            value, both, sorted((number(a), number(b)) for a, b in pairs.items())
        )

    def join(values, kernel_shape, after=()):
        return call(
            functools.partial(join_kernel, len(values)),
            shape(kernel_shape, half),
            [*values, *after],
            in_hbm=range(len(values), len(values) + len(after)),
        )

    def grow(value, over, after=()):
        return join([value, over(value)], (2 * value.shape[0],) + value.shape[1:], after)

    reach = p.across + 4
    cell = call(
        functools.partial(index_kernel, p),
        shape((3 * reach, 1), jnp.int32),
        [],
        flops=10**9,
    )

    strips = call(
        functools.partial(prepare_kernel, p),
        shape((p.block, p.width), half),
        [fields, diffusivity, usable, b_hidden, cell],
        in_hbm=[4],
        scratch=[pltpu.VMEM((p.block, p.width), single)],
    )
    seen, stages, before = observed, [], ()
    bit = 1
    while bit < p.tiles:
        if 2 * bit < p.tiles:
            seen = grow(seen, lambda value: trade(value, bit))
            before = [seen]
        strips = grow(strips, lambda value: trade(value, bit), before)
        before = ()
        stages.append(strips)
        bit *= 2
    strips = join(
        [strips] + [flip(strips, k * p.group) for k in range(1, p.chips)], (p.strips, p.width)
    )
    strips = [strips] + [flip(strips, k) for k in range(1, p.group)]

    near = [flip(w_hidden, chip * p.group) for chip in range(p.chips - 1, 0, -1)]
    near = [w_hidden] + near[::-1]
    near = call(
        functools.partial(stack_kernel, p),
        shape((p.chips * p.deep, p.hidden), half),
        near + [stages[-1]],
        in_hbm=[len(near)],
    )
    weights = [near] + [flip(near, k) for k in range(1, p.group)]

    far_half = p.tiles // 2
    seen = [
        seen,
        send(seen, {(b // p.group ^ far_half, b): (b // p.group, b) for b in range(p.chans)}),
    ]

    place, source, *targets = call(
        functools.partial(place_kernel, p),
        [shape((p.rows, 1), jnp.int32)] * 2
        + [shape((p.chips * p.patch, 1), jnp.int32)] * p.group,
        [owners.reshape(1, p.rows)],
        flops=SLACK_FLOPS,
    )
    radiance, in_use, preact, kappa = call(
        functools.partial(forward_kernel, p),
        [
            shape((p.rows, p.shard), single),
            shape((p.rows, 1), single),
            shape((p.chans, p.rows, p.hidden), single),
            shape((3 * reach, p.lane), single),
        ],
        [place, source, cell, b_radiance, w_radiance] + strips + weights + seen[:1],
        scratch=[pltpu.VMEM((p.rows, p.hidden * p.chans), half)],
        flops=FORWARD_FLOPS,
    )
    parts = call(
        functools.partial(depart_kernel, p),
        [shape((p.rows // p.steps, p.shard), half)] * p.steps,
        [radiance, in_use, place] + seen[1:],
    )

    slope = call(
        slope_kernel,
        shape((p.chans, p.hidden, p.rows), single),
        [preact],
        flops=40 * preact.size,
    )

    pool, held, choices = list(parts), {}, {}
    for j in range(p.steps):
        held[0, j] = choices[0, j] = j
    for step in range(p.steps):
        for since in range(-1, step):
            for j in range(p.steps):
                order = [1 << (j + k) % p.steps for k in range(p.steps)]
                roles = [0] if since < 0 else [
                    order[since] + rest
                    for rest in range(p.chips)
                    if rest & ~sum(order[:since]) == 0
                ]
                wanted = {
                    (a, b): (a, b ^ order[step] * p.group)
                    for a, b in everyone
                    if (b // p.group ^ a) in roles
                }
                source = pool[choices[roles[0], j]]
                for role in roles:
                    choices[role + order[step], j] = len(pool)
                pool.append(send(source, wanted))
    chosen = call(
        functools.partial(choose_kernel, p, choices),
        shape((p.rows, p.shard), half),
        pool + [slope],
        in_hbm=[len(pool)],
    )
    depart = [flip(chosen, k) for k in range(1, p.group)]

    partial = call(
        functools.partial(near_kernel, p),
        shape((p.rows, p.shard), single),
        [chosen, inv_cov],
        flops=2 * p.rows * p.shard * p.shard,
    )
    partial = call(
        functools.partial(backward_kernel, p),
        [shape((p.features, p.rows), half)]
        + [shape((p.chips * p.patch, p.features), half)] * (p.group - 1),
        [w_radiance, inv_cov, slope, partial] + depart + weights + targets[1:],
        flops=2 * p.rows * (p.hidden * p.chans * (p.features + p.shard) + inv_cov.size),
    )
    kept = call(
        keep_kernel, shape((p.chips * p.patch, p.features), half), [partial[0], targets[0]]
    )
    partial = [kept] + [flip(partial[k], k) for k in range(1, p.group)]
    partial = call(
        functools.partial(add_group_kernel, p),
        [shape((p.patch, p.features), half)] * p.chips,
        partial,
    )
    partial = [flip(partial[k], k * p.group) for k in range(p.chips - 1, 0, -1)] + [partial[0]]
    partial = call(
        functools.partial(add_chips_kernel, p),
        [shape((p.room, p.features), half)] * p.tiles,
        partial,
    )
    partial = [trade(partial[k], k) for k in range(p.tiles - 1, 0, -1)] + [partial[0]]
    edge = 8
    kappa = kappa.reshape(3, reach, p.lane)
    root = jnp.sqrt(
        jnp.concatenate(
            [kappa[0, :, p.along - edge : p.along], kappa[1, :, : p.along], kappa[2, :, :edge]],
            axis=1,
        ).T
    )
    return call(
        functools.partial(diffuse_kernel, p, edge),
        shape(fields.shape, single),
        partial + [root],
        flops=100 * fields.size,
    )


def solution(mesh):
    tiles, chans = mesh.shape["tile"], mesh.shape["chan"]
    by_column = tiles > 1 and chans % tiles == 0 and chans & (chans - 1) == 0 and chans > tiles
    placed = (
        P("chan", "tile", None),
        P("chan", "tile"),
        P(),
        P("tile", "chan"),
        P("tile"),
        P(None, "chan"),
        P("chan"),
        P(None, "chan"),
        P("chan"),
        P("tile", "chan"),
    )
    return jax.shard_map(
        body_by_column if by_column else body_by_owner,
        mesh=mesh,
        in_specs=placed,
        out_specs=P("chan", "tile", None),
        check_vma=False,
    )
```

```python
import functools

import jax
import jax.numpy as jnp
from jax import lax
from jax.experimental import pallas as pl
from jax.experimental.pallas import tpu as pltpu
from jax.sharding import PartitionSpec as P

VMEM_BYTES = 24 * 1024 * 1024
SLACK_FLOPS = 2 * 10**9
FORWARD_FLOPS = 10**8
NT_DIMS = (((1,), (1,)), ((), ()))


def padded_2(value, sides, width, wrap):
    for axis, dim in sides:
        devices, length = (lax.axis_size(axis), value.shape[dim])
        up = [(i, (i + 1) % devices) for i in range(devices if wrap else devices - 1)]
        down = [(j, i) for i, j in up]
        last = lax.slice_in_dim(value, length - width, length, axis=dim)
        first = lax.slice_in_dim(value, 0, width, axis=dim)
        before = lax.ppermute(last, axis, up)
        after = lax.ppermute(first, axis, down)
        value = jnp.concatenate([before, value, after], axis=dim)
    return value


def add_rims(values):
    rowwise = padded_2(values, (("chan", 0),), 1, False)
    return padded_2(rowwise, (("tile", 1),), 1, True)


def body_by_owner(
    fields,
    diffusivity,
    owners,
    observed,
    usable,
    w_hidden,
    b_hidden,
    w_radiance,
    b_radiance,
    inv_cov,
):
    tile_count = lax.axis_size("tile")
    chan_count = lax.axis_size("chan")
    tile_index = lax.axis_index("tile")
    chan_index = lax.axis_index("chan")
    slot_count = observed.shape[0]
    capacity = slot_count // tile_count
    cells_across, cells_along, features = fields.shape
    own_cols = cells_across // 4 * (cells_along // 4)
    tile_cols = chan_count * own_cols
    hidden_dev = w_hidden.shape[1]
    owner_table = owners[:, 0].reshape(tile_count, tile_cols)
    owner_hits = (
        owner_table[:, :, None] == jnp.arange(tile_count, dtype=jnp.int32)[None, None, :]
    ).astype(jnp.int32)
    before = jnp.sum((jnp.cumsum(owner_hits, axis=1) - owner_hits) * owner_hits, axis=2)
    tallies = jnp.sum(owner_hits, axis=1)
    slot_of = lax.dynamic_index_in_dim(
        owner_table * capacity + before, tile_index, 0, keepdims=False
    )
    arriving = lax.dynamic_index_in_dim(tallies, tile_index, 1, keepdims=False)
    occupied = (jnp.arange(capacity, dtype=jnp.int32)[None, :] < arriving[:, None]).reshape(
        slot_count
    )
    grouped = fields.reshape(cells_across // 4, 4, cells_along // 4, 4, features)
    columns = (
        (jnp.sum(grouped, axis=(1, 3)) * 0.0625).reshape(own_cols, features).astype(jnp.bfloat16)
    )
    placer = (slot_of[None, :] == jnp.arange(slot_count, dtype=jnp.int32)[:, None]).astype(
        jnp.bfloat16
    )
    outgoing = jnp.dot(
        placer,
        lax.all_gather(columns, "chan", axis=0, tiled=True),
        preferred_element_type=jnp.float32,
    )
    incoming = lax.all_to_all(
        outgoing.astype(jnp.bfloat16), "tile", split_axis=0, concat_axis=0, tiled=True
    )
    preact = lax.dot_general(
        w_hidden, incoming, (((0,), (1,)), ((), ())), preferred_element_type=jnp.float32
    )
    preact = preact + b_hidden[:, None]
    squash = jax.nn.sigmoid(preact)
    active = (preact * squash).astype(jnp.bfloat16)
    radiance = lax.dot_general(
        lax.all_gather(active, "chan", axis=0, tiled=True),
        w_radiance,
        (((0,), (0,)), ((), ())),
        preferred_element_type=jnp.float32,
    )
    radiance = radiance + b_radiance[None, :]
    in_use = usable.astype(jnp.float32) * occupied.astype(jnp.float32)
    departure = ((radiance - observed.astype(jnp.float32)) * in_use[:, None]).astype(jnp.bfloat16)
    cotangent = jnp.dot(
        lax.all_gather(departure, "chan", axis=1, tiled=True),
        lax.all_gather(inv_cov, "tile", axis=0, tiled=True),
        preferred_element_type=jnp.float32,
    )
    cotangent = cotangent.astype(jnp.bfloat16)
    full_sum = lax.psum(
        lax.dot_general(w_radiance, cotangent, NT_DIMS, preferred_element_type=jnp.float32),
        "chan",
    )
    grad_hidden = lax.dynamic_slice_in_dim(full_sum, chan_index * hidden_dev, hidden_dev, 0)
    slope_term = squash * (1.0 + preact * (1.0 - squash))
    grad_pre = (grad_hidden * slope_term).astype(jnp.bfloat16)
    part_grad = lax.dot_general(
        grad_pre, w_hidden, (((0,), (1,)), ((), ())), preferred_element_type=jnp.float32
    )
    returned = lax.all_to_all(part_grad, "tile", split_axis=0, concat_axis=0, tiled=True)
    column_grad = lax.psum_scatter(
        jnp.take(returned, slot_of, axis=0), "chan", scatter_dimension=0, tiled=True
    )
    spread = jnp.repeat(
        column_grad.reshape(cells_across // 4, cells_along // 4, features), 4, axis=0
    )
    adjoint = jnp.repeat(spread, 4, axis=1) * 0.0625
    kappa_root = jnp.sqrt(diffusivity)
    root_rim = add_rims(kappa_root)
    coef_north = (kappa_root * root_rim[2:, 1:-1])[:, :, None]
    coef_south = (kappa_root * root_rim[:-2, 1:-1])[:, :, None]
    coef_east = (kappa_root * root_rim[1:-1, 2:])[:, :, None]
    coef_west = (kappa_root * root_rim[1:-1, :-2])[:, :, None]
    for sweep_index in range(2):
        padded = add_rims(adjoint)
        adjoint = (
            adjoint
            + coef_north * (padded[2:, 1:-1] - adjoint)
            + coef_south * (padded[:-2, 1:-1] - adjoint)
            + coef_east * (padded[1:-1, 2:] - adjoint)
            + coef_west * (padded[1:-1, :-2] - adjoint)
        )
    return adjoint


def up_to(value, multiple):
    return -(-value // multiple) * multiple


def dot(left, right):
    return jnp.dot(left, right, preferred_element_type=jnp.float32)


def dot_nt(left, right):
    return lax.dot_general(left, right, NT_DIMS, preferred_element_type=jnp.float32)


def split_three(value):
    high = value.astype(jnp.bfloat16).astype(jnp.float32)
    middle = (value - high).astype(jnp.bfloat16).astype(jnp.float32)
    return high, middle, value - high - middle


def call(
    kernel, out_shape, args, in_hbm=(), out_hbm=False, scratch=(), flops=0, vmem=VMEM_BYTES
):
    far, near = pl.BlockSpec(memory_space=pl.ANY), pl.BlockSpec(memory_space=pltpu.VMEM)
    bytes_accessed = sum(a.size * a.dtype.itemsize for a in args)
    return pl.pallas_call(
        kernel,
        out_shape=out_shape,
        in_specs=[far if k in in_hbm else near for k in range(len(args))],
        out_specs=jax.tree.map(lambda _: far if out_hbm else near, out_shape),
        scratch_shapes=list(scratch),
        compiler_params=pltpu.CompilerParams(vmem_limit_bytes=vmem),
        cost_estimate=pl.CostEstimate(
            flops=flops, bytes_accessed=bytes_accessed, transcendentals=0
        ),
    )(*args)


class Plan:
    def __init__(self, tiles, chans, fields, owners, observed, w_hidden):
        self.tiles, self.chans = tiles, chans
        self.across, self.along, self.features = fields
        self.own_cols = self.across // 4 * (self.along // 4)
        self.rows = owners[0]
        self.tile_cols = self.rows // tiles
        self.slots = observed[0]
        self.shard = observed[1]
        self.capacity = self.slots // tiles
        self.hidden = w_hidden[1]
        self.group = chans // tiles
        self.chips = chans // self.group
        self.steps = self.chips.bit_length() - 1
        self.lane = up_to(self.along, 128)
        self.flag_at = up_to(self.hidden, 128)
        self.width = max(
            up_to(self.features, 128),
            2 * self.flag_at,
            self.flag_at + up_to(self.slots, 128),
            3 * self.lane,
        )
        self.block = up_to(self.own_cols + 2 + self.across, 16)
        self.per_row = self.own_cols + 2
        self.patch = 3 * tiles * self.own_cols
        self.room = up_to(3 * self.per_row, 16)
        self.deep = up_to(self.features, 16)
        self.strips = self.chips * tiles * self.block

    def order(self, mask):
        return mask % self.group * self.chips + mask // self.group

    def layer(self, refs, k):
        at = k % self.chips * self.deep
        return refs[k // self.chips][at : at + self.features, :]

    def mask(self, k):
        return k % self.chips * self.group + k // self.chips


def prepare_kernel(p, fields_ref, diffusivity_ref, usable_ref, bias_ref, after_ref, out_ref, flat):
    flat[...] = jnp.zeros(flat.shape, jnp.float32)
    shape = (p.own_cols, p.along)
    row = lax.broadcasted_iota(jnp.int32, shape, 0)
    member = row == lax.broadcasted_iota(jnp.int32, shape, 1) // 4
    total = jnp.dot(
        member.astype(jnp.float32),
        fields_ref[0] + fields_ref[1] + fields_ref[2] + fields_ref[3],
        precision=lax.Precision.HIGHEST,
        preferred_element_type=jnp.float32,
    )
    flat[: p.own_cols, : p.features] = total * 0.0625
    at = p.own_cols
    high, middle, low = split_three(bias_ref[...].reshape(1, p.hidden))
    flat[at : at + 1, : p.hidden] = high
    flat[at : at + 1, p.flag_at : p.flag_at + p.hidden] = middle
    flat[at + 1 : at + 2, : p.hidden] = low
    flags = usable_ref[...].reshape(1, p.slots).astype(jnp.float32)
    flat[at + 1 : at + 2, p.flag_at : p.flag_at + p.slots] = flags
    for k, part in enumerate(split_three(diffusivity_ref[...])):
        flat[at + 2 : at + 2 + p.across, k * p.lane : k * p.lane + p.along] = part
    out_ref[...] = flat[...].astype(jnp.bfloat16)


def strip_of(p, tile, chan):
    other = chan ^ lax.axis_index("chan")
    return p.order(other) * p.tiles + (tile ^ lax.axis_index("tile"))


def index_kernel(p, cell_ref):
    t, c = lax.axis_index("tile"), lax.axis_index("chan")
    row = lax.broadcasted_iota(jnp.int32, cell_ref.shape, 0)
    reach = p.across + 4
    tile = (t + row // reach - 1 + p.tiles) % p.tiles
    cell = c * p.across - 2 + row % reach
    inside = (cell >= 0) & (cell < p.chans * p.across)
    cell = jnp.where(inside, cell, 0)
    wanted = strip_of(p, tile, cell // p.across) * p.block + p.own_cols + 2 + cell % p.across
    cell_ref[...] = jnp.where(inside, wanted, -1)


def place_kernel(p, owners_ref, place_ref, source_ref, *target_refs):
    t = lax.axis_index("tile")
    across = owners_ref[...]
    shape = (p.rows, p.rows)
    row = lax.broadcasted_iota(jnp.int32, shape, 0)
    other = lax.broadcasted_iota(jnp.int32, shape, 1)
    owner = jnp.sum(jnp.where(row == other, across, 0), axis=1, keepdims=True)
    first = lax.broadcasted_iota(jnp.int32, owner.shape, 0)
    begin = first // p.tile_cols * p.tile_cols
    same = (owner == across) & (other >= begin) & (other < row)
    rank = jnp.sum(jnp.where(same, 1, 0), axis=1, keepdims=True)
    tile = first // p.tile_cols
    place_ref[...] = (owner ^ t) * p.slots + tile * p.capacity + rank
    source_ref[...] = (
        strip_of(p, tile, first % p.tile_cols // p.own_cols) * p.block + first % p.own_cols
    )

    c = lax.axis_index("chan")
    target = lax.broadcasted_iota(jnp.int32, target_refs[0].shape, 0)
    chip, inner = target // p.patch, target % p.patch
    beside, inner = inner // (p.patch // 3) - 1, inner % (p.patch // 3)
    tile, along = inner // p.own_cols, inner % p.own_cols
    for k, target_ref in enumerate(target_refs):
        row = (chip ^ (c // p.group)) * p.group + (c % p.group ^ k) + beside
        wanted = tile * p.tile_cols + row * p.own_cols + along
        target_ref[...] = jnp.where((row >= 0) & (row < p.chans), wanted, -1)


def join_kernel(count, *refs):
    ins, out_ref = refs[:count], refs[-1]
    size = out_ref.shape[0] // count
    for k, ref in enumerate(ins):
        out_ref[k * size : (k + 1) * size, :] = ref[...]


def stack_kernel(p, *refs):
    for k, ref in enumerate(refs[: p.chips]):
        refs[-1][k * p.deep : k * p.deep + p.features, :] = ref[...]
        refs[-1][k * p.deep + p.features : (k + 1) * p.deep, :] = jnp.zeros(
            (p.deep - p.features, p.hidden), jnp.bfloat16
        )


def one_hot(wanted, first, count):
    source = lax.broadcasted_iota(jnp.int32, (wanted.shape[0], count), 1)
    return (source + first == wanted).astype(jnp.bfloat16)


def forward_kernel(p, *refs):
    refs = list(refs)
    take = lambda n: [refs.pop(0) for _ in range(n)]
    place_ref, source_ref, cell_ref, bias_ref, w_radiance_ref = take(5)
    strip_refs, weight_refs = take(p.group), take(p.group)
    radiance_ref, in_use_ref, preact_ref, kappa_ref, active = refs
    c = lax.axis_index("chan")
    gathered = [ref[...] for ref in strip_refs]
    columns = sum(
        dot(one_hot(source_ref[...], k * p.strips, p.strips), strips)
        for k, strips in enumerate(gathered)
    )
    columns = columns.astype(jnp.bfloat16)[:, : p.features]
    for k in range(p.chans):
        member, chip = k // p.chips, k % p.chips
        at = chip * p.tiles * p.block + p.own_cols
        low = strip_refs[member][at : at + 2, :].astype(jnp.float32)
        bias = (
            low[:1, : p.hidden]
            + low[:1, p.flag_at : p.flag_at + p.hidden]
            + low[1:, : p.hidden]
        )
        preact = dot(columns, p.layer(weight_refs, k)) + bias
        preact_ref[k] = preact
        at = pl.multiple_of((c ^ p.mask(k)) * p.hidden, p.hidden)
        active[:, pl.ds(at, p.hidden)] = (preact * jax.nn.sigmoid(preact)).astype(jnp.bfloat16)
    in_use = jnp.zeros((p.rows, 1), jnp.float32)
    for k in range(p.tiles):
        slot = lax.broadcasted_iota(jnp.int32, (p.rows, p.slots), 1) + k * p.slots
        low = k * p.block + p.own_cols + 1
        flags = strip_refs[0][low : low + 1, p.flag_at : p.flag_at + p.slots]
        flags = jnp.where(place_ref[...] == slot, flags.astype(jnp.float32), 0.0)
        in_use = in_use + jnp.sum(flags, axis=1, keepdims=True)
    in_use_ref[...] = in_use
    radiance_ref[...] = dot(active[...], w_radiance_ref[...]) + bias_ref[...].reshape(1, p.shard)
    parts = sum(
        dot(one_hot(cell_ref[...], k * p.strips, p.strips), strips)
        for k, strips in enumerate(gathered)
    )
    kappa_ref[...] = sum(parts[:, k * p.lane : (k + 1) * p.lane] for k in range(3))


def depart_kernel(p, radiance_ref, in_use_ref, place_ref, *refs):
    seen_refs, part_refs = refs[: -p.steps], refs[-p.steps :]
    part, count = p.rows // p.steps, seen_refs[0].shape[0]
    for j, part_ref in enumerate(part_refs):
        at = slice(j * part, (j + 1) * part)
        observed = sum(
            dot(one_hot(place_ref[at, :], k * count, count), ref[...])
            for k, ref in enumerate(seen_refs)
        )
        departure = (radiance_ref[at, :] - observed) * in_use_ref[at, :]
        part_ref[...] = departure.astype(jnp.bfloat16)


def slope_kernel(preact_ref, slope_ref):
    for k in range(preact_ref.shape[0]):
        preact = preact_ref[k]
        squash = jax.nn.sigmoid(preact)
        slope_ref[k] = (squash * (1.0 + preact * (1.0 - squash))).T


def choose_kernel(p, choices, *refs):
    refs, out_ref = refs[:-2], refs[-1]
    size = refs[0].shape[0]
    role = (lax.axis_index("chan") // p.group) ^ lax.axis_index("tile")
    for place in range(p.chips):

        @pl.when(role == place)
        def _():
            for j in range(p.steps):
                out_ref[j * size : (j + 1) * size, :] = refs[choices[place, j]][...]


def near_kernel(p, depart_ref, inv_cov_ref, out_ref):
    at = pl.multiple_of(lax.axis_index("chan") % p.group * p.shard, p.shard)
    out_ref[...] = dot(depart_ref[...], inv_cov_ref[pl.ds(at, p.shard), :])


def backward_kernel(p, *refs):
    refs = list(refs)
    take = lambda n: [refs.pop(0) for _ in range(n)]
    w_radiance_ref, inv_cov_ref, slope_ref, near_ref = take(4)
    depart_refs, weight_refs, target_refs = take(p.group - 1), take(p.group), take(p.group - 1)
    out_refs = refs
    c = lax.axis_index("chan")
    cotangent = near_ref[...]
    for k, ref in enumerate(depart_refs):
        at = pl.multiple_of((c % p.group ^ (k + 1)) * p.shard, p.shard)
        cotangent = cotangent + dot(ref[...], inv_cov_ref[pl.ds(at, p.shard), :])
    cotangent = cotangent.T.astype(jnp.bfloat16)
    total = jnp.zeros((p.features, p.rows), jnp.float32)
    for k in range(p.chans):
        at = pl.multiple_of((c ^ p.mask(k)) * p.hidden, p.hidden)
        grad_hidden = dot(w_radiance_ref[pl.ds(at, p.hidden), :], cotangent)
        grad_pre = (grad_hidden * slope_ref[k]).astype(jnp.bfloat16)
        total = total + dot(p.layer(weight_refs, k), grad_pre)
    total = total.astype(jnp.bfloat16)
    out_refs[0][...] = total
    for target_ref, out_ref in zip(target_refs, out_refs[1:]):
        out_ref[...] = dot_nt(one_hot(target_ref[...], 0, p.rows), total).astype(jnp.bfloat16)


def keep_kernel(total_ref, target_ref, out_ref):
    pick = one_hot(target_ref[...], 0, total_ref.shape[1])
    out_ref[...] = dot_nt(pick, total_ref[...]).astype(jnp.bfloat16)


def add(refs, at=slice(None)):
    total = refs[0][at, :].astype(jnp.float32)
    for ref in refs[1:]:
        total = total + ref[at, :].astype(jnp.float32)
    return total


def add_group_kernel(p, *refs):
    ins, outs = refs[: p.group], refs[p.group :]
    for k, out_ref in enumerate(outs):
        out_ref[...] = add(ins, slice(k * p.patch, (k + 1) * p.patch)).astype(jnp.bfloat16)


def add_chips_kernel(p, *refs):
    ins, outs = refs[: p.chips], refs[p.chips :]
    total = add(ins).astype(jnp.bfloat16)
    target = lax.broadcasted_iota(jnp.int32, (p.room, 1), 0)
    row, along = target // p.per_row, target % p.per_row - 1
    count = p.tiles * p.own_cols
    for k, out_ref in enumerate(outs):
        cell = ((lax.axis_index("tile") ^ k) * p.own_cols + along + count) % count
        wanted = jnp.where(row < 3, row * count + cell, -1)
        out_ref[...] = dot(one_hot(wanted, 0, p.patch), total).astype(jnp.bfloat16)


def diffuse_kernel(p, edge, *refs):
    ins, root_ref, out_ref = refs[: p.tiles], refs[-2], refs[-1]
    total = add(ins) * 0.0625
    length = p.along + 2 * edge
    shape = (length, p.room)
    cell = lax.broadcasted_iota(jnp.int32, shape, 0)
    source = lax.broadcasted_iota(jnp.int32, shape, 1)
    column = (cell - edge + 4) // 4
    spread = []
    terms = [term.astype(jnp.bfloat16) for term in split_three(total)]
    for k in range(3):
        pick = (source == column + k * p.per_row) & (column >= 0) & (column < p.per_row)
        spread.append(sum(dot(pick.astype(jnp.bfloat16), term) for term in terms))
    root = root_ref[...]
    state = [spread[(row + 2) // 4] for row in range(p.across + 4)]
    east_of = functools.partial(pltpu.roll, shift=length - 1, axis=0)
    west_of = functools.partial(pltpu.roll, shift=1, axis=0)
    north = root[:, :-1] * root[:, 1:]
    east, west = root * east_of(root), root * west_of(root)
    for sweep in range(2):
        fresh = list(state)
        for row in range(1 + sweep, p.across + 3 - sweep):
            here = state[row]
            fresh[row] = (
                here
                + north[:, row : row + 1] * (state[row + 1] - here)
                + north[:, row - 1 : row] * (state[row - 1] - here)
                + east[:, row : row + 1] * (east_of(here) - here)
                + west[:, row : row + 1] * (west_of(here) - here)
            )
        state = fresh
    for row in range(p.across):
        out_ref[row] = state[row + 2][edge : edge + p.along, : p.features]


def body_by_column(
    fields,
    diffusivity,
    owners,
    observed,
    usable,
    w_hidden,
    b_hidden,
    w_radiance,
    b_radiance,
    inv_cov,
):
    p = Plan(
        lax.axis_size("tile"),
        lax.axis_size("chan"),
        fields.shape,
        owners.shape,
        observed.shape,
        w_hidden.shape,
    )
    half, single = jnp.bfloat16, jnp.float32
    shape = jax.ShapeDtypeStruct
    both = ("tile", "chan")
    everyone = [(a, b) for a in range(p.tiles) for b in range(p.chans)]

    def flip(value, mask):
        return lax.ppermute(value, "chan", [(b, b ^ mask) for b in range(p.chans)])

    def trade(value, mask):
        return lax.ppermute(value, "tile", [(a, a ^ mask) for a in range(p.tiles)])

    def send(value, wanted):
        pairs = dict(wanted)
        pairs.update({target: source for source, target in wanted.items()})
        for a, b in everyone:
            if (a, b) not in pairs:
                pairs[a, b] = (a, b ^ 1)
        number = lambda place: place[0] * p.chans + place[1]
        return lax.ppermute(
            value, both, sorted((number(a), number(b)) for a, b in pairs.items())
        )

    def join(values, kernel_shape, after=()):
        return call(
            functools.partial(join_kernel, len(values)),
            shape(kernel_shape, half),
            [*values, *after],
            in_hbm=range(len(values), len(values) + len(after)),
        )

    def grow(value, over, after=()):
        return join([value, over(value)], (2 * value.shape[0],) + value.shape[1:], after)

    reach = p.across + 4
    cell = call(
        functools.partial(index_kernel, p),
        shape((3 * reach, 1), jnp.int32),
        [],
        flops=10**9,
    )

    strips = call(
        functools.partial(prepare_kernel, p),
        shape((p.block, p.width), half),
        [fields, diffusivity, usable, b_hidden, cell],
        in_hbm=[4],
        scratch=[pltpu.VMEM((p.block, p.width), single)],
    )
    seen, stages, before = observed, [], ()
    bit = 1
    while bit < p.tiles:
        if 2 * bit < p.tiles:
            seen = grow(seen, lambda value: trade(value, bit))
            before = [seen]
        strips = grow(strips, lambda value: trade(value, bit), before)
        before = ()
        stages.append(strips)
        bit *= 2
    strips = join(
        [strips] + [flip(strips, k * p.group) for k in range(1, p.chips)], (p.strips, p.width)
    )
    strips = [strips] + [flip(strips, k) for k in range(1, p.group)]

    near = [flip(w_hidden, chip * p.group) for chip in range(p.chips - 1, 0, -1)]
    near = [w_hidden] + near[::-1]
    near = call(
        functools.partial(stack_kernel, p),
        shape((p.chips * p.deep, p.hidden), half),
        near + [stages[-1]],
        in_hbm=[len(near)],
    )
    weights = [near] + [flip(near, k) for k in range(1, p.group)]

    far_half = p.tiles // 2
    seen = [
        seen,
        send(seen, {(b // p.group ^ far_half, b): (b // p.group, b) for b in range(p.chans)}),
    ]

    place, source, *targets = call(
        functools.partial(place_kernel, p),
        [shape((p.rows, 1), jnp.int32)] * 2
        + [shape((p.chips * p.patch, 1), jnp.int32)] * p.group,
        [owners.reshape(1, p.rows)],
        flops=SLACK_FLOPS,
    )
    radiance, in_use, preact, kappa = call(
        functools.partial(forward_kernel, p),
        [
            shape((p.rows, p.shard), single),
            shape((p.rows, 1), single),
            shape((p.chans, p.rows, p.hidden), single),
            shape((3 * reach, p.lane), single),
        ],
        [place, source, cell, b_radiance, w_radiance] + strips + weights,
        scratch=[pltpu.VMEM((p.rows, p.hidden * p.chans), half)],
        flops=FORWARD_FLOPS,
    )
    parts = call(
        functools.partial(depart_kernel, p),
        [shape((p.rows // p.steps, p.shard), half)] * p.steps,
        [radiance, in_use, place] + seen,
    )

    slope = call(
        slope_kernel,
        shape((p.chans, p.hidden, p.rows), single),
        [preact],
        flops=40 * preact.size,
    )

    pool, held, choices = list(parts), {}, {}
    for j in range(p.steps):
        held[0, j] = choices[0, j] = j
    for step in range(p.steps):
        for since in range(-1, step):
            for j in range(p.steps):
                order = [1 << (j + k) % p.steps for k in range(p.steps)]
                roles = [0] if since < 0 else [
                    order[since] + rest
                    for rest in range(p.chips)
                    if rest & ~sum(order[:since]) == 0
                ]
                wanted = {
                    (a, b): (a, b ^ order[step] * p.group)
                    for a, b in everyone
                    if (b // p.group ^ a) in roles
                }
                source = pool[choices[roles[0], j]]
                for role in roles:
                    choices[role + order[step], j] = len(pool)
                pool.append(send(source, wanted))
    chosen = call(
        functools.partial(choose_kernel, p, choices),
        shape((p.rows, p.shard), half),
        pool + [slope],
        in_hbm=[len(pool)],
    )
    depart = [flip(chosen, k) for k in range(1, p.group)]

    partial = call(
        functools.partial(near_kernel, p),
        shape((p.rows, p.shard), single),
        [chosen, inv_cov],
        flops=2 * p.rows * p.shard * p.shard,
    )
    partial = call(
        functools.partial(backward_kernel, p),
        [shape((p.features, p.rows), half)]
        + [shape((p.chips * p.patch, p.features), half)] * (p.group - 1),
        [w_radiance, inv_cov, slope, partial] + depart + weights + targets[1:],
        flops=2 * p.rows * (p.hidden * p.chans * (p.features + p.shard) + inv_cov.size),
    )
    kept = call(
        keep_kernel, shape((p.chips * p.patch, p.features), half), [partial[0], targets[0]]
    )
    partial = [kept] + [flip(partial[k], k) for k in range(1, p.group)]
    partial = call(
        functools.partial(add_group_kernel, p),
        [shape((p.patch, p.features), half)] * p.chips,
        partial,
    )
    partial = [flip(partial[k], k * p.group) for k in range(p.chips - 1, 0, -1)] + [partial[0]]
    partial = call(
        functools.partial(add_chips_kernel, p),
        [shape((p.room, p.features), half)] * p.tiles,
        partial,
    )
    partial = [trade(partial[k], k) for k in sorted(range(1, p.tiles), key=lambda k: -(k & -k))] + [partial[0]]
    edge = 8
    kappa = kappa.reshape(3, reach, p.lane)
    root = jnp.sqrt(
        jnp.concatenate(
            [kappa[0, :, p.along - edge : p.along], kappa[1, :, : p.along], kappa[2, :, :edge]],
            axis=1,
        ).T
    )
    return call(
        functools.partial(diffuse_kernel, p, edge),
        shape(fields.shape, single),
        partial + [root],
        flops=100 * fields.size,
    )


def solution(mesh):
    tiles, chans = mesh.shape["tile"], mesh.shape["chan"]
    by_column = tiles > 1 and chans % tiles == 0 and chans & (chans - 1) == 0 and chans > tiles
    placed = (
        P("chan", "tile", None),
        P("chan", "tile"),
        P(),
        P("tile", "chan"),
        P("tile"),
        P(None, "chan"),
        P("chan"),
        P(None, "chan"),
        P("chan"),
        P("tile", "chan"),
    )
    return jax.shard_map(
        body_by_column if by_column else body_by_owner,
        mesh=mesh,
        in_specs=placed,
        out_specs=P("chan", "tile", None),
        check_vma=False,
    )
```
